32 devices in a mesh: groups: 2 (over y), space: 4 (over x, core), tm: 4 (over z).
Axes of the slice: x: 2, y: 2, z: 4, core: 2. Of those that a mesh axis runs over, the one named last changes fastest.
Arguments:
- couplings: float32 [9, 4, 4, 2, 4, 96, 192], P(None, 'tm', 'space'), may hold values from -0.15625 to 0.15625
- source: float32 [4, 4, 2, 4, 96, 256], P('tm', 'space'), may hold values from -6 to 6
- initial: float32 [4, 4, 2, 4, 96, 256], P('tm', 'space'), may hold values from -6 to 6
- vectors: float32 [512, 4, 4, 2, 4, 192], P(None, 'tm', 'space'), may hold values from -0.0390625 to 0.0390625
- inverse_eigen: float32 [2, 512], replicated, may hold values from -20 to 20
Outputs:
- solution: float32 [8, 4, 2, 4, 96, 256], P(('groups', 'tm'), 'space'), parts along dimension 0
- residual: float32 [8, 4, 2, 4, 96, 256], P(('groups', 'tm'), 'space'), parts along dimension 0
The draws below stay inside these ranges and needn't reach their ends.
There are 2 independent parts, one for each index of `groups`. The reference program is written for one: setup_inputs(seed, part) draws one part's arguments, and reference() takes and returns one part's arrays. A program takes and returns all parts, laid end to end along the dimension named above; an argument that names none is the same for every part. Nothing has to cross between parts.
All inputs are finite; a program needn't handle non-finite values.
Results may differ from the reference program's by a relative error of at most 0.0001.
Values sent between devices are 32-bit elements; how exact they have to be, the bound alone decides.
No kernel may reach another device: no remote copies, remote signals or barrier semaphores. Data moves between devices by JAX's collectives and lax.ppermute only.
A program may use at most 64 MiB of HBM per device.

```python
import jax
import jax.numpy as jnp
from jax import lax

NC = 96
NR = 128
NV = 512
LX = 4
LY = 2
ITERS = 2
NZ = 4
NT = 4


def block_scale(rng, shape, cuts, smallest, top_value):
    level, own = 1.0, jax.random.fold_in(rng, 6)
    for dim, blocks in cuts:
        steps = jnp.exp(jax.random.uniform(jax.random.fold_in(own, dim), (blocks,), jnp.float32, smallest / len(cuts), top_value / len(cuts)))
        level = level * jnp.repeat(steps, shape[dim] // blocks).reshape([-1 if axis == dim else 1 for axis in range(len(shape))])
    return level


def bell_draw(rng, dims, deviation, most, split=(), dtype=jnp.bfloat16):
    gain = block_scale(rng, dims, split, -0.22, 0.18) if split else 1.0
    drawn = jax.random.normal(rng, dims, jnp.float32) * deviation * gain
    return jnp.minimum(jnp.maximum(drawn, -most), most).astype(dtype)


def setup_inputs(seed: int = 0, part: int = 0) -> dict:
    streams_of = jax.random.split(jax.random.key(seed), 6)
    couplings = bell_draw(streams_of[0], (9, NT, NZ, LY, LX, NC, 2 * NC), (18 * NC) ** -0.5, 0.15625, ((1, 4), (2, 4)), jnp.float32)
    source = bell_draw(streams_of[1], (NT, NZ, LY, LX, NC, 2 * NR), 1.0, 6.0, ((0, 4), (1, 4)), jnp.float32)
    initial = bell_draw(streams_of[2], (NT, NZ, LY, LX, NC, 2 * NR), 1.0, 6.0, ((0, 4), (1, 4)), jnp.float32)
    vectors = bell_draw(streams_of[3], (NV, NT, NZ, LY, LX, 2 * NC), (2 * NC * LX * LY * NZ * NT) ** -0.5, 0.0390625, ((1, 4), (2, 4)), jnp.float32)
    inverse_eigen = jnp.clip(jax.random.uniform(streams_of[4], (2, NV), jnp.float32, -20.0, 20.0), -20.0, 20.0)
    return {"couplings": couplings, "source": source, "initial": initial, "vectors": vectors, "inverse_eigen": inverse_eigen}


def coupled(matrix, spinor):
    middle = spinor.shape[-1] // 2
    turned = jnp.concatenate([-spinor[..., middle:], spinor[..., :middle]], axis=-1)
    stacked = jnp.concatenate([spinor, turned], axis=-2)
    return jnp.einsum("tzyxij,tzyxjn->tzyxin", matrix, stacked, precision=lax.Precision.HIGHEST)


def apply_operator(spinor, couplings):
    forward_t = jnp.roll(spinor, -1, 0)
    forward_t = forward_t.at[-1].multiply(-1.0)
    backward_t = jnp.roll(spinor, 1, 0)
    backward_t = backward_t.at[0].multiply(-1.0)
    neighbours = [spinor, jnp.roll(spinor, -1, 3), jnp.roll(spinor, 1, 3), jnp.roll(spinor, -1, 2), jnp.roll(spinor, 1, 2), jnp.roll(spinor, -1, 1), jnp.roll(spinor, 1, 1), forward_t, backward_t]
    summed = jnp.zeros_like(spinor)
    for direction in range(9):
        summed = summed + coupled(couplings[direction], neighbours[direction])
    return summed


def deflate(residual, vectors, inverse_eigen):
    middle = residual.shape[-1] // 2
    number = vectors.shape[0]
    negated = jnp.concatenate([residual[..., middle:], -residual[..., :middle]], axis=-1)
    stacked = jnp.concatenate([residual, negated], axis=-2)
    coefficients = jnp.dot(vectors.reshape(number, -1), stacked.reshape(-1, stacked.shape[-1]), precision=lax.Precision.HIGHEST, preferred_element_type=jnp.float32)
    eigen_real = inverse_eigen[0][:, None]
    eigen_imag = inverse_eigen[1][:, None]
    coef_real = coefficients[:, :middle]
    coef_imag = coefficients[:, middle:]
    scaled_real = eigen_real * coef_real - eigen_imag * coef_imag
    scaled_imag = eigen_real * coef_imag + eigen_imag * coef_real
    dstack = jnp.stack([jnp.concatenate([scaled_real, scaled_imag], axis=-1), jnp.concatenate([-scaled_imag, scaled_real], axis=-1)])
    halves = vectors.reshape(vectors.shape[:-1] + (2, vectors.shape[-1] // 2))
    return jnp.einsum("ktzyxci,ckn->tzyxin", halves, dstack, precision=lax.Precision.HIGHEST)


def reference(couplings, source, initial, vectors, inverse_eigen):
    iterate = initial
    residual = source
    for sweep in range(ITERS):
        residual = source - apply_operator(iterate, couplings)
        iterate = iterate + deflate(residual, vectors, inverse_eigen) + 0.5 * residual
    return iterate, residual
```

```python
import functools

import jax
import jax.numpy as jnp
from jax import lax
from jax.experimental import pallas as pl
from jax.experimental.pallas import tpu as pltpu
from jax.sharding import PartitionSpec as P

ITERS = 2
F32 = jnp.float32
BF16 = jnp.bfloat16
VMEM_LIMIT = 48 * 1024 * 1024
LOCAL = 5


def params():
    return pltpu.CompilerParams(vmem_limit_bytes=VMEM_LIMIT)


def cost(flops, read):
    return pl.CostEstimate(flops=int(flops), bytes_accessed=int(read), transcendentals=0)


def low_lanes(value):
    lanes = lax.broadcasted_iota(jnp.int32, value.shape, value.ndim - 1)
    return lanes < value.shape[-1] // 2


def swap(value):
    return pltpu.roll(value, value.shape[-1] // 2, value.ndim - 1)


def turned(value):
    moved = swap(value)
    return jnp.where(low_lanes(value), -moved, moved)


def high_low(value):
    high = value.astype(BF16)
    low = (value - high.astype(F32)).astype(BF16)
    return high, low


def stack(value, sign):
    high, low = high_low(jnp.concatenate([value, sign * turned(value)], axis=0))
    return jnp.concatenate([high, low], axis=1)


def matmul(left, right):
    return jnp.dot(left, right, preferred_element_type=F32)


def fold(product):
    rows, lanes = product.shape[0] // 2, product.shape[1] // 2
    high = product[:rows, :lanes] + (product[:rows, lanes:] + product[rows:, :lanes])
    return high + product[rows:, lanes:]


def pick_half(value, group):
    middle = value.shape[-1] // 2
    real, imag = value[:, :middle], value[:, middle:]
    low = low_lanes(real)
    first = jnp.where(low, real, swap(imag))
    second = jnp.where(low, swap(real), imag)
    return jnp.where(group == 0, first, second)


def join_halves(own, other, group):
    first = jnp.where(group == 0, own, other)
    second = jnp.where(group == 0, other, own)
    low = low_lanes(own)
    real = jnp.where(low, first, swap(second))
    imag = jnp.where(low, swap(first), second)
    return jnp.concatenate([real, imag], axis=1)


def pack_kernel(place, full, half):
    for site in range(full.shape[0]):
        half[site] = pick_half(full[site], place[0])


def pack(place, full):
    sites, rows, lanes = full.shape
    return pl.pallas_call(
        pack_kernel,
        out_shape=jax.ShapeDtypeStruct((sites, rows, lanes // 2), F32),
        in_specs=[pl.BlockSpec(memory_space=pltpu.SMEM), pl.BlockSpec(memory_space=pltpu.VMEM)],
        out_specs=pl.BlockSpec(memory_space=pltpu.VMEM),
        compiler_params=params(),
        name="pack",
    )(place, full)


def around(site, ny, nx):
    y, x = site // nx, lax.rem(site, nx)
    right, left = lax.rem(x + 1, nx), lax.rem(x + nx - 1, nx)
    up, down = lax.rem(y + 1, ny), lax.rem(y + ny - 1, ny)
    return (site, y * nx + right, y * nx + left, up * nx + x, down * nx + x)


def local_sum(site, ny, nx, x_ref, stacks, matrix):
    @pl.when(site == 0)
    def _():
        for each in range(ny * nx):
            stacks[each] = stack(x_ref[each], 1.0)

    total = None
    for direction, neighbour in enumerate(around(site, ny, nx)):
        term = matmul(matrix(direction), stacks[neighbour])
        total = term if total is None else total + term
    return fold(total)


def first_kernel(ny, nx, place, x_ref, source, couplings, rest, half_source, local, halo, stacks):
    site = pl.program_id(0)
    own = pick_half(source[0], place[0])
    half_source[0] = own
    for direction in range(couplings.shape[0]):
        high, low = high_low(couplings[direction, 0])
        both = jnp.concatenate([high, low], axis=0)
        if direction < LOCAL:
            local[direction, 0] = both
        else:
            halo[direction - LOCAL, 0] = both
    rest[0] = own - local_sum(site, ny, nx, x_ref, stacks, lambda d: local[d, 0])


def first_local(place, x, source, couplings, ny, nx):
    sites, rows, lanes = x.shape
    directions, _, _, columns = couplings.shape
    outer = directions - LOCAL
    return pl.pallas_call(
        functools.partial(first_kernel, ny, nx),
        grid=(sites,),
        out_shape=(
            jax.ShapeDtypeStruct(x.shape, F32),
            jax.ShapeDtypeStruct(x.shape, F32),
            jax.ShapeDtypeStruct((LOCAL, sites, 2 * rows, columns), BF16),
            jax.ShapeDtypeStruct((outer, sites, 2 * rows, columns), BF16),
        ),
        in_specs=[
            pl.BlockSpec(memory_space=pltpu.SMEM),
            pl.BlockSpec((sites, rows, lanes), lambda s: (0, 0, 0)),
            pl.BlockSpec((1, rows, 2 * lanes), lambda s: (s, 0, 0)),
            pl.BlockSpec((directions, 1, rows, columns), lambda s: (0, s, 0, 0)),
        ],
        out_specs=(
            pl.BlockSpec((1, rows, lanes), lambda s: (s, 0, 0)),
            pl.BlockSpec((1, rows, lanes), lambda s: (s, 0, 0)),
            pl.BlockSpec((LOCAL, 1, 2 * rows, columns), lambda s: (0, s, 0, 0)),
            pl.BlockSpec((outer, 1, 2 * rows, columns), lambda s: (0, s, 0, 0)),
        ),
        scratch_shapes=[pltpu.VMEM((sites, 2 * rows, 2 * lanes), BF16)],
        compiler_params=params(),
        cost_estimate=cost(8e9, 16e6),
        name="first_local",
    )(place, x, source, couplings)


def local_kernel(ny, nx, x_ref, source, local, rest, stacks):
    site = pl.program_id(0)
    rest[0] = source[0] - local_sum(site, ny, nx, x_ref, stacks, lambda d: local[d, 0])


def local_part(x, source, local, ny, nx):
    sites, rows, lanes = x.shape
    columns = local.shape[-1]
    return pl.pallas_call(
        functools.partial(local_kernel, ny, nx),
        grid=(sites,),
        out_shape=jax.ShapeDtypeStruct(x.shape, F32),
        in_specs=[
            pl.BlockSpec((sites, rows, lanes), lambda s: (0, 0, 0)),
            pl.BlockSpec((1, rows, lanes), lambda s: (s, 0, 0)),
            pl.BlockSpec((LOCAL, 1, 2 * rows, columns), lambda s: (0, s, 0, 0)),
        ],
        out_specs=pl.BlockSpec((1, rows, lanes), lambda s: (s, 0, 0)),
        scratch_shapes=[pltpu.VMEM((sites, 2 * rows, 2 * lanes), BF16)],
        compiler_params=params(),
        cost_estimate=cost(8e9, 8e6),
        name="local_part",
    )(x, source, local)


def vectors_kernel(blocks, place, vectors, rows_out, columns_out, ordered):
    sites = rows_out.shape[0]
    rows = vectors.shape[1] // sites // 2
    size = vectors.shape[0] // blocks
    step = pl.program_id(0)

    @pl.when(step == 0)
    def _():
        for index in range(blocks):
            start = pl.multiple_of(place[1 + index] * size, size)
            ordered[index * size : (index + 1) * size] = vectors[pl.ds(start, size)]

    taken = rows_out.shape[2]
    part = ordered[pl.ds(pl.multiple_of(step * taken, taken), taken)]
    high, low = high_low(part)
    for site in range(sites):
        at = slice(site * 2 * rows, (site + 1) * 2 * rows)
        rows_out[site, 0] = high[:, at]
        rows_out[site, 1] = low[:, at]
    across = part.T
    for site in range(sites):
        for half in range(2):
            start = (2 * site + half) * rows
            high, low = high_low(across[start : start + rows])
            columns_out[0, site, half] = high
            columns_out[1, site, half] = low


def vectors_parts(place, vectors, blocks, sites):
    number, width = vectors.shape
    size = 128
    rows = width // sites // 2
    return pl.pallas_call(
        functools.partial(vectors_kernel, blocks),
        grid=(number // size,),
        out_shape=(
            jax.ShapeDtypeStruct((sites, 2, number, 2 * rows), BF16),
            jax.ShapeDtypeStruct((2, sites, 2, rows, number), BF16),
        ),
        in_specs=[
            pl.BlockSpec(memory_space=pltpu.SMEM),
            pl.BlockSpec((number, width), lambda b: (0, 0)),
        ],
        out_specs=(
            pl.BlockSpec((sites, 2, size, 2 * rows), lambda b: (0, 0, b, 0)),
            pl.BlockSpec((2, sites, 2, rows, size), lambda b: (0, 0, 0, 0, b)),
        ),
        scratch_shapes=[pltpu.VMEM((number, width), F32)],
        compiler_params=params(),
        cost_estimate=cost(1e9, 16e6),
        name="vectors_parts",
    )(place, vectors)


def halo_kernel(signs, rest, forward_z, backward_z, forward_t, backward_t, halo, vectors, residual, keep, send, total):
    site = pl.program_id(0)
    number, lanes = total.shape[0] // 2, total.shape[1] // 2
    fields = (forward_z[0], backward_z[0], signs[0] * forward_t[0], signs[1] * backward_t[0])
    summed = None
    for direction, field in enumerate(fields):
        term = matmul(halo[direction, 0], stack(field, 1.0))
        summed = term if summed is None else summed + term
    own = rest[0] - fold(summed)
    residual[0] = own
    rows = vectors.shape[3]
    left = vectors[0].reshape(2 * number, rows)
    product = matmul(left, stack(own, -1.0))

    @pl.when(site == 0)
    def _():
        total[...] = product

    @pl.when(site > 0)
    def _():
        total[...] += product

    @pl.when(site == pl.num_programs(0) - 1)
    def _():
        half = number // 2
        whole = fold(total[...])
        keep[...] = whole[:half]
        send[...] = whole[half:]


def halo_part(signs, rest, faces, halo, vectors):
    sites, rows, lanes = rest.shape
    outer, _, _, columns = halo.shape
    number = vectors.shape[2]
    field = pl.BlockSpec((1, rows, lanes), lambda s: (s, 0, 0))
    part = jax.ShapeDtypeStruct((number // 2, lanes), F32)
    whole = pl.BlockSpec((number // 2, lanes), lambda s: (0, 0))
    return pl.pallas_call(
        halo_kernel,
        grid=(sites,),
        out_shape=(jax.ShapeDtypeStruct(rest.shape, F32), part, part),
        in_specs=[
            pl.BlockSpec(memory_space=pltpu.SMEM),
            field,
            field,
            field,
            field,
            field,
            pl.BlockSpec((outer, 1, 2 * rows, columns), lambda s: (0, s, 0, 0)),
            pl.BlockSpec((1, 2, number, 2 * rows), lambda s: (s, 0, 0, 0)),
        ],
        out_specs=(field, whole, whole),
        scratch_shapes=[pltpu.VMEM((2 * number, 2 * lanes), F32)],
        compiler_params=params(),
        cost_estimate=cost(1e9, 8e6),
        name="halo_part",
    )(signs, rest, *faces, halo, vectors)


def scale_kernel(eigen, *refs):
    parts, out = refs[:-1], refs[-1]
    total = parts[0][...]
    for part in parts[1:]:
        total = total + part[...]
    out[...] = eigen[:, 0:1] * total + eigen[:, 1:2] * turned(total)


def scale(eigen, parts):
    return pl.pallas_call(
        scale_kernel,
        out_shape=jax.ShapeDtypeStruct(parts[0].shape, F32),
        compiler_params=params(),
        name="scale",
    )(eigen, *parts)


def update_kernel(x, residual, d, vectors, out, stacks):
    @pl.when(pl.program_id(0) == 0)
    def _():
        stacks[...] = stack(d[...], 1.0)

    rows = vectors.shape[3]
    number = vectors.shape[4]
    for site in range(vectors.shape[1]):
        total = None
        for half in range(2):
            left = vectors[:, site, half].reshape(2 * rows, number)
            term = matmul(left, stacks[half * number : (half + 1) * number, :])
            total = term if total is None else total + term
        out[site] = x[site] + 0.5 * residual[site] + fold(total)


def update(x, residual, d, vectors):
    sites, rows, lanes = x.shape
    number = vectors.shape[-1]
    step = 2
    field = pl.BlockSpec((step, rows, lanes), lambda s: (s, 0, 0))
    return pl.pallas_call(
        update_kernel,
        grid=(sites // step,),
        out_shape=jax.ShapeDtypeStruct(x.shape, F32),
        in_specs=[
            field,
            field,
            pl.BlockSpec((number, lanes), lambda s: (0, 0)),
            pl.BlockSpec((2, step, 2, rows, number), lambda s: (0, s, 0, 0, 0)),
        ],
        out_specs=field,
        scratch_shapes=[pltpu.VMEM((2 * number, 2 * lanes), BF16)],
        compiler_params=params(),
        cost_estimate=cost(1e9, 8e6),
        name="update",
    )(x, residual, d, vectors)


def join_kernel(place, x, other_x, residual, other_residual, base, full):
    own = x[0] + 0.5 * residual[0]
    other = other_x[0] + 0.5 * other_residual[0]
    base[0] = join_halves(own, other, place[0])
    full[0] = join_halves(residual[0], other_residual[0], place[0])


def join(place, x, other_x, residual, other_residual):
    sites, rows, lanes = x.shape
    field = pl.BlockSpec((1, rows, lanes), lambda s: (s, 0, 0))
    wide = pl.BlockSpec((1, rows, 2 * lanes), lambda s: (s, 0, 0))
    shape = jax.ShapeDtypeStruct((sites, rows, 2 * lanes), F32)
    return pl.pallas_call(
        join_kernel,
        grid=(sites,),
        out_shape=(shape, shape),
        in_specs=[pl.BlockSpec(memory_space=pltpu.SMEM), field, field, field, field],
        out_specs=(wide, wide),
        compiler_params=params(),
        cost_estimate=cost(1e6, 4e6),
        name="join",
    )(place, x, other_x, residual, other_residual)


def final_kernel(place, base, d, other_d, vectors, out, stacks):
    @pl.when(pl.program_id(0) == 0)
    def _():
        whole = join_halves(d[...], other_d[...], place[0])
        stacks[...] = stack(whole, 1.0)

    rows = vectors.shape[3]
    number = vectors.shape[4]
    for site in range(vectors.shape[1]):
        total = None
        for half in range(2):
            left = vectors[:, site, half].reshape(2 * rows, number)
            term = matmul(left, stacks[half * number : (half + 1) * number, :])
            total = term if total is None else total + term
        out[site] = base[site] + fold(total)


def final(place, base, d, other_d, vectors):
    sites, rows, lanes = base.shape
    number = vectors.shape[-1]
    step = 2
    field = pl.BlockSpec((step, rows, lanes), lambda s: (s, 0, 0))
    small = pl.BlockSpec((number, lanes // 2), lambda s: (0, 0))
    return pl.pallas_call(
        final_kernel,
        grid=(sites // step,),
        out_shape=jax.ShapeDtypeStruct(base.shape, F32),
        in_specs=[
            pl.BlockSpec(memory_space=pltpu.SMEM),
            field,
            small,
            small,
            pl.BlockSpec((2, step, 2, rows, number), lambda s: (0, s, 0, 0, 0)),
        ],
        out_specs=field,
        scratch_shapes=[pltpu.VMEM((2 * number, 2 * lanes), BF16)],
        compiler_params=params(),
        cost_estimate=cost(2e9, 8e6),
        name="final",
    )(place, base, d, other_d, vectors)


def shifted(value, axis, step):
    count = lax.axis_size(axis)
    return lax.ppermute(value, axis, [(i, (i + step) % count) for i in range(count)])


def crossed(value, axis, mask):
    count = lax.axis_size(axis)
    return lax.ppermute(value, axis, [(i, i ^ mask) for i in range(count)])


def faces_of(x):
    backward_t = shifted(x, "tm", 1)
    forward_t = shifted(x, "tm", -1)
    backward_z = shifted(x, "space", 1)
    forward_z = shifted(x, "space", -1)
    return forward_z, backward_z, forward_t, backward_t


def halving(keep, send):
    count = lax.axis_size("space")
    mask = 1
    while mask < count:
        part = keep + crossed(send, "space", mask)
        mask *= 2
        middle = part.shape[0] // 2
        keep, send = part[:middle], part[middle:]
    return part


def doubling(part):
    mask = lax.axis_size("space") // 2
    while mask:
        part = jnp.concatenate([part, crossed(part, "space", mask)], axis=0)
        mask //= 2
    return part


def over_time(part):
    count = lax.axis_size("tm")
    if count <= 4:
        return [part] + [shifted(part, "tm", step) for step in range(1, count)]
    mask = 1
    while mask < count:
        part = part + crossed(part, "tm", mask)
        mask *= 2
    return [part]


def block_order(count):
    bits = count.bit_length() - 1
    return [int(format(index, "b").zfill(bits)[::-1], 2) if bits else 0 for index in range(count)]


def shards(couplings, source, initial, vectors, inverse_eigen):
    directions = couplings.shape[0]
    ny, nx, rows, lanes = source.shape[2:]
    sites = ny * nx
    number = vectors.shape[0]
    width = vectors.shape[-1]
    group, space, time = (lax.axis_index(name) for name in ("groups", "space", "tm"))
    blocks, slices = lax.axis_size("space"), lax.axis_size("tm")

    order = jnp.array(block_order(blocks), jnp.int32) ^ space
    place = jnp.concatenate([jnp.full((1,), group, jnp.int32), order])
    signs = jnp.stack([jnp.where(time == slices - 1, -1.0, 1.0), jnp.where(time == 0, -1.0, 1.0)]).astype(F32)
    size = number // blocks
    eigen = lax.dynamic_slice_in_dim(inverse_eigen, space * size, size, 1).T

    x = pack(place, initial.reshape(sites, rows, lanes))
    faces = faces_of(x)
    matrices = couplings.reshape(directions, sites, rows, couplings.shape[-1])
    rest, half_source, local, halo = first_local(place, x, source.reshape(sites, rows, lanes), matrices, ny, nx)
    by_rows, by_columns = vectors_parts(place, vectors.reshape(number, sites * width), blocks, sites)

    for sweep in range(ITERS):
        if sweep:
            faces = faces_of(x)
            rest = local_part(x, half_source, local, ny, nx)
        residual, keep, send = halo_part(signs, rest, faces, halo, by_rows)
        part = halving(keep, send)
        d = scale(eigen, over_time(part))
        if sweep < ITERS - 1:
            x = update(x, residual, doubling(d), by_columns)
    other_x = crossed(x, "groups", 1)
    other_residual = crossed(residual, "groups", 1)
    other_d = crossed(d, "groups", 1)
    base, full_residual = join(place, x, other_x, residual, other_residual)
    whole = final(place, base, doubling(d), doubling(other_d), by_columns)
    shape = source.shape
    return whole.reshape(shape), full_residual.reshape(shape)


def solution(mesh):
    in_specs = (
        P(None, "tm", "space", None, None, None, None),
        P("tm", "space", None, None, None, None),
        P("tm", "space", None, None, None, None),
        P(None, "tm", "space", None, None, None),
        P(),
    )
    out_specs = (
        P(("groups", "tm"), "space", None, None, None, None),
        P(("groups", "tm"), "space", None, None, None, None),
    )
    return jax.shard_map(shards, mesh=mesh, in_specs=in_specs, out_specs=out_specs, check_vma=False)
```

```python
import functools

import jax
import jax.numpy as jnp
from jax import lax
from jax.experimental import pallas as pl
from jax.experimental.pallas import tpu as pltpu
from jax.sharding import PartitionSpec as P

ITERS = 2
F32 = jnp.float32
BF16 = jnp.bfloat16
LOCAL = 5


def params(mebibytes=12):
    return pltpu.CompilerParams(vmem_limit_bytes=mebibytes * 1024 * 1024)


def cost(flops, read):
    return pl.CostEstimate(flops=int(flops), bytes_accessed=int(read), transcendentals=0)


def low_lanes(value):
    lanes = lax.broadcasted_iota(jnp.int32, value.shape, value.ndim - 1)
    return lanes < value.shape[-1] // 2


def swap(value):
    return pltpu.roll(value, value.shape[-1] // 2, value.ndim - 1)


def turned(value):
    moved = swap(value)
    return jnp.where(low_lanes(value), -moved, moved)


def high_low(value):
    high = value.astype(BF16)
    low = (value - high.astype(F32)).astype(BF16)
    return high, low


def stack(value, sign):
    high, low = high_low(jnp.concatenate([value, sign * turned(value)], axis=0))
    return jnp.concatenate([high, low], axis=1)


def matmul(left, right):
    return jnp.dot(left, right, preferred_element_type=F32)


def fold(product):
    rows, lanes = product.shape[0] // 2, product.shape[1] // 2
    high = product[:rows, :lanes] + (product[:rows, lanes:] + product[rows:, :lanes])
    return high + product[rows:, lanes:]


def pick_half(value, group):
    middle = value.shape[-1] // 2
    real, imag = value[:, :middle], value[:, middle:]
    low = low_lanes(real)
    first = jnp.where(low, real, swap(imag))
    second = jnp.where(low, swap(real), imag)
    return jnp.where(group == 0, first, second)


def join_halves(own, other, group):
    first = jnp.where(group == 0, own, other)
    second = jnp.where(group == 0, other, own)
    low = low_lanes(own)
    real = jnp.where(low, first, swap(second))
    imag = jnp.where(low, swap(first), second)
    return jnp.concatenate([real, imag], axis=1)


def vmem(count):
    return [pl.BlockSpec(memory_space=pltpu.VMEM)] * count


def pack_kernel(full, half):
    group = lax.axis_index("groups")
    for site in range(full.shape[0]):
        half[site] = pick_half(full[site], group)


def pack(full):
    sites, rows, lanes = full.shape
    step = 2
    return pl.pallas_call(
        pack_kernel,
        grid=(sites // step,),
        out_shape=jax.ShapeDtypeStruct((sites, rows, lanes // 2), F32),
        in_specs=[pl.BlockSpec((step, rows, lanes), lambda s: (s, 0, 0))],
        out_specs=pl.BlockSpec((step, rows, lanes // 2), lambda s: (s, 0, 0)),
        compiler_params=params(),
        cost_estimate=cost(1e6, 1e6),
        name="pack",
    )(full)


def around(site, ny, nx):
    y, x = site // nx, lax.rem(site, nx)
    right, left = lax.rem(x + 1, nx), lax.rem(x + nx - 1, nx)
    up, down = lax.rem(y + 1, ny), lax.rem(y + ny - 1, ny)
    return (site, y * nx + right, y * nx + left, up * nx + x, down * nx + x)


def local_sum(site, ny, nx, x_ref, stacks, matrix):
    @pl.when(site == 0)
    def _():
        for each in range(ny * nx):
            stacks[each] = stack(x_ref[each], 1.0)

    total = None
    for direction, neighbour in enumerate(around(site, ny, nx)):
        term = matmul(matrix(direction), stacks[neighbour])
        total = term if total is None else total + term
    return fold(total)


def first_kernel(ny, nx, x_ref, source, couplings, rest, half_source, local, halo, stacks):
    site = pl.program_id(0)
    own = pick_half(source[0], lax.axis_index("groups"))
    half_source[0] = own
    for direction in range(couplings.shape[0]):
        high, low = high_low(couplings[direction, 0])
        both = jnp.concatenate([high, low], axis=0)
        if direction < LOCAL:
            local[direction, 0] = both
        else:
            halo[direction - LOCAL, 0] = both
    rest[0] = own - local_sum(site, ny, nx, x_ref, stacks, lambda d: local[d, 0])


def first_local(x, source, couplings, ny, nx):
    sites, rows, lanes = x.shape
    directions, _, _, columns = couplings.shape
    outer = directions - LOCAL
    return pl.pallas_call(
        functools.partial(first_kernel, ny, nx),
        grid=(sites,),
        out_shape=(
            jax.ShapeDtypeStruct(x.shape, F32),
            jax.ShapeDtypeStruct(x.shape, F32),
            jax.ShapeDtypeStruct((LOCAL, sites, 2 * rows, columns), BF16),
            jax.ShapeDtypeStruct((outer, sites, 2 * rows, columns), BF16),
        ),
        in_specs=[
            pl.BlockSpec((sites, rows, lanes), lambda s: (0, 0, 0)),
            pl.BlockSpec((1, rows, 2 * lanes), lambda s: (s, 0, 0)),
            pl.BlockSpec((directions, 1, rows, columns), lambda s: (0, s, 0, 0)),
        ],
        out_specs=(
            pl.BlockSpec((1, rows, lanes), lambda s: (s, 0, 0)),
            pl.BlockSpec((1, rows, lanes), lambda s: (s, 0, 0)),
            pl.BlockSpec((LOCAL, 1, 2 * rows, columns), lambda s: (0, s, 0, 0)),
            pl.BlockSpec((outer, 1, 2 * rows, columns), lambda s: (0, s, 0, 0)),
        ),
        scratch_shapes=[pltpu.VMEM((sites, 2 * rows, 2 * lanes), BF16)],
        compiler_params=params(),
        cost_estimate=cost(8e9, 16e6),
        name="first_local",
    )(x, source, couplings)


def local_kernel(ny, nx, x_ref, source, local, rest, stacks):
    site = pl.program_id(0)
    rest[0] = source[0] - local_sum(site, ny, nx, x_ref, stacks, lambda d: local[d, 0])


def local_part(x, source, local, ny, nx):
    sites, rows, lanes = x.shape
    columns = local.shape[-1]
    return pl.pallas_call(
        functools.partial(local_kernel, ny, nx),
        grid=(sites,),
        out_shape=jax.ShapeDtypeStruct(x.shape, F32),
        in_specs=[
            pl.BlockSpec((sites, rows, lanes), lambda s: (0, 0, 0)),
            pl.BlockSpec((1, rows, lanes), lambda s: (s, 0, 0)),
            pl.BlockSpec((LOCAL, 1, 2 * rows, columns), lambda s: (0, s, 0, 0)),
        ],
        out_specs=pl.BlockSpec((1, rows, lanes), lambda s: (s, 0, 0)),
        scratch_shapes=[pltpu.VMEM((sites, 2 * rows, 2 * lanes), BF16)],
        compiler_params=params(),
        cost_estimate=cost(8e9, 8e6),
        name="local_part",
    )(x, source, local)


def block_order(count):
    bits = count.bit_length() - 1
    return [int(format(index, "b").zfill(bits)[::-1], 2) if bits else 0 for index in range(count)]


def ordered_rows(vectors, chunk, taken):
    blocks = lax.axis_size("space")
    space = lax.axis_index("space")
    size = vectors.shape[0] // blocks
    unit = min(size, taken)
    parts = []
    for start in range(chunk * taken, (chunk + 1) * taken, unit):
        block = space ^ block_order(blocks)[start // size]
        parts.append(vectors[pl.ds(pl.multiple_of(block * size + start % size, unit), unit)])
    return parts[0] if len(parts) == 1 else jnp.concatenate(parts, axis=0)


def by_rows_kernel(vectors, out):
    taken = 128
    number = vectors.shape[0]
    for chunk in range(number // taken):
        high, low = high_low(ordered_rows(vectors, chunk, taken))
        out[chunk * taken : (chunk + 1) * taken] = high
        out[number + chunk * taken : number + (chunk + 1) * taken] = low


def by_rows_of(vectors):
    number, width = vectors.shape
    return pl.pallas_call(
        by_rows_kernel,
        out_shape=jax.ShapeDtypeStruct((2 * number, width), BF16),
        in_specs=vmem(1),
        out_specs=vmem(1)[0],
        compiler_params=params(),
        cost_estimate=cost(1e6, 6e6),
        name="by_rows",
    )(vectors)


def by_columns_kernel(vectors, out):
    taken = 128
    sites, rows = out.shape[0], out.shape[2] // 2
    for chunk in range(vectors.shape[0] // taken):
        across = ordered_rows(vectors, chunk, taken).T
        at = slice(chunk * taken, (chunk + 1) * taken)
        for site in range(sites):
            for half in range(2):
                start = (2 * site + half) * rows
                high, low = high_low(across[start : start + rows])
                out[site, half, :rows, at] = high
                out[site, half, rows:, at] = low


def by_columns_of(vectors, sites):
    number, width = vectors.shape
    rows = width // sites // 2
    return pl.pallas_call(
        by_columns_kernel,
        out_shape=jax.ShapeDtypeStruct((sites, 2, 2 * rows, number), BF16),
        in_specs=vmem(1),
        out_specs=vmem(1)[0],
        compiler_params=params(),
        cost_estimate=cost(1e6, 6e6),
        name="by_columns",
    )(vectors)


def apply_faces(site, faces, matrices):
    summed = None
    for face, matrix in zip(faces, matrices):
        term = matmul(matrix[site], stack(face(site), 1.0))
        summed = term if summed is None else summed + term
    return fold(summed)


def z_faces_kernel(rest, forward, backward, matrix, out):
    faces = (lambda s: forward[s], lambda s: backward[s])
    for site in range(rest.shape[0]):
        out[site] = rest[site] - apply_faces(site, faces, (matrix.at[0], matrix.at[1]))


def z_faces(rest, forward, backward, matrix):
    return pl.pallas_call(
        z_faces_kernel,
        out_shape=jax.ShapeDtypeStruct(rest.shape, F32),
        in_specs=vmem(4),
        out_specs=vmem(1)[0],
        compiler_params=params(),
        cost_estimate=cost(1e9, 4e6),
        name="z_faces",
    )(rest, forward, backward, matrix)


def edge_sign(last):
    count = lax.axis_size("tm")
    return jnp.where(lax.axis_index("tm") == (count - 1 if last else 0), -1.0, 1.0).astype(F32)


def backward_kernel(rest, backward, matrix, out):
    sign = edge_sign(False)
    for site in range(rest.shape[0]):
        out[site] = rest[site] - apply_faces(site, (lambda s: sign * backward[s],), (matrix.at[3],))


def backward_face(rest, backward, matrix):
    return pl.pallas_call(
        backward_kernel,
        out_shape=jax.ShapeDtypeStruct(rest.shape, F32),
        in_specs=vmem(3),
        out_specs=vmem(1)[0],
        compiler_params=params(),
        cost_estimate=cost(1e9, 4e6),
        name="backward_face",
    )(rest, backward, matrix)


def forward_kernel(rest, forward, matrix, vectors, residual, keep, send, stacks):
    sign = edge_sign(True)
    rows = 2 * rest.shape[1]
    for site in range(rest.shape[0]):
        own = rest[site] - apply_faces(site, (lambda s: sign * forward[s],), (matrix.at[2],))
        residual[site] = own
        stacks[site * rows : (site + 1) * rows] = stack(own, -1.0)
    whole = fold(matmul(vectors[...], stacks[...]))
    half = whole.shape[0] // 2
    keep[...] = whole[:half]
    send[...] = whole[half:]


def forward_face(rest, forward, matrix, vectors):
    sites, rows, lanes = rest.shape
    part = jax.ShapeDtypeStruct((vectors.shape[0] // 4, lanes), F32)
    return pl.pallas_call(
        forward_kernel,
        out_shape=(jax.ShapeDtypeStruct(rest.shape, F32), part, part),
        in_specs=vmem(4),
        out_specs=tuple(vmem(3)),
        scratch_shapes=[pltpu.VMEM((sites * 2 * rows, 2 * lanes), BF16)],
        compiler_params=params(),
        cost_estimate=cost(2e9, 8e6),
        name="forward_face",
    )(rest, forward, matrix, vectors)


def split_kernel(keep, received, next_keep, next_send):
    half = next_keep.shape[0]
    next_keep[...] = keep[:half] + received[:half]
    next_send[...] = keep[half:] + received[half:]


def add_split(keep, received):
    rows, lanes = keep.shape
    part = jax.ShapeDtypeStruct((rows // 2, lanes), F32)
    return pl.pallas_call(
        split_kernel,
        out_shape=(part, part),
        in_specs=vmem(2),
        out_specs=tuple(vmem(2)),
        compiler_params=params(),
        name="add_split",
    )(keep, received)


def scale_kernel(eigen, *refs):
    parts, out = refs[:-1], refs[-1]
    total = parts[0][...]
    for part in parts[1:]:
        total = total + part[...]
    out[...] = eigen[0] * total + eigen[1] * turned(total)


def scale(eigen, parts):
    return pl.pallas_call(
        scale_kernel,
        out_shape=jax.ShapeDtypeStruct(parts[0].shape, F32),
        in_specs=vmem(1 + len(parts)),
        out_specs=vmem(1)[0],
        compiler_params=params(),
        name="scale",
    )(eigen, *parts)


def expand(site, vectors, stacks):
    number = vectors.shape[3]
    total = None
    for half in range(2):
        term = matmul(vectors[site, half], stacks[half * number : (half + 1) * number])
        total = term if total is None else total + term
    return fold(total)


def update_kernel(x, residual, d, vectors, out, stacks):
    stacks[...] = stack(d[...], 1.0)
    for site in range(x.shape[0]):
        out[site] = x[site] + 0.5 * residual[site] + expand(site, vectors, stacks)


def update(x, residual, d, vectors):
    number = vectors.shape[-1]
    return pl.pallas_call(
        update_kernel,
        out_shape=jax.ShapeDtypeStruct(x.shape, F32),
        in_specs=vmem(4),
        out_specs=vmem(1)[0],
        scratch_shapes=[pltpu.VMEM((2 * number, 2 * x.shape[-1]), BF16)],
        compiler_params=params(),
        cost_estimate=cost(1e9, 8e6),
        name="update",
    )(x, residual, d, vectors)


def join_kernel(x, other_x, residual, other_residual, base, full):
    group = lax.axis_index("groups")
    own = x[0] + 0.5 * residual[0]
    other = other_x[0] + 0.5 * other_residual[0]
    base[0] = join_halves(own, other, group)
    full[0] = join_halves(residual[0], other_residual[0], group)


def join(x, other_x, residual, other_residual):
    sites, rows, lanes = x.shape
    field = pl.BlockSpec((1, rows, lanes), lambda s: (s, 0, 0))
    wide = pl.BlockSpec((1, rows, 2 * lanes), lambda s: (s, 0, 0))
    shape = jax.ShapeDtypeStruct((sites, rows, 2 * lanes), F32)
    return pl.pallas_call(
        join_kernel,
        grid=(sites,),
        out_shape=(shape, shape),
        in_specs=[field, field, field, field],
        out_specs=(wide, wide),
        compiler_params=params(),
        cost_estimate=cost(1e6, 4e6),
        name="join",
    )(x, other_x, residual, other_residual)


def final_kernel(base, d, other_d, vectors, out, stacks):
    @pl.when(pl.program_id(0) == 0)
    def _():
        stacks[...] = stack(join_halves(d[...], other_d[...], lax.axis_index("groups")), 1.0)

    for site in range(vectors.shape[0]):
        out[site] = base[site] + expand(site, vectors, stacks)


def final(base, d, other_d, vectors):
    sites, rows, lanes = base.shape
    number = vectors.shape[-1]
    step = 2
    field = pl.BlockSpec((step, rows, lanes), lambda s: (s, 0, 0))
    small = pl.BlockSpec((number, lanes // 2), lambda s: (0, 0))
    return pl.pallas_call(
        final_kernel,
        grid=(sites // step,),
        out_shape=jax.ShapeDtypeStruct(base.shape, F32),
        in_specs=[field, small, small, pl.BlockSpec((step, 2, 2 * rows, number), lambda s: (s, 0, 0, 0))],
        out_specs=field,
        scratch_shapes=[pltpu.VMEM((2 * number, 2 * lanes), BF16)],
        compiler_params=params(),
        cost_estimate=cost(2e9, 8e6),
        name="final",
    )(base, d, other_d, vectors)


def shifted(value, axis, step):
    count = lax.axis_size(axis)
    return lax.ppermute(value, axis, [(i, (i + step) % count) for i in range(count)])


def crossed(value, axis, mask):
    count = lax.axis_size(axis)
    return lax.ppermute(value, axis, [(i, i ^ mask) for i in range(count)])


def faces_of(x):
    backward_t = shifted(x, "tm", 1)
    forward_t = shifted(x, "tm", -1)
    backward_z = shifted(x, "space", 1)
    forward_z = shifted(x, "space", -1)
    return forward_z, backward_z, forward_t, backward_t


def halving(keep, send):
    count = lax.axis_size("space")
    mask = 1
    while True:
        received = crossed(send, "space", mask)
        mask *= 2
        if mask >= count:
            return keep + received
        keep, send = add_split(keep, received)


def doubling(part, mask):
    while mask:
        part = jnp.concatenate([part, crossed(part, "space", mask)], axis=0)
        mask //= 2
    return part


def both_doubling(part):
    groups, count = lax.axis_size("groups"), lax.axis_size("space")
    mask = count // 2
    pairs = [(g * count + s, (g ^ 1) * count + (s ^ mask)) for g in range(groups) for s in range(count)]
    across = lax.ppermute(part, ("groups", "space"), pairs)
    other = jnp.concatenate([crossed(part, "groups", 1), across], axis=0)
    own = jnp.concatenate([part, crossed(part, "space", mask)], axis=0)
    mask //= 2
    while mask:
        rows = own.shape[0]
        received = crossed(jnp.concatenate([own, other], axis=0), "space", mask)
        own = jnp.concatenate([own, received[:rows]], axis=0)
        other = jnp.concatenate([other, received[rows:]], axis=0)
        mask //= 2
    return own, other


def over_time(part):
    count = lax.axis_size("tm")
    if count <= 4:
        return [part] + [shifted(part, "tm", step) for step in range(1, count)]
    mask = 1
    while mask < count:
        part = part + crossed(part, "tm", mask)
        mask *= 2
    return [part]


def shards(couplings, source, initial, vectors, inverse_eigen):
    directions = couplings.shape[0]
    ny, nx, rows, lanes = source.shape[2:]
    sites = ny * nx
    number = vectors.shape[0]
    blocks = lax.axis_size("space")

    x = pack(initial.reshape(sites, rows, lanes))
    faces = faces_of(x)
    matrices = couplings.reshape(directions, sites, rows, couplings.shape[-1])
    rest, half_source, local, halo = first_local(x, source.reshape(sites, rows, lanes), matrices, ny, nx)
    flat = vectors.reshape(number, sites * vectors.shape[-1])
    by_rows = by_rows_of(flat)
    size = number // blocks
    eigen = lax.dynamic_slice_in_dim(inverse_eigen, lax.axis_index("space") * size, size, 1)
    eigen = jnp.broadcast_to(eigen[:, :, None], (2, size, lanes // 2))

    for sweep in range(ITERS):
        last = sweep == ITERS - 1
        if sweep:
            faces = faces_of(x)
            if last:
                other_x = crossed(x, "groups", 1)
            rest = local_part(x, half_source, local, ny, nx)
        forward_z, backward_z, forward_t, backward_t = faces
        rest = z_faces(rest, forward_z, backward_z, halo)
        if sweep and last:
            rest, other_x = lax.optimization_barrier((rest, other_x))
        rest = backward_face(rest, backward_t, halo)
        residual, keep, send = forward_face(rest, forward_t, halo, by_rows)
        if sweep == 0:
            flat, send = lax.optimization_barrier((flat, send))
            by_columns = by_columns_of(flat, sites)
        d = scale(eigen, over_time(halving(keep, send)))
        if not last:
            x = update(x, residual, doubling(d, blocks // 2), by_columns)
    other_residual = crossed(residual, "groups", 1)
    base, full_residual = join(x, other_x, residual, other_residual)
    d, other_d = both_doubling(d)
    whole = final(base, d, other_d, by_columns)
    shape = source.shape
    return whole.reshape(shape), full_residual.reshape(shape)


def solution(mesh):
    in_specs = (
        P(None, "tm", "space", None, None, None, None),
        P("tm", "space", None, None, None, None),
        P("tm", "space", None, None, None, None),
        P(None, "tm", "space", None, None, None),
        P(),
    )
    out_specs = (
        P(("groups", "tm"), "space", None, None, None, None),
        P(("groups", "tm"), "space", None, None, None, None),
    )
    return jax.shard_map(shards, mesh=mesh, in_specs=in_specs, out_specs=out_specs, check_vma=False)
```

```python
import functools

import jax
import jax.numpy as jnp
from jax import lax
from jax.experimental import pallas as pl
from jax.experimental.pallas import tpu as pltpu
from jax.sharding import PartitionSpec as P

ITERS = 2
F32 = jnp.float32
BF16 = jnp.bfloat16
LOCAL = 5


def params(mebibytes=12):
    return pltpu.CompilerParams(vmem_limit_bytes=mebibytes * 1024 * 1024)


def cost(flops, read):
    return pl.CostEstimate(flops=int(flops), bytes_accessed=int(read), transcendentals=0)


def low_lanes(value):
    lanes = lax.broadcasted_iota(jnp.int32, value.shape, value.ndim - 1)
    return lanes < value.shape[-1] // 2


def swap(value):
    return pltpu.roll(value, value.shape[-1] // 2, value.ndim - 1)


def turned(value):
    moved = swap(value)
    return jnp.where(low_lanes(value), -moved, moved)


def high_low(value):
    high = value.astype(BF16)
    low = (value - high.astype(F32)).astype(BF16)
    return high, low


def stack(value, sign):
    high, low = high_low(jnp.concatenate([value, sign * turned(value)], axis=0))
    return jnp.concatenate([high, low], axis=1)


def matmul(left, right):
    return jnp.dot(left, right, preferred_element_type=F32)


def fold(product):
    rows, lanes = product.shape[0] // 2, product.shape[1] // 2
    high = product[:rows, :lanes] + (product[:rows, lanes:] + product[rows:, :lanes])
    return high + product[rows:, lanes:]


def pick_half(value, group):
    middle = value.shape[-1] // 2
    real, imag = value[:, :middle], value[:, middle:]
    low = low_lanes(real)
    first = jnp.where(low, real, swap(imag))
    second = jnp.where(low, swap(real), imag)
    return jnp.where(group == 0, first, second)


def join_halves(own, other, group):
    first = jnp.where(group == 0, own, other)
    second = jnp.where(group == 0, other, own)
    low = low_lanes(own)
    real = jnp.where(low, first, swap(second))
    imag = jnp.where(low, swap(first), second)
    return jnp.concatenate([real, imag], axis=1)


def vmem(count):
    return [pl.BlockSpec(memory_space=pltpu.VMEM)] * count


def in_hbm(value):
    return pltpu.with_memory_space_constraint(value, pltpu.HBM)


def pack_kernel(full, half):
    group = lax.axis_index("groups")
    for site in range(full.shape[0]):
        half[site] = pick_half(full[site], group)


def pack(full):
    sites, rows, lanes = full.shape
    step = 2
    return pl.pallas_call(
        pack_kernel,
        grid=(sites // step,),
        out_shape=pltpu.VMEM((sites, rows, lanes // 2), F32),
        in_specs=[pl.BlockSpec((step, rows, lanes), lambda s: (s, 0, 0))],
        out_specs=pl.BlockSpec((step, rows, lanes // 2), lambda s: (s, 0, 0)),
        compiler_params=params(),
        cost_estimate=cost(1e6, 1e6),
        name="pack",
    )(in_hbm(full))


def around(site, ny, nx):
    y, x = site // nx, lax.rem(site, nx)
    right, left = lax.rem(x + 1, nx), lax.rem(x + nx - 1, nx)
    up, down = lax.rem(y + 1, ny), lax.rem(y + ny - 1, ny)
    return (site, y * nx + right, y * nx + left, up * nx + x, down * nx + x)


def local_sum(site, ny, nx, x_ref, stacks, matrix):
    @pl.when(site == 0)
    def _():
        for each in range(ny * nx):
            stacks[each] = stack(x_ref[each], 1.0)

    total = None
    for direction, neighbour in enumerate(around(site, ny, nx)):
        term = matmul(matrix(direction), stacks[neighbour])
        total = term if total is None else total + term
    return fold(total)


def first_kernel(ny, nx, x_ref, source, couplings, rest, half_source, local, halo, stacks):
    site = pl.program_id(0)
    own = pick_half(source[0], lax.axis_index("groups"))
    half_source[0] = own
    for direction in range(couplings.shape[0]):
        high, low = high_low(couplings[direction, 0])
        both = jnp.concatenate([high, low], axis=0)
        if direction < LOCAL:
            local[direction, 0] = both
        else:
            halo[direction - LOCAL, 0] = both
    rest[0] = own - local_sum(site, ny, nx, x_ref, stacks, lambda d: local[d, 0])


def first_local(x, source, couplings, ny, nx):
    sites, rows, lanes = x.shape
    directions, _, _, columns = couplings.shape
    outer = directions - LOCAL
    return pl.pallas_call(
        functools.partial(first_kernel, ny, nx),
        grid=(sites,),
        out_shape=(
            pltpu.VMEM(x.shape, F32),
            pltpu.VMEM(x.shape, F32),
            pltpu.VMEM((LOCAL, sites, 2 * rows, columns), BF16),
            pltpu.VMEM((outer, sites, 2 * rows, columns), BF16),
        ),
        in_specs=[
            pl.BlockSpec((sites, rows, lanes), lambda s: (0, 0, 0)),
            pl.BlockSpec((1, rows, 2 * lanes), lambda s: (s, 0, 0)),
            pl.BlockSpec((directions, 1, rows, columns), lambda s: (0, s, 0, 0)),
        ],
        out_specs=(
            pl.BlockSpec((1, rows, lanes), lambda s: (s, 0, 0)),
            pl.BlockSpec((1, rows, lanes), lambda s: (s, 0, 0)),
            pl.BlockSpec((LOCAL, 1, 2 * rows, columns), lambda s: (0, s, 0, 0)),
            pl.BlockSpec((outer, 1, 2 * rows, columns), lambda s: (0, s, 0, 0)),
        ),
        scratch_shapes=[pltpu.VMEM((sites, 2 * rows, 2 * lanes), BF16)],
        compiler_params=params(),
        cost_estimate=cost(8e9, 16e6),
        name="first_local",
    )(x, in_hbm(source), in_hbm(couplings))


def local_kernel(ny, nx, x_ref, source, local, rest, stacks):
    site = pl.program_id(0)
    rest[0] = source[0] - local_sum(site, ny, nx, x_ref, stacks, lambda d: local[d, 0])


def local_part(x, source, local, ny, nx):
    sites, rows, lanes = x.shape
    columns = local.shape[-1]
    return pl.pallas_call(
        functools.partial(local_kernel, ny, nx),
        grid=(sites,),
        out_shape=pltpu.VMEM(x.shape, F32),
        in_specs=[
            pl.BlockSpec((sites, rows, lanes), lambda s: (0, 0, 0)),
            pl.BlockSpec((1, rows, lanes), lambda s: (s, 0, 0)),
            pl.BlockSpec((LOCAL, 1, 2 * rows, columns), lambda s: (0, s, 0, 0)),
        ],
        out_specs=pl.BlockSpec((1, rows, lanes), lambda s: (s, 0, 0)),
        scratch_shapes=[pltpu.VMEM((sites, 2 * rows, 2 * lanes), BF16)],
        compiler_params=params(),
        cost_estimate=cost(8e9, 8e6),
        name="local_part",
    )(x, source, local)


def block_order(count):
    bits = count.bit_length() - 1
    return [int(format(index, "b").zfill(bits)[::-1], 2) if bits else 0 for index in range(count)]


def ordered_rows(vectors, chunk, taken):
    blocks = lax.axis_size("space")
    space = lax.axis_index("space")
    size = vectors.shape[0] // blocks
    unit = min(size, taken)
    parts = []
    for start in range(chunk * taken, (chunk + 1) * taken, unit):
        block = space ^ block_order(blocks)[start // size]
        parts.append(vectors[pl.ds(pl.multiple_of(block * size + start % size, unit), unit)])
    return parts[0] if len(parts) == 1 else jnp.concatenate(parts, axis=0)


def by_rows_kernel(vectors, out):
    taken = 128
    number = vectors.shape[0]
    for chunk in range(number // taken):
        high, low = high_low(ordered_rows(vectors, chunk, taken))
        out[chunk * taken : (chunk + 1) * taken] = high
        out[number + chunk * taken : number + (chunk + 1) * taken] = low


def by_rows_of(vectors):
    number, width = vectors.shape
    return pl.pallas_call(
        by_rows_kernel,
        out_shape=pltpu.VMEM((2 * number, width), BF16),
        in_specs=vmem(1),
        out_specs=vmem(1)[0],
        compiler_params=params(),
        cost_estimate=cost(1e6, 6e6),
        name="by_rows",
    )(vectors)


def by_columns_kernel(by_rows, out):
    taken = 128
    number = by_rows.shape[0] // 2
    sites, rows = out.shape[0], out.shape[2] // 2
    for part in range(2):
        for chunk in range(number // taken):
            start = part * number + chunk * taken
            across = by_rows[start : start + taken].astype(F32).T.astype(BF16)
            at = slice(chunk * taken, (chunk + 1) * taken)
            for site in range(sites):
                for half in range(2):
                    start = (2 * site + half) * rows
                    out[site, half, part * rows : (part + 1) * rows, at] = across[start : start + rows]


def by_columns_of(by_rows, sites):
    number, width = by_rows.shape[0] // 2, by_rows.shape[1]
    rows = width // sites // 2
    return pl.pallas_call(
        by_columns_kernel,
        out_shape=pltpu.VMEM((sites, 2, 2 * rows, number), BF16),
        in_specs=vmem(1),
        out_specs=vmem(1)[0],
        compiler_params=params(),
        cost_estimate=cost(1e6, 6e6),
        name="by_columns",
    )(by_rows)


def apply_faces(site, faces, matrices):
    summed = None
    for face, matrix in zip(faces, matrices):
        term = matmul(matrix[site], stack(face(site), 1.0))
        summed = term if summed is None else summed + term
    return fold(summed)


def z_faces_kernel(rest, forward, backward, matrix, out):
    faces = (lambda s: forward[s], lambda s: backward[s])
    for site in range(rest.shape[0]):
        out[site] = rest[site] - apply_faces(site, faces, (matrix.at[0], matrix.at[1]))


def z_faces(rest, forward, backward, matrix):
    return pl.pallas_call(
        z_faces_kernel,
        out_shape=pltpu.VMEM(rest.shape, F32),
        in_specs=vmem(4),
        out_specs=vmem(1)[0],
        compiler_params=params(),
        cost_estimate=cost(1e9, 4e6),
        name="z_faces",
    )(rest, forward, backward, matrix)


def edge_sign(last):
    count = lax.axis_size("tm")
    return jnp.where(lax.axis_index("tm") == (count - 1 if last else 0), -1.0, 1.0).astype(F32)


def backward_kernel(rest, backward, matrix, out):
    sign = edge_sign(False)
    for site in range(rest.shape[0]):
        out[site] = rest[site] - apply_faces(site, (lambda s: sign * backward[s],), (matrix.at[3],))


def backward_face(rest, backward, matrix):
    return pl.pallas_call(
        backward_kernel,
        out_shape=pltpu.VMEM(rest.shape, F32),
        in_specs=vmem(3),
        out_specs=vmem(1)[0],
        compiler_params=params(),
        cost_estimate=cost(1e9, 4e6),
        name="backward_face",
    )(rest, backward, matrix)


def forward_kernel(rest, forward, matrix, vectors, residual, keep, send, stacks):
    sign = edge_sign(True)
    rows = 2 * rest.shape[1]
    for site in range(rest.shape[0]):
        own = rest[site] - apply_faces(site, (lambda s: sign * forward[s],), (matrix.at[2],))
        residual[site] = own
        stacks[site * rows : (site + 1) * rows] = stack(own, -1.0)
    whole = fold(matmul(vectors[...], stacks[...]))
    half = whole.shape[0] // 2
    keep[...] = whole[:half]
    send[...] = whole[half:]


def forward_face(rest, forward, matrix, vectors):
    sites, rows, lanes = rest.shape
    part = pltpu.VMEM((vectors.shape[0] // 4, lanes), F32)
    return pl.pallas_call(
        forward_kernel,
        out_shape=(pltpu.VMEM(rest.shape, F32), part, part),
        in_specs=vmem(4),
        out_specs=tuple(vmem(3)),
        scratch_shapes=[pltpu.VMEM((sites * 2 * rows, 2 * lanes), BF16)],
        compiler_params=params(),
        cost_estimate=cost(2e9, 8e6),
        name="forward_face",
    )(rest, forward, matrix, vectors)


def split_kernel(keep, received, next_keep, next_send):
    half = next_keep.shape[0]
    next_keep[...] = keep[:half] + received[:half]
    next_send[...] = keep[half:] + received[half:]


def add_split(keep, received):
    rows, lanes = keep.shape
    part = pltpu.VMEM((rows // 2, lanes), F32)
    return pl.pallas_call(
        split_kernel,
        out_shape=(part, part),
        in_specs=vmem(2),
        out_specs=tuple(vmem(2)),
        compiler_params=params(),
        name="add_split",
    )(keep, received)


def add_kernel(left, right, out):
    out[...] = left[...] + right[...]


def add(left, right):
    return pl.pallas_call(
        add_kernel,
        out_shape=pltpu.VMEM(left.shape, F32),
        in_specs=vmem(2),
        out_specs=vmem(1)[0],
        compiler_params=params(),
        name="add",
    )(left, right)


def scale_kernel(eigen, *refs):
    parts, out = refs[:-1], refs[-1]
    total = parts[0][...]
    for part in parts[1:]:
        total = total + part[...]
    out[...] = eigen[0] * total + eigen[1] * turned(total)


def scale(eigen, parts):
    return pl.pallas_call(
        scale_kernel,
        out_shape=pltpu.VMEM(parts[0].shape, F32),
        in_specs=vmem(1 + len(parts)),
        out_specs=vmem(1)[0],
        compiler_params=params(),
        name="scale",
    )(eigen, *parts)


def expand(site, vectors, stacks):
    number = vectors.shape[3]
    total = None
    for half in range(2):
        term = matmul(vectors[site, half], stacks[half * number : (half + 1) * number])
        total = term if total is None else total + term
    return fold(total)


def assemble(pieces):
    return pieces[0][...] if len(pieces) == 1 else jnp.concatenate([piece[...] for piece in pieces], axis=0)


def update_kernel(x, residual, vectors, *refs):
    pieces, (out, stacks) = refs[:-2], refs[-2:]
    stacks[...] = stack(assemble(pieces), 1.0)
    for site in range(x.shape[0]):
        out[site] = x[site] + 0.5 * residual[site] + expand(site, vectors, stacks)


def update(x, residual, pieces, vectors):
    number = vectors.shape[-1]
    return pl.pallas_call(
        update_kernel,
        out_shape=pltpu.VMEM(x.shape, F32),
        in_specs=vmem(3 + len(pieces)),
        out_specs=vmem(1)[0],
        scratch_shapes=[pltpu.VMEM((2 * number, 2 * x.shape[-1]), BF16)],
        compiler_params=params(),
        cost_estimate=cost(1e9, 8e6),
        name="update",
    )(x, residual, vectors, *pieces)


def join_kernel(x, other_x, residual, other_residual, base, full):
    group = lax.axis_index("groups")
    for site in range(x.shape[0]):
        own = x[site] + 0.5 * residual[site]
        other = other_x[site] + 0.5 * other_residual[site]
        base[site] = join_halves(own, other, group)
        full[site] = join_halves(residual[site], other_residual[site], group)


def join(x, other_x, residual, other_residual):
    sites, rows, lanes = x.shape
    shape = (sites, rows, 2 * lanes)
    return pl.pallas_call(
        join_kernel,
        out_shape=(pltpu.VMEM(shape, F32), jax.ShapeDtypeStruct(shape, F32)),
        in_specs=vmem(4),
        out_specs=tuple(vmem(2)),
        compiler_params=params(),
        cost_estimate=cost(1e6, 4e6),
        name="join",
    )(x, other_x, residual, other_residual)


def final_kernel(count, base, vectors, *refs):
    own, other, (out, stacks) = refs[:count], refs[count:-2], refs[-2:]

    @pl.when(pl.program_id(0) == 0)
    def _():
        stacks[...] = stack(join_halves(assemble(own), assemble(other), lax.axis_index("groups")), 1.0)

    for site in range(vectors.shape[0]):
        out[site] = base[site] + expand(site, vectors, stacks)


def final(base, own, other, vectors):
    sites, rows, lanes = base.shape
    number = vectors.shape[-1]
    step = 2
    field = pl.BlockSpec((step, rows, lanes), lambda s: (s, 0, 0))
    return pl.pallas_call(
        functools.partial(final_kernel, len(own)),
        grid=(sites // step,),
        out_shape=jax.ShapeDtypeStruct(base.shape, F32),
        in_specs=[field, pl.BlockSpec((step, 2, 2 * rows, number), lambda s: (s, 0, 0, 0))] + vmem(len(own) + len(other)),
        out_specs=field,
        scratch_shapes=[pltpu.VMEM((2 * number, 2 * lanes), BF16)],
        compiler_params=params(),
        cost_estimate=cost(2e9, 8e6),
        name="final",
    )(base, vectors, *own, *other)


def shifted(value, axis, step):
    count = lax.axis_size(axis)
    return lax.ppermute(value, axis, [(i, (i + step) % count) for i in range(count)])


def crossed(value, axis, mask):
    count = lax.axis_size(axis)
    return lax.ppermute(value, axis, [(i, i ^ mask) for i in range(count)])


def faces_of(x):
    backward_t = shifted(x, "tm", 1)
    forward_t = shifted(x, "tm", -1)
    backward_z = shifted(x, "space", 1)
    forward_z = shifted(x, "space", -1)
    return forward_z, backward_z, forward_t, backward_t


def halving(keep, send):
    count = lax.axis_size("space")
    mask = 1
    while True:
        received = crossed(send, "space", mask)
        mask *= 2
        if mask >= count:
            return add(keep, received)
        keep, send = add_split(keep, received)


def doubling(pieces, mask):
    while mask:
        if len(pieces) > 2:
            pieces = [jnp.concatenate(pieces, axis=0)]
        pieces = pieces + [crossed(piece, "space", mask) for piece in pieces]
        mask //= 2
    return pieces


def both_doubling(part):
    groups, count = lax.axis_size("groups"), lax.axis_size("space")
    mask = count // 2
    pairs = [(g * count + s, (g ^ 1) * count + (s ^ mask)) for g in range(groups) for s in range(count)]
    across = lax.ppermute(part, ("groups", "space"), pairs)
    other = [crossed(part, "groups", 1), across]
    own = [part, crossed(part, "space", mask)]
    return doubling(own, mask // 2), doubling(other, mask // 2)


def over_time(part):
    count = lax.axis_size("tm")
    if count <= 4:
        return [part] + [shifted(part, "tm", step) for step in range(1, count)]
    mask = 1
    while mask < count:
        part = part + crossed(part, "tm", mask)
        mask *= 2
    return [part]


def shards(couplings, source, initial, vectors, inverse_eigen):
    directions = couplings.shape[0]
    ny, nx, rows, lanes = source.shape[2:]
    sites = ny * nx
    number = vectors.shape[0]
    blocks = lax.axis_size("space")

    x = pack(initial.reshape(sites, rows, lanes))
    faces = faces_of(x)
    matrices = couplings.reshape(directions, sites, rows, couplings.shape[-1])
    rest, half_source, local, halo = first_local(x, source.reshape(sites, rows, lanes), matrices, ny, nx)
    by_rows = by_rows_of(vectors.reshape(number, sites * vectors.shape[-1]))
    size = number // blocks
    eigen = lax.dynamic_slice_in_dim(inverse_eigen, lax.axis_index("space") * size, size, 1)
    eigen = jnp.broadcast_to(eigen[:, :, None], (2, size, lanes // 2))

    for sweep in range(ITERS):
        last = sweep == ITERS - 1
        if sweep:
            faces = faces_of(x)
            if last:
                other_x = crossed(x, "groups", 1)
            rest = local_part(x, half_source, local, ny, nx)
        forward_z, backward_z, forward_t, backward_t = faces
        rest = z_faces(rest, forward_z, backward_z, halo)
        if sweep and last:
            rest, other_x = lax.optimization_barrier((rest, other_x))
        rest = backward_face(rest, backward_t, halo)
        residual, keep, send = forward_face(rest, forward_t, halo, by_rows)
        if sweep == 0:
            by_rows, send = lax.optimization_barrier((by_rows, send))
            by_columns = by_columns_of(by_rows, sites)
        if last:
            other_residual = crossed(residual, "groups", 1)
        parts = over_time(halving(keep, send))
        if sweep == 0:
            parts, by_columns = lax.optimization_barrier((parts, by_columns))
        if last:
            parts, other_residual = lax.optimization_barrier((parts, other_residual))
        d = scale(eigen, parts)
        if not last:
            x = update(x, residual, doubling([d], blocks // 2), by_columns)
    base, full_residual = join(x, other_x, residual, other_residual)
    whole = final(base, *both_doubling(d), by_columns)
    shape = source.shape
    return whole.reshape(shape), full_residual.reshape(shape)


def solution(mesh):
    in_specs = (
        P(None, "tm", "space", None, None, None, None),
        P("tm", "space", None, None, None, None),
        P("tm", "space", None, None, None, None),
        P(None, "tm", "space", None, None, None),
        P(),
    )
    out_specs = (
        P(("groups", "tm"), "space", None, None, None, None),
        P(("groups", "tm"), "space", None, None, None, None),
    )
    return jax.shard_map(shards, mesh=mesh, in_specs=in_specs, out_specs=out_specs, check_vma=False)
```

```python
import functools

import jax
import jax.numpy as jnp
from jax import lax
from jax.experimental import pallas as pl
from jax.experimental.pallas import tpu as pltpu
from jax.sharding import PartitionSpec as P

ITERS = 2
F32 = jnp.float32
BF16 = jnp.bfloat16
LOCAL = 5


def params(mebibytes=12):
    return pltpu.CompilerParams(vmem_limit_bytes=mebibytes * 1024 * 1024)


def cost(flops, read):
    return pl.CostEstimate(flops=int(flops), bytes_accessed=int(read), transcendentals=0)


def low_lanes(value):
    lanes = lax.broadcasted_iota(jnp.int32, value.shape, value.ndim - 1)
    return lanes < value.shape[-1] // 2


def swap(value):
    return pltpu.roll(value, value.shape[-1] // 2, value.ndim - 1)


def turned(value):
    moved = swap(value)
    return jnp.where(low_lanes(value), -moved, moved)


def high_low(value):
    high = value.astype(BF16)
    low = (value - high.astype(F32)).astype(BF16)
    return high, low


def stack(value, sign):
    high, low = high_low(jnp.concatenate([value, sign * turned(value)], axis=0))
    return jnp.concatenate([high, low], axis=1)


def matmul(left, right):
    return jnp.dot(left, right, preferred_element_type=F32)


def fold(product):
    rows, lanes = product.shape[0] // 2, product.shape[1] // 2
    high = product[:rows, :lanes] + (product[:rows, lanes:] + product[rows:, :lanes])
    return high + product[rows:, lanes:]


def pick_half(value, group):
    middle = value.shape[-1] // 2
    real, imag = value[:, :middle], value[:, middle:]
    low = low_lanes(real)
    first = jnp.where(low, real, swap(imag))
    second = jnp.where(low, swap(real), imag)
    return jnp.where(group == 0, first, second)


def join_halves(own, other, group):
    first = jnp.where(group == 0, own, other)
    second = jnp.where(group == 0, other, own)
    low = low_lanes(own)
    real = jnp.where(low, first, swap(second))
    imag = jnp.where(low, swap(first), second)
    return jnp.concatenate([real, imag], axis=1)


def vmem(count):
    return [pl.BlockSpec(memory_space=pltpu.VMEM)] * count


def in_hbm(value):
    return pltpu.with_memory_space_constraint(value, pltpu.HBM)


def pack_kernel(full, half):
    group = lax.axis_index("groups")
    for site in range(full.shape[0]):
        half[site] = pick_half(full[site], group)


def pack(full):
    sites, rows, lanes = full.shape
    return pl.pallas_call(
        pack_kernel,
        out_shape=pltpu.VMEM((sites, rows, lanes // 2), F32),
        in_specs=vmem(1),
        out_specs=vmem(1)[0],
        compiler_params=params(),
        cost_estimate=cost(1e6, 1e6),
        name="pack",
    )(full)


def around(site, ny, nx):
    y, x = site // nx, lax.rem(site, nx)
    right, left = lax.rem(x + 1, nx), lax.rem(x + nx - 1, nx)
    up, down = lax.rem(y + 1, ny), lax.rem(y + ny - 1, ny)
    return (site, y * nx + right, y * nx + left, up * nx + x, down * nx + x)


def local_sum(site, ny, nx, x_ref, stacks, matrix):
    @pl.when(site == 0)
    def _():
        for each in range(ny * nx):
            stacks[each] = stack(x_ref[each], 1.0)

    total = None
    for direction, neighbour in enumerate(around(site, ny, nx)):
        term = matmul(matrix(direction), stacks[neighbour])
        total = term if total is None else total + term
    return fold(total)


def first_kernel(ny, nx, x_ref, source, couplings, rest, half_source, local, halo, stacks):
    site = pl.program_id(0)
    own = pick_half(source[0], lax.axis_index("groups"))
    half_source[0] = own
    for direction in range(couplings.shape[0]):
        high, low = high_low(couplings[direction, 0])
        both = jnp.concatenate([high, low], axis=0)
        if direction < LOCAL:
            local[direction, 0] = both
        else:
            halo[direction - LOCAL, 0] = both
    rest[0] = own - local_sum(site, ny, nx, x_ref, stacks, lambda d: local[d, 0])


def first_local(x, source, couplings, ny, nx):
    sites, rows, lanes = x.shape
    directions, _, _, columns = couplings.shape
    outer = directions - LOCAL
    return pl.pallas_call(
        functools.partial(first_kernel, ny, nx),
        grid=(sites,),
        out_shape=(
            pltpu.VMEM(x.shape, F32),
            pltpu.VMEM(x.shape, F32),
            pltpu.VMEM((LOCAL, sites, 2 * rows, columns), BF16),
            pltpu.VMEM((outer, sites, 2 * rows, columns), BF16),
        ),
        in_specs=[
            pl.BlockSpec((sites, rows, lanes), lambda s: (0, 0, 0)),
            pl.BlockSpec((1, rows, 2 * lanes), lambda s: (s, 0, 0)),
            pl.BlockSpec((directions, 1, rows, columns), lambda s: (0, s, 0, 0)),
        ],
        out_specs=(
            pl.BlockSpec((1, rows, lanes), lambda s: (s, 0, 0)),
            pl.BlockSpec((1, rows, lanes), lambda s: (s, 0, 0)),
            pl.BlockSpec((LOCAL, 1, 2 * rows, columns), lambda s: (0, s, 0, 0)),
            pl.BlockSpec((outer, 1, 2 * rows, columns), lambda s: (0, s, 0, 0)),
        ),
        scratch_shapes=[pltpu.VMEM((sites, 2 * rows, 2 * lanes), BF16)],
        compiler_params=params(),
        cost_estimate=cost(8e9, 16e6),
        name="first_local",
    )(x, in_hbm(source), in_hbm(couplings))


def local_kernel(ny, nx, x_ref, source, local, rest, stacks):
    site = pl.program_id(0)
    rest[0] = source[0] - local_sum(site, ny, nx, x_ref, stacks, lambda d: local[d, 0])


def local_part(x, source, local, ny, nx):
    sites, rows, lanes = x.shape
    columns = local.shape[-1]
    return pl.pallas_call(
        functools.partial(local_kernel, ny, nx),
        grid=(sites,),
        out_shape=pltpu.VMEM(x.shape, F32),
        in_specs=[
            pl.BlockSpec((sites, rows, lanes), lambda s: (0, 0, 0)),
            pl.BlockSpec((1, rows, lanes), lambda s: (s, 0, 0)),
            pl.BlockSpec((LOCAL, 1, 2 * rows, columns), lambda s: (0, s, 0, 0)),
        ],
        out_specs=pl.BlockSpec((1, rows, lanes), lambda s: (s, 0, 0)),
        scratch_shapes=[pltpu.VMEM((sites, 2 * rows, 2 * lanes), BF16)],
        compiler_params=params(),
        cost_estimate=cost(8e9, 8e6),
        name="local_part",
    )(x, source, local)


def block_order(count):
    bits = count.bit_length() - 1
    return [int(format(index, "b").zfill(bits)[::-1], 2) if bits else 0 for index in range(count)]


def block_starts(size):
    space = lax.axis_index("space")
    return [pl.multiple_of((space ^ block) * size, size) for block in block_order(lax.axis_size("space"))]


def vectors_kernel(across, by_rows, by_columns):
    sites, _, double, number = by_columns.shape
    rows = double // 2
    high, low = high_low(across[...].T)
    by_rows[:number] = high
    by_rows[number:] = low
    for site in range(sites):
        for half in range(2):
            start = (2 * site + half) * rows
            high, low = high_low(across[start : start + rows])
            by_columns[site, half, :rows] = high
            by_columns[site, half, rows:] = low


def vectors_parts(across, sites):
    width, number = across.shape
    rows = width // sites // 2
    step = 2
    return pl.pallas_call(
        vectors_kernel,
        grid=(sites // step,),
        out_shape=(pltpu.VMEM((2 * number, width), BF16), pltpu.VMEM((sites, 2, 2 * rows, number), BF16)),
        in_specs=[pl.BlockSpec((step * 2 * rows, number), lambda s: (s, 0))],
        out_specs=(
            pl.BlockSpec((2 * number, step * 2 * rows), lambda s: (0, s)),
            pl.BlockSpec((step, 2, 2 * rows, number), lambda s: (s, 0, 0, 0)),
        ),
        compiler_params=params(16),
        cost_estimate=cost(1e6, 9e6),
        name="vectors_parts",
    )(in_hbm(across))


def eigen_kernel(inverse, out):
    size, lanes = out.shape[1:]
    number = inverse.shape[1]
    start = lax.axis_index("space") * size
    row = lax.broadcasted_iota(jnp.int32, (size, number), 0) + start
    chosen = lax.broadcasted_iota(jnp.int32, (size, number), 1) == row
    for part in range(2):
        value = jnp.where(chosen, inverse[part : part + 1], 0.0)
        out[part] = jnp.broadcast_to(jnp.sum(value, axis=1, keepdims=True), (size, lanes))


def eigen_of(inverse, size, lanes):
    return pl.pallas_call(
        eigen_kernel,
        out_shape=pltpu.VMEM((2, size, lanes), F32),
        in_specs=vmem(1),
        out_specs=vmem(1)[0],
        compiler_params=params(),
        cost_estimate=cost(1e6, 1e6),
        name="eigen",
    )(inverse)


def apply_faces(site, faces, matrices):
    summed = None
    for face, matrix in zip(faces, matrices):
        term = matmul(matrix[site], stack(face(site), 1.0))
        summed = term if summed is None else summed + term
    return fold(summed)


def z_faces_kernel(rest, forward, backward, matrix, out):
    faces = (lambda s: forward[s], lambda s: backward[s])
    for site in range(rest.shape[0]):
        out[site] = rest[site] - apply_faces(site, faces, (matrix.at[0], matrix.at[1]))


def z_faces(rest, forward, backward, matrix):
    return pl.pallas_call(
        z_faces_kernel,
        out_shape=pltpu.VMEM(rest.shape, F32),
        in_specs=vmem(4),
        out_specs=vmem(1)[0],
        compiler_params=params(),
        cost_estimate=cost(1e9, 4e6),
        name="z_faces",
    )(rest, forward, backward, matrix)


def edge_sign(last):
    count = lax.axis_size("tm")
    return jnp.where(lax.axis_index("tm") == (count - 1 if last else 0), -1.0, 1.0).astype(F32)


def backward_kernel(rest, backward, matrix, out):
    sign = edge_sign(False)
    for site in range(rest.shape[0]):
        out[site] = rest[site] - apply_faces(site, (lambda s: sign * backward[s],), (matrix.at[3],))


def backward_face(rest, backward, matrix):
    return pl.pallas_call(
        backward_kernel,
        out_shape=pltpu.VMEM(rest.shape, F32),
        in_specs=vmem(3),
        out_specs=vmem(1)[0],
        compiler_params=params(),
        cost_estimate=cost(1e9, 4e6),
        name="backward_face",
    )(rest, backward, matrix)


def forward_kernel(rest, forward, matrix, vectors, residual, keep, send, stacks, whole):
    sign = edge_sign(True)
    rows = 2 * rest.shape[1]
    for site in range(rest.shape[0]):
        own = rest[site] - apply_faces(site, (lambda s: sign * forward[s],), (matrix.at[2],))
        residual[site] = own
        stacks[site * rows : (site + 1) * rows] = stack(own, -1.0)
    whole[...] = fold(matmul(vectors[...], stacks[...]))
    starts = block_starts(whole.shape[0] // lax.axis_size("space"))
    half = len(starts) // 2
    size = whole.shape[0] // len(starts)
    for index, start in enumerate(starts):
        part, at = (keep, index) if index < half else (send, index - half)
        part[at * size : (at + 1) * size] = whole[pl.ds(start, size)]


def forward_face(rest, forward, matrix, vectors):
    sites, rows, lanes = rest.shape
    part = pltpu.VMEM((vectors.shape[0] // 4, lanes), F32)
    return pl.pallas_call(
        forward_kernel,
        out_shape=(pltpu.VMEM(rest.shape, F32), part, part),
        in_specs=vmem(4),
        out_specs=tuple(vmem(3)),
        scratch_shapes=[
            pltpu.VMEM((sites * 2 * rows, 2 * lanes), BF16),
            pltpu.VMEM((vectors.shape[0] // 2, lanes), F32),
        ],
        compiler_params=params(),
        cost_estimate=cost(2e9, 8e6),
        name="forward_face",
    )(rest, forward, matrix, vectors)


def split_kernel(keep, received, next_keep, next_send):
    half = next_keep.shape[0]
    next_keep[...] = keep[:half] + received[:half]
    next_send[...] = keep[half:] + received[half:]


def add_split(keep, received):
    rows, lanes = keep.shape
    part = pltpu.VMEM((rows // 2, lanes), F32)
    return pl.pallas_call(
        split_kernel,
        out_shape=(part, part),
        in_specs=vmem(2),
        out_specs=tuple(vmem(2)),
        compiler_params=params(),
        name="add_split",
    )(keep, received)


def add_kernel(left, right, out):
    out[...] = left[...] + right[...]


def add(left, right):
    return pl.pallas_call(
        add_kernel,
        out_shape=pltpu.VMEM(left.shape, F32),
        in_specs=vmem(2),
        out_specs=vmem(1)[0],
        compiler_params=params(),
        name="add",
    )(left, right)


def scale_kernel(eigen, *refs):
    parts, out = refs[:-1], refs[-1]
    total = parts[0][...]
    for part in parts[1:]:
        total = total + part[...]
    out[...] = eigen[0] * total + eigen[1] * turned(total)


def scale(eigen, parts):
    return pl.pallas_call(
        scale_kernel,
        out_shape=pltpu.VMEM(parts[0].shape, F32),
        in_specs=vmem(1 + len(parts)),
        out_specs=vmem(1)[0],
        compiler_params=params(),
        name="scale",
    )(eigen, *parts)


def expand(site, vectors, stacks):
    number = vectors.shape[3]
    total = None
    for half in range(2):
        term = matmul(vectors[site, half], stacks[half * number : (half + 1) * number])
        total = term if total is None else total + term
    return fold(total)


def place_pieces(values, stacks):
    number = stacks.shape[0] // 2
    size = number // lax.axis_size("space")
    starts = iter(block_starts(size))
    for value in values:
        both = stack(value, 1.0)
        rows = value.shape[0]
        for at in range(0, rows, size):
            start = next(starts)
            stacks[pl.ds(start, size)] = both[at : at + size]
            stacks[pl.ds(start + number, size)] = both[rows + at : rows + at + size]


def update_kernel(x, residual, vectors, *refs):
    pieces, (out, stacks) = refs[:-2], refs[-2:]
    place_pieces([piece[...] for piece in pieces], stacks)
    for site in range(x.shape[0]):
        out[site] = x[site] + 0.5 * residual[site] + expand(site, vectors, stacks)


def update(x, residual, pieces, vectors):
    number = vectors.shape[-1]
    return pl.pallas_call(
        update_kernel,
        out_shape=pltpu.VMEM(x.shape, F32),
        in_specs=vmem(3 + len(pieces)),
        out_specs=vmem(1)[0],
        scratch_shapes=[pltpu.VMEM((2 * number, 2 * x.shape[-1]), BF16)],
        compiler_params=params(),
        cost_estimate=cost(1e9, 8e6),
        name="update",
    )(x, residual, vectors, *pieces)


def join_kernel(x, other_x, residual, other_residual, base, full):
    group = lax.axis_index("groups")
    for site in range(x.shape[0]):
        own = x[site] + 0.5 * residual[site]
        other = other_x[site] + 0.5 * other_residual[site]
        base[site] = join_halves(own, other, group)
        full[site] = join_halves(residual[site], other_residual[site], group)


def join(x, other_x, residual, other_residual):
    sites, rows, lanes = x.shape
    shape = (sites, rows, 2 * lanes)
    return pl.pallas_call(
        join_kernel,
        out_shape=(pltpu.VMEM(shape, F32), jax.ShapeDtypeStruct(shape, F32)),
        in_specs=vmem(4),
        out_specs=tuple(vmem(2)),
        compiler_params=params(),
        cost_estimate=cost(1e6, 4e6),
        name="join",
    )(x, other_x, residual, other_residual)


def final_kernel(count, base, vectors, *refs):
    own, other, (out, stacks) = refs[:count], refs[count:-2], refs[-2:]
    step = out.shape[0]
    first = pl.program_id(0) * step

    @pl.when(first == 0)
    def _():
        group = lax.axis_index("groups")
        place_pieces([join_halves(a[...], b[...], group) for a, b in zip(own, other)], stacks)

    for index in range(step):
        out[index] = base[first + index] + expand(first + index, vectors, stacks)


def final(base, own, other, vectors):
    sites, rows, lanes = base.shape
    number = vectors.shape[-1]
    step = 2
    return pl.pallas_call(
        functools.partial(final_kernel, len(own)),
        grid=(sites // step,),
        out_shape=jax.ShapeDtypeStruct(base.shape, F32),
        in_specs=vmem(2 + len(own) + len(other)),
        out_specs=pl.BlockSpec((step, rows, lanes), lambda s: (s, 0, 0)),
        scratch_shapes=[pltpu.VMEM((2 * number, 2 * lanes), BF16)],
        compiler_params=params(),
        cost_estimate=cost(2e9, 8e6),
        name="final",
    )(base, vectors, *own, *other)


def shifted(value, axis, step):
    count = lax.axis_size(axis)
    return lax.ppermute(value, axis, [(i, (i + step) % count) for i in range(count)])


def crossed(value, axis, mask):
    count = lax.axis_size(axis)
    return lax.ppermute(value, axis, [(i, i ^ mask) for i in range(count)])


def faces_of(x):
    backward_t = shifted(x, "tm", 1)
    forward_t = shifted(x, "tm", -1)
    backward_z = shifted(x, "space", 1)
    forward_z = shifted(x, "space", -1)
    return forward_z, backward_z, forward_t, backward_t


def halving(keep, send):
    count = lax.axis_size("space")
    mask = 1
    while True:
        received = crossed(send, "space", mask)
        mask *= 2
        if mask >= count:
            return add(keep, received)
        keep, send = add_split(keep, received)


def doubling(pieces, mask):
    while mask:
        if len(pieces) > 2:
            pieces = [jnp.concatenate(pieces, axis=0)]
        pieces = pieces + [crossed(piece, "space", mask) for piece in pieces]
        mask //= 2
    return pieces


def both_doubling(part):
    groups, count = lax.axis_size("groups"), lax.axis_size("space")
    mask = count // 2
    pairs = [(g * count + s, (g ^ 1) * count + (s ^ mask)) for g in range(groups) for s in range(count)]
    across = lax.ppermute(part, ("groups", "space"), pairs)
    other = [crossed(part, "groups", 1), across]
    own = [part, crossed(part, "space", mask)]
    return doubling(own, mask // 2), doubling(other, mask // 2)


def over_time(part):
    count = lax.axis_size("tm")
    if count <= 4:
        return [part] + [shifted(part, "tm", step) for step in range(1, count)]
    mask = 1
    while mask < count:
        part = part + crossed(part, "tm", mask)
        mask *= 2
    return [part]


def shards(couplings, source, initial, vectors, inverse_eigen):
    directions = couplings.shape[0]
    ny, nx, rows, lanes = source.shape[2:]
    sites = ny * nx
    number = vectors.shape[0]
    blocks = lax.axis_size("space")

    x = pack(initial.reshape(sites, rows, lanes))
    faces = faces_of(x)
    matrices = couplings.reshape(directions, sites, rows, couplings.shape[-1])
    rest, half_source, local, halo = first_local(x, source.reshape(sites, rows, lanes), matrices, ny, nx)
    across = jnp.transpose(vectors, (1, 2, 3, 4, 5, 0)).reshape(sites * vectors.shape[-1], number)
    by_rows, by_columns = vectors_parts(across, sites)
    eigen = eigen_of(inverse_eigen, number // blocks, lanes // 2)

    for sweep in range(ITERS):
        last = sweep == ITERS - 1
        if sweep:
            faces = faces_of(x)
            if last:
                other_x = crossed(x, "groups", 1)
            rest = local_part(x, half_source, local, ny, nx)
        forward_z, backward_z, forward_t, backward_t = faces
        rest = z_faces(rest, forward_z, backward_z, halo)
        if sweep and last:
            rest, other_x = lax.optimization_barrier((rest, other_x))
        rest = backward_face(rest, backward_t, halo)
        residual, keep, send = forward_face(rest, forward_t, halo, by_rows)
        part = halving(keep, send)
        if last:
            part, residual = lax.optimization_barrier((part, residual))
            other_residual = crossed(residual, "groups", 1)
        parts = over_time(part)
        if last:
            parts, other_residual = lax.optimization_barrier((parts, other_residual))
        d = scale(eigen, parts)
        if not last:
            x = update(x, residual, doubling([d], blocks // 2), by_columns)
    base, full_residual = join(x, other_x, residual, other_residual)
    whole = final(base, *both_doubling(d), by_columns)
    shape = source.shape
    return whole.reshape(shape), full_residual.reshape(shape)


def solution(mesh):
    in_specs = (
        P(None, "tm", "space", None, None, None, None),
        P("tm", "space", None, None, None, None),
        P("tm", "space", None, None, None, None),
        P(None, "tm", "space", None, None, None),
        P(),
    )
    out_specs = (
        P(("groups", "tm"), "space", None, None, None, None),
        P(("groups", "tm"), "space", None, None, None, None),
    )
    return jax.shard_map(shards, mesh=mesh, in_specs=in_specs, out_specs=out_specs, check_vma=False)
```

```python
import functools

import jax
import jax.numpy as jnp
from jax import lax
from jax.experimental import pallas as pl
from jax.experimental.pallas import tpu as pltpu
from jax.sharding import PartitionSpec as P

ITERS = 2
F32 = jnp.float32
BF16 = jnp.bfloat16
LOCAL = 5


def params(mebibytes=12):
    return pltpu.CompilerParams(vmem_limit_bytes=mebibytes * 1024 * 1024)


def cost(flops, read):
    return pl.CostEstimate(flops=int(flops), bytes_accessed=int(read), transcendentals=0)


def low_lanes(value):
    lanes = lax.broadcasted_iota(jnp.int32, value.shape, value.ndim - 1)
    return lanes < value.shape[-1] // 2


def swap(value):
    return pltpu.roll(value, value.shape[-1] // 2, value.ndim - 1)


def turned(value):
    moved = swap(value)
    return jnp.where(low_lanes(value), -moved, moved)


def high_low(value):
    high = value.astype(BF16)
    low = (value - high.astype(F32)).astype(BF16)
    return high, low


def stack(value, sign):
    high, low = high_low(jnp.concatenate([value, sign * turned(value)], axis=0))
    return jnp.concatenate([high, low], axis=1)


def matmul(left, right):
    return jnp.dot(left, right, preferred_element_type=F32)


def fold(product):
    rows, lanes = product.shape[0] // 2, product.shape[1] // 2
    high = product[:rows, :lanes] + (product[:rows, lanes:] + product[rows:, :lanes])
    return high + product[rows:, lanes:]


def pick_half(value, group):
    middle = value.shape[-1] // 2
    real, imag = value[:, :middle], value[:, middle:]
    low = low_lanes(real)
    first = jnp.where(low, real, swap(imag))
    second = jnp.where(low, swap(real), imag)
    return jnp.where(group == 0, first, second)


def join_halves(own, other, group):
    first = jnp.where(group == 0, own, other)
    second = jnp.where(group == 0, other, own)
    low = low_lanes(own)
    real = jnp.where(low, first, swap(second))
    imag = jnp.where(low, swap(first), second)
    return jnp.concatenate([real, imag], axis=1)


def vmem(count):
    return [pl.BlockSpec(memory_space=pltpu.VMEM)] * count


def in_hbm(value):
    return pltpu.with_memory_space_constraint(value, pltpu.HBM)


def pack_kernel(full, half):
    group = lax.axis_index("groups")
    for site in range(full.shape[0]):
        half[site] = pick_half(full[site], group)


def pack(full):
    sites, rows, lanes = full.shape
    return pl.pallas_call(
        pack_kernel,
        out_shape=pltpu.VMEM((sites, rows, lanes // 2), F32),
        in_specs=vmem(1),
        out_specs=vmem(1)[0],
        compiler_params=params(),
        cost_estimate=cost(1e6, 1e6),
        name="pack",
    )(full)


def around(site, ny, nx):
    y, x = site // nx, lax.rem(site, nx)
    right, left = lax.rem(x + 1, nx), lax.rem(x + nx - 1, nx)
    up, down = lax.rem(y + 1, ny), lax.rem(y + ny - 1, ny)
    return (site, y * nx + right, y * nx + left, up * nx + x, down * nx + x)


def local_sum(site, ny, nx, x_ref, stacks, matrix):
    @pl.when(site == 0)
    def _():
        for each in range(ny * nx):
            stacks[each] = stack(x_ref[each], 1.0)

    total = None
    for direction, neighbour in enumerate(around(site, ny, nx)):
        term = matmul(matrix(direction), stacks[neighbour])
        total = term if total is None else total + term
    return fold(total)


def first_kernel(ny, nx, x_ref, source, couplings, rest, half_source, local, halo, stacks):
    site = pl.program_id(0)
    own = pick_half(source[0], lax.axis_index("groups"))
    half_source[0] = own
    for direction in range(couplings.shape[0]):
        high, low = high_low(couplings[direction, 0])
        both = jnp.concatenate([high, low], axis=0)
        if direction < LOCAL:
            local[direction, 0] = both
        else:
            halo[direction - LOCAL, 0] = both
    rest[0] = own - local_sum(site, ny, nx, x_ref, stacks, lambda d: local[d, 0])


def first_local(x, source, couplings, ny, nx):
    sites, rows, lanes = x.shape
    directions, _, _, columns = couplings.shape
    outer = directions - LOCAL
    return pl.pallas_call(
        functools.partial(first_kernel, ny, nx),
        grid=(sites,),
        out_shape=(
            pltpu.VMEM(x.shape, F32),
            pltpu.VMEM(x.shape, F32),
            pltpu.VMEM((LOCAL, sites, 2 * rows, columns), BF16),
            pltpu.VMEM((outer, sites, 2 * rows, columns), BF16),
        ),
        in_specs=[
            pl.BlockSpec((sites, rows, lanes), lambda s: (0, 0, 0)),
            pl.BlockSpec((1, rows, 2 * lanes), lambda s: (s, 0, 0)),
            pl.BlockSpec((directions, 1, rows, columns), lambda s: (0, s, 0, 0)),
        ],
        out_specs=(
            pl.BlockSpec((1, rows, lanes), lambda s: (s, 0, 0)),
            pl.BlockSpec((1, rows, lanes), lambda s: (s, 0, 0)),
            pl.BlockSpec((LOCAL, 1, 2 * rows, columns), lambda s: (0, s, 0, 0)),
            pl.BlockSpec((outer, 1, 2 * rows, columns), lambda s: (0, s, 0, 0)),
        ),
        scratch_shapes=[pltpu.VMEM((sites, 2 * rows, 2 * lanes), BF16)],
        compiler_params=params(),
        cost_estimate=cost(1e11, 16e6),
        name="first_local",
    )(x, in_hbm(source), in_hbm(couplings))


def local_kernel(ny, nx, x_ref, source, local, rest, stacks):
    site = pl.program_id(0)
    rest[0] = source[0] - local_sum(site, ny, nx, x_ref, stacks, lambda d: local[d, 0])


def local_part(x, source, local, ny, nx):
    sites, rows, lanes = x.shape
    columns = local.shape[-1]
    return pl.pallas_call(
        functools.partial(local_kernel, ny, nx),
        grid=(sites,),
        out_shape=pltpu.VMEM(x.shape, F32),
        in_specs=[
            pl.BlockSpec((sites, rows, lanes), lambda s: (0, 0, 0)),
            pl.BlockSpec((1, rows, lanes), lambda s: (s, 0, 0)),
            pl.BlockSpec((LOCAL, 1, 2 * rows, columns), lambda s: (0, s, 0, 0)),
        ],
        out_specs=pl.BlockSpec((1, rows, lanes), lambda s: (s, 0, 0)),
        scratch_shapes=[pltpu.VMEM((sites, 2 * rows, 2 * lanes), BF16)],
        compiler_params=params(),
        cost_estimate=cost(1e11, 8e6),
        name="local_part",
    )(x, source, local)


def block_order(count):
    bits = count.bit_length() - 1
    return [int(format(index, "b").zfill(bits)[::-1], 2) if bits else 0 for index in range(count)]


def block_starts(size):
    space = lax.axis_index("space")
    return [pl.multiple_of((space ^ block) * size, size) for block in block_order(lax.axis_size("space"))]


def vectors_kernel(across, by_rows, by_columns):
    sites, _, double, number = by_columns.shape
    rows = double // 2
    high, low = high_low(across[...].T)
    by_rows[:number] = high
    by_rows[number:] = low
    for site in range(sites):
        for half in range(2):
            start = (2 * site + half) * rows
            high, low = high_low(across[start : start + rows])
            by_columns[site, half, :rows] = high
            by_columns[site, half, rows:] = low


def vectors_parts(across, sites):
    width, number = across.shape
    rows = width // sites // 2
    step = 2
    return pl.pallas_call(
        vectors_kernel,
        grid=(sites // step,),
        out_shape=(pltpu.VMEM((2 * number, width), BF16), pltpu.VMEM((sites, 2, 2 * rows, number), BF16)),
        in_specs=[pl.BlockSpec((step * 2 * rows, number), lambda s: (s, 0))],
        out_specs=(
            pl.BlockSpec((2 * number, step * 2 * rows), lambda s: (0, s)),
            pl.BlockSpec((step, 2, 2 * rows, number), lambda s: (s, 0, 0, 0)),
        ),
        compiler_params=params(16),
        cost_estimate=cost(1e6, 9e6),
        name="vectors_parts",
    )(in_hbm(across))


def eigen_kernel(inverse, out):
    size, lanes = out.shape[1:]
    number = inverse.shape[1]
    start = lax.axis_index("space") * size
    row = lax.broadcasted_iota(jnp.int32, (size, number), 0) + start
    chosen = lax.broadcasted_iota(jnp.int32, (size, number), 1) == row
    for part in range(2):
        value = jnp.where(chosen, inverse[part : part + 1], 0.0)
        out[part] = jnp.broadcast_to(jnp.sum(value, axis=1, keepdims=True), (size, lanes))


def eigen_of(inverse, size, lanes):
    return pl.pallas_call(
        eigen_kernel,
        out_shape=pltpu.VMEM((2, size, lanes), F32),
        in_specs=vmem(1),
        out_specs=vmem(1)[0],
        compiler_params=params(),
        cost_estimate=cost(1e6, 1e6),
        name="eigen",
    )(inverse)


def apply_faces(site, faces, matrices):
    summed = None
    for face, matrix in zip(faces, matrices):
        term = matmul(matrix[site], stack(face(site), 1.0))
        summed = term if summed is None else summed + term
    return fold(summed)


def z_faces_kernel(rest, forward, backward, matrix, out):
    faces = (lambda s: forward[s], lambda s: backward[s])
    for site in range(rest.shape[0]):
        out[site] = rest[site] - apply_faces(site, faces, (matrix.at[0], matrix.at[1]))


def z_faces(rest, forward, backward, matrix):
    return pl.pallas_call(
        z_faces_kernel,
        out_shape=pltpu.VMEM(rest.shape, F32),
        in_specs=vmem(4),
        out_specs=vmem(1)[0],
        compiler_params=params(),
        cost_estimate=cost(1e9, 4e6),
        name="z_faces",
    )(rest, forward, backward, matrix)


def edge_sign(last):
    count = lax.axis_size("tm")
    return jnp.where(lax.axis_index("tm") == (count - 1 if last else 0), -1.0, 1.0).astype(F32)


def backward_kernel(rest, backward, matrix, out):
    sign = edge_sign(False)
    for site in range(rest.shape[0]):
        out[site] = rest[site] - apply_faces(site, (lambda s: sign * backward[s],), (matrix.at[3],))


def backward_face(rest, backward, matrix):
    return pl.pallas_call(
        backward_kernel,
        out_shape=pltpu.VMEM(rest.shape, F32),
        in_specs=vmem(3),
        out_specs=vmem(1)[0],
        compiler_params=params(),
        cost_estimate=cost(1e9, 4e6),
        name="backward_face",
    )(rest, backward, matrix)


def forward_kernel(rest, forward, matrix, vectors, residual, keep, send, stacks, whole):
    sign = edge_sign(True)
    rows = 2 * rest.shape[1]
    for site in range(rest.shape[0]):
        own = rest[site] - apply_faces(site, (lambda s: sign * forward[s],), (matrix.at[2],))
        residual[site] = own
        stacks[site * rows : (site + 1) * rows] = stack(own, -1.0)
    whole[...] = fold(matmul(vectors[...], stacks[...]))
    starts = block_starts(whole.shape[0] // lax.axis_size("space"))
    half = len(starts) // 2
    size = whole.shape[0] // len(starts)
    for index, start in enumerate(starts):
        part, at = (keep, index) if index < half else (send, index - half)
        part[at * size : (at + 1) * size] = whole[pl.ds(start, size)]


def forward_face(rest, forward, matrix, vectors):
    sites, rows, lanes = rest.shape
    part = pltpu.VMEM((vectors.shape[0] // 4, lanes), F32)
    return pl.pallas_call(
        forward_kernel,
        out_shape=(pltpu.VMEM(rest.shape, F32), part, part),
        in_specs=vmem(4),
        out_specs=tuple(vmem(3)),
        scratch_shapes=[
            pltpu.VMEM((sites * 2 * rows, 2 * lanes), BF16),
            pltpu.VMEM((vectors.shape[0] // 2, lanes), F32),
        ],
        compiler_params=params(),
        cost_estimate=cost(2e9, 8e6),
        name="forward_face",
    )(rest, forward, matrix, vectors)


def split_kernel(keep, received, next_keep, next_send):
    half = next_keep.shape[0]
    next_keep[...] = keep[:half] + received[:half]
    next_send[...] = keep[half:] + received[half:]


def add_split(keep, received):
    rows, lanes = keep.shape
    part = pltpu.VMEM((rows // 2, lanes), F32)
    return pl.pallas_call(
        split_kernel,
        out_shape=(part, part),
        in_specs=vmem(2),
        out_specs=tuple(vmem(2)),
        compiler_params=params(),
        name="add_split",
    )(keep, received)


def add_kernel(left, right, out):
    out[...] = left[...] + right[...]


def add(left, right):
    return pl.pallas_call(
        add_kernel,
        out_shape=pltpu.VMEM(left.shape, F32),
        in_specs=vmem(2),
        out_specs=vmem(1)[0],
        compiler_params=params(),
        name="add",
    )(left, right)


def scale_kernel(eigen, *refs):
    parts, out = refs[:-1], refs[-1]
    total = parts[0][...]
    for part in parts[1:]:
        total = total + part[...]
    out[...] = eigen[0] * total + eigen[1] * turned(total)


def scale(eigen, parts):
    return pl.pallas_call(
        scale_kernel,
        out_shape=pltpu.VMEM(parts[0].shape, F32),
        in_specs=vmem(1 + len(parts)),
        out_specs=vmem(1)[0],
        compiler_params=params(),
        name="scale",
    )(eigen, *parts)


def expand(site, vectors, stacks):
    number = vectors.shape[3]
    total = None
    for half in range(2):
        term = matmul(vectors[site, half], stacks[half * number : (half + 1) * number])
        total = term if total is None else total + term
    return fold(total)


def place_pieces(values, stacks):
    number = stacks.shape[0] // 2
    size = number // lax.axis_size("space")
    starts = iter(block_starts(size))
    for value in values:
        both = stack(value, 1.0)
        rows = value.shape[0]
        for at in range(0, rows, size):
            start = next(starts)
            stacks[pl.ds(start, size)] = both[at : at + size]
            stacks[pl.ds(start + number, size)] = both[rows + at : rows + at + size]


def update_kernel(x, residual, vectors, *refs):
    pieces, (out, stacks) = refs[:-2], refs[-2:]
    place_pieces([piece[...] for piece in pieces], stacks)
    for site in range(x.shape[0]):
        out[site] = x[site] + 0.5 * residual[site] + expand(site, vectors, stacks)


def update(x, residual, pieces, vectors):
    number = vectors.shape[-1]
    return pl.pallas_call(
        update_kernel,
        out_shape=pltpu.VMEM(x.shape, F32),
        in_specs=vmem(3 + len(pieces)),
        out_specs=vmem(1)[0],
        scratch_shapes=[pltpu.VMEM((2 * number, 2 * x.shape[-1]), BF16)],
        compiler_params=params(),
        cost_estimate=cost(1e9, 8e6),
        name="update",
    )(x, residual, vectors, *pieces)


def join_kernel(x, other_x, residual, other_residual, base, full):
    group = lax.axis_index("groups")
    for site in range(x.shape[0]):
        own = x[site] + 0.5 * residual[site]
        other = other_x[site] + 0.5 * other_residual[site]
        base[site] = join_halves(own, other, group)
        full[site] = join_halves(residual[site], other_residual[site], group)


def join(x, other_x, residual, other_residual):
    sites, rows, lanes = x.shape
    shape = (sites, rows, 2 * lanes)
    return pl.pallas_call(
        join_kernel,
        out_shape=(pltpu.VMEM(shape, F32), jax.ShapeDtypeStruct(shape, F32)),
        in_specs=vmem(4),
        out_specs=tuple(vmem(2)),
        compiler_params=params(),
        cost_estimate=cost(1e6, 4e6),
        name="join",
    )(x, other_x, residual, other_residual)


def final_kernel(count, base, vectors, *refs):
    own, other, (out, stacks) = refs[:count], refs[count:-2], refs[-2:]
    step, _, lanes = out.shape
    first = pl.program_id(0) * step

    @pl.when(first == 0)
    def _():
        group = lax.axis_index("groups")
        place_pieces([join_halves(a[...], b[...], group) for a, b in zip(own, other)], stacks)

    number, rows = vectors.shape[3], out.shape[1]
    for index in range(step):
        total = base[first + index]
        for half in range(2):
            left = vectors[first + index, half]
            right = stacks[half * number : (half + 1) * number]
            total = total + (matmul(left[:rows], right[:, :lanes]) + (matmul(left[:rows], right[:, lanes:]) + matmul(left[rows:], right[:, :lanes])))
        out[index] = total


def final(base, own, other, vectors):
    sites, rows, lanes = base.shape
    number = vectors.shape[-1]
    step = 2
    return pl.pallas_call(
        functools.partial(final_kernel, len(own)),
        grid=(sites // step,),
        out_shape=jax.ShapeDtypeStruct(base.shape, F32),
        in_specs=vmem(2 + len(own) + len(other)),
        out_specs=pl.BlockSpec((step, rows, lanes), lambda s: (s, 0, 0)),
        scratch_shapes=[pltpu.VMEM((2 * number, 2 * lanes), BF16)],
        compiler_params=params(),
        cost_estimate=cost(2e9, 8e6),
        name="final",
    )(base, vectors, *own, *other)


def shifted(value, axis, step):
    count = lax.axis_size(axis)
    return lax.ppermute(value, axis, [(i, (i + step) % count) for i in range(count)])


def crossed(value, axis, mask):
    count = lax.axis_size(axis)
    return lax.ppermute(value, axis, [(i, i ^ mask) for i in range(count)])


def faces_of(x):
    backward_t = shifted(x, "tm", 1)
    forward_t = shifted(x, "tm", -1)
    backward_z = shifted(x, "space", 1)
    forward_z = shifted(x, "space", -1)
    return forward_z, backward_z, forward_t, backward_t


def halving(keep, send):
    count = lax.axis_size("space")
    mask = 1
    while True:
        received = crossed(send, "space", mask)
        mask *= 2
        if mask >= count:
            return add(keep, received)
        keep, send = add_split(keep, received)


def doubling(pieces, mask):
    while mask:
        if len(pieces) > 2:
            pieces = [jnp.concatenate(pieces, axis=0)]
        pieces = pieces + [crossed(piece, "space", mask) for piece in pieces]
        mask //= 2
    return pieces


def across_groups(part, mask):
    groups, count = lax.axis_size("groups"), lax.axis_size("space")
    pairs = [(g * count + s, (g ^ 1) * count + (s ^ mask)) for g in range(groups) for s in range(count)]
    return [crossed(part, "groups", 1), lax.ppermute(part, ("groups", "space"), pairs)]


def over_time(part):
    count = lax.axis_size("tm")
    if count <= 4:
        return [part] + [crossed(part, "tm", mask) for mask in range(1, count)]
    mask = 1
    while mask < count:
        part = part + crossed(part, "tm", mask)
        mask *= 2
    return [part]


def shards(couplings, source, initial, vectors, inverse_eigen):
    directions = couplings.shape[0]
    ny, nx, rows, lanes = source.shape[2:]
    sites = ny * nx
    number = vectors.shape[0]
    blocks = lax.axis_size("space")

    x = pack(initial.reshape(sites, rows, lanes))
    faces = faces_of(x)
    matrices = couplings.reshape(directions, sites, rows, couplings.shape[-1])
    rest, half_source, local, halo = first_local(x, source.reshape(sites, rows, lanes), matrices, ny, nx)
    across = jnp.transpose(vectors, (1, 2, 3, 4, 5, 0)).reshape(sites * vectors.shape[-1], number)
    by_rows, by_columns = vectors_parts(across, sites)
    eigen = eigen_of(inverse_eigen, number // blocks, lanes // 2)

    for sweep in range(ITERS):
        last = sweep == ITERS - 1
        if sweep:
            faces = faces_of(x)
            if last:
                other_x = crossed(x, "groups", 1)
            rest = local_part(x, half_source, local, ny, nx)
        forward_z, backward_z, forward_t, backward_t = faces
        rest = backward_face(rest, backward_t, halo)
        rest = z_faces(rest, forward_z, backward_z, halo)
        if sweep and last:
            rest, other_x = lax.optimization_barrier((rest, other_x))
        residual, keep, send = forward_face(rest, forward_t, halo, by_rows)
        part = halving(keep, send)
        if last:
            part, residual = lax.optimization_barrier((part, residual))
            other_residual = crossed(residual, "groups", 1)
        parts = over_time(part)
        if last:
            parts, other_residual = lax.optimization_barrier((parts, other_residual))
        d = scale(eigen, parts)
        if not last:
            x = update(x, residual, doubling([d], blocks // 2), by_columns)
    base, full_residual = join(x, other_x, residual, other_residual)
    mask = blocks // 2
    other = across_groups(d, mask)
    own = [d, crossed(d, "space", mask)]
    other[1], base = lax.optimization_barrier((other[1], base))
    whole = final(base, doubling(own, mask // 2), doubling(other, mask // 2), by_columns)
    shape = source.shape
    return whole.reshape(shape), full_residual.reshape(shape)


def solution(mesh):
    in_specs = (
        P(None, "tm", "space", None, None, None, None),
        P("tm", "space", None, None, None, None),
        P("tm", "space", None, None, None, None),
        P(None, "tm", "space", None, None, None),
        P(),
    )
    out_specs = (
        P(("groups", "tm"), "space", None, None, None, None),
        P(("groups", "tm"), "space", None, None, None, None),
    )
    return jax.shard_map(shards, mesh=mesh, in_specs=in_specs, out_specs=out_specs, check_vma=False)
```

```python
import functools

import jax
import jax.numpy as jnp
from jax import lax
from jax.experimental import pallas as pl
from jax.experimental.pallas import tpu as pltpu
from jax.sharding import PartitionSpec as P

ITERS = 2
F32 = jnp.float32
BF16 = jnp.bfloat16
LOCAL = 5


def params(mebibytes=12):
    return pltpu.CompilerParams(vmem_limit_bytes=mebibytes * 1024 * 1024)


def cost(flops, read):
    return pl.CostEstimate(flops=int(flops), bytes_accessed=int(read), transcendentals=0)


def low_lanes(value):
    lanes = lax.broadcasted_iota(jnp.int32, value.shape, value.ndim - 1)
    return lanes < value.shape[-1] // 2


def swap(value):
    return pltpu.roll(value, value.shape[-1] // 2, value.ndim - 1)


def turned(value):
    moved = swap(value)
    return jnp.where(low_lanes(value), -moved, moved)


def high_low(value):
    high = value.astype(BF16)
    low = (value - high.astype(F32)).astype(BF16)
    return high, low


def stack(value, sign):
    high, low = high_low(jnp.concatenate([value, sign * turned(value)], axis=0))
    return jnp.concatenate([high, low], axis=1)


def matmul(left, right):
    return jnp.dot(left, right, preferred_element_type=F32)


def fold(product):
    rows, lanes = product.shape[0] // 2, product.shape[1] // 2
    high = product[:rows, :lanes] + (product[:rows, lanes:] + product[rows:, :lanes])
    return high + product[rows:, lanes:]


def pick_half(value, group):
    middle = value.shape[-1] // 2
    real, imag = value[:, :middle], value[:, middle:]
    low = low_lanes(real)
    first = jnp.where(low, real, swap(imag))
    second = jnp.where(low, swap(real), imag)
    return jnp.where(group == 0, first, second)


def join_halves(own, other, group):
    first = jnp.where(group == 0, own, other)
    second = jnp.where(group == 0, other, own)
    low = low_lanes(own)
    real = jnp.where(low, first, swap(second))
    imag = jnp.where(low, swap(first), second)
    return jnp.concatenate([real, imag], axis=1)


def vmem(count):
    return [pl.BlockSpec(memory_space=pltpu.VMEM)] * count


def in_hbm(value):
    return pltpu.with_memory_space_constraint(value, pltpu.HBM)


def pack_kernel(full, half):
    group = lax.axis_index("groups")
    for site in range(full.shape[0]):
        half[site] = pick_half(full[site], group)


def pack(full):
    sites, rows, lanes = full.shape
    return pl.pallas_call(
        pack_kernel,
        out_shape=pltpu.VMEM((sites, rows, lanes // 2), F32),
        in_specs=vmem(1),
        out_specs=vmem(1)[0],
        compiler_params=params(),
        cost_estimate=cost(1e6, 1e6),
        name="pack",
    )(full)


def around(site, ny, nx):
    y, x = site // nx, lax.rem(site, nx)
    right, left = lax.rem(x + 1, nx), lax.rem(x + nx - 1, nx)
    up, down = lax.rem(y + 1, ny), lax.rem(y + ny - 1, ny)
    return (site, y * nx + right, y * nx + left, up * nx + x, down * nx + x)


def local_sum(site, ny, nx, x_ref, stacks, matrix):
    @pl.when(site == 0)
    def _():
        for each in range(ny * nx):
            stacks[each] = stack(x_ref[each], 1.0)

    total = None
    for direction, neighbour in enumerate(around(site, ny, nx)):
        term = matmul(matrix(direction), stacks[neighbour])
        total = term if total is None else total + term
    return fold(total)


def first_kernel(ny, nx, x_ref, source, couplings, rest, half_source, local, halo, stacks):
    site = pl.program_id(0)
    own = pick_half(source[0], lax.axis_index("groups"))
    half_source[0] = own
    for direction in range(couplings.shape[0]):
        high, low = high_low(couplings[direction, 0])
        both = jnp.concatenate([high, low], axis=0)
        if direction < LOCAL:
            local[direction, 0] = both
        else:
            halo[direction - LOCAL, 0] = both
    rest[0] = own - local_sum(site, ny, nx, x_ref, stacks, lambda d: local[d, 0])


def first_local(x, source, couplings, ny, nx):
    sites, rows, lanes = x.shape
    directions, _, _, columns = couplings.shape
    outer = directions - LOCAL
    return pl.pallas_call(
        functools.partial(first_kernel, ny, nx),
        grid=(sites,),
        out_shape=(
            pltpu.VMEM(x.shape, F32),
            pltpu.VMEM(x.shape, F32),
            pltpu.VMEM((LOCAL, sites, 2 * rows, columns), BF16),
            pltpu.VMEM((outer, sites, 2 * rows, columns), BF16),
        ),
        in_specs=[
            pl.BlockSpec((sites, rows, lanes), lambda s: (0, 0, 0)),
            pl.BlockSpec((1, rows, 2 * lanes), lambda s: (s, 0, 0)),
            pl.BlockSpec((directions, 1, rows, columns), lambda s: (0, s, 0, 0)),
        ],
        out_specs=(
            pl.BlockSpec((1, rows, lanes), lambda s: (s, 0, 0)),
            pl.BlockSpec((1, rows, lanes), lambda s: (s, 0, 0)),
            pl.BlockSpec((LOCAL, 1, 2 * rows, columns), lambda s: (0, s, 0, 0)),
            pl.BlockSpec((outer, 1, 2 * rows, columns), lambda s: (0, s, 0, 0)),
        ),
        scratch_shapes=[pltpu.VMEM((sites, 2 * rows, 2 * lanes), BF16)],
        compiler_params=params(),
        cost_estimate=cost(8e9, 16e6),
        name="first_local",
    )(x, in_hbm(source), in_hbm(couplings))


def local_kernel(ny, nx, x_ref, source, local, rest, stacks):
    site = pl.program_id(0)
    rest[0] = source[0] - local_sum(site, ny, nx, x_ref, stacks, lambda d: local[d, 0])


def local_part(x, source, local, ny, nx):
    sites, rows, lanes = x.shape
    columns = local.shape[-1]
    return pl.pallas_call(
        functools.partial(local_kernel, ny, nx),
        grid=(sites,),
        out_shape=pltpu.VMEM(x.shape, F32),
        in_specs=[
            pl.BlockSpec((sites, rows, lanes), lambda s: (0, 0, 0)),
            pl.BlockSpec((1, rows, lanes), lambda s: (s, 0, 0)),
            pl.BlockSpec((LOCAL, 1, 2 * rows, columns), lambda s: (0, s, 0, 0)),
        ],
        out_specs=pl.BlockSpec((1, rows, lanes), lambda s: (s, 0, 0)),
        scratch_shapes=[pltpu.VMEM((sites, 2 * rows, 2 * lanes), BF16)],
        compiler_params=params(),
        cost_estimate=cost(8e9, 8e6),
        name="local_part",
    )(x, source, local)


def block_order(count):
    bits = count.bit_length() - 1
    return [int(format(index, "b").zfill(bits)[::-1], 2) if bits else 0 for index in range(count)]


def block_starts(size):
    space = lax.axis_index("space")
    return [pl.multiple_of((space ^ block) * size, size) for block in block_order(lax.axis_size("space"))]


def vectors_kernel(across, by_rows, by_columns):
    sites, _, double, number = by_columns.shape
    rows = double // 2
    high, low = high_low(across[...].T)
    by_rows[:number] = high
    by_rows[number:] = low
    for site in range(sites):
        for half in range(2):
            start = (2 * site + half) * rows
            high, low = high_low(across[start : start + rows])
            by_columns[site, half, :rows] = high
            by_columns[site, half, rows:] = low


def vectors_parts(across, sites):
    width, number = across.shape
    rows = width // sites // 2
    step = 2
    return pl.pallas_call(
        vectors_kernel,
        grid=(sites // step,),
        out_shape=(pltpu.VMEM((2 * number, width), BF16), pltpu.VMEM((sites, 2, 2 * rows, number), BF16)),
        in_specs=[pl.BlockSpec((step * 2 * rows, number), lambda s: (s, 0))],
        out_specs=(
            pl.BlockSpec((2 * number, step * 2 * rows), lambda s: (0, s)),
            pl.BlockSpec((step, 2, 2 * rows, number), lambda s: (s, 0, 0, 0)),
        ),
        compiler_params=params(16),
        cost_estimate=cost(1e6, 9e6),
        name="vectors_parts",
    )(in_hbm(across))


def eigen_kernel(inverse, out):
    size, lanes = out.shape[1:]
    number = inverse.shape[1]
    start = lax.axis_index("space") * size
    row = lax.broadcasted_iota(jnp.int32, (size, number), 0) + start
    chosen = lax.broadcasted_iota(jnp.int32, (size, number), 1) == row
    for part in range(2):
        value = jnp.where(chosen, inverse[part : part + 1], 0.0)
        out[part] = jnp.broadcast_to(jnp.sum(value, axis=1, keepdims=True), (size, lanes))


def eigen_of(inverse, size, lanes):
    return pl.pallas_call(
        eigen_kernel,
        out_shape=pltpu.VMEM((2, size, lanes), F32),
        in_specs=vmem(1),
        out_specs=vmem(1)[0],
        compiler_params=params(),
        cost_estimate=cost(1e6, 1e6),
        name="eigen",
    )(inverse)


def apply_faces(site, faces, matrices):
    summed = None
    for face, matrix in zip(faces, matrices):
        term = matmul(matrix[site], stack(face(site), 1.0))
        summed = term if summed is None else summed + term
    return fold(summed)


def z_faces_kernel(rest, forward, backward, matrix, out):
    faces = (lambda s: forward[s], lambda s: backward[s])
    for site in range(rest.shape[0]):
        out[site] = rest[site] - apply_faces(site, faces, (matrix.at[0], matrix.at[1]))


def z_faces(rest, forward, backward, matrix):
    return pl.pallas_call(
        z_faces_kernel,
        out_shape=pltpu.VMEM(rest.shape, F32),
        in_specs=vmem(4),
        out_specs=vmem(1)[0],
        compiler_params=params(),
        cost_estimate=cost(1e9, 4e6),
        name="z_faces",
    )(rest, forward, backward, matrix)


def edge_sign(last):
    count = lax.axis_size("tm")
    return jnp.where(lax.axis_index("tm") == (count - 1 if last else 0), -1.0, 1.0).astype(F32)


def backward_kernel(rest, backward, matrix, out):
    sign = edge_sign(False)
    for site in range(rest.shape[0]):
        out[site] = rest[site] - apply_faces(site, (lambda s: sign * backward[s],), (matrix.at[3],))


def backward_face(rest, backward, matrix):
    return pl.pallas_call(
        backward_kernel,
        out_shape=pltpu.VMEM(rest.shape, F32),
        in_specs=vmem(3),
        out_specs=vmem(1)[0],
        compiler_params=params(),
        cost_estimate=cost(1e9, 4e6),
        name="backward_face",
    )(rest, backward, matrix)


def forward_kernel(rest, forward, matrix, vectors, residual, keep, send, stacks, whole):
    sign = edge_sign(True)
    rows = 2 * rest.shape[1]
    for site in range(rest.shape[0]):
        own = rest[site] - apply_faces(site, (lambda s: sign * forward[s],), (matrix.at[2],))
        residual[site] = own
        stacks[site * rows : (site + 1) * rows] = stack(own, -1.0)
    whole[...] = fold(matmul(vectors[...], stacks[...]))
    starts = block_starts(whole.shape[0] // lax.axis_size("space"))
    half = len(starts) // 2
    size = whole.shape[0] // len(starts)
    for index, start in enumerate(starts):
        part, at = (keep, index) if index < half else (send, index - half)
        part[at * size : (at + 1) * size] = whole[pl.ds(start, size)]


def forward_face(rest, forward, matrix, vectors):
    sites, rows, lanes = rest.shape
    part = pltpu.VMEM((vectors.shape[0] // 4, lanes), F32)
    return pl.pallas_call(
        forward_kernel,
        out_shape=(pltpu.VMEM(rest.shape, F32), part, part),
        in_specs=vmem(4),
        out_specs=tuple(vmem(3)),
        scratch_shapes=[
            pltpu.VMEM((sites * 2 * rows, 2 * lanes), BF16),
            pltpu.VMEM((vectors.shape[0] // 2, lanes), F32),
        ],
        compiler_params=params(),
        cost_estimate=cost(2e9, 8e6),
        name="forward_face",
    )(rest, forward, matrix, vectors)


def split_kernel(keep, received, next_keep, next_send):
    half = next_keep.shape[0]
    next_keep[...] = keep[:half] + received[:half]
    next_send[...] = keep[half:] + received[half:]


def add_split(keep, received):
    rows, lanes = keep.shape
    part = pltpu.VMEM((rows // 2, lanes), F32)
    return pl.pallas_call(
        split_kernel,
        out_shape=(part, part),
        in_specs=vmem(2),
        out_specs=tuple(vmem(2)),
        compiler_params=params(),
        name="add_split",
    )(keep, received)


def add_kernel(left, right, out):
    out[...] = left[...] + right[...]


def add(left, right):
    return pl.pallas_call(
        add_kernel,
        out_shape=pltpu.VMEM(left.shape, F32),
        in_specs=vmem(2),
        out_specs=vmem(1)[0],
        compiler_params=params(),
        name="add",
    )(left, right)


def scale_kernel(eigen, *refs):
    parts, out = refs[:-1], refs[-1]
    total = parts[0][...]
    for part in parts[1:]:
        total = total + part[...]
    out[...] = eigen[0] * total + eigen[1] * turned(total)


def scale(eigen, parts):
    return pl.pallas_call(
        scale_kernel,
        out_shape=pltpu.VMEM(parts[0].shape, F32),
        in_specs=vmem(1 + len(parts)),
        out_specs=vmem(1)[0],
        compiler_params=params(),
        name="scale",
    )(eigen, *parts)


def expand(site, vectors, stacks):
    number = vectors.shape[3]
    total = None
    for half in range(2):
        term = matmul(vectors[site, half], stacks[half * number : (half + 1) * number])
        total = term if total is None else total + term
    return fold(total)


def place_pieces(values, stacks):
    number = stacks.shape[0] // 2
    size = number // lax.axis_size("space")
    starts = iter(block_starts(size))
    for value in values:
        both = stack(value, 1.0)
        rows = value.shape[0]
        for at in range(0, rows, size):
            start = next(starts)
            stacks[pl.ds(start, size)] = both[at : at + size]
            stacks[pl.ds(start + number, size)] = both[rows + at : rows + at + size]


def update_kernel(x, residual, vectors, *refs):
    pieces, (out, stacks) = refs[:-2], refs[-2:]
    place_pieces([piece[...] for piece in pieces], stacks)
    for site in range(x.shape[0]):
        out[site] = x[site] + 0.5 * residual[site] + expand(site, vectors, stacks)


def update(x, residual, pieces, vectors):
    number = vectors.shape[-1]
    return pl.pallas_call(
        update_kernel,
        out_shape=pltpu.VMEM(x.shape, F32),
        in_specs=vmem(3 + len(pieces)),
        out_specs=vmem(1)[0],
        scratch_shapes=[pltpu.VMEM((2 * number, 2 * x.shape[-1]), BF16)],
        compiler_params=params(),
        cost_estimate=cost(1e9, 8e6),
        name="update",
    )(x, residual, vectors, *pieces)


def join_kernel(own, other, out):
    group = lax.axis_index("groups")
    for site in range(own.shape[0]):
        out[site] = join_halves(own[site], other[site], group)


def join(own, other):
    sites, rows, lanes = own.shape
    return pl.pallas_call(
        join_kernel,
        out_shape=pltpu.VMEM((sites, rows, 2 * lanes), F32),
        in_specs=vmem(2),
        out_specs=vmem(1)[0],
        compiler_params=params(),
        cost_estimate=cost(1e6, 2e6),
        name="join",
    )(own, other)


def final_kernel(count, base, residual, other_residual, vectors, *refs):
    own, other = refs[:count], refs[count : 2 * count]
    out, full, stacks, held, held_full, sems = refs[2 * count :]
    group = lax.axis_index("groups")
    copies = []
    for site in range(base.shape[0]):
        held_full[site] = join_halves(residual[site], other_residual[site], group)
        copies.append(pltpu.make_async_copy(held_full.at[site], full.at[site], sems.at[0, site]))
        copies[-1].start()
    place_pieces([join_halves(a[...], b[...], group) for a, b in zip(own, other)], stacks)
    for site in range(base.shape[0]):
        held[site] = base[site] + 0.5 * held_full[site] + expand(site, vectors, stacks)
        copies.append(pltpu.make_async_copy(held.at[site], out.at[site], sems.at[1, site]))
        copies[-1].start()
    for copy in copies:
        copy.wait()


def final(base, residual, other_residual, own, other, vectors):
    sites, _, lanes = base.shape
    number = vectors.shape[-1]
    shape = jax.ShapeDtypeStruct(base.shape, F32)
    return pl.pallas_call(
        functools.partial(final_kernel, len(own)),
        out_shape=(shape, shape),
        in_specs=vmem(4 + len(own) + len(other)),
        out_specs=(pl.BlockSpec(memory_space=pl.ANY),) * 2,
        scratch_shapes=[
            pltpu.VMEM((2 * number, 2 * lanes), BF16),
            pltpu.VMEM(base.shape, F32),
            pltpu.VMEM(base.shape, F32),
            pltpu.SemaphoreType.DMA((2, sites)),
        ],
        compiler_params=params(),
        cost_estimate=cost(2e9, 8e6),
        name="final",
    )(base, residual, other_residual, vectors, *own, *other)


def shifted(value, axis, step):
    count = lax.axis_size(axis)
    return lax.ppermute(value, axis, [(i, (i + step) % count) for i in range(count)])


def crossed(value, axis, mask):
    count = lax.axis_size(axis)
    return lax.ppermute(value, axis, [(i, i ^ mask) for i in range(count)])


def faces_of(x):
    backward_t = shifted(x, "tm", 1)
    forward_t = shifted(x, "tm", -1)
    backward_z = shifted(x, "space", 1)
    forward_z = shifted(x, "space", -1)
    return forward_z, backward_z, forward_t, backward_t


def halving(keep, send):
    count = lax.axis_size("space")
    mask = 1
    while True:
        received = crossed(send, "space", mask)
        mask *= 2
        if mask >= count:
            return add(keep, received)
        keep, send = add_split(keep, received)


def doubling(pieces, mask):
    while mask:
        if len(pieces) > 2:
            pieces = [jnp.concatenate(pieces, axis=0)]
        pieces = pieces + [crossed(piece, "space", mask) for piece in pieces]
        mask //= 2
    return pieces


def across_groups(part, mask):
    groups, count = lax.axis_size("groups"), lax.axis_size("space")
    pairs = [(g * count + s, (g ^ 1) * count + (s ^ mask)) for g in range(groups) for s in range(count)]
    return [crossed(part, "groups", 1), lax.ppermute(part, ("groups", "space"), pairs)]


def over_time(part):
    count = lax.axis_size("tm")
    if count <= 4:
        return [part] + [crossed(part, "tm", mask) for mask in range(1, count)]
    mask = 1
    while mask < count:
        part = part + crossed(part, "tm", mask)
        mask *= 2
    return [part]


def shards(couplings, source, initial, vectors, inverse_eigen):
    directions = couplings.shape[0]
    ny, nx, rows, lanes = source.shape[2:]
    sites = ny * nx
    number = vectors.shape[0]
    blocks = lax.axis_size("space")

    x = pack(initial.reshape(sites, rows, lanes))
    faces = faces_of(x)
    matrices = couplings.reshape(directions, sites, rows, couplings.shape[-1])
    rest, half_source, local, halo = first_local(x, source.reshape(sites, rows, lanes), matrices, ny, nx)
    across = jnp.transpose(vectors, (1, 2, 3, 4, 5, 0)).reshape(sites * vectors.shape[-1], number)
    by_rows, by_columns = vectors_parts(across, sites)
    eigen = eigen_of(inverse_eigen, number // blocks, lanes // 2)

    for sweep in range(ITERS):
        last = sweep == ITERS - 1
        if sweep:
            faces = faces_of(x)
            if last:
                other_x = crossed(x, "groups", 1)
            rest = local_part(x, half_source, local, ny, nx)
        forward_z, backward_z, forward_t, backward_t = faces
        rest = backward_face(rest, backward_t, halo)
        rest = z_faces(rest, forward_z, backward_z, halo)
        if sweep and last:
            base, rest = lax.optimization_barrier((join(x, other_x), rest))
        residual, keep, send = forward_face(rest, forward_t, halo, by_rows)
        part = halving(keep, send)
        if last:
            part, residual = lax.optimization_barrier((part, residual))
            other_residual = crossed(residual, "groups", 1)
        parts = over_time(part)
        d = scale(eigen, parts)
        if not last:
            x = update(x, residual, doubling([d], blocks // 2), by_columns)
    mask = blocks // 2
    other = across_groups(d, mask)
    own = [d, crossed(d, "space", mask)]
    whole, full_residual = final(base, residual, other_residual, doubling(own, mask // 2), doubling(other, mask // 2), by_columns)
    shape = source.shape
    return whole.reshape(shape), full_residual.reshape(shape)


def solution(mesh):
    in_specs = (
        P(None, "tm", "space", None, None, None, None),
        P("tm", "space", None, None, None, None),
        P("tm", "space", None, None, None, None),
        P(None, "tm", "space", None, None, None),
        P(),
    )
    out_specs = (
        P(("groups", "tm"), "space", None, None, None, None),
        P(("groups", "tm"), "space", None, None, None, None),
    )
    return jax.shard_map(shards, mesh=mesh, in_specs=in_specs, out_specs=out_specs, check_vma=False)
```

```python
import functools

import jax
import jax.numpy as jnp
from jax import lax
from jax.experimental import pallas as pl
from jax.experimental.pallas import tpu as pltpu
from jax.sharding import PartitionSpec as P

ITERS = 2
F32 = jnp.float32
BF16 = jnp.bfloat16
LOCAL = 5


def params(mebibytes=12):
    return pltpu.CompilerParams(vmem_limit_bytes=mebibytes * 1024 * 1024)


def cost(flops, read):
    return pl.CostEstimate(flops=int(flops), bytes_accessed=int(read), transcendentals=0)


def low_lanes(value):
    lanes = lax.broadcasted_iota(jnp.int32, value.shape, value.ndim - 1)
    return lanes < value.shape[-1] // 2


def swap(value):
    return pltpu.roll(value, value.shape[-1] // 2, value.ndim - 1)


def turned(value):
    moved = swap(value)
    return jnp.where(low_lanes(value), -moved, moved)


def high_low(value):
    high = value.astype(BF16)
    low = (value - high.astype(F32)).astype(BF16)
    return high, low


def stack(value, sign):
    high, low = high_low(jnp.concatenate([value, sign * turned(value)], axis=0))
    return jnp.concatenate([high, low], axis=1)


def matmul(left, right):
    return jnp.dot(left, right, preferred_element_type=F32)


def fold(product):
    rows, lanes = product.shape[0] // 2, product.shape[1] // 2
    high = product[:rows, :lanes] + (product[:rows, lanes:] + product[rows:, :lanes])
    return high + product[rows:, lanes:]


def pick_half(value, group):
    middle = value.shape[-1] // 2
    real, imag = value[:, :middle], value[:, middle:]
    low = low_lanes(real)
    first = jnp.where(low, real, swap(imag))
    second = jnp.where(low, swap(real), imag)
    return jnp.where(group == 0, first, second)


def join_halves(own, other, group):
    first = jnp.where(group == 0, own, other)
    second = jnp.where(group == 0, other, own)
    low = low_lanes(own)
    real = jnp.where(low, first, swap(second))
    imag = jnp.where(low, swap(first), second)
    return jnp.concatenate([real, imag], axis=1)


def vmem(count):
    return [pl.BlockSpec(memory_space=pltpu.VMEM)] * count


def in_hbm(value):
    return pltpu.with_memory_space_constraint(value, pltpu.HBM)


def pack_kernel(full, half, held, sems):
    group = lax.axis_index("groups")
    copies = [pltpu.make_async_copy(full.at[site], held.at[site], sems.at[site]) for site in range(half.shape[0])]
    for copy in copies:
        copy.start()
    for site, copy in enumerate(copies):
        copy.wait()
        half[site] = pick_half(held[site], group)


def pack(full):
    sites, rows, lanes = full.shape
    return pl.pallas_call(
        pack_kernel,
        out_shape=pltpu.VMEM((sites, rows, lanes // 2), F32),
        in_specs=[pl.BlockSpec(memory_space=pl.ANY)],
        out_specs=vmem(1)[0],
        scratch_shapes=[pltpu.VMEM(full.shape, F32), pltpu.SemaphoreType.DMA((sites,))],
        compiler_params=params(),
        cost_estimate=cost(1e6, 1e6),
        name="pack",
    )(in_hbm(full))


def around(site, ny, nx):
    y, x = site // nx, lax.rem(site, nx)
    right, left = lax.rem(x + 1, nx), lax.rem(x + nx - 1, nx)
    up, down = lax.rem(y + 1, ny), lax.rem(y + ny - 1, ny)
    return (site, y * nx + right, y * nx + left, up * nx + x, down * nx + x)


def local_sum(site, ny, nx, x_ref, stacks, matrix):
    @pl.when(site == 0)
    def _():
        for each in range(ny * nx):
            stacks[each] = stack(x_ref[each], 1.0)

    total = None
    for direction, neighbour in enumerate(around(site, ny, nx)):
        term = matmul(matrix(direction), stacks[neighbour])
        total = term if total is None else total + term
    return fold(total)


def first_kernel(ny, nx, x_ref, source, couplings, rest, half_source, local, halo, stacks):
    site = pl.program_id(0)
    own = pick_half(source[0], lax.axis_index("groups"))
    half_source[0] = own
    for direction in range(couplings.shape[0]):
        high, low = high_low(couplings[direction, 0])
        both = jnp.concatenate([high, low], axis=0)
        if direction < LOCAL:
            local[direction, 0] = both
        else:
            halo[direction - LOCAL, 0] = both
    rest[0] = own - local_sum(site, ny, nx, x_ref, stacks, lambda d: local[d, 0])


def first_local(x, source, couplings, ny, nx):
    sites, rows, lanes = x.shape
    directions, _, _, columns = couplings.shape
    outer = directions - LOCAL
    return pl.pallas_call(
        functools.partial(first_kernel, ny, nx),
        grid=(sites,),
        out_shape=(
            pltpu.VMEM(x.shape, F32),
            pltpu.VMEM(x.shape, F32),
            pltpu.VMEM((LOCAL, sites, 2 * rows, columns), BF16),
            pltpu.VMEM((outer, sites, 2 * rows, columns), BF16),
        ),
        in_specs=[
            pl.BlockSpec((sites, rows, lanes), lambda s: (0, 0, 0)),
            pl.BlockSpec((1, rows, 2 * lanes), lambda s: (s, 0, 0)),
            pl.BlockSpec((directions, 1, rows, columns), lambda s: (0, s, 0, 0)),
        ],
        out_specs=(
            pl.BlockSpec((1, rows, lanes), lambda s: (s, 0, 0)),
            pl.BlockSpec((1, rows, lanes), lambda s: (s, 0, 0)),
            pl.BlockSpec((LOCAL, 1, 2 * rows, columns), lambda s: (0, s, 0, 0)),
            pl.BlockSpec((outer, 1, 2 * rows, columns), lambda s: (0, s, 0, 0)),
        ),
        scratch_shapes=[pltpu.VMEM((sites, 2 * rows, 2 * lanes), BF16)],
        compiler_params=params(),
        cost_estimate=cost(8e9, 16e6),
        name="first_local",
    )(x, in_hbm(source), in_hbm(couplings))


def local_kernel(ny, nx, x_ref, source, local, rest, stacks):
    site = pl.program_id(0)
    rest[0] = source[0] - local_sum(site, ny, nx, x_ref, stacks, lambda d: local[d, 0])


def local_part(x, source, local, ny, nx):
    sites, rows, lanes = x.shape
    columns = local.shape[-1]
    return pl.pallas_call(
        functools.partial(local_kernel, ny, nx),
        grid=(sites,),
        out_shape=pltpu.VMEM(x.shape, F32),
        in_specs=[
            pl.BlockSpec((sites, rows, lanes), lambda s: (0, 0, 0)),
            pl.BlockSpec((1, rows, lanes), lambda s: (s, 0, 0)),
            pl.BlockSpec((LOCAL, 1, 2 * rows, columns), lambda s: (0, s, 0, 0)),
        ],
        out_specs=pl.BlockSpec((1, rows, lanes), lambda s: (s, 0, 0)),
        scratch_shapes=[pltpu.VMEM((sites, 2 * rows, 2 * lanes), BF16)],
        compiler_params=params(),
        cost_estimate=cost(8e9, 8e6),
        name="local_part",
    )(x, source, local)


def block_order(count):
    bits = count.bit_length() - 1
    return [int(format(index, "b").zfill(bits)[::-1], 2) if bits else 0 for index in range(count)]


def ordered_rows(rows, chunk, taken):
    blocks = lax.axis_size("space")
    space = lax.axis_index("space")
    size = rows.shape[0] // blocks
    unit = min(size, taken)
    parts = []
    for start in range(chunk * taken, (chunk + 1) * taken, unit):
        block = space ^ block_order(blocks)[start // size]
        parts.append(rows[pl.ds(pl.multiple_of(block * size + start % size, unit), unit)])
    return parts[0] if len(parts) == 1 else jnp.concatenate(parts, axis=0)


def vectors_kernel(across, by_rows, by_columns, turned_rows):
    sites, _, double, number = by_columns.shape
    rows = double // 2
    taken = 128
    turned_rows[...] = across[...].T
    for chunk in range(number // taken):
        part = ordered_rows(turned_rows, chunk, taken)
        high, low = high_low(part)
        at = slice(chunk * taken, (chunk + 1) * taken)
        by_rows[at] = high
        by_rows[number + chunk * taken : number + (chunk + 1) * taken] = low
        back = part.T
        for site in range(sites):
            for half in range(2):
                start = (2 * site + half) * rows
                high, low = high_low(back[start : start + rows])
                by_columns[site, half, :rows, at] = high
                by_columns[site, half, rows:, at] = low


def vectors_parts(across, sites):
    width, number = across.shape
    rows = width // sites // 2
    step = 2
    return pl.pallas_call(
        vectors_kernel,
        grid=(sites // step,),
        out_shape=(pltpu.VMEM((2 * number, width), BF16), pltpu.VMEM((sites, 2, 2 * rows, number), BF16)),
        in_specs=[pl.BlockSpec((step * 2 * rows, number), lambda s: (s, 0))],
        out_specs=(
            pl.BlockSpec((2 * number, step * 2 * rows), lambda s: (0, s)),
            pl.BlockSpec((step, 2, 2 * rows, number), lambda s: (s, 0, 0, 0)),
        ),
        scratch_shapes=[pltpu.VMEM((number, step * 2 * rows), F32)],
        compiler_params=params(16),
        cost_estimate=cost(1e6, 9e6),
        name="vectors_parts",
    )(in_hbm(across))


def eigen_kernel(inverse, out):
    size, lanes = out.shape[1:]
    number = inverse.shape[1]
    start = lax.axis_index("space") * size
    row = lax.broadcasted_iota(jnp.int32, (size, number), 0) + start
    chosen = lax.broadcasted_iota(jnp.int32, (size, number), 1) == row
    for part in range(2):
        value = jnp.where(chosen, inverse[part : part + 1], 0.0)
        out[part] = jnp.broadcast_to(jnp.sum(value, axis=1, keepdims=True), (size, lanes))


def eigen_of(inverse, size, lanes):
    return pl.pallas_call(
        eigen_kernel,
        out_shape=pltpu.VMEM((2, size, lanes), F32),
        in_specs=vmem(1),
        out_specs=vmem(1)[0],
        compiler_params=params(),
        cost_estimate=cost(1e6, 1e6),
        name="eigen",
    )(inverse)


def apply_faces(site, faces, matrices):
    summed = None
    for face, matrix in zip(faces, matrices):
        term = matmul(matrix[site], stack(face(site), 1.0))
        summed = term if summed is None else summed + term
    return fold(summed)


def z_faces_kernel(rest, forward, backward, matrix, out):
    faces = (lambda s: forward[s], lambda s: backward[s])
    for site in range(rest.shape[0]):
        out[site] = rest[site] - apply_faces(site, faces, (matrix.at[0], matrix.at[1]))


def z_faces(rest, forward, backward, matrix):
    return pl.pallas_call(
        z_faces_kernel,
        out_shape=pltpu.VMEM(rest.shape, F32),
        in_specs=vmem(4),
        out_specs=vmem(1)[0],
        compiler_params=params(),
        cost_estimate=cost(1e9, 4e6),
        name="z_faces",
    )(rest, forward, backward, matrix)


def edge_sign(last):
    count = lax.axis_size("tm")
    return jnp.where(lax.axis_index("tm") == (count - 1 if last else 0), -1.0, 1.0).astype(F32)


def backward_kernel(rest, backward, matrix, out):
    sign = edge_sign(False)
    for site in range(rest.shape[0]):
        out[site] = rest[site] - apply_faces(site, (lambda s: sign * backward[s],), (matrix.at[3],))


def backward_face(rest, backward, matrix):
    return pl.pallas_call(
        backward_kernel,
        out_shape=pltpu.VMEM(rest.shape, F32),
        in_specs=vmem(3),
        out_specs=vmem(1)[0],
        compiler_params=params(),
        cost_estimate=cost(1e9, 4e6),
        name="backward_face",
    )(rest, backward, matrix)


def forward_kernel(rest, forward, matrix, vectors, residual, keep, send, stacks):
    sign = edge_sign(True)
    rows = 2 * rest.shape[1]
    for site in range(rest.shape[0]):
        own = rest[site] - apply_faces(site, (lambda s: sign * forward[s],), (matrix.at[2],))
        residual[site] = own
        stacks[site * rows : (site + 1) * rows] = stack(own, -1.0)
    whole = fold(matmul(vectors[...], stacks[...]))
    half = whole.shape[0] // 2
    keep[...] = whole[:half]
    send[...] = whole[half:]


def forward_face(rest, forward, matrix, vectors):
    sites, rows, lanes = rest.shape
    part = pltpu.VMEM((vectors.shape[0] // 4, lanes), F32)
    return pl.pallas_call(
        forward_kernel,
        out_shape=(pltpu.VMEM(rest.shape, F32), part, part),
        in_specs=vmem(4),
        out_specs=tuple(vmem(3)),
        scratch_shapes=[pltpu.VMEM((sites * 2 * rows, 2 * lanes), BF16)],
        compiler_params=params(),
        cost_estimate=cost(2e9, 8e6),
        name="forward_face",
    )(rest, forward, matrix, vectors)


def split_kernel(keep, received, next_keep, next_send):
    half = next_keep.shape[0]
    next_keep[...] = keep[:half] + received[:half]
    next_send[...] = keep[half:] + received[half:]


def add_split(keep, received):
    rows, lanes = keep.shape
    part = pltpu.VMEM((rows // 2, lanes), F32)
    return pl.pallas_call(
        split_kernel,
        out_shape=(part, part),
        in_specs=vmem(2),
        out_specs=tuple(vmem(2)),
        compiler_params=params(),
        name="add_split",
    )(keep, received)


def add_kernel(left, right, out):
    out[...] = left[...] + right[...]


def add(left, right):
    return pl.pallas_call(
        add_kernel,
        out_shape=pltpu.VMEM(left.shape, F32),
        in_specs=vmem(2),
        out_specs=vmem(1)[0],
        compiler_params=params(),
        name="add",
    )(left, right)


def scale_kernel(eigen, *refs):
    parts, out = refs[:-1], refs[-1]
    total = parts[0][...]
    for part in parts[1:]:
        total = total + part[...]
    out[...] = eigen[0] * total + eigen[1] * turned(total)


def scale(eigen, parts):
    return pl.pallas_call(
        scale_kernel,
        out_shape=pltpu.VMEM(parts[0].shape, F32),
        in_specs=vmem(1 + len(parts)),
        out_specs=vmem(1)[0],
        compiler_params=params(),
        name="scale",
    )(eigen, *parts)


def expand(site, vectors, part, stacks):
    depth = stacks.shape[0] // 2
    total = None
    for half in range(2):
        left = vectors[site, half, :, part * depth : (part + 1) * depth]
        term = matmul(left, stacks[half * depth : (half + 1) * depth])
        total = term if total is None else total + term
    return fold(total)


def place_pieces(pieces, stacks):
    values = [piece[...] for piece in pieces]
    stacks[...] = stack(values[0] if len(values) == 1 else jnp.concatenate(values, axis=0), 1.0)


def first_half_kernel(x, residual, vectors, *refs):
    pieces, (out, stacks) = refs[:-2], refs[-2:]
    place_pieces(pieces, stacks)
    for site in range(x.shape[0]):
        out[site] = x[site] + 0.5 * residual[site] + expand(site, vectors, 0, stacks)


def first_half(x, residual, pieces, vectors):
    return pl.pallas_call(
        first_half_kernel,
        out_shape=pltpu.VMEM(x.shape, F32),
        in_specs=vmem(3 + len(pieces)),
        out_specs=vmem(1)[0],
        scratch_shapes=[pltpu.VMEM((vectors.shape[-1], 2 * x.shape[-1]), BF16)],
        compiler_params=params(),
        cost_estimate=cost(1e9, 4e6),
        name="first_half",
    )(x, residual, vectors, *pieces)


def second_half_kernel(base, vectors, *refs):
    pieces, (out, stacks) = refs[:-2], refs[-2:]
    place_pieces(pieces, stacks)
    for site in range(base.shape[0]):
        out[site] = base[site] + expand(site, vectors, 1, stacks)


def second_half(base, pieces, vectors):
    return pl.pallas_call(
        second_half_kernel,
        out_shape=pltpu.VMEM(base.shape, F32),
        in_specs=vmem(2 + len(pieces)),
        out_specs=vmem(1)[0],
        scratch_shapes=[pltpu.VMEM((vectors.shape[-1], 2 * base.shape[-1]), BF16)],
        compiler_params=params(),
        cost_estimate=cost(1e9, 4e6),
        name="second_half",
    )(base, vectors, *pieces)


def join_kernel(own, other, full, held, sems):
    group = lax.axis_index("groups")
    copies = []
    for site in range(own.shape[0]):
        held[site] = join_halves(own[site], other[site], group)
        copies.append(pltpu.make_async_copy(held.at[site], full.at[site], sems.at[site]))
        copies[-1].start()
    for copy in copies:
        copy.wait()


def join(own, other):
    sites, rows, lanes = own.shape
    shape = (sites, rows, 2 * lanes)
    return pl.pallas_call(
        join_kernel,
        out_shape=jax.ShapeDtypeStruct(shape, F32),
        in_specs=vmem(2),
        out_specs=pl.BlockSpec(memory_space=pl.ANY),
        scratch_shapes=[pltpu.VMEM(shape, F32), pltpu.SemaphoreType.DMA((sites,))],
        compiler_params=params(),
        cost_estimate=cost(1e6, 2e6),
        name="join",
    )(own, other)


def final_kernel(own, other, vectors, *refs):
    pieces, (full, stacks, held, sems) = refs[:-4], refs[-4:]
    group = lax.axis_index("groups")
    place_pieces(pieces, stacks)
    copies = []
    for site in range(own.shape[0]):
        held[site] = join_halves(own[site], other[site] + expand(site, vectors, 1, stacks), group)
        copies.append(pltpu.make_async_copy(held.at[site], full.at[site], sems.at[site]))
        copies[-1].start()
    for copy in copies:
        copy.wait()


def final(own, other, pieces, vectors):
    sites, rows, lanes = own.shape
    shape = (sites, rows, 2 * lanes)
    return pl.pallas_call(
        final_kernel,
        out_shape=jax.ShapeDtypeStruct(shape, F32),
        in_specs=vmem(3 + len(pieces)),
        out_specs=pl.BlockSpec(memory_space=pl.ANY),
        scratch_shapes=[
            pltpu.VMEM((vectors.shape[-1], 2 * lanes), BF16),
            pltpu.VMEM(shape, F32),
            pltpu.SemaphoreType.DMA((sites,)),
        ],
        compiler_params=params(),
        cost_estimate=cost(1e9, 4e6),
        name="final",
    )(own, other, vectors, *pieces)


def shifted(value, axis, step):
    count = lax.axis_size(axis)
    return lax.ppermute(value, axis, [(i, (i + step) % count) for i in range(count)])


def crossed(value, axis, mask):
    count = lax.axis_size(axis)
    return lax.ppermute(value, axis, [(i, i ^ mask) for i in range(count)])


def faces_of(x):
    backward_t = shifted(x, "tm", 1)
    forward_t = shifted(x, "tm", -1)
    backward_z = shifted(x, "space", 1)
    forward_z = shifted(x, "space", -1)
    return forward_z, backward_z, forward_t, backward_t


def halving(keep, send):
    count = lax.axis_size("space")
    mask = 1
    while True:
        received = crossed(send, "space", mask)
        mask *= 2
        if mask >= count:
            return add(keep, received)
        keep, send = add_split(keep, received)


def doubling(pieces, mask):
    while mask > 1:
        if len(pieces) > 2:
            pieces = [jnp.concatenate(pieces, axis=0)]
        pieces = pieces + [crossed(piece, "space", mask) for piece in pieces]
        mask //= 2
    return pieces


def paired(pieces):
    return [crossed(piece, "space", 1) for piece in pieces]


def across_groups(part, mask):
    groups, count = lax.axis_size("groups"), lax.axis_size("space")
    pairs = [(g * count + s, (g ^ 1) * count + (s ^ mask)) for g in range(groups) for s in range(count)]
    return [crossed(part, "groups", 1), lax.ppermute(part, ("groups", "space"), pairs)]


def over_time(part):
    count = lax.axis_size("tm")
    if count <= 4:
        return [part] + [crossed(part, "tm", mask) for mask in range(1, count)]
    mask = 1
    while mask < count:
        part = part + crossed(part, "tm", mask)
        mask *= 2
    return [part]


def shards(couplings, source, initial, vectors, inverse_eigen):
    directions = couplings.shape[0]
    ny, nx, rows, lanes = source.shape[2:]
    sites = ny * nx
    number = vectors.shape[0]
    blocks = lax.axis_size("space")

    x = pack(initial.reshape(sites, rows, lanes))
    faces = faces_of(x)
    matrices = couplings.reshape(directions, sites, rows, couplings.shape[-1])
    rest, half_source, local, halo = first_local(x, source.reshape(sites, rows, lanes), matrices, ny, nx)
    across = jnp.transpose(vectors, (1, 2, 3, 4, 5, 0)).reshape(sites * vectors.shape[-1], number)
    by_rows, by_columns = vectors_parts(across, sites)
    eigen = eigen_of(inverse_eigen, number // blocks, lanes // 2)

    for sweep in range(ITERS):
        last = sweep == ITERS - 1
        if sweep:
            faces = faces_of(x)
            if last:
                other_x = crossed(x, "groups", 1)
            rest = local_part(x, half_source, local, ny, nx)
        forward_z, backward_z, forward_t, backward_t = faces
        rest = backward_face(rest, backward_t, halo)
        rest = z_faces(rest, forward_z, backward_z, halo)
        if sweep and last:
            rest, other_x = lax.optimization_barrier((rest, other_x))
        residual, keep, send = forward_face(rest, forward_t, halo, by_rows)
        part = halving(keep, send)
        if last:
            part, residual = lax.optimization_barrier((part, residual))
            other_residual = crossed(residual, "groups", 1)
        parts = over_time(part)
        d = scale(eigen, parts)
        if not last:
            pieces = doubling([d], blocks // 2)
            base = first_half(x, residual, pieces, by_columns)
            x = second_half(base, paired(pieces), by_columns)
    mask = blocks // 2
    other = across_groups(d, mask)
    own = [d, crossed(d, "space", mask)]
    other, own = doubling(other, mask // 2), doubling(own, mask // 2)
    full_residual = join(residual, other_residual)
    own[-1], full_residual = lax.optimization_barrier((own[-1], full_residual))
    own_x = first_half(x, residual, own, by_columns)
    other[0], own_x = lax.optimization_barrier((other[0], own_x))
    own_x = second_half(own_x, paired(own), by_columns)
    other[-1], own_x = lax.optimization_barrier((other[-1], own_x))
    other_second = paired(other)
    other_x = first_half(other_x, other_residual, other, by_columns)
    whole = final(own_x, other_x, other_second, by_columns)
    shape = source.shape
    return whole.reshape(shape), full_residual.reshape(shape)


def solution(mesh):
    in_specs = (
        P(None, "tm", "space", None, None, None, None),
        P("tm", "space", None, None, None, None),
        P("tm", "space", None, None, None, None),
        P(None, "tm", "space", None, None, None),
        P(),
    )
    out_specs = (
        P(("groups", "tm"), "space", None, None, None, None),
        P(("groups", "tm"), "space", None, None, None, None),
    )
    return jax.shard_map(shards, mesh=mesh, in_specs=in_specs, out_specs=out_specs, check_vma=False)
```

```python
import functools

import jax
import jax.numpy as jnp
from jax import lax
from jax.experimental import pallas as pl
from jax.experimental.pallas import tpu as pltpu
from jax.sharding import PartitionSpec as P

ITERS = 2
F32 = jnp.float32
BF16 = jnp.bfloat16
LOCAL = 5


def params(mebibytes=12):
    return pltpu.CompilerParams(vmem_limit_bytes=mebibytes * 1024 * 1024)


def cost(flops, read):
    return pl.CostEstimate(flops=int(flops), bytes_accessed=int(read), transcendentals=0)


def low_lanes(value):
    lanes = lax.broadcasted_iota(jnp.int32, value.shape, value.ndim - 1)
    return lanes < value.shape[-1] // 2


def swap(value):
    return pltpu.roll(value, value.shape[-1] // 2, value.ndim - 1)


def turned(value):
    moved = swap(value)
    return jnp.where(low_lanes(value), -moved, moved)


def high_low(value):
    high = value.astype(BF16)
    low = (value - high.astype(F32)).astype(BF16)
    return high, low


def stack(value, sign):
    high, low = high_low(jnp.concatenate([value, sign * turned(value)], axis=0))
    return jnp.concatenate([high, low], axis=1)


def matmul(left, right):
    return jnp.dot(left, right, preferred_element_type=F32)


def fold(product):
    rows, lanes = product.shape[0] // 2, product.shape[1] // 2
    high = product[:rows, :lanes] + (product[:rows, lanes:] + product[rows:, :lanes])
    return high + product[rows:, lanes:]


def pick_half(value, group):
    middle = value.shape[-1] // 2
    real, imag = value[:, :middle], value[:, middle:]
    low = low_lanes(real)
    first = jnp.where(low, real, swap(imag))
    second = jnp.where(low, swap(real), imag)
    return jnp.where(group == 0, first, second)


def join_halves(own, other, group):
    first = jnp.where(group == 0, own, other)
    second = jnp.where(group == 0, other, own)
    low = low_lanes(own)
    real = jnp.where(low, first, swap(second))
    imag = jnp.where(low, swap(first), second)
    return jnp.concatenate([real, imag], axis=1)


def vmem(count):
    return [pl.BlockSpec(memory_space=pltpu.VMEM)] * count


def in_hbm(value):
    return pltpu.with_memory_space_constraint(value, pltpu.HBM)


def pack_kernel(full, half):
    group = lax.axis_index("groups")
    for site in range(full.shape[0]):
        half[site] = pick_half(full[site], group)


def pack(full):
    sites, rows, lanes = full.shape
    return pl.pallas_call(
        pack_kernel,
        out_shape=pltpu.VMEM((sites, rows, lanes // 2), F32),
        in_specs=vmem(1),
        out_specs=vmem(1)[0],
        compiler_params=params(),
        cost_estimate=cost(1e6, 1e6),
        name="pack",
    )(full)


def around(site, ny, nx):
    y, x = site // nx, lax.rem(site, nx)
    right, left = lax.rem(x + 1, nx), lax.rem(x + nx - 1, nx)
    up, down = lax.rem(y + 1, ny), lax.rem(y + ny - 1, ny)
    return (site, y * nx + right, y * nx + left, up * nx + x, down * nx + x)


def local_sum(site, ny, nx, x_ref, stacks, matrix):
    @pl.when(site == 0)
    def _():
        for each in range(ny * nx):
            stacks[each] = stack(x_ref[each], 1.0)

    total = None
    for direction, neighbour in enumerate(around(site, ny, nx)):
        term = matmul(matrix(direction), stacks[neighbour])
        total = term if total is None else total + term
    return fold(total)


def first_kernel(ny, nx, x_ref, source, couplings, rest, half_source, local, halo, stacks):
    site = pl.program_id(0)
    own = pick_half(source[0], lax.axis_index("groups"))
    half_source[0] = own
    for direction in range(couplings.shape[0]):
        high, low = high_low(couplings[direction, 0])
        both = jnp.concatenate([high, low], axis=0)
        if direction < LOCAL:
            local[direction, 0] = both
        else:
            halo[direction - LOCAL, 0] = both
    rest[0] = own - local_sum(site, ny, nx, x_ref, stacks, lambda d: local[d, 0])


def first_local(x, source, couplings, ny, nx):
    sites, rows, lanes = x.shape
    directions, _, _, columns = couplings.shape
    outer = directions - LOCAL
    return pl.pallas_call(
        functools.partial(first_kernel, ny, nx),
        grid=(sites,),
        out_shape=(
            pltpu.VMEM(x.shape, F32),
            pltpu.VMEM(x.shape, F32),
            pltpu.VMEM((LOCAL, sites, 2 * rows, columns), BF16),
            pltpu.VMEM((outer, sites, 2 * rows, columns), BF16),
        ),
        in_specs=[
            pl.BlockSpec((sites, rows, lanes), lambda s: (0, 0, 0)),
            pl.BlockSpec((1, rows, 2 * lanes), lambda s: (s, 0, 0)),
            pl.BlockSpec((directions, 1, rows, columns), lambda s: (0, s, 0, 0)),
        ],
        out_specs=(
            pl.BlockSpec((1, rows, lanes), lambda s: (s, 0, 0)),
            pl.BlockSpec((1, rows, lanes), lambda s: (s, 0, 0)),
            pl.BlockSpec((LOCAL, 1, 2 * rows, columns), lambda s: (0, s, 0, 0)),
            pl.BlockSpec((outer, 1, 2 * rows, columns), lambda s: (0, s, 0, 0)),
        ),
        scratch_shapes=[pltpu.VMEM((sites, 2 * rows, 2 * lanes), BF16)],
        compiler_params=params(),
        cost_estimate=cost(8e9, 16e6),
        name="first_local",
    )(x, in_hbm(source), in_hbm(couplings))


def local_kernel(ny, nx, x_ref, source, local, rest, stacks):
    site = pl.program_id(0)
    rest[0] = source[0] - local_sum(site, ny, nx, x_ref, stacks, lambda d: local[d, 0])


def local_part(x, source, local, ny, nx):
    sites, rows, lanes = x.shape
    columns = local.shape[-1]
    return pl.pallas_call(
        functools.partial(local_kernel, ny, nx),
        grid=(sites,),
        out_shape=pltpu.VMEM(x.shape, F32),
        in_specs=[
            pl.BlockSpec((sites, rows, lanes), lambda s: (0, 0, 0)),
            pl.BlockSpec((1, rows, lanes), lambda s: (s, 0, 0)),
            pl.BlockSpec((LOCAL, 1, 2 * rows, columns), lambda s: (0, s, 0, 0)),
        ],
        out_specs=pl.BlockSpec((1, rows, lanes), lambda s: (s, 0, 0)),
        scratch_shapes=[pltpu.VMEM((sites, 2 * rows, 2 * lanes), BF16)],
        compiler_params=params(),
        cost_estimate=cost(8e9, 8e6),
        name="local_part",
    )(x, source, local)


def block_order(count):
    bits = count.bit_length() - 1
    return [int(format(index, "b").zfill(bits)[::-1], 2) if bits else 0 for index in range(count)]


def ordered_rows(rows, chunk, taken):
    blocks = lax.axis_size("space")
    space = lax.axis_index("space")
    size = rows.shape[0] // blocks
    unit = min(size, taken)
    parts = []
    for start in range(chunk * taken, (chunk + 1) * taken, unit):
        block = space ^ block_order(blocks)[start // size]
        parts.append(rows[pl.ds(pl.multiple_of(block * size + start % size, unit), unit)])
    return parts[0] if len(parts) == 1 else jnp.concatenate(parts, axis=0)


def vectors_kernel(across, by_rows, by_columns, turned_rows):
    sites, _, double, number = by_columns.shape
    rows = double // 2
    taken = 128
    turned_rows[...] = across[...].T
    for chunk in range(number // taken):
        part = ordered_rows(turned_rows, chunk, taken)
        high, low = high_low(part)
        at = slice(chunk * taken, (chunk + 1) * taken)
        by_rows[at] = high
        by_rows[number + chunk * taken : number + (chunk + 1) * taken] = low
        back = part.T
        for site in range(sites):
            for half in range(2):
                start = (2 * site + half) * rows
                high, low = high_low(back[start : start + rows])
                by_columns[site, half, :rows, at] = high
                by_columns[site, half, rows:, at] = low


def vectors_parts(across, sites):
    width, number = across.shape
    rows = width // sites // 2
    step = 2
    return pl.pallas_call(
        vectors_kernel,
        grid=(sites // step,),
        out_shape=(pltpu.VMEM((2 * number, width), BF16), pltpu.VMEM((sites, 2, 2 * rows, number), BF16)),
        in_specs=[pl.BlockSpec((step * 2 * rows, number), lambda s: (s, 0))],
        out_specs=(
            pl.BlockSpec((2 * number, step * 2 * rows), lambda s: (0, s)),
            pl.BlockSpec((step, 2, 2 * rows, number), lambda s: (s, 0, 0, 0)),
        ),
        scratch_shapes=[pltpu.VMEM((number, step * 2 * rows), F32)],
        compiler_params=params(16),
        cost_estimate=cost(1e6, 9e6),
        name="vectors_parts",
    )(in_hbm(across))


def eigen_kernel(inverse, out):
    size, lanes = out.shape[1:]
    number = inverse.shape[1]
    start = lax.axis_index("space") * size
    row = lax.broadcasted_iota(jnp.int32, (size, number), 0) + start
    chosen = lax.broadcasted_iota(jnp.int32, (size, number), 1) == row
    for part in range(2):
        value = jnp.where(chosen, inverse[part : part + 1], 0.0)
        out[part] = jnp.broadcast_to(jnp.sum(value, axis=1, keepdims=True), (size, lanes))


def eigen_of(inverse, size, lanes):
    return pl.pallas_call(
        eigen_kernel,
        out_shape=pltpu.VMEM((2, size, lanes), F32),
        in_specs=vmem(1),
        out_specs=vmem(1)[0],
        compiler_params=params(),
        cost_estimate=cost(1e6, 1e6),
        name="eigen",
    )(inverse)


def apply_faces(site, faces, matrices):
    summed = None
    for face, matrix in zip(faces, matrices):
        term = matmul(matrix[site], stack(face(site), 1.0))
        summed = term if summed is None else summed + term
    return fold(summed)


def z_faces_kernel(rest, near, far, matrix, out):
    parity = lax.rem(lax.axis_index("space"), 2)
    faces = (lambda s: near[s], lambda s: far[s])
    for site in range(rest.shape[0]):
        out[site] = rest[site] - apply_faces(site, faces, (matrix.at[parity], matrix.at[1 - parity]))


def z_faces(rest, near, far, matrix):
    return pl.pallas_call(
        z_faces_kernel,
        out_shape=pltpu.VMEM(rest.shape, F32),
        in_specs=vmem(4),
        out_specs=vmem(1)[0],
        compiler_params=params(),
        cost_estimate=cost(1e9, 4e6),
        name="z_faces",
    )(rest, near, far, matrix)


def edge_sign(last):
    count = lax.axis_size("tm")
    return jnp.where(lax.axis_index("tm") == (count - 1 if last else 0), -1.0, 1.0).astype(F32)


def backward_kernel(rest, backward, matrix, out):
    sign = edge_sign(False)
    for site in range(rest.shape[0]):
        out[site] = rest[site] - apply_faces(site, (lambda s: sign * backward[s],), (matrix.at[3],))


def backward_face(rest, backward, matrix):
    return pl.pallas_call(
        backward_kernel,
        out_shape=pltpu.VMEM(rest.shape, F32),
        in_specs=vmem(3),
        out_specs=vmem(1)[0],
        compiler_params=params(),
        cost_estimate=cost(1e9, 4e6),
        name="backward_face",
    )(rest, backward, matrix)


def forward_kernel(rest, forward, matrix, vectors, residual, keep, send, stacks):
    sign = edge_sign(True)
    rows = 2 * rest.shape[1]
    for site in range(rest.shape[0]):
        own = rest[site] - apply_faces(site, (lambda s: sign * forward[s],), (matrix.at[2],))
        residual[site] = own
        stacks[site * rows : (site + 1) * rows] = stack(own, -1.0)
    whole = fold(matmul(vectors[...], stacks[...]))
    half = whole.shape[0] // 2
    keep[...] = whole[:half]
    send[...] = whole[half:]


def forward_face(rest, forward, matrix, vectors):
    sites, rows, lanes = rest.shape
    part = pltpu.VMEM((vectors.shape[0] // 4, lanes), F32)
    return pl.pallas_call(
        forward_kernel,
        out_shape=(pltpu.VMEM(rest.shape, F32), part, part),
        in_specs=vmem(4),
        out_specs=tuple(vmem(3)),
        scratch_shapes=[pltpu.VMEM((sites * 2 * rows, 2 * lanes), BF16)],
        compiler_params=params(),
        cost_estimate=cost(2e9, 8e6),
        name="forward_face",
    )(rest, forward, matrix, vectors)


def split_kernel(keep, received, next_keep, next_send):
    half = next_keep.shape[0]
    next_keep[...] = keep[:half] + received[:half]
    next_send[...] = keep[half:] + received[half:]


def add_split(keep, received):
    rows, lanes = keep.shape
    part = pltpu.VMEM((rows // 2, lanes), F32)
    return pl.pallas_call(
        split_kernel,
        out_shape=(part, part),
        in_specs=vmem(2),
        out_specs=tuple(vmem(2)),
        compiler_params=params(),
        name="add_split",
    )(keep, received)


def add_kernel(left, right, out):
    out[...] = left[...] + right[...]


def add(left, right):
    return pl.pallas_call(
        add_kernel,
        out_shape=pltpu.VMEM(left.shape, F32),
        in_specs=vmem(2),
        out_specs=vmem(1)[0],
        compiler_params=params(),
        name="add",
    )(left, right)


def scaled_sum(keep, send, eigen):
    blocks, slices = lax.axis_size("space"), lax.axis_size("tm")
    if blocks != 4 or slices != 4:
        return doubling([scale(eigen, over_time(halving(keep, send)))], blocks // 2)
    keep, send = add_split(keep, crossed(send, "space", 1))
    parts = [crossed(send, "space", 2), crossed(keep, "tm", 2), crossed_both(send, "space", 2, "tm", 2)]
    d = scale(eigen, [keep] + parts)
    moved, across = crossed(d, "space", 2), crossed_both(d, "space", 2, "tm", 1)
    return [add(d, crossed(d, "tm", 1)), add(moved, across)]


def scale_kernel(eigen, *refs):
    parts, out = refs[:-1], refs[-1]
    total = parts[0][...]
    for part in parts[1:]:
        total = total + part[...]
    out[...] = eigen[0] * total + eigen[1] * turned(total)


def scale(eigen, parts):
    return pl.pallas_call(
        scale_kernel,
        out_shape=pltpu.VMEM(parts[0].shape, F32),
        in_specs=vmem(1 + len(parts)),
        out_specs=vmem(1)[0],
        compiler_params=params(),
        name="scale",
    )(eigen, *parts)


def expand(site, vectors, part, stacks):
    depth = stacks.shape[0] // 2
    total = None
    for half in range(2):
        left = vectors[site, half, :, part * depth : (part + 1) * depth]
        term = matmul(left, stacks[half * depth : (half + 1) * depth])
        total = term if total is None else total + term
    return fold(total)


def place_pieces(pieces, stacks):
    values = [piece[...] for piece in pieces]
    stacks[...] = stack(values[0] if len(values) == 1 else jnp.concatenate(values, axis=0), 1.0)


def first_half_kernel(x, residual, vectors, *refs):
    pieces, (out, stacks) = refs[:-2], refs[-2:]
    place_pieces(pieces, stacks)
    for site in range(x.shape[0]):
        out[site] = x[site] + 0.5 * residual[site] + expand(site, vectors, 0, stacks)


def first_half(x, residual, pieces, vectors):
    return pl.pallas_call(
        first_half_kernel,
        out_shape=pltpu.VMEM(x.shape, F32),
        in_specs=vmem(3 + len(pieces)),
        out_specs=vmem(1)[0],
        scratch_shapes=[pltpu.VMEM((vectors.shape[-1], 2 * x.shape[-1]), BF16)],
        compiler_params=params(),
        cost_estimate=cost(1e9, 4e6),
        name="first_half",
    )(x, residual, vectors, *pieces)


def second_half_kernel(base, vectors, *refs):
    pieces, (out, stacks) = refs[:-2], refs[-2:]
    place_pieces(pieces, stacks)
    for site in range(base.shape[0]):
        out[site] = base[site] + expand(site, vectors, 1, stacks)


def second_half(base, pieces, vectors):
    return pl.pallas_call(
        second_half_kernel,
        out_shape=pltpu.VMEM(base.shape, F32),
        in_specs=vmem(2 + len(pieces)),
        out_specs=vmem(1)[0],
        scratch_shapes=[pltpu.VMEM((vectors.shape[-1], 2 * base.shape[-1]), BF16)],
        compiler_params=params(),
        cost_estimate=cost(1e9, 4e6),
        name="second_half",
    )(base, vectors, *pieces)


def join_kernel(own, other, full, held, sems):
    group = lax.axis_index("groups")
    copies = []
    for site in range(own.shape[0]):
        held[site] = join_halves(own[site], other[site], group)
        copies.append(pltpu.make_async_copy(held.at[site], full.at[site], sems.at[site]))
        copies[-1].start()
    for copy in copies:
        copy.wait()


def join(own, other):
    sites, rows, lanes = own.shape
    shape = (sites, rows, 2 * lanes)
    return pl.pallas_call(
        join_kernel,
        out_shape=jax.ShapeDtypeStruct(shape, F32),
        in_specs=vmem(2),
        out_specs=pl.BlockSpec(memory_space=pl.ANY),
        scratch_shapes=[pltpu.VMEM(shape, F32), pltpu.SemaphoreType.DMA((sites,))],
        compiler_params=params(),
        cost_estimate=cost(1e6, 2e6),
        name="join",
    )(own, other)


def final_kernel(own, other, vectors, *refs):
    pieces, (full, stacks, held, sems) = refs[:-4], refs[-4:]
    group = lax.axis_index("groups")
    place_pieces(pieces, stacks)
    copies = []
    for site in range(own.shape[0]):
        held[site] = join_halves(own[site], other[site] + expand(site, vectors, 1, stacks), group)
        copies.append(pltpu.make_async_copy(held.at[site], full.at[site], sems.at[site]))
        copies[-1].start()
    for copy in copies:
        copy.wait()


def final(own, other, pieces, vectors):
    sites, rows, lanes = own.shape
    shape = (sites, rows, 2 * lanes)
    return pl.pallas_call(
        final_kernel,
        out_shape=jax.ShapeDtypeStruct(shape, F32),
        in_specs=vmem(3 + len(pieces)),
        out_specs=pl.BlockSpec(memory_space=pl.ANY),
        scratch_shapes=[
            pltpu.VMEM((vectors.shape[-1], 2 * lanes), BF16),
            pltpu.VMEM(shape, F32),
            pltpu.SemaphoreType.DMA((sites,)),
        ],
        compiler_params=params(),
        cost_estimate=cost(1e9, 4e6),
        name="final",
    )(own, other, vectors, *pieces)


def shifted(value, axis, step):
    count = lax.axis_size(axis)
    return lax.ppermute(value, axis, [(i, (i + step) % count) for i in range(count)])


def crossed(value, axis, mask):
    count = lax.axis_size(axis)
    return lax.ppermute(value, axis, [(i, i ^ mask) for i in range(count)])


def crossed_both(value, first, first_mask, second, second_mask):
    count, inner = lax.axis_size(first), lax.axis_size(second)
    pairs = [(i * inner + j, (i ^ first_mask) * inner + (j ^ second_mask)) for i in range(count) for j in range(inner)]
    return lax.ppermute(value, (first, second), pairs)


def faces_of(x):
    count = lax.axis_size("space")
    near = crossed(x, "space", 1)
    far = lax.ppermute(x, "space", [(i, (i + 1 if i % 2 else i - 1) % count) for i in range(count)])
    return near, far, shifted(x, "tm", -1), shifted(x, "tm", 1)


def halving(keep, send):
    count = lax.axis_size("space")
    mask = 1
    while True:
        received = crossed(send, "space", mask)
        mask *= 2
        if mask >= count:
            return add(keep, received)
        keep, send = add_split(keep, received)


def doubling(pieces, mask):
    while mask > 1:
        if len(pieces) > 2:
            pieces = [jnp.concatenate(pieces, axis=0)]
        pieces = pieces + [crossed(piece, "space", mask) for piece in pieces]
        mask //= 2
    return pieces


def paired(pieces):
    return [crossed(piece, "space", 1) for piece in pieces]


def across_groups(part, mask):
    return [crossed(part, "groups", 1), crossed_both(part, "groups", 1, "space", mask)]


def over_time(part):
    count = lax.axis_size("tm")
    if count <= 4:
        return [part] + [crossed(part, "tm", mask) for mask in range(1, count)]
    mask = 1
    while mask < count:
        part = part + crossed(part, "tm", mask)
        mask *= 2
    return [part]


def shards(couplings, source, initial, vectors, inverse_eigen):
    directions = couplings.shape[0]
    ny, nx, rows, lanes = source.shape[2:]
    sites = ny * nx
    number = vectors.shape[0]
    blocks = lax.axis_size("space")

    x = pack(initial.reshape(sites, rows, lanes))
    faces = faces_of(x)
    matrices = couplings.reshape(directions, sites, rows, couplings.shape[-1])
    rest, half_source, local, halo = first_local(x, source.reshape(sites, rows, lanes), matrices, ny, nx)
    across = jnp.transpose(vectors, (1, 2, 3, 4, 5, 0)).reshape(sites * vectors.shape[-1], number)
    by_rows, by_columns = vectors_parts(across, sites)
    eigen = eigen_of(inverse_eigen, number // blocks, lanes // 2)

    for sweep in range(ITERS):
        last = sweep == ITERS - 1
        if sweep:
            faces = faces_of(x)
            rest = local_part(x, half_source, local, ny, nx)
        near, far, forward_t, backward_t = faces
        if last:
            near, x = lax.optimization_barrier((near, x))
            other_x = crossed(x, "groups", 1)
        rest = backward_face(rest, backward_t, halo)
        rest = z_faces(rest, near, far, halo)
        if last:
            rest, other_x = lax.optimization_barrier((rest, other_x))
        residual, keep, send = forward_face(rest, forward_t, halo, by_rows)
        if not last:
            pieces = scaled_sum(keep, send, eigen)
            base = first_half(x, residual, pieces, by_columns)
            x = second_half(base, paired(pieces), by_columns)
    part, residual = lax.optimization_barrier((halving(keep, send), residual))
    other_residual = crossed(residual, "groups", 1)
    d = scale(eigen, over_time(part))
    mask = blocks // 2
    other = across_groups(d, mask)
    own = [d, crossed(d, "space", mask)]
    other, own = doubling(other, mask // 2), doubling(own, mask // 2)
    full_residual = join(residual, other_residual)
    own[-1], full_residual = lax.optimization_barrier((own[-1], full_residual))
    own_x = first_half(x, residual, own, by_columns)
    other[0], own_x = lax.optimization_barrier((other[0], own_x))
    own_x = second_half(own_x, paired(own), by_columns)
    other[-1], own_x = lax.optimization_barrier((other[-1], own_x))
    other_second = paired(other)
    other_x = first_half(other_x, other_residual, other, by_columns)
    whole = final(own_x, other_x, other_second, by_columns)
    shape = source.shape
    return whole.reshape(shape), full_residual.reshape(shape)


def solution(mesh):
    in_specs = (
        P(None, "tm", "space", None, None, None, None),
        P("tm", "space", None, None, None, None),
        P("tm", "space", None, None, None, None),
        P(None, "tm", "space", None, None, None),
        P(),
    )
    out_specs = (
        P(("groups", "tm"), "space", None, None, None, None),
        P(("groups", "tm"), "space", None, None, None, None),
    )
    return jax.shard_map(shards, mesh=mesh, in_specs=in_specs, out_specs=out_specs, check_vma=False)
```

```python
import functools

import jax
import jax.numpy as jnp
from jax import lax
from jax.experimental import pallas as pl
from jax.experimental.pallas import tpu as pltpu
from jax.sharding import PartitionSpec as P

ITERS = 2
F32 = jnp.float32
BF16 = jnp.bfloat16
LOCAL = 5


def params(mebibytes=12):
    return pltpu.CompilerParams(vmem_limit_bytes=mebibytes * 1024 * 1024)


def cost(flops, read):
    return pl.CostEstimate(flops=int(flops), bytes_accessed=int(read), transcendentals=0)


def low_lanes(value):
    lanes = lax.broadcasted_iota(jnp.int32, value.shape, value.ndim - 1)
    return lanes < value.shape[-1] // 2


def swap(value):
    return pltpu.roll(value, value.shape[-1] // 2, value.ndim - 1)


def turned(value):
    moved = swap(value)
    return jnp.where(low_lanes(value), -moved, moved)


def high_low(value):
    high = value.astype(BF16)
    low = (value - high.astype(F32)).astype(BF16)
    return high, low


def stack(value, sign):
    high, low = high_low(jnp.concatenate([value, sign * turned(value)], axis=0))
    return jnp.concatenate([high, low], axis=1)


def matmul(left, right):
    return jnp.dot(left, right, preferred_element_type=F32)


def fold(product):
    rows, lanes = product.shape[0] // 2, product.shape[1] // 2
    high = product[:rows, :lanes] + (product[:rows, lanes:] + product[rows:, :lanes])
    return high + product[rows:, lanes:]


def pick_half(value, group):
    middle = value.shape[-1] // 2
    real, imag = value[:, :middle], value[:, middle:]
    low = low_lanes(real)
    first = jnp.where(low, real, swap(imag))
    second = jnp.where(low, swap(real), imag)
    return jnp.where(group == 0, first, second)


def join_halves(own, other, group):
    first = jnp.where(group == 0, own, other)
    second = jnp.where(group == 0, other, own)
    low = low_lanes(own)
    real = jnp.where(low, first, swap(second))
    imag = jnp.where(low, swap(first), second)
    return jnp.concatenate([real, imag], axis=1)


def vmem(count):
    return [pl.BlockSpec(memory_space=pltpu.VMEM)] * count


def in_hbm(value):
    return pltpu.with_memory_space_constraint(value, pltpu.HBM)


def pack_kernel(full, half):
    group = lax.axis_index("groups")
    for site in range(full.shape[0]):
        half[site] = pick_half(full[site], group)


def pack(full):
    sites, rows, lanes = full.shape
    return pl.pallas_call(
        pack_kernel,
        out_shape=pltpu.VMEM((sites, rows, lanes // 2), F32),
        in_specs=vmem(1),
        out_specs=vmem(1)[0],
        compiler_params=params(),
        cost_estimate=cost(1e6, 1e6),
        name="pack",
    )(full)


def around(site, ny, nx):
    y, x = site // nx, lax.rem(site, nx)
    right, left = lax.rem(x + 1, nx), lax.rem(x + nx - 1, nx)
    up, down = lax.rem(y + 1, ny), lax.rem(y + ny - 1, ny)
    return (site, y * nx + right, y * nx + left, up * nx + x, down * nx + x)


def local_sum(site, ny, nx, x_ref, stacks, matrix):
    @pl.when(site == 0)
    def _():
        for each in range(ny * nx):
            stacks[each] = stack(x_ref[each], 1.0)

    total = None
    for direction, neighbour in enumerate(around(site, ny, nx)):
        term = matmul(matrix(direction), stacks[neighbour])
        total = term if total is None else total + term
    return fold(total)


def first_kernel(ny, nx, x_ref, source, couplings, rest, half_source, local, halo, stacks):
    site = pl.program_id(0)
    own = pick_half(source[0], lax.axis_index("groups"))
    half_source[0] = own
    for direction in range(couplings.shape[0]):
        high, low = high_low(couplings[direction, 0])
        both = jnp.concatenate([high, low], axis=0)
        if direction < LOCAL:
            local[direction, 0] = both
        else:
            halo[direction - LOCAL, 0] = both
    rest[0] = own - local_sum(site, ny, nx, x_ref, stacks, lambda d: local[d, 0])


def first_local(x, source, couplings, ny, nx):
    sites, rows, lanes = x.shape
    directions, _, _, columns = couplings.shape
    outer = directions - LOCAL
    return pl.pallas_call(
        functools.partial(first_kernel, ny, nx),
        grid=(sites,),
        out_shape=(
            pltpu.VMEM(x.shape, F32),
            pltpu.VMEM(x.shape, F32),
            pltpu.VMEM((LOCAL, sites, 2 * rows, columns), BF16),
            pltpu.VMEM((outer, sites, 2 * rows, columns), BF16),
        ),
        in_specs=[
            pl.BlockSpec((sites, rows, lanes), lambda s: (0, 0, 0)),
            pl.BlockSpec((1, rows, 2 * lanes), lambda s: (s, 0, 0)),
            pl.BlockSpec((directions, 1, rows, columns), lambda s: (0, s, 0, 0)),
        ],
        out_specs=(
            pl.BlockSpec((1, rows, lanes), lambda s: (s, 0, 0)),
            pl.BlockSpec((1, rows, lanes), lambda s: (s, 0, 0)),
            pl.BlockSpec((LOCAL, 1, 2 * rows, columns), lambda s: (0, s, 0, 0)),
            pl.BlockSpec((outer, 1, 2 * rows, columns), lambda s: (0, s, 0, 0)),
        ),
        scratch_shapes=[pltpu.VMEM((sites, 2 * rows, 2 * lanes), BF16)],
        compiler_params=params(),
        cost_estimate=cost(8e9, 16e6),
        name="first_local",
    )(x, in_hbm(source), in_hbm(couplings))


def local_kernel(ny, nx, x_ref, source, local, rest, stacks):
    site = pl.program_id(0)
    rest[0] = source[0] - local_sum(site, ny, nx, x_ref, stacks, lambda d: local[d, 0])


def local_part(x, source, local, ny, nx):
    sites, rows, lanes = x.shape
    columns = local.shape[-1]
    return pl.pallas_call(
        functools.partial(local_kernel, ny, nx),
        grid=(sites,),
        out_shape=pltpu.VMEM(x.shape, F32),
        in_specs=[
            pl.BlockSpec((sites, rows, lanes), lambda s: (0, 0, 0)),
            pl.BlockSpec((1, rows, lanes), lambda s: (s, 0, 0)),
            pl.BlockSpec((LOCAL, 1, 2 * rows, columns), lambda s: (0, s, 0, 0)),
        ],
        out_specs=pl.BlockSpec((1, rows, lanes), lambda s: (s, 0, 0)),
        scratch_shapes=[pltpu.VMEM((sites, 2 * rows, 2 * lanes), BF16)],
        compiler_params=params(),
        cost_estimate=cost(8e9, 8e6),
        name="local_part",
    )(x, source, local)


def block_order(count):
    bits = count.bit_length() - 1
    return [int(format(index, "b").zfill(bits)[::-1], 2) if bits else 0 for index in range(count)]


def ordered_rows(rows, chunk, taken):
    blocks = lax.axis_size("space")
    space = lax.axis_index("space")
    size = rows.shape[0] // blocks
    unit = min(size, taken)
    parts = []
    for start in range(chunk * taken, (chunk + 1) * taken, unit):
        block = space ^ block_order(blocks)[start // size]
        parts.append(rows[pl.ds(pl.multiple_of(block * size + start % size, unit), unit)])
    return parts[0] if len(parts) == 1 else jnp.concatenate(parts, axis=0)


def vectors_kernel(across, by_rows, by_columns, turned_rows):
    sites, _, double, number = by_columns.shape
    rows = double // 2
    taken = 128
    turned_rows[...] = across[...].T
    for chunk in range(number // taken):
        part = ordered_rows(turned_rows, chunk, taken)
        high, low = high_low(part)
        at = slice(chunk * taken, (chunk + 1) * taken)
        by_rows[at] = high
        by_rows[number + chunk * taken : number + (chunk + 1) * taken] = low
        back = part.T
        for site in range(sites):
            for half in range(2):
                start = (2 * site + half) * rows
                high, low = high_low(back[start : start + rows])
                by_columns[site, half, :rows, at] = high
                by_columns[site, half, rows:, at] = low


def vectors_parts(across, sites):
    width, number = across.shape
    rows = width // sites // 2
    step = 2
    return pl.pallas_call(
        vectors_kernel,
        grid=(sites // step,),
        out_shape=(pltpu.VMEM((2 * number, width), BF16), pltpu.VMEM((sites, 2, 2 * rows, number), BF16)),
        in_specs=[pl.BlockSpec((step * 2 * rows, number), lambda s: (s, 0))],
        out_specs=(
            pl.BlockSpec((2 * number, step * 2 * rows), lambda s: (0, s)),
            pl.BlockSpec((step, 2, 2 * rows, number), lambda s: (s, 0, 0, 0)),
        ),
        scratch_shapes=[pltpu.VMEM((number, step * 2 * rows), F32)],
        compiler_params=params(16),
        cost_estimate=cost(1e6, 9e6),
        name="vectors_parts",
    )(in_hbm(across))


def eigen_kernel(inverse, out):
    size, lanes = out.shape[1:]
    number = inverse.shape[1]
    start = lax.axis_index("space") * size
    row = lax.broadcasted_iota(jnp.int32, (size, number), 0) + start
    chosen = lax.broadcasted_iota(jnp.int32, (size, number), 1) == row
    for part in range(2):
        value = jnp.where(chosen, inverse[part : part + 1], 0.0)
        out[part] = jnp.broadcast_to(jnp.sum(value, axis=1, keepdims=True), (size, lanes))


def eigen_of(inverse, size, lanes):
    return pl.pallas_call(
        eigen_kernel,
        out_shape=pltpu.VMEM((2, size, lanes), F32),
        in_specs=vmem(1),
        out_specs=vmem(1)[0],
        compiler_params=params(),
        cost_estimate=cost(1e6, 1e6),
        name="eigen",
    )(inverse)


def apply_faces(site, faces, matrices):
    summed = None
    for face, matrix in zip(faces, matrices):
        term = matmul(matrix[site], stack(face(site), 1.0))
        summed = term if summed is None else summed + term
    return fold(summed)


def z_faces_kernel(rest, near, far, matrix, out):
    parity = lax.rem(lax.axis_index("space"), 2)
    faces = (lambda s: near[s], lambda s: far[s])
    for site in range(rest.shape[0]):
        out[site] = rest[site] - apply_faces(site, faces, (matrix.at[parity], matrix.at[1 - parity]))


def z_faces(rest, near, far, matrix):
    return pl.pallas_call(
        z_faces_kernel,
        out_shape=pltpu.VMEM(rest.shape, F32),
        in_specs=vmem(4),
        out_specs=vmem(1)[0],
        compiler_params=params(),
        cost_estimate=cost(1e9, 4e6),
        name="z_faces",
    )(rest, near, far, matrix)


def edge_sign(last):
    count = lax.axis_size("tm")
    return jnp.where(lax.axis_index("tm") == (count - 1 if last else 0), -1.0, 1.0).astype(F32)


def backward_kernel(rest, backward, matrix, out):
    sign = edge_sign(False)
    for site in range(rest.shape[0]):
        out[site] = rest[site] - apply_faces(site, (lambda s: sign * backward[s],), (matrix.at[3],))


def backward_face(rest, backward, matrix):
    return pl.pallas_call(
        backward_kernel,
        out_shape=pltpu.VMEM(rest.shape, F32),
        in_specs=vmem(3),
        out_specs=vmem(1)[0],
        compiler_params=params(),
        cost_estimate=cost(1e9, 4e6),
        name="backward_face",
    )(rest, backward, matrix)


def forward_kernel(rest, forward, matrix, vectors, residual, keep, send, stacks):
    sign = edge_sign(True)
    rows = 2 * rest.shape[1]
    for site in range(rest.shape[0]):
        own = rest[site] - apply_faces(site, (lambda s: sign * forward[s],), (matrix.at[2],))
        residual[site] = own
        stacks[site * rows : (site + 1) * rows] = stack(own, -1.0)
    whole = fold(matmul(vectors[...], stacks[...]))
    half = whole.shape[0] // 2
    keep[...] = whole[:half]
    send[...] = whole[half:]


def forward_face(rest, forward, matrix, vectors):
    sites, rows, lanes = rest.shape
    part = pltpu.VMEM((vectors.shape[0] // 4, lanes), F32)
    return pl.pallas_call(
        forward_kernel,
        out_shape=(pltpu.VMEM(rest.shape, F32), part, part),
        in_specs=vmem(4),
        out_specs=tuple(vmem(3)),
        scratch_shapes=[pltpu.VMEM((sites * 2 * rows, 2 * lanes), BF16)],
        compiler_params=params(),
        cost_estimate=cost(2e9, 8e6),
        name="forward_face",
    )(rest, forward, matrix, vectors)


def split_kernel(keep, received, next_keep, next_send):
    half = next_keep.shape[0]
    next_keep[...] = keep[:half] + received[:half]
    next_send[...] = keep[half:] + received[half:]


def add_split(keep, received):
    rows, lanes = keep.shape
    part = pltpu.VMEM((rows // 2, lanes), F32)
    return pl.pallas_call(
        split_kernel,
        out_shape=(part, part),
        in_specs=vmem(2),
        out_specs=tuple(vmem(2)),
        compiler_params=params(),
        name="add_split",
    )(keep, received)


def add_kernel(left, right, out):
    out[...] = left[...] + right[...]


def add(left, right):
    return pl.pallas_call(
        add_kernel,
        out_shape=pltpu.VMEM(left.shape, F32),
        in_specs=vmem(2),
        out_specs=vmem(1)[0],
        compiler_params=params(),
        name="add",
    )(left, right)


def scaled_sum(keep, send, eigen):
    blocks, slices = lax.axis_size("space"), lax.axis_size("tm")
    if blocks != 4 or slices != 4:
        return doubling([scale(eigen, over_time(halving(keep, send)))], blocks // 2)
    keep, send = add_split(keep, crossed(send, "space", 1))
    parts = [crossed(send, "space", 2), crossed(keep, "tm", 2), crossed_both(send, "space", 2, "tm", 2)]
    d = scale(eigen, [keep] + parts)
    moved, across = crossed(d, "space", 2), crossed_both(d, "space", 2, "tm", 1)
    return [add(d, crossed(d, "tm", 1)), add(moved, across)]


def scale_kernel(eigen, *refs):
    parts, out = refs[:-1], refs[-1]
    total = parts[0][...]
    for part in parts[1:]:
        total = total + part[...]
    out[...] = eigen[0] * total + eigen[1] * turned(total)


def scale(eigen, parts):
    return pl.pallas_call(
        scale_kernel,
        out_shape=pltpu.VMEM(parts[0].shape, F32),
        in_specs=vmem(1 + len(parts)),
        out_specs=vmem(1)[0],
        compiler_params=params(),
        name="scale",
    )(eigen, *parts)


def expand(site, vectors, part, stacks):
    depth = stacks.shape[0] // 2
    total = None
    for half in range(2):
        left = vectors[site, half, :, part * depth : (part + 1) * depth]
        term = matmul(left, stacks[half * depth : (half + 1) * depth])
        total = term if total is None else total + term
    return fold(total)


def place_pieces(pieces, stacks):
    values = [piece[...] for piece in pieces]
    stacks[...] = stack(values[0] if len(values) == 1 else jnp.concatenate(values, axis=0), 1.0)


def first_half_kernel(x, residual, vectors, *refs):
    pieces, (out, stacks) = refs[:-2], refs[-2:]
    place_pieces(pieces, stacks)
    for site in range(x.shape[0]):
        out[site] = x[site] + 0.5 * residual[site] + expand(site, vectors, 0, stacks)


def first_half(x, residual, pieces, vectors):
    return pl.pallas_call(
        first_half_kernel,
        out_shape=pltpu.VMEM(x.shape, F32),
        in_specs=vmem(3 + len(pieces)),
        out_specs=vmem(1)[0],
        scratch_shapes=[pltpu.VMEM((vectors.shape[-1], 2 * x.shape[-1]), BF16)],
        compiler_params=params(),
        cost_estimate=cost(1e9, 4e6),
        name="first_half",
    )(x, residual, vectors, *pieces)


def second_half_kernel(base, vectors, *refs):
    pieces, (out, stacks) = refs[:-2], refs[-2:]
    place_pieces(pieces, stacks)
    for site in range(base.shape[0]):
        out[site] = base[site] + expand(site, vectors, 1, stacks)


def second_half(base, pieces, vectors):
    return pl.pallas_call(
        second_half_kernel,
        out_shape=pltpu.VMEM(base.shape, F32),
        in_specs=vmem(2 + len(pieces)),
        out_specs=vmem(1)[0],
        scratch_shapes=[pltpu.VMEM((vectors.shape[-1], 2 * base.shape[-1]), BF16)],
        compiler_params=params(),
        cost_estimate=cost(1e9, 4e6),
        name="second_half",
    )(base, vectors, *pieces)


def join_kernel(own, other, full, held, sems):
    group = lax.axis_index("groups")
    copies = []
    for site in range(own.shape[0]):
        held[site] = join_halves(own[site], other[site], group)
        copies.append(pltpu.make_async_copy(held.at[site], full.at[site], sems.at[site]))
        copies[-1].start()
    for copy in copies:
        copy.wait()


def join(own, other):
    sites, rows, lanes = own.shape
    shape = (sites, rows, 2 * lanes)
    return pl.pallas_call(
        join_kernel,
        out_shape=jax.ShapeDtypeStruct(shape, F32),
        in_specs=vmem(2),
        out_specs=pl.BlockSpec(memory_space=pl.ANY),
        scratch_shapes=[pltpu.VMEM(shape, F32), pltpu.SemaphoreType.DMA((sites,))],
        compiler_params=params(),
        cost_estimate=cost(1e6, 2e6),
        name="join",
    )(own, other)


def final_kernel(own, other, vectors, *refs):
    pieces, (full, stacks, held, sems) = refs[:-4], refs[-4:]
    group = lax.axis_index("groups")
    place_pieces(pieces, stacks)
    copies = []
    for site in range(own.shape[0]):
        held[site] = join_halves(own[site], other[site] + expand(site, vectors, 1, stacks), group)
        copies.append(pltpu.make_async_copy(held.at[site], full.at[site], sems.at[site]))
        copies[-1].start()
    for copy in copies:
        copy.wait()


def final(own, other, pieces, vectors):
    sites, rows, lanes = own.shape
    shape = (sites, rows, 2 * lanes)
    return pl.pallas_call(
        final_kernel,
        out_shape=jax.ShapeDtypeStruct(shape, F32),
        in_specs=vmem(3 + len(pieces)),
        out_specs=pl.BlockSpec(memory_space=pl.ANY),
        scratch_shapes=[
            pltpu.VMEM((vectors.shape[-1], 2 * lanes), BF16),
            pltpu.VMEM(shape, F32),
            pltpu.SemaphoreType.DMA((sites,)),
        ],
        compiler_params=params(),
        cost_estimate=cost(1e9, 4e6),
        name="final",
    )(own, other, vectors, *pieces)


def shifted(value, axis, step):
    count = lax.axis_size(axis)
    return lax.ppermute(value, axis, [(i, (i + step) % count) for i in range(count)])


def crossed(value, axis, mask):
    count = lax.axis_size(axis)
    return lax.ppermute(value, axis, [(i, i ^ mask) for i in range(count)])


def crossed_both(value, first, first_mask, second, second_mask):
    count, inner = lax.axis_size(first), lax.axis_size(second)
    pairs = [(i * inner + j, (i ^ first_mask) * inner + (j ^ second_mask)) for i in range(count) for j in range(inner)]
    return lax.ppermute(value, (first, second), pairs)


def faces_of(x):
    count = lax.axis_size("space")
    backward_t, forward_t = shifted(x, "tm", 1), shifted(x, "tm", -1)
    near, x = lax.optimization_barrier((crossed(x, "space", 1), x))
    far = lax.ppermute(x, "space", [(i, (i + 1 if i % 2 else i - 1) % count) for i in range(count)])
    return near, far, forward_t, backward_t


def halving(keep, send):
    count = lax.axis_size("space")
    mask = 1
    while True:
        received = crossed(send, "space", mask)
        mask *= 2
        if mask >= count:
            return add(keep, received)
        keep, send = add_split(keep, received)


def doubling(pieces, mask):
    while mask > 1:
        if len(pieces) > 2:
            pieces = [jnp.concatenate(pieces, axis=0)]
        pieces = pieces + [crossed(piece, "space", mask) for piece in pieces]
        mask //= 2
    return pieces


def paired(pieces):
    return [crossed(piece, "space", 1) for piece in pieces]


def across_groups(part, mask):
    return [crossed(part, "groups", 1), crossed_both(part, "groups", 1, "space", mask)]


def over_time(part):
    count = lax.axis_size("tm")
    if count <= 4:
        return [part] + [crossed(part, "tm", mask) for mask in range(1, count)]
    mask = 1
    while mask < count:
        part = part + crossed(part, "tm", mask)
        mask *= 2
    return [part]


def shards(couplings, source, initial, vectors, inverse_eigen):
    directions = couplings.shape[0]
    ny, nx, rows, lanes = source.shape[2:]
    sites = ny * nx
    number = vectors.shape[0]
    blocks = lax.axis_size("space")

    x = pack(initial.reshape(sites, rows, lanes))
    faces = faces_of(x)
    matrices = couplings.reshape(directions, sites, rows, couplings.shape[-1])
    rest, half_source, local, halo = first_local(x, source.reshape(sites, rows, lanes), matrices, ny, nx)
    across = jnp.transpose(vectors, (1, 2, 3, 4, 5, 0)).reshape(sites * vectors.shape[-1], number)
    by_rows, by_columns = vectors_parts(across, sites)
    eigen = eigen_of(inverse_eigen, number // blocks, lanes // 2)

    for sweep in range(ITERS):
        last = sweep == ITERS - 1
        if sweep:
            faces = faces_of(x)
            rest = local_part(x, half_source, local, ny, nx)
        near, far, forward_t, backward_t = faces
        if last:
            near, x = lax.optimization_barrier((near, x))
            other_x = crossed(x, "groups", 1)
        rest = z_faces(rest, near, far, halo)
        rest = backward_face(rest, backward_t, halo)
        if last:
            rest, other_x = lax.optimization_barrier((rest, other_x))
        residual, keep, send = forward_face(rest, forward_t, halo, by_rows)
        if not last:
            pieces = scaled_sum(keep, send, eigen)
            base = first_half(x, residual, pieces, by_columns)
            x = second_half(base, paired(pieces), by_columns)
    part, residual = lax.optimization_barrier((halving(keep, send), residual))
    other_residual = crossed(residual, "groups", 1)
    d = scale(eigen, over_time(part))
    mask = blocks // 2
    other = across_groups(d, mask)
    own = [d, crossed(d, "space", mask)]
    other, own = doubling(other, mask // 2), doubling(own, mask // 2)
    full_residual = join(residual, other_residual)
    own[-1], full_residual = lax.optimization_barrier((own[-1], full_residual))
    own_x = first_half(x, residual, own, by_columns)
    other[0], own_x = lax.optimization_barrier((other[0], own_x))
    own_x = second_half(own_x, paired(own), by_columns)
    other[-1], own_x = lax.optimization_barrier((other[-1], own_x))
    other_second = paired(other)
    other_x = first_half(other_x, other_residual, other, by_columns)
    whole = final(own_x, other_x, other_second, by_columns)
    shape = source.shape
    return whole.reshape(shape), full_residual.reshape(shape)


def solution(mesh):
    in_specs = (
        P(None, "tm", "space", None, None, None, None),
        P("tm", "space", None, None, None, None),
        P("tm", "space", None, None, None, None),
        P(None, "tm", "space", None, None, None),
        P(),
    )
    out_specs = (
        P(("groups", "tm"), "space", None, None, None, None),
        P(("groups", "tm"), "space", None, None, None, None),
    )
    return jax.shard_map(shards, mesh=mesh, in_specs=in_specs, out_specs=out_specs, check_vma=False)
```

```python
import functools

import jax
import jax.numpy as jnp
from jax import lax
from jax.experimental import pallas as pl
from jax.experimental.pallas import tpu as pltpu
from jax.sharding import PartitionSpec as P

ITERS = 2
F32 = jnp.float32
BF16 = jnp.bfloat16
LOCAL = 5


def params(mebibytes=12):
    return pltpu.CompilerParams(vmem_limit_bytes=mebibytes * 1024 * 1024)


def cost(flops, read):
    return pl.CostEstimate(flops=int(flops), bytes_accessed=int(read), transcendentals=0)


def low_lanes(value):
    lanes = lax.broadcasted_iota(jnp.int32, value.shape, value.ndim - 1)
    return lanes < value.shape[-1] // 2


def swap(value):
    return pltpu.roll(value, value.shape[-1] // 2, value.ndim - 1)


def turned(value):
    moved = swap(value)
    return jnp.where(low_lanes(value), -moved, moved)


def high_low(value):
    high = value.astype(BF16)
    low = (value - high.astype(F32)).astype(BF16)
    return high, low


def stack(value, sign):
    high, low = high_low(jnp.concatenate([value, sign * turned(value)], axis=0))
    return jnp.concatenate([high, low], axis=1)


def matmul(left, right):
    return jnp.dot(left, right, preferred_element_type=F32)


def fold(product):
    rows, lanes = product.shape[0] // 2, product.shape[1] // 2
    high = product[:rows, :lanes] + (product[:rows, lanes:] + product[rows:, :lanes])
    return high + product[rows:, lanes:]


def pick_half(value, group):
    middle = value.shape[-1] // 2
    real, imag = value[:, :middle], value[:, middle:]
    low = low_lanes(real)
    first = jnp.where(low, real, swap(imag))
    second = jnp.where(low, swap(real), imag)
    return jnp.where(group == 0, first, second)


def join_halves(own, other, group):
    first = jnp.where(group == 0, own, other)
    second = jnp.where(group == 0, other, own)
    low = low_lanes(own)
    real = jnp.where(low, first, swap(second))
    imag = jnp.where(low, swap(first), second)
    return jnp.concatenate([real, imag], axis=1)


def vmem(count):
    return [pl.BlockSpec(memory_space=pltpu.VMEM)] * count


def in_hbm(value):
    return pltpu.with_memory_space_constraint(value, pltpu.HBM)


def put(site, value, whole, front, back):
    count = front.shape[0]
    whole[site] = value
    if site < count:
        front[site] = value
    else:
        back[site - count] = value


def with_halves(shape):
    part = pltpu.VMEM((shape[0] // 2,) + tuple(shape[1:]), F32)
    return pltpu.VMEM(shape, F32), part, part


def pack_kernel(full, half, front, back):
    group = lax.axis_index("groups")
    for site in range(full.shape[0]):
        put(site, pick_half(full[site], group), half, front, back)


def pack(full):
    sites, rows, lanes = full.shape
    return pl.pallas_call(
        pack_kernel,
        out_shape=with_halves((sites, rows, lanes // 2)),
        in_specs=vmem(1),
        out_specs=tuple(vmem(3)),
        compiler_params=params(),
        cost_estimate=cost(1e6, 1e6),
        name="pack",
    )(full)


def around(site, ny, nx):
    y, x = site // nx, lax.rem(site, nx)
    right, left = lax.rem(x + 1, nx), lax.rem(x + nx - 1, nx)
    up, down = lax.rem(y + 1, ny), lax.rem(y + ny - 1, ny)
    return (site, y * nx + right, y * nx + left, up * nx + x, down * nx + x)


def local_sum(site, ny, nx, x_ref, stacks, matrix):
    @pl.when(site == 0)
    def _():
        for each in range(ny * nx):
            stacks[each] = stack(x_ref[each], 1.0)

    total = None
    for direction, neighbour in enumerate(around(site, ny, nx)):
        term = matmul(matrix(direction), stacks[neighbour])
        total = term if total is None else total + term
    return fold(total)


def first_kernel(ny, nx, x_ref, source, couplings, rest, half_source, local, halo, stacks):
    site = pl.program_id(0)
    own = pick_half(source[0], lax.axis_index("groups"))
    half_source[0] = own
    for direction in range(couplings.shape[0]):
        high, low = high_low(couplings[direction, 0])
        both = jnp.concatenate([high, low], axis=0)
        if direction < LOCAL:
            local[direction, 0] = both
        else:
            halo[direction - LOCAL, 0] = both
    rest[0] = own - local_sum(site, ny, nx, x_ref, stacks, lambda d: local[d, 0])


def first_local(x, source, couplings, ny, nx):
    sites, rows, lanes = x.shape
    directions, _, _, columns = couplings.shape
    outer = directions - LOCAL
    return pl.pallas_call(
        functools.partial(first_kernel, ny, nx),
        grid=(sites,),
        out_shape=(
            pltpu.VMEM(x.shape, F32),
            pltpu.VMEM(x.shape, F32),
            pltpu.VMEM((LOCAL, sites, 2 * rows, columns), BF16),
            pltpu.VMEM((outer, sites, 2 * rows, columns), BF16),
        ),
        in_specs=[
            pl.BlockSpec((sites, rows, lanes), lambda s: (0, 0, 0)),
            pl.BlockSpec((1, rows, 2 * lanes), lambda s: (s, 0, 0)),
            pl.BlockSpec((directions, 1, rows, columns), lambda s: (0, s, 0, 0)),
        ],
        out_specs=(
            pl.BlockSpec((1, rows, lanes), lambda s: (s, 0, 0)),
            pl.BlockSpec((1, rows, lanes), lambda s: (s, 0, 0)),
            pl.BlockSpec((LOCAL, 1, 2 * rows, columns), lambda s: (0, s, 0, 0)),
            pl.BlockSpec((outer, 1, 2 * rows, columns), lambda s: (0, s, 0, 0)),
        ),
        scratch_shapes=[pltpu.VMEM((sites, 2 * rows, 2 * lanes), BF16)],
        compiler_params=params(),
        cost_estimate=cost(8e9, 16e6),
        name="first_local",
    )(x, in_hbm(source), in_hbm(couplings))


def local_kernel(ny, nx, x_ref, source, local, rest, stacks):
    site = pl.program_id(0)
    rest[0] = source[0] - local_sum(site, ny, nx, x_ref, stacks, lambda d: local[d, 0])


def local_part(x, source, local, ny, nx):
    sites, rows, lanes = x.shape
    columns = local.shape[-1]
    return pl.pallas_call(
        functools.partial(local_kernel, ny, nx),
        grid=(sites,),
        out_shape=pltpu.VMEM(x.shape, F32),
        in_specs=[
            pl.BlockSpec((sites, rows, lanes), lambda s: (0, 0, 0)),
            pl.BlockSpec((1, rows, lanes), lambda s: (s, 0, 0)),
            pl.BlockSpec((LOCAL, 1, 2 * rows, columns), lambda s: (0, s, 0, 0)),
        ],
        out_specs=pl.BlockSpec((1, rows, lanes), lambda s: (s, 0, 0)),
        scratch_shapes=[pltpu.VMEM((sites, 2 * rows, 2 * lanes), BF16)],
        compiler_params=params(),
        cost_estimate=cost(8e9, 8e6),
        name="local_part",
    )(x, source, local)


def block_order(count):
    bits = count.bit_length() - 1
    return [int(format(index, "b").zfill(bits)[::-1], 2) if bits else 0 for index in range(count)]


def ordered_rows(rows, chunk, taken):
    blocks = lax.axis_size("space")
    space = lax.axis_index("space")
    size = rows.shape[0] // blocks
    unit = min(size, taken)
    parts = []
    for start in range(chunk * taken, (chunk + 1) * taken, unit):
        block = space ^ block_order(blocks)[start // size]
        parts.append(rows[pl.ds(pl.multiple_of(block * size + start % size, unit), unit)])
    return parts[0] if len(parts) == 1 else jnp.concatenate(parts, axis=0)


def vectors_kernel(across, by_rows, by_columns, turned_rows):
    sites, _, double, number = by_columns.shape
    rows = double // 2
    taken = 128
    turned_rows[...] = across[...].T
    for chunk in range(number // taken):
        part = ordered_rows(turned_rows, chunk, taken)
        high, low = high_low(part)
        at = slice(chunk * taken, (chunk + 1) * taken)
        by_rows[at] = high
        by_rows[number + chunk * taken : number + (chunk + 1) * taken] = low
        back = part.T
        for site in range(sites):
            for half in range(2):
                start = (2 * site + half) * rows
                high, low = high_low(back[start : start + rows])
                by_columns[site, half, :rows, at] = high
                by_columns[site, half, rows:, at] = low


def vectors_parts(across, sites):
    width, number = across.shape
    rows = width // sites // 2
    step = 2
    return pl.pallas_call(
        vectors_kernel,
        grid=(sites // step,),
        out_shape=(pltpu.VMEM((2 * number, width), BF16), pltpu.VMEM((sites, 2, 2 * rows, number), BF16)),
        in_specs=[pl.BlockSpec((step * 2 * rows, number), lambda s: (s, 0))],
        out_specs=(
            pl.BlockSpec((2 * number, step * 2 * rows), lambda s: (0, s)),
            pl.BlockSpec((step, 2, 2 * rows, number), lambda s: (s, 0, 0, 0)),
        ),
        scratch_shapes=[pltpu.VMEM((number, step * 2 * rows), F32)],
        compiler_params=params(16),
        cost_estimate=cost(1e6, 9e6),
        name="vectors_parts",
    )(in_hbm(across))


def eigen_kernel(inverse, out):
    size, lanes = out.shape[1:]
    number = inverse.shape[1]
    start = lax.axis_index("space") * size
    row = lax.broadcasted_iota(jnp.int32, (size, number), 0) + start
    chosen = lax.broadcasted_iota(jnp.int32, (size, number), 1) == row
    for part in range(2):
        value = jnp.where(chosen, inverse[part : part + 1], 0.0)
        out[part] = jnp.broadcast_to(jnp.sum(value, axis=1, keepdims=True), (size, lanes))


def eigen_of(inverse, size, lanes):
    return pl.pallas_call(
        eigen_kernel,
        out_shape=pltpu.VMEM((2, size, lanes), F32),
        in_specs=vmem(1),
        out_specs=vmem(1)[0],
        compiler_params=params(),
        cost_estimate=cost(1e6, 1e6),
        name="eigen",
    )(inverse)


def apply_faces(*pairs):
    summed = None
    for matrix, face in pairs:
        term = matmul(matrix, stack(face, 1.0))
        summed = term if summed is None else summed + term
    return fold(summed)


def edge_sign(last):
    count = lax.axis_size("tm")
    return jnp.where(lax.axis_index("tm") == (count - 1 if last else 0), -1.0, 1.0).astype(F32)


def front_kernel(backward, forward, matrix, out):
    behind, ahead = edge_sign(False), edge_sign(True)
    for site in range(out.shape[0]):
        out[site] = apply_faces((matrix[2, site], ahead * forward[site]), (matrix[3, site], behind * backward[site]))


def front_faces(backward, forward, matrix):
    return pl.pallas_call(
        front_kernel,
        out_shape=pltpu.VMEM(forward.shape, F32),
        in_specs=vmem(3),
        out_specs=vmem(1)[0],
        compiler_params=params(),
        cost_estimate=cost(1e3, 1e3),
        name="front_faces",
    )(backward, forward, matrix)


def middle_kernel(rest, near, far, front, matrix, vectors, back, residual, partial, stacks):
    parity = lax.rem(lax.axis_index("space"), 2)
    sites, rows, _ = front.shape
    for site in range(rest.shape[0]):
        own = rest[site] - apply_faces((matrix[parity, site], near[site]), (matrix[1 - parity, site], far[site]))
        if site < sites:
            own = own - front[site]
            residual[site] = own
            stacks[site * 2 * rows : (site + 1) * 2 * rows] = stack(own, -1.0)
        else:
            back[site - sites] = own
    partial[...] = fold(matmul(vectors[:, : stacks.shape[0]], stacks[...]))


def middle(rest, near, far, front, matrix, vectors):
    sites, rows, lanes = front.shape
    half = pltpu.VMEM(front.shape, F32)
    return pl.pallas_call(
        middle_kernel,
        out_shape=(half, half, pltpu.VMEM((vectors.shape[0] // 2, lanes), F32)),
        in_specs=vmem(6),
        out_specs=tuple(vmem(3)),
        scratch_shapes=[pltpu.VMEM((sites * 2 * rows, 2 * lanes), BF16)],
        compiler_params=params(),
        cost_estimate=cost(1e3, 1e3),
        name="middle",
    )(rest, near, far, front, matrix, vectors)


def backward_kernel(rest, backward, matrix, out):
    sign = edge_sign(False)
    sites = backward.shape[0]
    for site in range(sites):
        out[site] = rest[site] - apply_faces((matrix[3, sites + site], sign * backward[site]))


def backward_face(rest, backward, matrix):
    return pl.pallas_call(
        backward_kernel,
        out_shape=pltpu.VMEM(backward.shape, F32),
        in_specs=vmem(3),
        out_specs=vmem(1)[0],
        compiler_params=params(),
        cost_estimate=cost(1e3, 1e3),
        name="backward_face",
    )(rest, backward, matrix)


def forward_kernel(front, partial, rest, forward, matrix, vectors, residual, keep, send, stacks):
    sign = edge_sign(True)
    sites, rows, _ = forward.shape
    for site in range(sites):
        own = rest[site] - apply_faces((matrix[2, sites + site], sign * forward[site]))
        residual[site] = front[site]
        residual[sites + site] = own
        stacks[site * 2 * rows : (site + 1) * 2 * rows] = stack(own, -1.0)
    whole = partial[...] + fold(matmul(vectors[:, stacks.shape[0] :], stacks[...]))
    half = whole.shape[0] // 2
    keep[...] = whole[:half]
    send[...] = whole[half:]


def forward_face(front, partial, rest, forward, matrix, vectors):
    sites, rows, lanes = forward.shape
    part = pltpu.VMEM((vectors.shape[0] // 4, lanes), F32)
    return pl.pallas_call(
        forward_kernel,
        out_shape=(pltpu.VMEM((2 * sites, rows, lanes), F32), part, part),
        in_specs=vmem(6),
        out_specs=tuple(vmem(3)),
        scratch_shapes=[pltpu.VMEM((sites * 2 * rows, 2 * lanes), BF16)],
        compiler_params=params(),
        cost_estimate=cost(2e9, 8e6),
        name="forward_face",
    )(front, partial, rest, forward, matrix, vectors)


def split_kernel(keep, received, next_keep, next_send):
    half = next_keep.shape[0]
    next_keep[...] = keep[:half] + received[:half]
    next_send[...] = keep[half:] + received[half:]


def add_split(keep, received):
    rows, lanes = keep.shape
    part = pltpu.VMEM((rows // 2, lanes), F32)
    return pl.pallas_call(
        split_kernel,
        out_shape=(part, part),
        in_specs=vmem(2),
        out_specs=tuple(vmem(2)),
        compiler_params=params(),
        name="add_split",
    )(keep, received)


def add_kernel(left, right, out):
    out[...] = left[...] + right[...]


def add(left, right):
    return pl.pallas_call(
        add_kernel,
        out_shape=pltpu.VMEM(left.shape, F32),
        in_specs=vmem(2),
        out_specs=vmem(1)[0],
        compiler_params=params(),
        name="add",
    )(left, right)


def scaled_sum(keep, send, eigen):
    blocks, slices = lax.axis_size("space"), lax.axis_size("tm")
    if blocks != 4 or slices != 4:
        return doubling([scale(eigen, over_time(halving(keep, send)))], blocks // 2)
    keep, send = add_split(keep, crossed(send, "space", 1))
    parts = [crossed(send, "space", 2), crossed(keep, "tm", 2), crossed_both(send, "space", 2, "tm", 2)]
    d = scale(eigen, [keep] + parts)
    moved, across = crossed(d, "space", 2), crossed_both(d, "space", 2, "tm", 1)
    return [add(d, crossed(d, "tm", 1)), add(moved, across)]


def scale_kernel(eigen, *refs):
    parts, out = refs[:-1], refs[-1]
    total = parts[0][...]
    for part in parts[1:]:
        total = total + part[...]
    out[...] = eigen[0] * total + eigen[1] * turned(total)


def scale(eigen, parts):
    return pl.pallas_call(
        scale_kernel,
        out_shape=pltpu.VMEM(parts[0].shape, F32),
        in_specs=vmem(1 + len(parts)),
        out_specs=vmem(1)[0],
        compiler_params=params(),
        name="scale",
    )(eigen, *parts)


def expand(site, vectors, part, stacks):
    depth = stacks.shape[0] // 2
    total = None
    for half in range(2):
        left = vectors[site, half, :, part * depth : (part + 1) * depth]
        term = matmul(left, stacks[half * depth : (half + 1) * depth])
        total = term if total is None else total + term
    return fold(total)


def place_pieces(pieces, stacks):
    values = [piece[...] for piece in pieces]
    stacks[...] = stack(values[0] if len(values) == 1 else jnp.concatenate(values, axis=0), 1.0)


def first_half_kernel(x, residual, vectors, *refs):
    pieces, (out, stacks) = refs[:-2], refs[-2:]
    place_pieces(pieces, stacks)
    for site in range(x.shape[0]):
        out[site] = x[site] + 0.5 * residual[site] + expand(site, vectors, 0, stacks)


def first_half(x, residual, pieces, vectors):
    return pl.pallas_call(
        first_half_kernel,
        out_shape=pltpu.VMEM(x.shape, F32),
        in_specs=vmem(3 + len(pieces)),
        out_specs=vmem(1)[0],
        scratch_shapes=[pltpu.VMEM((vectors.shape[-1], 2 * x.shape[-1]), BF16)],
        compiler_params=params(),
        cost_estimate=cost(1e9, 4e6),
        name="first_half",
    )(x, residual, vectors, *pieces)


def second_half_kernel(base, vectors, *refs):
    pieces, (out, front, back, stacks) = refs[:-4], refs[-4:]
    place_pieces(pieces, stacks)
    for site in range(base.shape[0]):
        put(site, base[site] + expand(site, vectors, 1, stacks), out, front, back)


def second_half(base, pieces, vectors):
    return pl.pallas_call(
        second_half_kernel,
        out_shape=with_halves(base.shape),
        in_specs=vmem(2 + len(pieces)),
        out_specs=tuple(vmem(3)),
        scratch_shapes=[pltpu.VMEM((vectors.shape[-1], 2 * base.shape[-1]), BF16)],
        compiler_params=params(),
        cost_estimate=cost(1e9, 4e6),
        name="second_half",
    )(base, vectors, *pieces)


def join_kernel(own, other, full, held, sems):
    group = lax.axis_index("groups")
    copies = []
    for site in range(own.shape[0]):
        held[site] = join_halves(own[site], other[site], group)
        copies.append(pltpu.make_async_copy(held.at[site], full.at[site], sems.at[site]))
        copies[-1].start()
    for copy in copies:
        copy.wait()


def join(own, other):
    sites, rows, lanes = own.shape
    shape = (sites, rows, 2 * lanes)
    return pl.pallas_call(
        join_kernel,
        out_shape=jax.ShapeDtypeStruct(shape, F32),
        in_specs=vmem(2),
        out_specs=pl.BlockSpec(memory_space=pl.ANY),
        scratch_shapes=[pltpu.VMEM(shape, F32), pltpu.SemaphoreType.DMA((sites,))],
        compiler_params=params(),
        cost_estimate=cost(1e6, 2e6),
        name="join",
    )(own, other)


def final_kernel(own, other, vectors, *refs):
    pieces, (full, stacks, held, sems) = refs[:-4], refs[-4:]
    group = lax.axis_index("groups")
    place_pieces(pieces, stacks)
    copies = []
    for site in range(own.shape[0]):
        held[site] = join_halves(own[site], other[site] + expand(site, vectors, 1, stacks), group)
        copies.append(pltpu.make_async_copy(held.at[site], full.at[site], sems.at[site]))
        copies[-1].start()
    for copy in copies:
        copy.wait()


def final(own, other, pieces, vectors):
    sites, rows, lanes = own.shape
    shape = (sites, rows, 2 * lanes)
    return pl.pallas_call(
        final_kernel,
        out_shape=jax.ShapeDtypeStruct(shape, F32),
        in_specs=vmem(3 + len(pieces)),
        out_specs=pl.BlockSpec(memory_space=pl.ANY),
        scratch_shapes=[
            pltpu.VMEM((vectors.shape[-1], 2 * lanes), BF16),
            pltpu.VMEM(shape, F32),
            pltpu.SemaphoreType.DMA((sites,)),
        ],
        compiler_params=params(),
        cost_estimate=cost(1e9, 4e6),
        name="final",
    )(own, other, vectors, *pieces)


def shifted(value, axis, step):
    count = lax.axis_size(axis)
    return lax.ppermute(value, axis, [(i, (i + step) % count) for i in range(count)])


def crossed(value, axis, mask):
    count = lax.axis_size(axis)
    return lax.ppermute(value, axis, [(i, i ^ mask) for i in range(count)])


def crossed_both(value, first, first_mask, second, second_mask):
    count, inner = lax.axis_size(first), lax.axis_size(second)
    pairs = [(i * inner + j, (i ^ first_mask) * inner + (j ^ second_mask)) for i in range(count) for j in range(inner)]
    return lax.ppermute(value, (first, second), pairs)


def faces_of(x, front, back):
    count = lax.axis_size("space")
    early = shifted(front, "tm", 1), shifted(front, "tm", -1)
    near, back = lax.optimization_barrier((crossed(x, "space", 1), back))
    far = lax.ppermute(x, "space", [(i, (i + 1 if i % 2 else i - 1) % count) for i in range(count)])
    late = shifted(back, "tm", 1), shifted(back, "tm", -1)
    return near, far, early, late


def halving(keep, send):
    count = lax.axis_size("space")
    mask = 1
    while True:
        received = crossed(send, "space", mask)
        mask *= 2
        if mask >= count:
            return add(keep, received)
        keep, send = add_split(keep, received)


def doubling(pieces, mask):
    while mask > 1:
        if len(pieces) > 2:
            pieces = [jnp.concatenate(pieces, axis=0)]
        pieces = pieces + [crossed(piece, "space", mask) for piece in pieces]
        mask //= 2
    return pieces


def paired(pieces):
    return [crossed(piece, "space", 1) for piece in pieces]


def across_groups(part, mask):
    return [crossed(part, "groups", 1), crossed_both(part, "groups", 1, "space", mask)]


def over_time(part):
    count = lax.axis_size("tm")
    if count <= 4:
        return [part] + [crossed(part, "tm", mask) for mask in range(1, count)]
    mask = 1
    while mask < count:
        part = part + crossed(part, "tm", mask)
        mask *= 2
    return [part]


def shards(couplings, source, initial, vectors, inverse_eigen):
    directions = couplings.shape[0]
    ny, nx, rows, lanes = source.shape[2:]
    sites = ny * nx
    number = vectors.shape[0]
    blocks = lax.axis_size("space")

    x, front, back = pack(initial.reshape(sites, rows, lanes))
    faces = faces_of(x, front, back)
    matrices = couplings.reshape(directions, sites, rows, couplings.shape[-1])
    rest, half_source, local, halo = first_local(x, source.reshape(sites, rows, lanes), matrices, ny, nx)
    across = jnp.transpose(vectors, (1, 2, 3, 4, 5, 0)).reshape(sites * vectors.shape[-1], number)
    by_rows, by_columns = vectors_parts(across, sites)
    eigen = eigen_of(inverse_eigen, number // blocks, lanes // 2)

    for sweep in range(ITERS):
        last = sweep == ITERS - 1
        if sweep:
            faces = faces_of(x, front, back)
            rest = local_part(x, half_source, local, ny, nx)
        near, far, early, late = faces
        back_rest, own, partial = middle(rest, near, far, front_faces(*early, halo), halo, by_rows)
        if last:
            partial, x = lax.optimization_barrier((partial, x))
            other_x = crossed(x, "groups", 1)
        back_rest = backward_face(back_rest, late[0], halo)
        residual, keep, send = forward_face(own, partial, back_rest, late[1], halo, by_rows)
        if not last:
            pieces = scaled_sum(keep, send, eigen)
            base = first_half(x, residual, pieces, by_columns)
            x, front, back = second_half(base, paired(pieces), by_columns)
    part, residual, other_x = lax.optimization_barrier((halving(keep, send), residual, other_x))
    other_residual = crossed(residual, "groups", 1)
    d = scale(eigen, over_time(part))
    mask = blocks // 2
    other = across_groups(d, mask)
    own = [d, crossed(d, "space", mask)]
    other, own = doubling(other, mask // 2), doubling(own, mask // 2)
    full_residual = join(residual, other_residual)
    own[-1], full_residual = lax.optimization_barrier((own[-1], full_residual))
    own_x = first_half(x, residual, own, by_columns)
    other[0], own_x = lax.optimization_barrier((other[0], own_x))
    own_x, _, _ = second_half(own_x, paired(own), by_columns)
    other[-1], own_x = lax.optimization_barrier((other[-1], own_x))
    other_second = paired(other)
    other_x = first_half(other_x, other_residual, other, by_columns)
    whole = final(own_x, other_x, other_second, by_columns)
    shape = source.shape
    return whole.reshape(shape), full_residual.reshape(shape)


def solution(mesh):
    in_specs = (
        P(None, "tm", "space", None, None, None, None),
        P("tm", "space", None, None, None, None),
        P("tm", "space", None, None, None, None),
        P(None, "tm", "space", None, None, None),
        P(),
    )
    out_specs = (
        P(("groups", "tm"), "space", None, None, None, None),
        P(("groups", "tm"), "space", None, None, None, None),
    )
    return jax.shard_map(shards, mesh=mesh, in_specs=in_specs, out_specs=out_specs, check_vma=False)
```

```python
import functools

import jax
import jax.numpy as jnp
from jax import lax
from jax.experimental import pallas as pl
from jax.experimental.pallas import tpu as pltpu
from jax.sharding import PartitionSpec as P

ITERS = 2
F32 = jnp.float32
BF16 = jnp.bfloat16
LOCAL = 5


def params(mebibytes=12):
    return pltpu.CompilerParams(vmem_limit_bytes=mebibytes * 1024 * 1024)


def cost(flops, read):
    return pl.CostEstimate(flops=int(flops), bytes_accessed=int(read), transcendentals=0)


def low_lanes(value):
    lanes = lax.broadcasted_iota(jnp.int32, value.shape, value.ndim - 1)
    return lanes < value.shape[-1] // 2


def swap(value):
    return pltpu.roll(value, value.shape[-1] // 2, value.ndim - 1)


def turned(value):
    moved = swap(value)
    return jnp.where(low_lanes(value), -moved, moved)


def high_low(value):
    high = value.astype(BF16)
    low = (value - high.astype(F32)).astype(BF16)
    return high, low


def stack(value, sign):
    high, low = high_low(jnp.concatenate([value, sign * turned(value)], axis=0))
    return jnp.concatenate([high, low], axis=1)


def matmul(left, right):
    return jnp.dot(left, right, preferred_element_type=F32)


def fold(product):
    rows, lanes = product.shape[0] // 2, product.shape[1] // 2
    high = product[:rows, :lanes] + (product[:rows, lanes:] + product[rows:, :lanes])
    return high + product[rows:, lanes:]


def pick_half(value, group):
    middle = value.shape[-1] // 2
    real, imag = value[:, :middle], value[:, middle:]
    low = low_lanes(real)
    first = jnp.where(low, real, swap(imag))
    second = jnp.where(low, swap(real), imag)
    return jnp.where(group == 0, first, second)


def join_halves(own, other, group):
    first = jnp.where(group == 0, own, other)
    second = jnp.where(group == 0, other, own)
    low = low_lanes(own)
    real = jnp.where(low, first, swap(second))
    imag = jnp.where(low, swap(first), second)
    return jnp.concatenate([real, imag], axis=1)


def vmem(count):
    return [pl.BlockSpec(memory_space=pltpu.VMEM)] * count


def in_hbm(value):
    return pltpu.with_memory_space_constraint(value, pltpu.HBM)


def put(site, value, whole, front, back):
    count = front.shape[0]
    whole[site] = value
    if site < count:
        front[site] = value
    else:
        back[site - count] = value


def with_halves(shape):
    part = pltpu.VMEM((shape[0] // 2,) + tuple(shape[1:]), F32)
    return pltpu.VMEM(shape, F32), part, part


def pack_kernel(full, half, front, back):
    group = lax.axis_index("groups")
    for site in range(full.shape[0]):
        put(site, pick_half(full[site], group), half, front, back)


def pack(full):
    sites, rows, lanes = full.shape
    return pl.pallas_call(
        pack_kernel,
        out_shape=with_halves((sites, rows, lanes // 2)),
        in_specs=vmem(1),
        out_specs=tuple(vmem(3)),
        compiler_params=params(),
        cost_estimate=cost(1e6, 1e6),
        name="pack",
    )(full)


def around(site, ny, nx):
    y, x = site // nx, site % nx
    right, left = (x + 1) % nx, (x - 1) % nx
    up, down = (y + 1) % ny, (y - 1) % ny
    return (site, y * nx + right, y * nx + left, up * nx + x, down * nx + x)


def local_sum(site, ny, nx, stacks, local):
    total = None
    for direction, neighbour in enumerate(around(site, ny, nx)):
        term = matmul(local[direction, site], stacks[neighbour])
        total = term if total is None else total + term
    return fold(total)


def first_kernel(ny, nx, x_ref, source, couplings, rest, half_source, local, halo, stacks, held, held_source, sems):
    group = lax.axis_index("groups")
    sites = x_ref.shape[0]
    copies = []
    for site in range(sites):
        copies.append(pltpu.make_async_copy(couplings.at[:, site], held.at[site], sems.at[site]))
        copies[-1].start()
    bring = pltpu.make_async_copy(source, held_source, sems.at[sites])
    bring.start()
    for site in range(sites):
        stacks[site] = stack(x_ref[site], 1.0)
    bring.wait()
    for site in range(sites):
        half_source[site] = pick_half(held_source[site], group)
    for site in range(sites):
        copies[site].wait()
        for direction in range(couplings.shape[0]):
            high, low = high_low(held[site, direction])
            both = jnp.concatenate([high, low], axis=0)
            if direction < LOCAL:
                local[direction, site] = both
            else:
                halo[direction - LOCAL, site] = both
        rest[site] = half_source[site] - local_sum(site, ny, nx, stacks, local)


def first_local(x, source, couplings, ny, nx):
    sites, rows, lanes = x.shape
    directions, _, _, columns = couplings.shape
    outer = directions - LOCAL
    in_place = pl.BlockSpec(memory_space=pl.ANY)
    return pl.pallas_call(
        functools.partial(first_kernel, ny, nx),
        out_shape=(
            pltpu.VMEM(x.shape, F32),
            pltpu.VMEM(x.shape, F32),
            pltpu.VMEM((LOCAL, sites, 2 * rows, columns), BF16),
            pltpu.VMEM((outer, sites, 2 * rows, columns), BF16),
        ),
        in_specs=vmem(1) + [in_place, in_place],
        out_specs=tuple(vmem(4)),
        scratch_shapes=[
            pltpu.VMEM((sites, 2 * rows, 2 * lanes), BF16),
            pltpu.VMEM((sites, directions, rows, columns), F32),
            pltpu.VMEM(source.shape, F32),
            pltpu.SemaphoreType.DMA((sites + 1,)),
        ],
        compiler_params=params(20),
        cost_estimate=cost(8e9, 16e6),
        name="first_local",
    )(x, in_hbm(source), in_hbm(couplings))


def local_kernel(ny, nx, x_ref, source, local, rest, stacks):
    for site in range(x_ref.shape[0]):
        stacks[site] = stack(x_ref[site], 1.0)
    for site in range(x_ref.shape[0]):
        rest[site] = source[site] - local_sum(site, ny, nx, stacks, local)


def local_part(x, source, local, ny, nx):
    sites, rows, lanes = x.shape
    return pl.pallas_call(
        functools.partial(local_kernel, ny, nx),
        out_shape=pltpu.VMEM(x.shape, F32),
        in_specs=vmem(3),
        out_specs=vmem(1)[0],
        scratch_shapes=[pltpu.VMEM((sites, 2 * rows, 2 * lanes), BF16)],
        compiler_params=params(),
        cost_estimate=cost(8e9, 8e6),
        name="local_part",
    )(x, source, local)


def block_order(count):
    bits = count.bit_length() - 1
    return [int(format(index, "b").zfill(bits)[::-1], 2) if bits else 0 for index in range(count)]


def ordered_rows(rows, chunk, taken):
    blocks = lax.axis_size("space")
    space = lax.axis_index("space")
    size = rows.shape[0] // blocks
    unit = min(size, taken)
    parts = []
    for start in range(chunk * taken, (chunk + 1) * taken, unit):
        block = space ^ block_order(blocks)[start // size]
        parts.append(rows[pl.ds(pl.multiple_of(block * size + start % size, unit), unit)])
    return parts[0] if len(parts) == 1 else jnp.concatenate(parts, axis=0)


def by_rows_kernel(across, by_rows, held, turned_rows, sems):
    number = held.shape[1]
    taken = 128
    step = turned_rows.shape[1]
    copies = []
    for index in range(across.shape[0] // step):
        at = pl.ds(index * step, step)
        copies.append(pltpu.make_async_copy(across.at[at], held.at[at], sems.at[index]))
        copies[-1].start()
    for index, copy in enumerate(copies):
        copy.wait()
        at = slice(index * step, (index + 1) * step)
        turned_rows[...] = held[at].T
        for chunk in range(number // taken):
            high, low = high_low(ordered_rows(turned_rows, chunk, taken))
            by_rows[chunk * taken : (chunk + 1) * taken, at] = high
            by_rows[number + chunk * taken : number + (chunk + 1) * taken, at] = low


def by_rows_of(across, sites):
    width, number = across.shape
    step = width // (sites // 2)
    return pl.pallas_call(
        by_rows_kernel,
        out_shape=pltpu.VMEM((2 * number, width), BF16),
        in_specs=[pl.BlockSpec(memory_space=pl.ANY)],
        out_specs=vmem(1)[0],
        scratch_shapes=[
            pltpu.VMEM((width, number), F32),
            pltpu.VMEM((number, step), F32),
            pltpu.SemaphoreType.DMA((width // step,)),
        ],
        compiler_params=params(),
        cost_estimate=cost(1e6, 9e6),
        name="by_rows",
    )(in_hbm(across))


def by_columns_kernel(by_rows, by_columns):
    sites, _, double, number = by_columns.shape
    rows = double // 2
    taken = 128
    for part in range(2):
        for chunk in range(number // taken):
            start = part * number + chunk * taken
            back = by_rows[start : start + taken].astype(F32).T.astype(BF16)
            at = slice(chunk * taken, (chunk + 1) * taken)
            for site in range(sites):
                for half in range(2):
                    start = (2 * site + half) * rows
                    by_columns[site, half, part * rows : (part + 1) * rows, at] = back[start : start + rows]


def by_columns_of(by_rows, sites):
    number, width = by_rows.shape[0] // 2, by_rows.shape[1]
    return pl.pallas_call(
        by_columns_kernel,
        out_shape=pltpu.VMEM((sites, 2, width // sites, number), BF16),
        in_specs=vmem(1),
        out_specs=vmem(1)[0],
        compiler_params=params(),
        cost_estimate=cost(1e6, 6e6),
        name="by_columns",
    )(by_rows)


def eigen_kernel(inverse, out):
    size, lanes = out.shape[1:]
    number = inverse.shape[1]
    start = lax.axis_index("space") * size
    row = lax.broadcasted_iota(jnp.int32, (size, number), 0) + start
    chosen = lax.broadcasted_iota(jnp.int32, (size, number), 1) == row
    for part in range(2):
        value = jnp.where(chosen, inverse[part : part + 1], 0.0)
        out[part] = jnp.broadcast_to(jnp.sum(value, axis=1, keepdims=True), (size, lanes))


def eigen_of(inverse, size, lanes):
    return pl.pallas_call(
        eigen_kernel,
        out_shape=pltpu.VMEM((2, size, lanes), F32),
        in_specs=vmem(1),
        out_specs=vmem(1)[0],
        compiler_params=params(),
        cost_estimate=cost(1e6, 1e6),
        name="eigen",
    )(inverse)


def apply_faces(*pairs):
    summed = None
    for matrix, face in pairs:
        term = matmul(matrix, stack(face, 1.0))
        summed = term if summed is None else summed + term
    return fold(summed)


def edge_sign(last):
    count = lax.axis_size("tm")
    return jnp.where(lax.axis_index("tm") == (count - 1 if last else 0), -1.0, 1.0).astype(F32)


def front_kernel(backward, forward, matrix, out):
    behind, ahead = edge_sign(False), edge_sign(True)
    for site in range(out.shape[0]):
        out[site] = apply_faces((matrix[2, site], ahead * forward[site]), (matrix[3, site], behind * backward[site]))


def front_faces(backward, forward, matrix):
    return pl.pallas_call(
        front_kernel,
        out_shape=pltpu.VMEM(forward.shape, F32),
        in_specs=vmem(3),
        out_specs=vmem(1)[0],
        compiler_params=params(),
        cost_estimate=cost(1e3, 1e3),
        name="front_faces",
    )(backward, forward, matrix)


def middle_kernel(rest, near, far, front, matrix, vectors, back, residual, partial, stacks):
    parity = lax.rem(lax.axis_index("space"), 2)
    sites, rows, _ = front.shape
    for site in range(rest.shape[0]):
        own = rest[site] - apply_faces((matrix[parity, site], near[site]), (matrix[1 - parity, site], far[site]))
        if site < sites:
            own = own - front[site]
            residual[site] = own
            stacks[site * 2 * rows : (site + 1) * 2 * rows] = stack(own, -1.0)
        else:
            back[site - sites] = own
    partial[...] = fold(matmul(vectors[:, : stacks.shape[0]], stacks[...]))


def middle(rest, near, far, front, matrix, vectors):
    sites, rows, lanes = front.shape
    half = pltpu.VMEM(front.shape, F32)
    return pl.pallas_call(
        middle_kernel,
        out_shape=(half, half, pltpu.VMEM((vectors.shape[0] // 2, lanes), F32)),
        in_specs=vmem(6),
        out_specs=tuple(vmem(3)),
        scratch_shapes=[pltpu.VMEM((sites * 2 * rows, 2 * lanes), BF16)],
        compiler_params=params(),
        cost_estimate=cost(1e3, 1e3),
        name="middle",
    )(rest, near, far, front, matrix, vectors)


def backward_kernel(rest, backward, matrix, out):
    sign = edge_sign(False)
    sites = backward.shape[0]
    for site in range(sites):
        out[site] = rest[site] - apply_faces((matrix[3, sites + site], sign * backward[site]))


def backward_face(rest, backward, matrix):
    return pl.pallas_call(
        backward_kernel,
        out_shape=pltpu.VMEM(backward.shape, F32),
        in_specs=vmem(3),
        out_specs=vmem(1)[0],
        compiler_params=params(),
        cost_estimate=cost(1e3, 1e3),
        name="backward_face",
    )(rest, backward, matrix)


def forward_kernel(front, partial, rest, forward, matrix, vectors, residual, keep, send, stacks):
    sign = edge_sign(True)
    sites, rows, _ = forward.shape
    for site in range(sites):
        own = rest[site] - apply_faces((matrix[2, sites + site], sign * forward[site]))
        residual[site] = front[site]
        residual[sites + site] = own
        stacks[site * 2 * rows : (site + 1) * 2 * rows] = stack(own, -1.0)
    whole = partial[...] + fold(matmul(vectors[:, stacks.shape[0] :], stacks[...]))
    half = whole.shape[0] // 2
    keep[...] = whole[:half]
    send[...] = whole[half:]


def forward_face(front, partial, rest, forward, matrix, vectors):
    sites, rows, lanes = forward.shape
    part = pltpu.VMEM((vectors.shape[0] // 4, lanes), F32)
    return pl.pallas_call(
        forward_kernel,
        out_shape=(pltpu.VMEM((2 * sites, rows, lanes), F32), part, part),
        in_specs=vmem(6),
        out_specs=tuple(vmem(3)),
        scratch_shapes=[pltpu.VMEM((sites * 2 * rows, 2 * lanes), BF16)],
        compiler_params=params(),
        cost_estimate=cost(2e9, 8e6),
        name="forward_face",
    )(front, partial, rest, forward, matrix, vectors)


def split_kernel(keep, received, next_keep, next_send):
    half = next_keep.shape[0]
    next_keep[...] = keep[:half] + received[:half]
    next_send[...] = keep[half:] + received[half:]


def add_split(keep, received):
    rows, lanes = keep.shape
    part = pltpu.VMEM((rows // 2, lanes), F32)
    return pl.pallas_call(
        split_kernel,
        out_shape=(part, part),
        in_specs=vmem(2),
        out_specs=tuple(vmem(2)),
        compiler_params=params(),
        name="add_split",
    )(keep, received)


def add_kernel(left, right, out):
    out[...] = left[...] + right[...]


def add(left, right):
    return pl.pallas_call(
        add_kernel,
        out_shape=pltpu.VMEM(left.shape, F32),
        in_specs=vmem(2),
        out_specs=vmem(1)[0],
        compiler_params=params(),
        name="add",
    )(left, right)


def scaled_sum(keep, send, eigen, by_rows, sites):
    blocks, slices = lax.axis_size("space"), lax.axis_size("tm")
    by_rows, send = lax.optimization_barrier((by_rows, send))
    by_columns = by_columns_of(by_rows, sites)
    if blocks != 4 or slices != 4:
        return doubling([scale(eigen, over_time(halving(keep, send)))], blocks // 2), by_columns
    keep, send = add_split(keep, crossed(send, "space", 1))
    parts = [crossed(send, "space", 2), crossed(keep, "tm", 2), crossed_both(send, "space", 2, "tm", 2)]
    parts[-1], by_columns = lax.optimization_barrier((parts[-1], by_columns))
    d = scale(eigen, [keep] + parts)
    moved, across = crossed(d, "space", 2), crossed_both(d, "space", 2, "tm", 1)
    return [add(d, crossed(d, "tm", 1)), add(moved, across)], by_columns


def scale_kernel(eigen, *refs):
    parts, out = refs[:-1], refs[-1]
    total = parts[0][...]
    for part in parts[1:]:
        total = total + part[...]
    out[...] = eigen[0] * total + eigen[1] * turned(total)


def scale(eigen, parts):
    return pl.pallas_call(
        scale_kernel,
        out_shape=pltpu.VMEM(parts[0].shape, F32),
        in_specs=vmem(1 + len(parts)),
        out_specs=vmem(1)[0],
        compiler_params=params(),
        name="scale",
    )(eigen, *parts)


def expand(site, vectors, part, stacks):
    depth = stacks.shape[0] // 2
    total = None
    for half in range(2):
        left = vectors[site, half, :, part * depth : (part + 1) * depth]
        term = matmul(left, stacks[half * depth : (half + 1) * depth])
        total = term if total is None else total + term
    return fold(total)


def place_pieces(pieces, stacks):
    values = [piece[...] for piece in pieces]
    stacks[...] = stack(values[0] if len(values) == 1 else jnp.concatenate(values, axis=0), 1.0)


def first_half_kernel(x, residual, vectors, *refs):
    pieces, (out, stacks) = refs[:-2], refs[-2:]
    place_pieces(pieces, stacks)
    for site in range(x.shape[0]):
        out[site] = x[site] + 0.5 * residual[site] + expand(site, vectors, 0, stacks)


def first_half(x, residual, pieces, vectors):
    return pl.pallas_call(
        first_half_kernel,
        out_shape=pltpu.VMEM(x.shape, F32),
        in_specs=vmem(3 + len(pieces)),
        out_specs=vmem(1)[0],
        scratch_shapes=[pltpu.VMEM((vectors.shape[-1], 2 * x.shape[-1]), BF16)],
        compiler_params=params(),
        cost_estimate=cost(1e9, 4e6),
        name="first_half",
    )(x, residual, vectors, *pieces)


def second_half_kernel(base, vectors, *refs):
    pieces, (out, front, back, stacks) = refs[:-4], refs[-4:]
    place_pieces(pieces, stacks)
    for site in range(base.shape[0]):
        put(site, base[site] + expand(site, vectors, 1, stacks), out, front, back)


def second_half(base, pieces, vectors):
    return pl.pallas_call(
        second_half_kernel,
        out_shape=with_halves(base.shape),
        in_specs=vmem(2 + len(pieces)),
        out_specs=tuple(vmem(3)),
        scratch_shapes=[pltpu.VMEM((vectors.shape[-1], 2 * base.shape[-1]), BF16)],
        compiler_params=params(),
        cost_estimate=cost(1e9, 4e6),
        name="second_half",
    )(base, vectors, *pieces)


def join_kernel(own, other, full, held, sems):
    group = lax.axis_index("groups")
    copies = []
    for site in range(own.shape[0]):
        held[site] = join_halves(own[site], other[site], group)
        copies.append(pltpu.make_async_copy(held.at[site], full.at[site], sems.at[site]))
        copies[-1].start()
    for copy in copies:
        copy.wait()


def join(own, other):
    sites, rows, lanes = own.shape
    shape = (sites, rows, 2 * lanes)
    return pl.pallas_call(
        join_kernel,
        out_shape=jax.ShapeDtypeStruct(shape, F32),
        in_specs=vmem(2),
        out_specs=pl.BlockSpec(memory_space=pl.ANY),
        scratch_shapes=[pltpu.VMEM(shape, F32), pltpu.SemaphoreType.DMA((sites,))],
        compiler_params=params(),
        cost_estimate=cost(1e6, 2e6),
        name="join",
    )(own, other)


def final_kernel(own, other, vectors, *refs):
    pieces, (full, stacks, held, sems) = refs[:-4], refs[-4:]
    group = lax.axis_index("groups")
    place_pieces(pieces, stacks)
    copies = []
    for site in range(own.shape[0]):
        held[site] = join_halves(own[site], other[site] + expand(site, vectors, 1, stacks), group)
        copies.append(pltpu.make_async_copy(held.at[site], full.at[site], sems.at[site]))
        copies[-1].start()
    for copy in copies:
        copy.wait()


def final(own, other, pieces, vectors):
    sites, rows, lanes = own.shape
    shape = (sites, rows, 2 * lanes)
    return pl.pallas_call(
        final_kernel,
        out_shape=jax.ShapeDtypeStruct(shape, F32),
        in_specs=vmem(3 + len(pieces)),
        out_specs=pl.BlockSpec(memory_space=pl.ANY),
        scratch_shapes=[
            pltpu.VMEM((vectors.shape[-1], 2 * lanes), BF16),
            pltpu.VMEM(shape, F32),
            pltpu.SemaphoreType.DMA((sites,)),
        ],
        compiler_params=params(),
        cost_estimate=cost(1e9, 4e6),
        name="final",
    )(own, other, vectors, *pieces)


def shifted(value, axis, step):
    count = lax.axis_size(axis)
    return lax.ppermute(value, axis, [(i, (i + step) % count) for i in range(count)])


def crossed(value, axis, mask):
    count = lax.axis_size(axis)
    return lax.ppermute(value, axis, [(i, i ^ mask) for i in range(count)])


def crossed_both(value, first, first_mask, second, second_mask):
    count, inner = lax.axis_size(first), lax.axis_size(second)
    pairs = [(i * inner + j, (i ^ first_mask) * inner + (j ^ second_mask)) for i in range(count) for j in range(inner)]
    return lax.ppermute(value, (first, second), pairs)


def faces_of(x, front, back):
    count = lax.axis_size("space")
    early = shifted(front, "tm", 1), shifted(front, "tm", -1)
    near, back, x = lax.optimization_barrier((crossed(x, "space", 1), back, x))
    far = lax.ppermute(x, "space", [(i, (i + 1 if i % 2 else i - 1) % count) for i in range(count)])
    late = shifted(back, "tm", 1), shifted(back, "tm", -1)
    return near, far, early, late


def halving(keep, send):
    count = lax.axis_size("space")
    mask = 1
    while True:
        received = crossed(send, "space", mask)
        mask *= 2
        if mask >= count:
            return add(keep, received)
        keep, send = add_split(keep, received)


def doubling(pieces, mask):
    while mask > 1:
        if len(pieces) > 2:
            pieces = [jnp.concatenate(pieces, axis=0)]
        pieces = pieces + [crossed(piece, "space", mask) for piece in pieces]
        mask //= 2
    return pieces


def paired(pieces):
    return [crossed(piece, "space", 1) for piece in pieces]


def across_groups(part, mask):
    return [crossed(part, "groups", 1), crossed_both(part, "groups", 1, "space", mask)]


def over_time(part):
    count = lax.axis_size("tm")
    if count <= 4:
        return [part] + [crossed(part, "tm", mask) for mask in range(1, count)]
    mask = 1
    while mask < count:
        part = part + crossed(part, "tm", mask)
        mask *= 2
    return [part]


def shards(couplings, source, initial, vectors, inverse_eigen):
    directions = couplings.shape[0]
    ny, nx, rows, lanes = source.shape[2:]
    sites = ny * nx
    number = vectors.shape[0]
    blocks = lax.axis_size("space")

    x, early_x, late_x = pack(initial.reshape(sites, rows, lanes))
    faces = faces_of(x, early_x, late_x)
    matrices = couplings.reshape(directions, sites, rows, couplings.shape[-1])
    rest, half_source, local, halo = first_local(x, source.reshape(sites, rows, lanes), matrices, ny, nx)
    across = jnp.transpose(vectors, (1, 2, 3, 4, 5, 0)).reshape(sites * vectors.shape[-1], number)
    by_rows = by_rows_of(across, sites)
    eigen = eigen_of(inverse_eigen, number // blocks, lanes // 2)

    for sweep in range(ITERS):
        last = sweep == ITERS - 1
        if sweep:
            faces = faces_of(x, early_x, late_x)
            rest = local_part(x, half_source, local, ny, nx)
        near, far, early, late = faces
        back_rest, own, partial = middle(rest, near, far, front_faces(*early, halo), halo, by_rows)
        if last:
            partial, x = lax.optimization_barrier((partial, x))
            other_x = crossed(x, "groups", 1)
        back_rest = backward_face(back_rest, late[0], halo)
        residual, keep, send = forward_face(own, partial, back_rest, late[1], halo, by_rows)
        if not last:
            pieces, by_columns = scaled_sum(keep, send, eigen, by_rows, sites)
            base = first_half(x, residual, pieces, by_columns)
            x, early_x, late_x = second_half(base, paired(pieces), by_columns)
    part, residual, other_x = lax.optimization_barrier((halving(keep, send), residual, other_x))
    other_residual = crossed(residual, "groups", 1)
    d = scale(eigen, over_time(part))
    mask = blocks // 2
    other = across_groups(d, mask)
    own = [d, crossed(d, "space", mask)]
    other, own = doubling(other, mask // 2), doubling(own, mask // 2)
    full_residual = join(residual, other_residual)
    own[-1], full_residual = lax.optimization_barrier((own[-1], full_residual))
    own_x = first_half(x, residual, own, by_columns)
    other[0], own_x = lax.optimization_barrier((other[0], own_x))
    own_x, _, _ = second_half(own_x, paired(own), by_columns)
    other[-1], own_x = lax.optimization_barrier((other[-1], own_x))
    other_second = paired(other)
    other_x = first_half(other_x, other_residual, other, by_columns)
    whole = final(own_x, other_x, other_second, by_columns)
    shape = source.shape
    return whole.reshape(shape), full_residual.reshape(shape)


def solution(mesh):
    in_specs = (
        P(None, "tm", "space", None, None, None, None),
        P("tm", "space", None, None, None, None),
        P("tm", "space", None, None, None, None),
        P(None, "tm", "space", None, None, None),
        P(),
    )
    out_specs = (
        P(("groups", "tm"), "space", None, None, None, None),
        P(("groups", "tm"), "space", None, None, None, None),
    )
    return jax.shard_map(shards, mesh=mesh, in_specs=in_specs, out_specs=out_specs, check_vma=False)
```

```python
import functools

import jax
import jax.numpy as jnp
from jax import lax
from jax.experimental import pallas as pl
from jax.experimental.pallas import tpu as pltpu
from jax.sharding import PartitionSpec as P

ITERS = 2
F32 = jnp.float32
BF16 = jnp.bfloat16
LOCAL = 5


def params(mebibytes=12):
    return pltpu.CompilerParams(vmem_limit_bytes=mebibytes * 1024 * 1024)


def cost(flops, read):
    return pl.CostEstimate(flops=int(flops), bytes_accessed=int(read), transcendentals=0)


def low_lanes(value):
    lanes = lax.broadcasted_iota(jnp.int32, value.shape, value.ndim - 1)
    return lanes < value.shape[-1] // 2


def swap(value):
    return pltpu.roll(value, value.shape[-1] // 2, value.ndim - 1)


def turned(value):
    moved = swap(value)
    return jnp.where(low_lanes(value), -moved, moved)


def high_low(value):
    high = value.astype(BF16)
    low = (value - high.astype(F32)).astype(BF16)
    return high, low


def stack(value, sign):
    high, low = high_low(jnp.concatenate([value, sign * turned(value)], axis=0))
    return jnp.concatenate([high, low], axis=1)


def matmul(left, right):
    return jnp.dot(left, right, preferred_element_type=F32)


def fold(product):
    rows, lanes = product.shape[0] // 2, product.shape[1] // 2
    high = product[:rows, :lanes] + (product[:rows, lanes:] + product[rows:, :lanes])
    return high + product[rows:, lanes:]


def pick_half(value, group):
    middle = value.shape[-1] // 2
    real, imag = value[:, :middle], value[:, middle:]
    low = low_lanes(real)
    first = jnp.where(low, real, swap(imag))
    second = jnp.where(low, swap(real), imag)
    return jnp.where(group == 0, first, second)


def join_halves(own, other, group):
    first = jnp.where(group == 0, own, other)
    second = jnp.where(group == 0, other, own)
    low = low_lanes(own)
    real = jnp.where(low, first, swap(second))
    imag = jnp.where(low, swap(first), second)
    return jnp.concatenate([real, imag], axis=1)


def vmem(count):
    return [pl.BlockSpec(memory_space=pltpu.VMEM)] * count


def in_hbm(value):
    return pltpu.with_memory_space_constraint(value, pltpu.HBM)


def put(site, value, whole, front, back):
    count = front.shape[0]
    whole[site] = value
    if site < count:
        front[site] = value
    else:
        back[site - count] = value


def with_halves(shape):
    part = pltpu.VMEM((shape[0] // 2,) + tuple(shape[1:]), F32)
    return pltpu.VMEM(shape, F32), part, part


def pack_kernel(full, half, front, back):
    group = lax.axis_index("groups")
    for site in range(full.shape[0]):
        put(site, pick_half(full[site], group), half, front, back)


def pack(full):
    sites, rows, lanes = full.shape
    return pl.pallas_call(
        pack_kernel,
        out_shape=with_halves((sites, rows, lanes // 2)),
        in_specs=vmem(1),
        out_specs=tuple(vmem(3)),
        compiler_params=params(),
        cost_estimate=cost(1e6, 1e6),
        name="pack",
    )(full)


def around(site, ny, nx):
    y, x = site // nx, site % nx
    right, left = (x + 1) % nx, (x - 1) % nx
    up, down = (y + 1) % ny, (y - 1) % ny
    return (site, y * nx + right, y * nx + left, up * nx + x, down * nx + x)


def local_sum(site, ny, nx, stacks, local):
    total = None
    for direction, neighbour in enumerate(around(site, ny, nx)):
        term = matmul(local[direction, site], stacks[neighbour])
        total = term if total is None else total + term
    return fold(total)


def first_kernel(ny, nx, x_ref, source, couplings, rest, half_source, local, halo, stacks, held, held_source, sems):
    group = lax.axis_index("groups")
    sites = x_ref.shape[0]
    copies = []
    for site in range(sites):
        copies.append(pltpu.make_async_copy(couplings.at[:, site], held.at[site], sems.at[site]))
        copies[-1].start()
    bring = pltpu.make_async_copy(source, held_source, sems.at[sites])
    bring.start()
    for site in range(sites):
        stacks[site] = stack(x_ref[site], 1.0)
    bring.wait()
    for site in range(sites):
        half_source[site] = pick_half(held_source[site], group)
    for site in range(sites):
        copies[site].wait()
        for direction in range(couplings.shape[0]):
            high, low = high_low(held[site, direction])
            both = jnp.concatenate([high, low], axis=0)
            if direction < LOCAL:
                local[direction, site] = both
            else:
                halo[direction - LOCAL, site] = both
        rest[site] = half_source[site] - local_sum(site, ny, nx, stacks, local)


def first_local(x, source, couplings, ny, nx):
    sites, rows, lanes = x.shape
    directions, _, _, columns = couplings.shape
    outer = directions - LOCAL
    in_place = pl.BlockSpec(memory_space=pl.ANY)
    return pl.pallas_call(
        functools.partial(first_kernel, ny, nx),
        out_shape=(
            pltpu.VMEM(x.shape, F32),
            pltpu.VMEM(x.shape, F32),
            pltpu.VMEM((LOCAL, sites, 2 * rows, columns), BF16),
            pltpu.VMEM((outer, sites, 2 * rows, columns), BF16),
        ),
        in_specs=vmem(1) + [in_place, in_place],
        out_specs=tuple(vmem(4)),
        scratch_shapes=[
            pltpu.VMEM((sites, 2 * rows, 2 * lanes), BF16),
            pltpu.VMEM((sites, directions, rows, columns), F32),
            pltpu.VMEM(source.shape, F32),
            pltpu.SemaphoreType.DMA((sites + 1,)),
        ],
        compiler_params=params(20),
        cost_estimate=cost(8e9, 16e6),
        name="first_local",
    )(x, in_hbm(source), in_hbm(couplings))


def local_kernel(ny, nx, x_ref, source, local, rest, stacks):
    for site in range(x_ref.shape[0]):
        stacks[site] = stack(x_ref[site], 1.0)
    for site in range(x_ref.shape[0]):
        rest[site] = source[site] - local_sum(site, ny, nx, stacks, local)


def local_part(x, source, local, ny, nx):
    sites, rows, lanes = x.shape
    return pl.pallas_call(
        functools.partial(local_kernel, ny, nx),
        out_shape=pltpu.VMEM(x.shape, F32),
        in_specs=vmem(3),
        out_specs=vmem(1)[0],
        scratch_shapes=[pltpu.VMEM((sites, 2 * rows, 2 * lanes), BF16)],
        compiler_params=params(),
        cost_estimate=cost(8e9, 8e6),
        name="local_part",
    )(x, source, local)


def block_order(count):
    bits = count.bit_length() - 1
    return [int(format(index, "b").zfill(bits)[::-1], 2) if bits else 0 for index in range(count)]


def ordered_rows(rows, chunk, taken):
    blocks = lax.axis_size("space")
    space = lax.axis_index("space")
    size = rows.shape[0] // blocks
    unit = min(size, taken)
    parts = []
    for start in range(chunk * taken, (chunk + 1) * taken, unit):
        block = space ^ block_order(blocks)[start // size]
        parts.append(rows[pl.ds(pl.multiple_of(block * size + start % size, unit), unit)])
    return parts[0] if len(parts) == 1 else jnp.concatenate(parts, axis=0)


def vectors_kernel(across, by_rows, by_columns, turned_rows):
    sites, _, double, number = by_columns.shape
    rows = double // 2
    taken = 128
    turned_rows[...] = across[...].T
    for chunk in range(number // taken):
        part = ordered_rows(turned_rows, chunk, taken)
        high, low = high_low(part)
        at = slice(chunk * taken, (chunk + 1) * taken)
        by_rows[at] = high
        by_rows[number + chunk * taken : number + (chunk + 1) * taken] = low
        back = part.T
        for site in range(sites):
            for half in range(2):
                start = (2 * site + half) * rows
                high, low = high_low(back[start : start + rows])
                by_columns[site, half, :rows, at] = high
                by_columns[site, half, rows:, at] = low


def vectors_parts(across, sites):
    width, number = across.shape
    rows = width // sites // 2
    step = 2
    return pl.pallas_call(
        vectors_kernel,
        grid=(sites // step,),
        out_shape=(pltpu.VMEM((2 * number, width), BF16), pltpu.VMEM((sites, 2, 2 * rows, number), BF16)),
        in_specs=[pl.BlockSpec((step * 2 * rows, number), lambda s: (s, 0))],
        out_specs=(
            pl.BlockSpec((2 * number, step * 2 * rows), lambda s: (0, s)),
            pl.BlockSpec((step, 2, 2 * rows, number), lambda s: (s, 0, 0, 0)),
        ),
        scratch_shapes=[pltpu.VMEM((number, step * 2 * rows), F32)],
        compiler_params=params(16),
        cost_estimate=cost(1e6, 9e6),
        name="vectors_parts",
    )(in_hbm(across))


def eigen_kernel(inverse, out):
    size, lanes = out.shape[1:]
    number = inverse.shape[1]
    start = lax.axis_index("space") * size
    row = lax.broadcasted_iota(jnp.int32, (size, number), 0) + start
    chosen = lax.broadcasted_iota(jnp.int32, (size, number), 1) == row
    for part in range(2):
        value = jnp.where(chosen, inverse[part : part + 1], 0.0)
        out[part] = jnp.broadcast_to(jnp.sum(value, axis=1, keepdims=True), (size, lanes))


def eigen_of(inverse, size, lanes):
    return pl.pallas_call(
        eigen_kernel,
        out_shape=pltpu.VMEM((2, size, lanes), F32),
        in_specs=vmem(1),
        out_specs=vmem(1)[0],
        compiler_params=params(),
        cost_estimate=cost(1e6, 1e6),
        name="eigen",
    )(inverse)


def apply_faces(*pairs):
    summed = None
    for matrix, face in pairs:
        term = matmul(matrix, stack(face, 1.0))
        summed = term if summed is None else summed + term
    return fold(summed)


def edge_sign(last):
    count = lax.axis_size("tm")
    return jnp.where(lax.axis_index("tm") == (count - 1 if last else 0), -1.0, 1.0).astype(F32)


def front_kernel(backward, forward, matrix, out):
    behind, ahead = edge_sign(False), edge_sign(True)
    for site in range(out.shape[0]):
        out[site] = apply_faces((matrix[2, site], ahead * forward[site]), (matrix[3, site], behind * backward[site]))


def front_faces(backward, forward, matrix):
    return pl.pallas_call(
        front_kernel,
        out_shape=pltpu.VMEM(forward.shape, F32),
        in_specs=vmem(3),
        out_specs=vmem(1)[0],
        compiler_params=params(),
        cost_estimate=cost(1e3, 1e3),
        name="front_faces",
    )(backward, forward, matrix)


def middle_kernel(rest, near, far, front, matrix, vectors, back, residual, partial, stacks):
    parity = lax.rem(lax.axis_index("space"), 2)
    sites, rows, _ = front.shape
    for site in range(rest.shape[0]):
        own = rest[site] - apply_faces((matrix[parity, site], near[site]), (matrix[1 - parity, site], far[site]))
        if site < sites:
            own = own - front[site]
            residual[site] = own
            stacks[site * 2 * rows : (site + 1) * 2 * rows] = stack(own, -1.0)
        else:
            back[site - sites] = own
    partial[...] = fold(matmul(vectors[:, : stacks.shape[0]], stacks[...]))


def middle(rest, near, far, front, matrix, vectors):
    sites, rows, lanes = front.shape
    half = pltpu.VMEM(front.shape, F32)
    return pl.pallas_call(
        middle_kernel,
        out_shape=(half, half, pltpu.VMEM((vectors.shape[0] // 2, lanes), F32)),
        in_specs=vmem(6),
        out_specs=tuple(vmem(3)),
        scratch_shapes=[pltpu.VMEM((sites * 2 * rows, 2 * lanes), BF16)],
        compiler_params=params(),
        cost_estimate=cost(1e3, 1e3),
        name="middle",
    )(rest, near, far, front, matrix, vectors)


def backward_kernel(rest, backward, matrix, out):
    sign = edge_sign(False)
    sites = backward.shape[0]
    for site in range(sites):
        out[site] = rest[site] - apply_faces((matrix[3, sites + site], sign * backward[site]))


def backward_face(rest, backward, matrix):
    return pl.pallas_call(
        backward_kernel,
        out_shape=pltpu.VMEM(backward.shape, F32),
        in_specs=vmem(3),
        out_specs=vmem(1)[0],
        compiler_params=params(),
        cost_estimate=cost(1e3, 1e3),
        name="backward_face",
    )(rest, backward, matrix)


def forward_kernel(front, partial, rest, forward, matrix, vectors, residual, keep, send, stacks):
    sign = edge_sign(True)
    sites, rows, _ = forward.shape
    for site in range(sites):
        own = rest[site] - apply_faces((matrix[2, sites + site], sign * forward[site]))
        residual[site] = front[site]
        residual[sites + site] = own
        stacks[site * 2 * rows : (site + 1) * 2 * rows] = stack(own, -1.0)
    whole = partial[...] + fold(matmul(vectors[:, stacks.shape[0] :], stacks[...]))
    half = whole.shape[0] // 2
    keep[...] = whole[:half]
    send[...] = whole[half:]


def forward_face(front, partial, rest, forward, matrix, vectors):
    sites, rows, lanes = forward.shape
    part = pltpu.VMEM((vectors.shape[0] // 4, lanes), F32)
    return pl.pallas_call(
        forward_kernel,
        out_shape=(pltpu.VMEM((2 * sites, rows, lanes), F32), part, part),
        in_specs=vmem(6),
        out_specs=tuple(vmem(3)),
        scratch_shapes=[pltpu.VMEM((sites * 2 * rows, 2 * lanes), BF16)],
        compiler_params=params(),
        cost_estimate=cost(2e9, 8e6),
        name="forward_face",
    )(front, partial, rest, forward, matrix, vectors)


def split_kernel(keep, received, next_keep, next_send):
    half = next_keep.shape[0]
    next_keep[...] = keep[:half] + received[:half]
    next_send[...] = keep[half:] + received[half:]


def add_split(keep, received):
    rows, lanes = keep.shape
    part = pltpu.VMEM((rows // 2, lanes), F32)
    return pl.pallas_call(
        split_kernel,
        out_shape=(part, part),
        in_specs=vmem(2),
        out_specs=tuple(vmem(2)),
        compiler_params=params(),
        name="add_split",
    )(keep, received)


def add_kernel(left, right, out):
    out[...] = left[...] + right[...]


def add(left, right):
    return pl.pallas_call(
        add_kernel,
        out_shape=pltpu.VMEM(left.shape, F32),
        in_specs=vmem(2),
        out_specs=vmem(1)[0],
        compiler_params=params(),
        name="add",
    )(left, right)


def scaled_sum(keep, send, eigen):
    blocks, slices = lax.axis_size("space"), lax.axis_size("tm")
    if blocks != 4 or slices != 4:
        return doubling([scale(eigen, over_time(halving(keep, send)))], blocks // 2)
    keep, send = add_split(keep, crossed(send, "space", 1))
    parts = [crossed(send, "space", 2), crossed(keep, "tm", 2), crossed_both(send, "space", 2, "tm", 2)]
    d = scale(eigen, [keep] + parts)
    moved, across = crossed(d, "space", 2), crossed_both(d, "space", 2, "tm", 1)
    return [add(d, crossed(d, "tm", 1)), add(moved, across)]


def scale_kernel(eigen, *refs):
    parts, out = refs[:-1], refs[-1]
    total = parts[0][...]
    for part in parts[1:]:
        total = total + part[...]
    out[...] = eigen[0] * total + eigen[1] * turned(total)


def scale(eigen, parts):
    return pl.pallas_call(
        scale_kernel,
        out_shape=pltpu.VMEM(parts[0].shape, F32),
        in_specs=vmem(1 + len(parts)),
        out_specs=vmem(1)[0],
        compiler_params=params(),
        name="scale",
    )(eigen, *parts)


def expand(site, vectors, part, stacks):
    depth = stacks.shape[0] // 2
    total = None
    for half in range(2):
        left = vectors[site, half, :, part * depth : (part + 1) * depth]
        term = matmul(left, stacks[half * depth : (half + 1) * depth])
        total = term if total is None else total + term
    return fold(total)


def place_pieces(pieces, stacks):
    values = [piece[...] for piece in pieces]
    stacks[...] = stack(values[0] if len(values) == 1 else jnp.concatenate(values, axis=0), 1.0)


def first_half_kernel(x, residual, vectors, *refs):
    pieces, (out, stacks) = refs[:-2], refs[-2:]
    place_pieces(pieces, stacks)
    for site in range(x.shape[0]):
        out[site] = x[site] + 0.5 * residual[site] + expand(site, vectors, 0, stacks)


def first_half(x, residual, pieces, vectors):
    return pl.pallas_call(
        first_half_kernel,
        out_shape=pltpu.VMEM(x.shape, F32),
        in_specs=vmem(3 + len(pieces)),
        out_specs=vmem(1)[0],
        scratch_shapes=[pltpu.VMEM((vectors.shape[-1], 2 * x.shape[-1]), BF16)],
        compiler_params=params(),
        cost_estimate=cost(1e9, 4e6),
        name="first_half",
    )(x, residual, vectors, *pieces)


def second_half_kernel(count, base, vectors, *refs):
    pieces, (outs, stacks) = refs[:count], (refs[count:-1], refs[-1])
    place_pieces(pieces, stacks)
    for site in range(base.shape[0]):
        value = base[site] + expand(site, vectors, 1, stacks)
        if len(outs) == 1:
            outs[0][site] = value
        else:
            put(site, value, *outs)


def second_half(base, pieces, vectors, halves):
    return pl.pallas_call(
        functools.partial(second_half_kernel, len(pieces)),
        out_shape=with_halves(base.shape) if halves else pltpu.VMEM(base.shape, F32),
        in_specs=vmem(2 + len(pieces)),
        out_specs=tuple(vmem(3)) if halves else vmem(1)[0],
        scratch_shapes=[pltpu.VMEM((vectors.shape[-1], 2 * base.shape[-1]), BF16)],
        compiler_params=params(),
        cost_estimate=cost(1e9, 4e6),
        name="second_half",
    )(base, vectors, *pieces)


def join_kernel(own, other, full, held, sems):
    group = lax.axis_index("groups")
    copies = []
    for site in range(own.shape[0]):
        held[site] = join_halves(own[site], other[site], group)
        copies.append(pltpu.make_async_copy(held.at[site], full.at[site], sems.at[site]))
        copies[-1].start()
    for copy in copies:
        copy.wait()


def join(own, other):
    sites, rows, lanes = own.shape
    shape = (sites, rows, 2 * lanes)
    return pl.pallas_call(
        join_kernel,
        out_shape=jax.ShapeDtypeStruct(shape, F32),
        in_specs=vmem(2),
        out_specs=pl.BlockSpec(memory_space=pl.ANY),
        scratch_shapes=[pltpu.VMEM(shape, F32), pltpu.SemaphoreType.DMA((sites,))],
        compiler_params=params(),
        cost_estimate=cost(1e6, 2e6),
        name="join",
    )(own, other)


def final_kernel(own, other, vectors, *refs):
    pieces, (full, stacks, held, sems) = refs[:-4], refs[-4:]
    group = lax.axis_index("groups")
    place_pieces(pieces, stacks)
    copies = []
    for site in range(own.shape[0]):
        held[site] = join_halves(own[site], other[site] + expand(site, vectors, 1, stacks), group)
        copies.append(pltpu.make_async_copy(held.at[site], full.at[site], sems.at[site]))
        copies[-1].start()
    for copy in copies:
        copy.wait()


def final(own, other, pieces, vectors):
    sites, rows, lanes = own.shape
    shape = (sites, rows, 2 * lanes)
    return pl.pallas_call(
        final_kernel,
        out_shape=jax.ShapeDtypeStruct(shape, F32),
        in_specs=vmem(3 + len(pieces)),
        out_specs=pl.BlockSpec(memory_space=pl.ANY),
        scratch_shapes=[
            pltpu.VMEM((vectors.shape[-1], 2 * lanes), BF16),
            pltpu.VMEM(shape, F32),
            pltpu.SemaphoreType.DMA((sites,)),
        ],
        compiler_params=params(),
        cost_estimate=cost(1e9, 4e6),
        name="final",
    )(own, other, vectors, *pieces)


def shifted(value, axis, step):
    count = lax.axis_size(axis)
    return lax.ppermute(value, axis, [(i, (i + step) % count) for i in range(count)])


def crossed(value, axis, mask):
    count = lax.axis_size(axis)
    return lax.ppermute(value, axis, [(i, i ^ mask) for i in range(count)])


def crossed_both(value, first, first_mask, second, second_mask):
    count, inner = lax.axis_size(first), lax.axis_size(second)
    pairs = [(i * inner + j, (i ^ first_mask) * inner + (j ^ second_mask)) for i in range(count) for j in range(inner)]
    return lax.ppermute(value, (first, second), pairs)


def faces_of(x, front, back):
    count = lax.axis_size("space")
    early = shifted(front, "tm", 1), shifted(front, "tm", -1)
    near, back = lax.optimization_barrier((crossed(x, "space", 1), back))
    far = lax.ppermute(x, "space", [(i, (i + 1 if i % 2 else i - 1) % count) for i in range(count)])
    late = shifted(back, "tm", 1), shifted(back, "tm", -1)
    return near, far, early, late


def halving(keep, send):
    count = lax.axis_size("space")
    mask = 1
    while True:
        received = crossed(send, "space", mask)
        mask *= 2
        if mask >= count:
            return add(keep, received)
        keep, send = add_split(keep, received)


def doubling(pieces, mask):
    while mask > 1:
        if len(pieces) > 2:
            pieces = [jnp.concatenate(pieces, axis=0)]
        pieces = pieces + [crossed(piece, "space", mask) for piece in pieces]
        mask //= 2
    return pieces


def paired(pieces):
    return [crossed(piece, "space", 1) for piece in pieces]


def across_groups(part, mask):
    return [crossed(part, "groups", 1), crossed_both(part, "groups", 1, "space", mask)]


def over_time(part):
    count = lax.axis_size("tm")
    if count <= 4:
        return [part] + [crossed(part, "tm", mask) for mask in range(1, count)]
    mask = 1
    while mask < count:
        part = part + crossed(part, "tm", mask)
        mask *= 2
    return [part]


def shards(couplings, source, initial, vectors, inverse_eigen):
    directions = couplings.shape[0]
    ny, nx, rows, lanes = source.shape[2:]
    sites = ny * nx
    number = vectors.shape[0]
    blocks = lax.axis_size("space")

    x, early_x, late_x = pack(initial.reshape(sites, rows, lanes))
    faces = faces_of(x, early_x, late_x)
    matrices = couplings.reshape(directions, sites, rows, couplings.shape[-1])
    rest, half_source, local, halo = first_local(x, source.reshape(sites, rows, lanes), matrices, ny, nx)
    across = jnp.transpose(vectors, (1, 2, 3, 4, 5, 0)).reshape(sites * vectors.shape[-1], number)
    by_rows, by_columns = vectors_parts(across, sites)
    eigen = eigen_of(inverse_eigen, number // blocks, lanes // 2)

    for sweep in range(ITERS):
        last = sweep == ITERS - 1
        if sweep:
            faces = faces_of(x, early_x, late_x)
            rest = local_part(x, half_source, local, ny, nx)
        if last:
            rest, x = lax.optimization_barrier((rest, x))
            other_x = crossed(x, "groups", 1)
        near, far, early, late = faces
        back_rest, own, partial = middle(rest, near, far, front_faces(*early, halo), halo, by_rows)
        back_rest = backward_face(back_rest, late[0], halo)
        residual, keep, send = forward_face(own, partial, back_rest, late[1], halo, by_rows)
        if not last:
            pieces = scaled_sum(keep, send, eigen)
            base = first_half(x, residual, pieces, by_columns)
            x, early_x, late_x = second_half(base, paired(pieces), by_columns, True)
    part, residual, other_x = lax.optimization_barrier((halving(keep, send), residual, other_x))
    other_residual = crossed(residual, "groups", 1)
    d = scale(eigen, over_time(part))
    mask = blocks // 2
    other = across_groups(d, mask)
    own = [d, crossed(d, "space", mask)]
    other, own = doubling(other, mask // 2), doubling(own, mask // 2)
    full_residual = join(residual, other_residual)
    own[-1], full_residual = lax.optimization_barrier((own[-1], full_residual))
    own_x = first_half(x, residual, own, by_columns)
    other[0], own_x = lax.optimization_barrier((other[0], own_x))
    own_x = second_half(own_x, paired(own), by_columns, False)
    other[-1], own_x = lax.optimization_barrier((other[-1], own_x))
    other_second = paired(other)
    other_x = first_half(other_x, other_residual, other, by_columns)
    whole = final(own_x, other_x, other_second, by_columns)
    shape = source.shape
    return whole.reshape(shape), full_residual.reshape(shape)


def solution(mesh):
    in_specs = (
        P(None, "tm", "space", None, None, None, None),
        P("tm", "space", None, None, None, None),
        P("tm", "space", None, None, None, None),
        P(None, "tm", "space", None, None, None),
        P(),
    )
    out_specs = (
        P(("groups", "tm"), "space", None, None, None, None),
        P(("groups", "tm"), "space", None, None, None, None),
    )
    return jax.shard_map(shards, mesh=mesh, in_specs=in_specs, out_specs=out_specs, check_vma=False)
```

```python
import functools

import jax
import jax.numpy as jnp
from jax import lax
from jax.experimental import pallas as pl
from jax.experimental.pallas import tpu as pltpu
from jax.sharding import PartitionSpec as P

ITERS = 2
F32 = jnp.float32
BF16 = jnp.bfloat16
LOCAL = 5


def params(mebibytes=12):
    return pltpu.CompilerParams(vmem_limit_bytes=mebibytes * 1024 * 1024)


def cost(flops, read):
    return pl.CostEstimate(flops=int(flops), bytes_accessed=int(read), transcendentals=0)


def low_lanes(value):
    lanes = lax.broadcasted_iota(jnp.int32, value.shape, value.ndim - 1)
    return lanes < value.shape[-1] // 2


def swap(value):
    return pltpu.roll(value, value.shape[-1] // 2, value.ndim - 1)


def turned(value):
    moved = swap(value)
    return jnp.where(low_lanes(value), -moved, moved)


def high_low(value):
    high = value.astype(BF16)
    low = (value - high.astype(F32)).astype(BF16)
    return high, low


def stack(value, sign):
    high, low = high_low(jnp.concatenate([value, sign * turned(value)], axis=0))
    return jnp.concatenate([high, low], axis=1)


def matmul(left, right):
    return jnp.dot(left, right, preferred_element_type=F32)


def fold(product):
    rows, lanes = product.shape[0] // 2, product.shape[1] // 2
    high = product[:rows, :lanes] + (product[:rows, lanes:] + product[rows:, :lanes])
    return high + product[rows:, lanes:]


def pick_half(value, group):
    middle = value.shape[-1] // 2
    real, imag = value[:, :middle], value[:, middle:]
    low = low_lanes(real)
    first = jnp.where(low, real, swap(imag))
    second = jnp.where(low, swap(real), imag)
    return jnp.where(group == 0, first, second)


def join_halves(own, other, group):
    first = jnp.where(group == 0, own, other)
    second = jnp.where(group == 0, other, own)
    low = low_lanes(own)
    real = jnp.where(low, first, swap(second))
    imag = jnp.where(low, swap(first), second)
    return jnp.concatenate([real, imag], axis=1)


def vmem(count):
    return [pl.BlockSpec(memory_space=pltpu.VMEM)] * count


def in_hbm(value):
    return pltpu.with_memory_space_constraint(value, pltpu.HBM)


def put(site, value, whole, front, back):
    count = front.shape[0]
    whole[site] = value
    if site < count:
        front[site] = value
    else:
        back[site - count] = value


def with_halves(shape):
    part = pltpu.VMEM((shape[0] // 2,) + tuple(shape[1:]), F32)
    return pltpu.VMEM(shape, F32), part, part


def pack_kernel(full, half, front, back):
    group = lax.axis_index("groups")
    for site in range(full.shape[0]):
        put(site, pick_half(full[site], group), half, front, back)


def pack(full):
    sites, rows, lanes = full.shape
    return pl.pallas_call(
        pack_kernel,
        out_shape=with_halves((sites, rows, lanes // 2)),
        in_specs=vmem(1),
        out_specs=tuple(vmem(3)),
        compiler_params=params(),
        cost_estimate=cost(1e6, 1e6),
        name="pack",
    )(full)


def around(site, ny, nx):
    y, x = site // nx, site % nx
    right, left = (x + 1) % nx, (x - 1) % nx
    up, down = (y + 1) % ny, (y - 1) % ny
    return (site, y * nx + right, y * nx + left, up * nx + x, down * nx + x)


def local_sum(site, ny, nx, stacks, local):
    total = None
    for direction, neighbour in enumerate(around(site, ny, nx)):
        term = matmul(local[direction, site], stacks[neighbour])
        total = term if total is None else total + term
    return fold(total)


def local_kernel(ny, nx, x_ref, source, local, rest, stacks):
    for site in range(x_ref.shape[0]):
        stacks[site] = stack(x_ref[site], 1.0)
    for site in range(x_ref.shape[0]):
        rest[site] = source[site] - local_sum(site, ny, nx, stacks, local)


def local_part(x, source, local, ny, nx):
    sites, rows, lanes = x.shape
    return pl.pallas_call(
        functools.partial(local_kernel, ny, nx),
        out_shape=pltpu.VMEM(x.shape, F32),
        in_specs=vmem(3),
        out_specs=vmem(1)[0],
        scratch_shapes=[pltpu.VMEM((sites, 2 * rows, 2 * lanes), BF16)],
        compiler_params=params(),
        cost_estimate=cost(8e9, 8e6),
        name="local_part",
    )(x, source, local)


def block_order(count):
    bits = count.bit_length() - 1
    return [int(format(index, "b").zfill(bits)[::-1], 2) if bits else 0 for index in range(count)]


def ordered_rows(rows, chunk, taken):
    blocks = lax.axis_size("space")
    space = lax.axis_index("space")
    size = rows.shape[0] // blocks
    unit = min(size, taken)
    parts = []
    for start in range(chunk * taken, (chunk + 1) * taken, unit):
        block = space ^ block_order(blocks)[start // size]
        parts.append(rows[pl.ds(pl.multiple_of(block * size + start % size, unit), unit)])
    return parts[0] if len(parts) == 1 else jnp.concatenate(parts, axis=0)


def prepare_kernel(ny, nx, x_ref, source, couplings, across, rest, half_source, local, halo, by_rows, by_columns, stacks, held, held_source, held_across, turned_rows, sems):
    group = lax.axis_index("groups")
    sites, directions, rows = held.shape[:3]
    number = held_across.shape[1]
    taken, step = 128, turned_rows.shape[1]
    arriving = []
    for site in range(sites):
        arriving.append(pltpu.make_async_copy(couplings.at[:, site], held.at[site], sems.at[site]))
    arriving.append(pltpu.make_async_copy(source, held_source, sems.at[sites]))
    for index in range(held_across.shape[0] // step):
        at = pl.ds(index * step, step)
        arriving.append(pltpu.make_async_copy(across.at[at], held_across.at[at], sems.at[sites + 1 + index]))
    for copy in arriving:
        copy.start()
    for site in range(sites):
        stacks[site] = stack(x_ref[site], 1.0)
    for site in range(sites):
        arriving[site].wait()
        for direction in range(directions):
            high, low = high_low(held[site, direction])
            both = jnp.concatenate([high, low], axis=0)
            if direction < LOCAL:
                local[direction, site] = both
            else:
                halo[direction - LOCAL, site] = both
        if site == 0:
            arriving[sites].wait()
        own = pick_half(held_source[site], group)
        half_source[site] = own
        rest[site] = own - local_sum(site, ny, nx, stacks, local)
    for index, copy in enumerate(arriving[sites + 1 :]):
        copy.wait()
        at = slice(index * step, (index + 1) * step)
        turned_rows[...] = held_across[at].T
        for chunk in range(number // taken):
            part = ordered_rows(turned_rows, chunk, taken)
            high, low = high_low(part)
            by_rows[chunk * taken : (chunk + 1) * taken, at] = high
            by_rows[number + chunk * taken : number + (chunk + 1) * taken, at] = low
            back = part.T
            for half in range(step // rows):
                high, low = high_low(back[half * rows : (half + 1) * rows])
                site, which = divmod(index * (step // rows) + half, 2)
                lanes = slice(chunk * taken, (chunk + 1) * taken)
                by_columns[site, which, :rows, lanes] = high
                by_columns[site, which, rows:, lanes] = low


def prepare(x, source, couplings, across, ny, nx):
    sites, rows, lanes = x.shape
    directions, _, _, columns = couplings.shape
    width, number = across.shape
    outer = directions - LOCAL
    step = width // (sites // 2)
    return pl.pallas_call(
        functools.partial(prepare_kernel, ny, nx),
        out_shape=(
            pltpu.VMEM(x.shape, F32),
            pltpu.VMEM(x.shape, F32),
            pltpu.VMEM((LOCAL, sites, 2 * rows, columns), BF16),
            pltpu.VMEM((outer, sites, 2 * rows, columns), BF16),
            pltpu.VMEM((2 * number, width), BF16),
            pltpu.VMEM((sites, 2, 2 * rows, number), BF16),
        ),
        in_specs=vmem(1) + [pl.BlockSpec(memory_space=pl.ANY)] * 3,
        out_specs=tuple(vmem(6)),
        scratch_shapes=[
            pltpu.VMEM((sites, 2 * rows, 2 * lanes), BF16),
            pltpu.VMEM((sites, directions, rows, columns), F32),
            pltpu.VMEM(source.shape, F32),
            pltpu.VMEM(across.shape, F32),
            pltpu.VMEM((number, step), F32),
            pltpu.SemaphoreType.DMA((sites + 1 + width // step,)),
        ],
        compiler_params=params(24),
        cost_estimate=cost(8e9, 25e6),
        name="prepare",
    )(x, in_hbm(source), in_hbm(couplings), in_hbm(across))


def eigen_kernel(inverse, out):
    size, lanes = out.shape[1:]
    number = inverse.shape[1]
    start = lax.axis_index("space") * size
    row = lax.broadcasted_iota(jnp.int32, (size, number), 0) + start
    chosen = lax.broadcasted_iota(jnp.int32, (size, number), 1) == row
    for part in range(2):
        value = jnp.where(chosen, inverse[part : part + 1], 0.0)
        out[part] = jnp.broadcast_to(jnp.sum(value, axis=1, keepdims=True), (size, lanes))


def eigen_of(inverse, size, lanes):
    return pl.pallas_call(
        eigen_kernel,
        out_shape=pltpu.VMEM((2, size, lanes), F32),
        in_specs=vmem(1),
        out_specs=vmem(1)[0],
        compiler_params=params(),
        cost_estimate=cost(1e6, 1e6),
        name="eigen",
    )(inverse)


def apply_faces(*pairs):
    summed = None
    for matrix, face in pairs:
        term = matmul(matrix, stack(face, 1.0))
        summed = term if summed is None else summed + term
    return fold(summed)


def edge_sign(last):
    count = lax.axis_size("tm")
    return jnp.where(lax.axis_index("tm") == (count - 1 if last else 0), -1.0, 1.0).astype(F32)


def front_kernel(backward, forward, matrix, out):
    behind, ahead = edge_sign(False), edge_sign(True)
    for site in range(out.shape[0]):
        out[site] = apply_faces((matrix[2, site], ahead * forward[site]), (matrix[3, site], behind * backward[site]))


def front_faces(backward, forward, matrix):
    return pl.pallas_call(
        front_kernel,
        out_shape=pltpu.VMEM(forward.shape, F32),
        in_specs=vmem(3),
        out_specs=vmem(1)[0],
        compiler_params=params(),
        cost_estimate=cost(1e3, 1e3),
        name="front_faces",
    )(backward, forward, matrix)


def middle_kernel(rest, near, far, front, matrix, vectors, back, residual, partial, stacks):
    parity = lax.rem(lax.axis_index("space"), 2)
    sites, rows, _ = front.shape
    for site in range(rest.shape[0]):
        own = rest[site] - apply_faces((matrix[parity, site], near[site]), (matrix[1 - parity, site], far[site]))
        if site < sites:
            own = own - front[site]
            residual[site] = own
            stacks[site * 2 * rows : (site + 1) * 2 * rows] = stack(own, -1.0)
        else:
            back[site - sites] = own
    partial[...] = fold(matmul(vectors[:, : stacks.shape[0]], stacks[...]))


def middle(rest, near, far, front, matrix, vectors):
    sites, rows, lanes = front.shape
    half = pltpu.VMEM(front.shape, F32)
    return pl.pallas_call(
        middle_kernel,
        out_shape=(half, half, pltpu.VMEM((vectors.shape[0] // 2, lanes), F32)),
        in_specs=vmem(6),
        out_specs=tuple(vmem(3)),
        scratch_shapes=[pltpu.VMEM((sites * 2 * rows, 2 * lanes), BF16)],
        compiler_params=params(),
        cost_estimate=cost(1e3, 1e3),
        name="middle",
    )(rest, near, far, front, matrix, vectors)


def backward_kernel(rest, backward, matrix, out):
    sign = edge_sign(False)
    sites = backward.shape[0]
    for site in range(sites):
        out[site] = rest[site] - apply_faces((matrix[3, sites + site], sign * backward[site]))


def backward_face(rest, backward, matrix):
    return pl.pallas_call(
        backward_kernel,
        out_shape=pltpu.VMEM(backward.shape, F32),
        in_specs=vmem(3),
        out_specs=vmem(1)[0],
        compiler_params=params(),
        cost_estimate=cost(1e3, 1e3),
        name="backward_face",
    )(rest, backward, matrix)


def forward_kernel(front, partial, rest, forward, matrix, vectors, residual, keep, send, stacks):
    sign = edge_sign(True)
    sites, rows, _ = forward.shape
    for site in range(sites):
        own = rest[site] - apply_faces((matrix[2, sites + site], sign * forward[site]))
        residual[site] = front[site]
        residual[sites + site] = own
        stacks[site * 2 * rows : (site + 1) * 2 * rows] = stack(own, -1.0)
    whole = partial[...] + fold(matmul(vectors[:, stacks.shape[0] :], stacks[...]))
    half = whole.shape[0] // 2
    keep[...] = whole[:half]
    send[...] = whole[half:]


def forward_face(front, partial, rest, forward, matrix, vectors):
    sites, rows, lanes = forward.shape
    part = pltpu.VMEM((vectors.shape[0] // 4, lanes), F32)
    return pl.pallas_call(
        forward_kernel,
        out_shape=(pltpu.VMEM((2 * sites, rows, lanes), F32), part, part),
        in_specs=vmem(6),
        out_specs=tuple(vmem(3)),
        scratch_shapes=[pltpu.VMEM((sites * 2 * rows, 2 * lanes), BF16)],
        compiler_params=params(),
        cost_estimate=cost(2e9, 8e6),
        name="forward_face",
    )(front, partial, rest, forward, matrix, vectors)


def split_kernel(keep, received, next_keep, next_send):
    half = next_keep.shape[0]
    next_keep[...] = keep[:half] + received[:half]
    next_send[...] = keep[half:] + received[half:]


def add_split(keep, received):
    rows, lanes = keep.shape
    part = pltpu.VMEM((rows // 2, lanes), F32)
    return pl.pallas_call(
        split_kernel,
        out_shape=(part, part),
        in_specs=vmem(2),
        out_specs=tuple(vmem(2)),
        compiler_params=params(),
        name="add_split",
    )(keep, received)


def add_kernel(left, right, out):
    out[...] = left[...] + right[...]


def add(left, right):
    return pl.pallas_call(
        add_kernel,
        out_shape=pltpu.VMEM(left.shape, F32),
        in_specs=vmem(2),
        out_specs=vmem(1)[0],
        compiler_params=params(),
        name="add",
    )(left, right)


def scaled_sum(keep, send, eigen):
    blocks, slices = lax.axis_size("space"), lax.axis_size("tm")
    if blocks != 4 or slices != 4:
        return doubling([scale(eigen, over_time(halving(keep, send)))], blocks // 2)
    keep, send = add_split(keep, crossed(send, "space", 1))
    parts = [crossed(send, "space", 2), crossed(keep, "tm", 2), crossed_both(send, "space", 2, "tm", 2)]
    d = scale(eigen, [keep] + parts)
    moved, across = crossed(d, "space", 2), crossed_both(d, "space", 2, "tm", 1)
    return [add(d, crossed(d, "tm", 1)), add(moved, across)]


def scale_kernel(eigen, *refs):
    parts, out = refs[:-1], refs[-1]
    total = parts[0][...]
    for part in parts[1:]:
        total = total + part[...]
    out[...] = eigen[0] * total + eigen[1] * turned(total)


def scale(eigen, parts):
    return pl.pallas_call(
        scale_kernel,
        out_shape=pltpu.VMEM(parts[0].shape, F32),
        in_specs=vmem(1 + len(parts)),
        out_specs=vmem(1)[0],
        compiler_params=params(),
        name="scale",
    )(eigen, *parts)


def expand(site, vectors, part, stacks):
    depth = stacks.shape[0] // 2
    total = None
    for half in range(2):
        left = vectors[site, half, :, part * depth : (part + 1) * depth]
        term = matmul(left, stacks[half * depth : (half + 1) * depth])
        total = term if total is None else total + term
    return fold(total)


def place_pieces(pieces, stacks):
    values = [piece[...] for piece in pieces]
    stacks[...] = stack(values[0] if len(values) == 1 else jnp.concatenate(values, axis=0), 1.0)


def first_half_kernel(x, residual, vectors, *refs):
    pieces, (out, stacks) = refs[:-2], refs[-2:]
    place_pieces(pieces, stacks)
    for site in range(x.shape[0]):
        out[site] = x[site] + 0.5 * residual[site] + expand(site, vectors, 0, stacks)


def first_half(x, residual, pieces, vectors):
    return pl.pallas_call(
        first_half_kernel,
        out_shape=pltpu.VMEM(x.shape, F32),
        in_specs=vmem(3 + len(pieces)),
        out_specs=vmem(1)[0],
        scratch_shapes=[pltpu.VMEM((vectors.shape[-1], 2 * x.shape[-1]), BF16)],
        compiler_params=params(),
        cost_estimate=cost(1e9, 4e6),
        name="first_half",
    )(x, residual, vectors, *pieces)


def second_half_kernel(count, base, vectors, *refs):
    pieces, (outs, stacks) = refs[:count], (refs[count:-1], refs[-1])
    place_pieces(pieces, stacks)
    for site in range(base.shape[0]):
        value = base[site] + expand(site, vectors, 1, stacks)
        if len(outs) == 1:
            outs[0][site] = value
        else:
            put(site, value, *outs)


def second_half(base, pieces, vectors, halves):
    return pl.pallas_call(
        functools.partial(second_half_kernel, len(pieces)),
        out_shape=with_halves(base.shape) if halves else pltpu.VMEM(base.shape, F32),
        in_specs=vmem(2 + len(pieces)),
        out_specs=tuple(vmem(3)) if halves else vmem(1)[0],
        scratch_shapes=[pltpu.VMEM((vectors.shape[-1], 2 * base.shape[-1]), BF16)],
        compiler_params=params(),
        cost_estimate=cost(1e9, 4e6),
        name="second_half",
    )(base, vectors, *pieces)


def join_kernel(own, other, full, held, sems):
    group = lax.axis_index("groups")
    copies = []
    for site in range(own.shape[0]):
        held[site] = join_halves(own[site], other[site], group)
        copies.append(pltpu.make_async_copy(held.at[site], full.at[site], sems.at[site]))
        copies[-1].start()
    for copy in copies:
        copy.wait()


def join(own, other):
    sites, rows, lanes = own.shape
    shape = (sites, rows, 2 * lanes)
    return pl.pallas_call(
        join_kernel,
        out_shape=jax.ShapeDtypeStruct(shape, F32),
        in_specs=vmem(2),
        out_specs=pl.BlockSpec(memory_space=pl.ANY),
        scratch_shapes=[pltpu.VMEM(shape, F32), pltpu.SemaphoreType.DMA((sites,))],
        compiler_params=params(),
        cost_estimate=cost(1e6, 2e6),
        name="join",
    )(own, other)


def final_kernel(own, other, vectors, *refs):
    pieces, (full, stacks, held, sems) = refs[:-4], refs[-4:]
    group = lax.axis_index("groups")
    place_pieces(pieces, stacks)
    copies = []
    for site in range(own.shape[0]):
        held[site] = join_halves(own[site], other[site] + expand(site, vectors, 1, stacks), group)
        copies.append(pltpu.make_async_copy(held.at[site], full.at[site], sems.at[site]))
        copies[-1].start()
    for copy in copies:
        copy.wait()


def final(own, other, pieces, vectors):
    sites, rows, lanes = own.shape
    shape = (sites, rows, 2 * lanes)
    return pl.pallas_call(
        final_kernel,
        out_shape=jax.ShapeDtypeStruct(shape, F32),
        in_specs=vmem(3 + len(pieces)),
        out_specs=pl.BlockSpec(memory_space=pl.ANY),
        scratch_shapes=[
            pltpu.VMEM((vectors.shape[-1], 2 * lanes), BF16),
            pltpu.VMEM(shape, F32),
            pltpu.SemaphoreType.DMA((sites,)),
        ],
        compiler_params=params(),
        cost_estimate=cost(1e9, 4e6),
        name="final",
    )(own, other, vectors, *pieces)


def shifted(value, axis, step):
    count = lax.axis_size(axis)
    return lax.ppermute(value, axis, [(i, (i + step) % count) for i in range(count)])


def crossed(value, axis, mask):
    count = lax.axis_size(axis)
    return lax.ppermute(value, axis, [(i, i ^ mask) for i in range(count)])


def crossed_both(value, first, first_mask, second, second_mask):
    count, inner = lax.axis_size(first), lax.axis_size(second)
    pairs = [(i * inner + j, (i ^ first_mask) * inner + (j ^ second_mask)) for i in range(count) for j in range(inner)]
    return lax.ppermute(value, (first, second), pairs)


def faces_of(x, front, back):
    count = lax.axis_size("space")
    early = shifted(front, "tm", 1), shifted(front, "tm", -1)
    near, back = lax.optimization_barrier((crossed(x, "space", 1), back))
    far = lax.ppermute(x, "space", [(i, (i + 1 if i % 2 else i - 1) % count) for i in range(count)])
    late = shifted(back, "tm", 1), shifted(back, "tm", -1)
    return near, far, early, late


def halving(keep, send):
    count = lax.axis_size("space")
    mask = 1
    while True:
        received = crossed(send, "space", mask)
        mask *= 2
        if mask >= count:
            return add(keep, received)
        keep, send = add_split(keep, received)


def doubling(pieces, mask):
    while mask > 1:
        if len(pieces) > 2:
            pieces = [jnp.concatenate(pieces, axis=0)]
        pieces = pieces + [crossed(piece, "space", mask) for piece in pieces]
        mask //= 2
    return pieces


def paired(pieces):
    return [crossed(piece, "space", 1) for piece in pieces]


def across_groups(part, mask):
    return [crossed(part, "groups", 1), crossed_both(part, "groups", 1, "space", mask)]


def over_time(part):
    count = lax.axis_size("tm")
    if count <= 4:
        return [part] + [crossed(part, "tm", mask) for mask in range(1, count)]
    mask = 1
    while mask < count:
        part = part + crossed(part, "tm", mask)
        mask *= 2
    return [part]


def shards(couplings, source, initial, vectors, inverse_eigen):
    directions = couplings.shape[0]
    ny, nx, rows, lanes = source.shape[2:]
    sites = ny * nx
    number = vectors.shape[0]
    blocks = lax.axis_size("space")

    x, early_x, late_x = pack(initial.reshape(sites, rows, lanes))
    faces = faces_of(x, early_x, late_x)
    matrices = couplings.reshape(directions, sites, rows, couplings.shape[-1])
    across = jnp.transpose(vectors, (1, 2, 3, 4, 5, 0)).reshape(sites * vectors.shape[-1], number)
    rest, half_source, local, halo, by_rows, by_columns = prepare(
        x, source.reshape(sites, rows, lanes), matrices, across, ny, nx
    )
    eigen = eigen_of(inverse_eigen, number // blocks, lanes // 2)

    for sweep in range(ITERS):
        last = sweep == ITERS - 1
        if sweep:
            faces = faces_of(x, early_x, late_x)
            rest = local_part(x, half_source, local, ny, nx)
        if last:
            rest, x = lax.optimization_barrier((rest, x))
            other_x = crossed(x, "groups", 1)
        near, far, early, late = faces
        back_rest, own, partial = middle(rest, near, far, front_faces(*early, halo), halo, by_rows)
        back_rest = backward_face(back_rest, late[0], halo)
        residual, keep, send = forward_face(own, partial, back_rest, late[1], halo, by_rows)
        if not last:
            pieces = scaled_sum(keep, send, eigen)
            base = first_half(x, residual, pieces, by_columns)
            x, early_x, late_x = second_half(base, paired(pieces), by_columns, True)
    part, residual, other_x = lax.optimization_barrier((halving(keep, send), residual, other_x))
    other_residual = crossed(residual, "groups", 1)
    d = scale(eigen, over_time(part))
    mask = blocks // 2
    other = across_groups(d, mask)
    own = [d, crossed(d, "space", mask)]
    other, own = doubling(other, mask // 2), doubling(own, mask // 2)
    full_residual = join(residual, other_residual)
    own[-1], full_residual = lax.optimization_barrier((own[-1], full_residual))
    own_x = first_half(x, residual, own, by_columns)
    other[0], own_x = lax.optimization_barrier((other[0], own_x))
    own_x = second_half(own_x, paired(own), by_columns, False)
    other[-1], own_x = lax.optimization_barrier((other[-1], own_x))
    other_second = paired(other)
    other_x = first_half(other_x, other_residual, other, by_columns)
    whole = final(own_x, other_x, other_second, by_columns)
    shape = source.shape
    return whole.reshape(shape), full_residual.reshape(shape)


def solution(mesh):
    in_specs = (
        P(None, "tm", "space", None, None, None, None),
        P("tm", "space", None, None, None, None),
        P("tm", "space", None, None, None, None),
        P(None, "tm", "space", None, None, None),
        P(),
    )
    out_specs = (
        P(("groups", "tm"), "space", None, None, None, None),
        P(("groups", "tm"), "space", None, None, None, None),
    )
    return jax.shard_map(shards, mesh=mesh, in_specs=in_specs, out_specs=out_specs, check_vma=False)
```

```python
import functools

import jax
import jax.numpy as jnp
from jax import lax
from jax.experimental import pallas as pl
from jax.experimental.pallas import tpu as pltpu
from jax.sharding import PartitionSpec as P

ITERS = 2
F32 = jnp.float32
BF16 = jnp.bfloat16
LOCAL = 5


def params(mebibytes=12):
    return pltpu.CompilerParams(vmem_limit_bytes=mebibytes * 1024 * 1024)


def cost(flops, read):
    return pl.CostEstimate(flops=int(flops), bytes_accessed=int(read), transcendentals=0)


def low_lanes(value):
    lanes = lax.broadcasted_iota(jnp.int32, value.shape, value.ndim - 1)
    return lanes < value.shape[-1] // 2


def swap(value):
    return pltpu.roll(value, value.shape[-1] // 2, value.ndim - 1)


def turned(value):
    moved = swap(value)
    return jnp.where(low_lanes(value), -moved, moved)


def high_low(value):
    high = value.astype(BF16)
    low = (value - high.astype(F32)).astype(BF16)
    return high, low


def stack(value, sign):
    high, low = high_low(jnp.concatenate([value, sign * turned(value)], axis=0))
    return jnp.concatenate([high, low], axis=1)


def matmul(left, right):
    return jnp.dot(left, right, preferred_element_type=F32)


def fold(product):
    rows, lanes = product.shape[0] // 2, product.shape[1] // 2
    high = product[:rows, :lanes] + (product[:rows, lanes:] + product[rows:, :lanes])
    return high + product[rows:, lanes:]


def pick_half(value, group):
    middle = value.shape[-1] // 2
    real, imag = value[:, :middle], value[:, middle:]
    low = low_lanes(real)
    first = jnp.where(low, real, swap(imag))
    second = jnp.where(low, swap(real), imag)
    return jnp.where(group == 0, first, second)


def join_halves(own, other, group):
    first = jnp.where(group == 0, own, other)
    second = jnp.where(group == 0, other, own)
    low = low_lanes(own)
    real = jnp.where(low, first, swap(second))
    imag = jnp.where(low, swap(first), second)
    return jnp.concatenate([real, imag], axis=1)


def vmem(count):
    return [pl.BlockSpec(memory_space=pltpu.VMEM)] * count


def in_hbm(value):
    return pltpu.with_memory_space_constraint(value, pltpu.HBM)


def put(site, value, whole, front, back):
    count = front.shape[0]
    whole[site] = value
    if site < count:
        front[site] = value
    else:
        back[site - count] = value


def with_halves(shape):
    part = pltpu.VMEM((shape[0] // 2,) + tuple(shape[1:]), F32)
    return pltpu.VMEM(shape, F32), part, part


def pack_kernel(full, half, front, back):
    group = lax.axis_index("groups")
    for site in range(full.shape[0]):
        put(site, pick_half(full[site], group), half, front, back)


def pack(full):
    sites, rows, lanes = full.shape
    return pl.pallas_call(
        pack_kernel,
        out_shape=with_halves((sites, rows, lanes // 2)),
        in_specs=vmem(1),
        out_specs=tuple(vmem(3)),
        compiler_params=params(),
        cost_estimate=cost(1e6, 1e6),
        name="pack",
    )(full)


def around(site, ny, nx):
    y, x = site // nx, site % nx
    right, left = (x + 1) % nx, (x - 1) % nx
    up, down = (y + 1) % ny, (y - 1) % ny
    return (site, y * nx + right, y * nx + left, up * nx + x, down * nx + x)


def local_sum(site, ny, nx, stacks, local):
    total = None
    for direction, neighbour in enumerate(around(site, ny, nx)):
        term = matmul(local[direction, site], stacks[neighbour])
        total = term if total is None else total + term
    return fold(total)


def local_kernel(ny, nx, x_ref, source, local, rest, stacks):
    for site in range(x_ref.shape[0]):
        stacks[site] = stack(x_ref[site], 1.0)
    for site in range(x_ref.shape[0]):
        rest[site] = source[site] - local_sum(site, ny, nx, stacks, local)


def local_part(x, source, local, ny, nx):
    sites, rows, lanes = x.shape
    return pl.pallas_call(
        functools.partial(local_kernel, ny, nx),
        out_shape=pltpu.VMEM(x.shape, F32),
        in_specs=vmem(3),
        out_specs=vmem(1)[0],
        scratch_shapes=[pltpu.VMEM((sites, 2 * rows, 2 * lanes), BF16)],
        compiler_params=params(),
        cost_estimate=cost(8e9, 8e6),
        name="local_part",
    )(x, source, local)


def block_order(count):
    bits = count.bit_length() - 1
    return [int(format(index, "b").zfill(bits)[::-1], 2) if bits else 0 for index in range(count)]


def ordered_rows(rows, chunk, taken):
    blocks = lax.axis_size("space")
    space = lax.axis_index("space")
    size = rows.shape[0] // blocks
    unit = min(size, taken)
    parts = []
    for start in range(chunk * taken, (chunk + 1) * taken, unit):
        block = space ^ block_order(blocks)[start // size]
        parts.append(rows[pl.ds(pl.multiple_of(block * size + start % size, unit), unit)])
    return parts[0] if len(parts) == 1 else jnp.concatenate(parts, axis=0)


def prepare_kernel(ny, nx, x_ref, source, couplings, across, rest, half_source, local, halo, by_rows, by_columns, stacks, held, held_source, held_across, turned_rows, sems):
    group = lax.axis_index("groups")
    sites, directions, rows = held.shape[:3]
    number = held_across.shape[1]
    taken, step = 128, turned_rows.shape[1]
    arriving = []
    for site in range(sites):
        arriving.append(pltpu.make_async_copy(couplings.at[:, site], held.at[site], sems.at[site]))
    arriving.append(pltpu.make_async_copy(source, held_source, sems.at[sites]))
    for index in range(held_across.shape[0] // step):
        at = pl.ds(index * step, step)
        arriving.append(pltpu.make_async_copy(across.at[at], held_across.at[at], sems.at[sites + 1 + index]))
    for copy in arriving:
        copy.start()
    for site in range(sites):
        stacks[site] = stack(x_ref[site], 1.0)
    for site in range(sites):
        arriving[site].wait()
        for direction in range(directions):
            high, low = high_low(held[site, direction])
            both = jnp.concatenate([high, low], axis=0)
            if direction < LOCAL:
                local[direction, site] = both
            else:
                halo[direction - LOCAL, site] = both
        if site == 0:
            arriving[sites].wait()
        own = pick_half(held_source[site], group)
        half_source[site] = own
        rest[site] = own - local_sum(site, ny, nx, stacks, local)
    for index, copy in enumerate(arriving[sites + 1 :]):
        copy.wait()
        at = slice(index * step, (index + 1) * step)
        turned_rows[...] = held_across[at].T
        for chunk in range(number // taken):
            part = ordered_rows(turned_rows, chunk, taken)
            high, low = high_low(part)
            by_rows[chunk * taken : (chunk + 1) * taken, at] = high
            by_rows[number + chunk * taken : number + (chunk + 1) * taken, at] = low
            back = part.T
            for half in range(step // rows):
                high, low = high_low(back[half * rows : (half + 1) * rows])
                site, which = divmod(index * (step // rows) + half, 2)
                lanes = slice(chunk * taken, (chunk + 1) * taken)
                by_columns[site, which, :rows, lanes] = high
                by_columns[site, which, rows:, lanes] = low


def prepare(x, source, couplings, across, ny, nx):
    sites, rows, lanes = x.shape
    directions, _, _, columns = couplings.shape
    width, number = across.shape
    outer = directions - LOCAL
    step = width // (sites // 2)
    return pl.pallas_call(
        functools.partial(prepare_kernel, ny, nx),
        out_shape=(
            pltpu.VMEM(x.shape, F32),
            pltpu.VMEM(x.shape, F32),
            pltpu.VMEM((LOCAL, sites, 2 * rows, columns), BF16),
            pltpu.VMEM((outer, sites, 2 * rows, columns), BF16),
            pltpu.VMEM((2 * number, width), BF16),
            pltpu.VMEM((sites, 2, 2 * rows, number), BF16),
        ),
        in_specs=vmem(1) + [pl.BlockSpec(memory_space=pl.ANY)] * 3,
        out_specs=tuple(vmem(6)),
        scratch_shapes=[
            pltpu.VMEM((sites, 2 * rows, 2 * lanes), BF16),
            pltpu.VMEM((sites, directions, rows, columns), F32),
            pltpu.VMEM(source.shape, F32),
            pltpu.VMEM(across.shape, F32),
            pltpu.VMEM((number, step), F32),
            pltpu.SemaphoreType.DMA((sites + 1 + width // step,)),
        ],
        compiler_params=params(24),
        cost_estimate=cost(8e9, 25e6),
        name="prepare",
    )(x, in_hbm(source), in_hbm(couplings), in_hbm(across))


def eigen_kernel(inverse, out):
    size, lanes = out.shape[1:]
    number = inverse.shape[1]
    start = lax.axis_index("space") * size
    row = lax.broadcasted_iota(jnp.int32, (size, number), 0) + start
    chosen = lax.broadcasted_iota(jnp.int32, (size, number), 1) == row
    for part in range(2):
        value = jnp.where(chosen, inverse[part : part + 1], 0.0)
        out[part] = jnp.broadcast_to(jnp.sum(value, axis=1, keepdims=True), (size, lanes))


def eigen_of(inverse, size, lanes):
    return pl.pallas_call(
        eigen_kernel,
        out_shape=pltpu.VMEM((2, size, lanes), F32),
        in_specs=vmem(1),
        out_specs=vmem(1)[0],
        compiler_params=params(),
        cost_estimate=cost(1e6, 1e6),
        name="eigen",
    )(inverse)


def apply_faces(*pairs):
    summed = None
    for matrix, face in pairs:
        term = matmul(matrix, stack(face, 1.0))
        summed = term if summed is None else summed + term
    return fold(summed)


def edge_sign(last):
    count = lax.axis_size("tm")
    return jnp.where(lax.axis_index("tm") == (count - 1 if last else 0), -1.0, 1.0).astype(F32)


def front_kernel(backward, forward, matrix, out):
    behind, ahead = edge_sign(False), edge_sign(True)
    for site in range(out.shape[0]):
        out[site] = apply_faces((matrix[2, site], ahead * forward[site]), (matrix[3, site], behind * backward[site]))


def front_faces(backward, forward, matrix):
    return pl.pallas_call(
        front_kernel,
        out_shape=pltpu.VMEM(forward.shape, F32),
        in_specs=vmem(3),
        out_specs=vmem(1)[0],
        compiler_params=params(),
        cost_estimate=cost(1e3, 1e3),
        name="front_faces",
    )(backward, forward, matrix)


def middle_kernel(rest, near, far, front, matrix, vectors, back, residual, partial, stacks):
    parity = lax.rem(lax.axis_index("space"), 2)
    sites, rows, _ = front.shape
    for site in range(rest.shape[0]):
        own = rest[site] - apply_faces((matrix[parity, site], near[site]), (matrix[1 - parity, site], far[site]))
        if site < sites:
            own = own - front[site]
            residual[site] = own
            stacks[site * 2 * rows : (site + 1) * 2 * rows] = stack(own, -1.0)
        else:
            back[site - sites] = own
    partial[...] = fold(matmul(vectors[:, : stacks.shape[0]], stacks[...]))


def middle(rest, near, far, front, matrix, vectors):
    sites, rows, lanes = front.shape
    half = pltpu.VMEM(front.shape, F32)
    return pl.pallas_call(
        middle_kernel,
        out_shape=(half, half, pltpu.VMEM((vectors.shape[0] // 2, lanes), F32)),
        in_specs=vmem(6),
        out_specs=tuple(vmem(3)),
        scratch_shapes=[pltpu.VMEM((sites * 2 * rows, 2 * lanes), BF16)],
        compiler_params=params(),
        cost_estimate=cost(1e3, 1e3),
        name="middle",
    )(rest, near, far, front, matrix, vectors)


def backward_kernel(rest, backward, matrix, out):
    sign = edge_sign(False)
    sites = backward.shape[0]
    for site in range(sites):
        out[site] = rest[site] - apply_faces((matrix[3, sites + site], sign * backward[site]))


def backward_face(rest, backward, matrix):
    return pl.pallas_call(
        backward_kernel,
        out_shape=pltpu.VMEM(backward.shape, F32),
        in_specs=vmem(3),
        out_specs=vmem(1)[0],
        compiler_params=params(),
        cost_estimate=cost(1e3, 1e3),
        name="backward_face",
    )(rest, backward, matrix)


def forward_kernel(front, partial, rest, forward, matrix, vectors, residual, back, keep, send, stacks):
    sign = edge_sign(True)
    sites, rows, _ = forward.shape
    for site in range(sites):
        own = rest[site] - apply_faces((matrix[2, sites + site], sign * forward[site]))
        residual[site] = front[site]
        residual[sites + site] = own
        back[site] = own
        stacks[site * 2 * rows : (site + 1) * 2 * rows] = stack(own, -1.0)
    whole = partial[...] + fold(matmul(vectors[:, stacks.shape[0] :], stacks[...]))
    half = whole.shape[0] // 2
    keep[...] = whole[:half]
    send[...] = whole[half:]


def forward_face(front, partial, rest, forward, matrix, vectors):
    sites, rows, lanes = forward.shape
    part = pltpu.VMEM((vectors.shape[0] // 4, lanes), F32)
    return pl.pallas_call(
        forward_kernel,
        out_shape=(pltpu.VMEM((2 * sites, rows, lanes), F32), pltpu.VMEM(forward.shape, F32), part, part),
        in_specs=vmem(6),
        out_specs=tuple(vmem(4)),
        scratch_shapes=[pltpu.VMEM((sites * 2 * rows, 2 * lanes), BF16)],
        compiler_params=params(),
        cost_estimate=cost(2e9, 8e6),
        name="forward_face",
    )(front, partial, rest, forward, matrix, vectors)


def split_kernel(keep, received, next_keep, next_send):
    half = next_keep.shape[0]
    next_keep[...] = keep[:half] + received[:half]
    next_send[...] = keep[half:] + received[half:]


def add_split(keep, received):
    rows, lanes = keep.shape
    part = pltpu.VMEM((rows // 2, lanes), F32)
    return pl.pallas_call(
        split_kernel,
        out_shape=(part, part),
        in_specs=vmem(2),
        out_specs=tuple(vmem(2)),
        compiler_params=params(),
        name="add_split",
    )(keep, received)


def add_kernel(left, right, out):
    out[...] = left[...] + right[...]


def add(left, right):
    return pl.pallas_call(
        add_kernel,
        out_shape=pltpu.VMEM(left.shape, F32),
        in_specs=vmem(2),
        out_specs=vmem(1)[0],
        compiler_params=params(),
        name="add",
    )(left, right)


def scaled_sum(keep, send, eigen):
    blocks, slices = lax.axis_size("space"), lax.axis_size("tm")
    if blocks != 4 or slices != 4:
        return doubling([scale(eigen, over_time(halving(keep, send)))], blocks // 2)
    keep, send = add_split(keep, crossed(send, "space", 1))
    parts = [crossed(send, "space", 2), crossed(keep, "tm", 2), crossed_both(send, "space", 2, "tm", 2)]
    d = scale(eigen, [keep] + parts)
    moved, across = crossed(d, "space", 2), crossed_both(d, "space", 2, "tm", 1)
    return [add(d, crossed(d, "tm", 1)), add(moved, across)]


def scale_kernel(eigen, *refs):
    parts, out = refs[:-1], refs[-1]
    total = parts[0][...]
    for part in parts[1:]:
        total = total + part[...]
    out[...] = eigen[0] * total + eigen[1] * turned(total)


def scale(eigen, parts):
    return pl.pallas_call(
        scale_kernel,
        out_shape=pltpu.VMEM(parts[0].shape, F32),
        in_specs=vmem(1 + len(parts)),
        out_specs=vmem(1)[0],
        compiler_params=params(),
        name="scale",
    )(eigen, *parts)


def expand(site, vectors, part, stacks):
    depth = stacks.shape[0] // 2
    total = None
    for half in range(2):
        left = vectors[site, half, :, part * depth : (part + 1) * depth]
        term = matmul(left, stacks[half * depth : (half + 1) * depth])
        total = term if total is None else total + term
    return fold(total)


def place_pieces(pieces, stacks):
    values = [piece[...] for piece in pieces]
    stacks[...] = stack(values[0] if len(values) == 1 else jnp.concatenate(values, axis=0), 1.0)


def site_of(parts, site):
    count = parts[0].shape[0]
    return parts[site // count][site % count]


def first_half_kernel(count, x, vectors, *refs):
    residual, pieces, (out, stacks) = refs[:count], refs[count:-2], refs[-2:]
    place_pieces(pieces, stacks)
    for site in range(x.shape[0]):
        out[site] = x[site] + 0.5 * site_of(residual, site) + expand(site, vectors, 0, stacks)


def first_half(x, residual, pieces, vectors):
    return pl.pallas_call(
        functools.partial(first_half_kernel, len(residual)),
        out_shape=pltpu.VMEM(x.shape, F32),
        in_specs=vmem(2 + len(residual) + len(pieces)),
        out_specs=vmem(1)[0],
        scratch_shapes=[pltpu.VMEM((vectors.shape[-1], 2 * x.shape[-1]), BF16)],
        compiler_params=params(),
        cost_estimate=cost(1e9, 4e6),
        name="first_half",
    )(x, vectors, *residual, *pieces)


def second_half_kernel(count, base, vectors, *refs):
    pieces, (outs, stacks) = refs[:count], (refs[count:-1], refs[-1])
    place_pieces(pieces, stacks)
    for site in range(base.shape[0]):
        value = base[site] + expand(site, vectors, 1, stacks)
        if len(outs) == 1:
            outs[0][site] = value
        else:
            put(site, value, *outs)


def second_half(base, pieces, vectors, halves):
    return pl.pallas_call(
        functools.partial(second_half_kernel, len(pieces)),
        out_shape=with_halves(base.shape) if halves else pltpu.VMEM(base.shape, F32),
        in_specs=vmem(2 + len(pieces)),
        out_specs=tuple(vmem(3)) if halves else vmem(1)[0],
        scratch_shapes=[pltpu.VMEM((vectors.shape[-1], 2 * base.shape[-1]), BF16)],
        compiler_params=params(),
        cost_estimate=cost(1e9, 4e6),
        name="second_half",
    )(base, vectors, *pieces)


def join_kernel(own, front, back, full, held, sems):
    group = lax.axis_index("groups")
    copies = []
    for site in range(own.shape[0]):
        held[site] = join_halves(own[site], site_of((front, back), site), group)
        copies.append(pltpu.make_async_copy(held.at[site], full.at[site], sems.at[site]))
        copies[-1].start()
    for copy in copies:
        copy.wait()


def join(own, front, back):
    sites, rows, lanes = own.shape
    shape = (sites, rows, 2 * lanes)
    return pl.pallas_call(
        join_kernel,
        out_shape=jax.ShapeDtypeStruct(shape, F32),
        in_specs=vmem(3),
        out_specs=pl.BlockSpec(memory_space=pl.ANY),
        scratch_shapes=[pltpu.VMEM(shape, F32), pltpu.SemaphoreType.DMA((sites,))],
        compiler_params=params(),
        cost_estimate=cost(1e6, 2e6),
        name="join",
    )(own, front, back)


def final_kernel(own, other, vectors, *refs):
    pieces, (full, stacks, held, sems) = refs[:-4], refs[-4:]
    group = lax.axis_index("groups")
    place_pieces(pieces, stacks)
    copies = []
    for site in range(own.shape[0]):
        held[site] = join_halves(own[site], other[site] + expand(site, vectors, 1, stacks), group)
        copies.append(pltpu.make_async_copy(held.at[site], full.at[site], sems.at[site]))
        copies[-1].start()
    for copy in copies:
        copy.wait()


def final(own, other, pieces, vectors):
    sites, rows, lanes = own.shape
    shape = (sites, rows, 2 * lanes)
    return pl.pallas_call(
        final_kernel,
        out_shape=jax.ShapeDtypeStruct(shape, F32),
        in_specs=vmem(3 + len(pieces)),
        out_specs=pl.BlockSpec(memory_space=pl.ANY),
        scratch_shapes=[
            pltpu.VMEM((vectors.shape[-1], 2 * lanes), BF16),
            pltpu.VMEM(shape, F32),
            pltpu.SemaphoreType.DMA((sites,)),
        ],
        compiler_params=params(),
        cost_estimate=cost(1e9, 4e6),
        name="final",
    )(own, other, vectors, *pieces)


def shifted(value, axis, step):
    count = lax.axis_size(axis)
    return lax.ppermute(value, axis, [(i, (i + step) % count) for i in range(count)])


def crossed(value, axis, mask):
    count = lax.axis_size(axis)
    return lax.ppermute(value, axis, [(i, i ^ mask) for i in range(count)])


def crossed_both(value, first, first_mask, second, second_mask):
    count, inner = lax.axis_size(first), lax.axis_size(second)
    pairs = [(i * inner + j, (i ^ first_mask) * inner + (j ^ second_mask)) for i in range(count) for j in range(inner)]
    return lax.ppermute(value, (first, second), pairs)


def faces_of(x, front, back):
    count = lax.axis_size("space")
    early = shifted(front, "tm", 1), shifted(front, "tm", -1)
    near, back = lax.optimization_barrier((crossed(x, "space", 1), back))
    far = lax.ppermute(x, "space", [(i, (i + 1 if i % 2 else i - 1) % count) for i in range(count)])
    late = shifted(back, "tm", 1), shifted(back, "tm", -1)
    return near, far, early, late


def halving(keep, send):
    count = lax.axis_size("space")
    mask = 1
    while True:
        received = crossed(send, "space", mask)
        mask *= 2
        if mask >= count:
            return add(keep, received)
        keep, send = add_split(keep, received)


def doubling(pieces, mask):
    while mask > 1:
        if len(pieces) > 2:
            pieces = [jnp.concatenate(pieces, axis=0)]
        pieces = pieces + [crossed(piece, "space", mask) for piece in pieces]
        mask //= 2
    return pieces


def paired(pieces):
    return [crossed(piece, "space", 1) for piece in pieces]


def across_groups(part, mask):
    return [crossed(part, "groups", 1), crossed_both(part, "groups", 1, "space", mask)]


def over_time(part):
    count = lax.axis_size("tm")
    if count <= 4:
        return [part] + [crossed(part, "tm", mask) for mask in range(1, count)]
    mask = 1
    while mask < count:
        part = part + crossed(part, "tm", mask)
        mask *= 2
    return [part]


def shards(couplings, source, initial, vectors, inverse_eigen):
    directions = couplings.shape[0]
    ny, nx, rows, lanes = source.shape[2:]
    sites = ny * nx
    number = vectors.shape[0]
    blocks = lax.axis_size("space")

    x, early_x, late_x = pack(initial.reshape(sites, rows, lanes))
    faces = faces_of(x, early_x, late_x)
    matrices = couplings.reshape(directions, sites, rows, couplings.shape[-1])
    across = jnp.transpose(vectors, (1, 2, 3, 4, 5, 0)).reshape(sites * vectors.shape[-1], number)
    rest, half_source, local, halo, by_rows, by_columns = prepare(
        x, source.reshape(sites, rows, lanes), matrices, across, ny, nx
    )
    eigen = eigen_of(inverse_eigen, number // blocks, lanes // 2)

    for sweep in range(ITERS):
        last = sweep == ITERS - 1
        if sweep:
            faces = faces_of(x, early_x, late_x)
            rest = local_part(x, half_source, local, ny, nx)
        if last:
            rest, x = lax.optimization_barrier((rest, x))
            other_x = crossed(x, "groups", 1)
        near, far, early, late = faces
        back_rest, own, partial = middle(rest, near, far, front_faces(*early, halo), halo, by_rows)
        if last:
            other_front = crossed(own, "groups", 1)
        back_rest = backward_face(back_rest, late[0], halo)
        residual, back, keep, send = forward_face(own, partial, back_rest, late[1], halo, by_rows)
        if not last:
            pieces = scaled_sum(keep, send, eigen)
            base = first_half(x, [residual], pieces, by_columns)
            x, early_x, late_x = second_half(base, paired(pieces), by_columns, True)
    part, other_x = lax.optimization_barrier((halving(keep, send), other_x))
    other_back = crossed(back, "groups", 1)
    d, other_front = lax.optimization_barrier((scale(eigen, over_time(part)), other_front))
    mask = blocks // 2
    other = across_groups(d, mask)
    own = [d, crossed(d, "space", mask)]
    other, own = doubling(other, mask // 2), doubling(own, mask // 2)
    full_residual = join(residual, other_front, other_back)
    own[-1], full_residual = lax.optimization_barrier((own[-1], full_residual))
    own_x = first_half(x, [residual], own, by_columns)
    other[0], own_x = lax.optimization_barrier((other[0], own_x))
    own_x = second_half(own_x, paired(own), by_columns, False)
    other[-1], own_x = lax.optimization_barrier((other[-1], own_x))
    other_second = paired(other)
    other_x = first_half(other_x, [other_front, other_back], other, by_columns)
    whole = final(own_x, other_x, other_second, by_columns)
    shape = source.shape
    return whole.reshape(shape), full_residual.reshape(shape)


def solution(mesh):
    in_specs = (
        P(None, "tm", "space", None, None, None, None),
        P("tm", "space", None, None, None, None),
        P("tm", "space", None, None, None, None),
        P(None, "tm", "space", None, None, None),
        P(),
    )
    out_specs = (
        P(("groups", "tm"), "space", None, None, None, None),
        P(("groups", "tm"), "space", None, None, None, None),
    )
    return jax.shard_map(shards, mesh=mesh, in_specs=in_specs, out_specs=out_specs, check_vma=False)
```

```python
import functools

import jax
import jax.numpy as jnp
from jax import lax
from jax.experimental import pallas as pl
from jax.experimental.pallas import tpu as pltpu
from jax.sharding import PartitionSpec as P

ITERS = 2
F32 = jnp.float32
BF16 = jnp.bfloat16
LOCAL = 5


def params(mebibytes=12):
    return pltpu.CompilerParams(vmem_limit_bytes=mebibytes * 1024 * 1024)


def cost(flops, read):
    return pl.CostEstimate(flops=int(flops), bytes_accessed=int(read), transcendentals=0)


def low_lanes(value):
    lanes = lax.broadcasted_iota(jnp.int32, value.shape, value.ndim - 1)
    return lanes < value.shape[-1] // 2


def swap(value):
    return pltpu.roll(value, value.shape[-1] // 2, value.ndim - 1)


def turned(value):
    moved = swap(value)
    return jnp.where(low_lanes(value), -moved, moved)


def high_low(value):
    high = value.astype(BF16)
    low = (value - high.astype(F32)).astype(BF16)
    return high, low


def stack(value, sign):
    high, low = high_low(jnp.concatenate([value, sign * turned(value)], axis=0))
    return jnp.concatenate([high, low], axis=1)


def matmul(left, right):
    return jnp.dot(left, right, preferred_element_type=F32)


def fold(product):
    rows, lanes = product.shape[0] // 2, product.shape[1] // 2
    high = product[:rows, :lanes] + (product[:rows, lanes:] + product[rows:, :lanes])
    return high + product[rows:, lanes:]


def pick_half(value, group):
    middle = value.shape[-1] // 2
    real, imag = value[:, :middle], value[:, middle:]
    low = low_lanes(real)
    first = jnp.where(low, real, swap(imag))
    second = jnp.where(low, swap(real), imag)
    return jnp.where(group == 0, first, second)


def join_halves(own, other, group):
    first = jnp.where(group == 0, own, other)
    second = jnp.where(group == 0, other, own)
    low = low_lanes(own)
    real = jnp.where(low, first, swap(second))
    imag = jnp.where(low, swap(first), second)
    return jnp.concatenate([real, imag], axis=1)


def vmem(count):
    return [pl.BlockSpec(memory_space=pltpu.VMEM)] * count


def in_hbm(value):
    return pltpu.with_memory_space_constraint(value, pltpu.HBM)


def put(site, value, whole, front, back):
    count = front.shape[0]
    whole[site] = value
    if site < count:
        front[site] = value
    else:
        back[site - count] = value


def with_halves(shape):
    part = pltpu.VMEM((shape[0] // 2,) + tuple(shape[1:]), F32)
    return pltpu.VMEM(shape, F32), part, part


def pack_kernel(full, half, front, back):
    group = lax.axis_index("groups")
    for site in range(full.shape[0]):
        put(site, pick_half(full[site], group), half, front, back)


def pack(full):
    sites, rows, lanes = full.shape
    return pl.pallas_call(
        pack_kernel,
        out_shape=with_halves((sites, rows, lanes // 2)),
        in_specs=vmem(1),
        out_specs=tuple(vmem(3)),
        compiler_params=params(),
        cost_estimate=cost(1e6, 1e6),
        name="pack",
    )(full)


def around(site, ny, nx):
    y, x = site // nx, site % nx
    right, left = (x + 1) % nx, (x - 1) % nx
    up, down = (y + 1) % ny, (y - 1) % ny
    return (site, y * nx + right, y * nx + left, up * nx + x, down * nx + x)


def local_sum(site, ny, nx, stacks, local):
    total = None
    for direction, neighbour in enumerate(around(site, ny, nx)):
        term = matmul(local[direction, site], stacks[neighbour])
        total = term if total is None else total + term
    return fold(total)


def local_kernel(ny, nx, x_ref, source, local, rest, stacks):
    for site in range(x_ref.shape[0]):
        stacks[site] = stack(x_ref[site], 1.0)
    for site in range(x_ref.shape[0]):
        rest[site] = source[site] - local_sum(site, ny, nx, stacks, local)


def local_part(x, source, local, ny, nx):
    sites, rows, lanes = x.shape
    return pl.pallas_call(
        functools.partial(local_kernel, ny, nx),
        out_shape=pltpu.VMEM(x.shape, F32),
        in_specs=vmem(3),
        out_specs=vmem(1)[0],
        scratch_shapes=[pltpu.VMEM((sites, 2 * rows, 2 * lanes), BF16)],
        compiler_params=params(),
        cost_estimate=cost(8e9, 8e6),
        name="local_part",
    )(x, source, local)


def block_order(count):
    bits = count.bit_length() - 1
    return [int(format(index, "b").zfill(bits)[::-1], 2) if bits else 0 for index in range(count)]


def ordered_rows(rows, chunk, taken):
    blocks = lax.axis_size("space")
    space = lax.axis_index("space")
    size = rows.shape[0] // blocks
    unit = min(size, taken)
    parts = []
    for start in range(chunk * taken, (chunk + 1) * taken, unit):
        block = space ^ block_order(blocks)[start // size]
        parts.append(rows[pl.ds(pl.multiple_of(block * size + start % size, unit), unit)])
    return parts[0] if len(parts) == 1 else jnp.concatenate(parts, axis=0)


def prepare_kernel(ny, nx, x_ref, source, couplings, across, rest, half_source, local, halo, by_rows, by_columns, stacks, held, held_source, held_across, turned_rows, sems):
    group = lax.axis_index("groups")
    sites, directions, rows = held.shape[:3]
    number = held_across.shape[1]
    taken, step = 128, turned_rows.shape[1]
    arriving = []
    for site in range(sites):
        arriving.append(pltpu.make_async_copy(couplings.at[:, site], held.at[site], sems.at[site]))
    arriving.append(pltpu.make_async_copy(source, held_source, sems.at[sites]))
    for index in range(held_across.shape[0] // step):
        at = pl.ds(index * step, step)
        arriving.append(pltpu.make_async_copy(across.at[at], held_across.at[at], sems.at[sites + 1 + index]))
    for copy in arriving:
        copy.start()
    for site in range(sites):
        stacks[site] = stack(x_ref[site], 1.0)
    for site in range(sites):
        arriving[site].wait()
        for direction in range(directions):
            high, low = high_low(held[site, direction])
            both = jnp.concatenate([high, low], axis=0)
            if direction < LOCAL:
                local[direction, site] = both
            else:
                halo[direction - LOCAL, site] = both
        if site == 0:
            arriving[sites].wait()
        own = pick_half(held_source[site], group)
        half_source[site] = own
        rest[site] = own - local_sum(site, ny, nx, stacks, local)
    for index, copy in enumerate(arriving[sites + 1 :]):
        copy.wait()
        at = slice(index * step, (index + 1) * step)
        turned_rows[...] = held_across[at].T
        for chunk in range(number // taken):
            part = ordered_rows(turned_rows, chunk, taken)
            high, low = high_low(part)
            by_rows[chunk * taken : (chunk + 1) * taken, at] = high
            by_rows[number + chunk * taken : number + (chunk + 1) * taken, at] = low
            back = part.T
            for half in range(step // rows):
                high, low = high_low(back[half * rows : (half + 1) * rows])
                site, which = divmod(index * (step // rows) + half, 2)
                lanes = slice(chunk * taken, (chunk + 1) * taken)
                by_columns[site, which, :rows, lanes] = high
                by_columns[site, which, rows:, lanes] = low


def prepare(x, source, couplings, across, ny, nx):
    sites, rows, lanes = x.shape
    directions, _, _, columns = couplings.shape
    width, number = across.shape
    outer = directions - LOCAL
    step = width // (sites // 2)
    return pl.pallas_call(
        functools.partial(prepare_kernel, ny, nx),
        out_shape=(
            pltpu.VMEM(x.shape, F32),
            pltpu.VMEM(x.shape, F32),
            pltpu.VMEM((LOCAL, sites, 2 * rows, columns), BF16),
            pltpu.VMEM((outer, sites, 2 * rows, columns), BF16),
            pltpu.VMEM((2 * number, width), BF16),
            pltpu.VMEM((sites, 2, 2 * rows, number), BF16),
        ),
        in_specs=vmem(1) + [pl.BlockSpec(memory_space=pl.ANY)] * 3,
        out_specs=tuple(vmem(6)),
        scratch_shapes=[
            pltpu.VMEM((sites, 2 * rows, 2 * lanes), BF16),
            pltpu.VMEM((sites, directions, rows, columns), F32),
            pltpu.VMEM(source.shape, F32),
            pltpu.VMEM(across.shape, F32),
            pltpu.VMEM((number, step), F32),
            pltpu.SemaphoreType.DMA((sites + 1 + width // step,)),
        ],
        compiler_params=params(24),
        cost_estimate=cost(8e9, 25e6),
        name="prepare",
    )(x, in_hbm(source), in_hbm(couplings), in_hbm(across))


def eigen_kernel(inverse, out):
    size, lanes = out.shape[1:]
    number = inverse.shape[1]
    start = lax.axis_index("space") * size
    row = lax.broadcasted_iota(jnp.int32, (size, number), 0) + start
    chosen = lax.broadcasted_iota(jnp.int32, (size, number), 1) == row
    for part in range(2):
        value = jnp.where(chosen, inverse[part : part + 1], 0.0)
        out[part] = jnp.broadcast_to(jnp.sum(value, axis=1, keepdims=True), (size, lanes))


def eigen_of(inverse, size, lanes):
    return pl.pallas_call(
        eigen_kernel,
        out_shape=pltpu.VMEM((2, size, lanes), F32),
        in_specs=vmem(1),
        out_specs=vmem(1)[0],
        compiler_params=params(),
        cost_estimate=cost(1e6, 1e6),
        name="eigen",
    )(inverse)


def apply_faces(*pairs):
    summed = None
    for matrix, face in pairs:
        term = matmul(matrix, stack(face, 1.0))
        summed = term if summed is None else summed + term
    return fold(summed)


def edge_sign(last):
    count = lax.axis_size("tm")
    return jnp.where(lax.axis_index("tm") == (count - 1 if last else 0), -1.0, 1.0).astype(F32)


def front_kernel(backward, forward, matrix, out):
    behind, ahead = edge_sign(False), edge_sign(True)
    for site in range(out.shape[0]):
        out[site] = apply_faces((matrix[2, site], ahead * forward[site]), (matrix[3, site], behind * backward[site]))


def front_faces(backward, forward, matrix):
    return pl.pallas_call(
        front_kernel,
        out_shape=pltpu.VMEM(forward.shape, F32),
        in_specs=vmem(3),
        out_specs=vmem(1)[0],
        compiler_params=params(),
        cost_estimate=cost(1e3, 1e3),
        name="front_faces",
    )(backward, forward, matrix)


def middle_kernel(rest, near, far, front, matrix, vectors, back, residual, partial, stacks):
    parity = lax.rem(lax.axis_index("space"), 2)
    sites, rows, _ = front.shape
    for site in range(rest.shape[0]):
        own = rest[site] - apply_faces((matrix[parity, site], near[site]), (matrix[1 - parity, site], far[site]))
        if site < sites:
            own = own - front[site]
            residual[site] = own
            stacks[site * 2 * rows : (site + 1) * 2 * rows] = stack(own, -1.0)
        else:
            back[site - sites] = own
    partial[...] = fold(matmul(vectors[:, : stacks.shape[0]], stacks[...]))


def middle(rest, near, far, front, matrix, vectors):
    sites, rows, lanes = front.shape
    half = pltpu.VMEM(front.shape, F32)
    return pl.pallas_call(
        middle_kernel,
        out_shape=(half, half, pltpu.VMEM((vectors.shape[0] // 2, lanes), F32)),
        in_specs=vmem(6),
        out_specs=tuple(vmem(3)),
        scratch_shapes=[pltpu.VMEM((sites * 2 * rows, 2 * lanes), BF16)],
        compiler_params=params(),
        cost_estimate=cost(1e3, 1e3),
        name="middle",
    )(rest, near, far, front, matrix, vectors)


def backward_kernel(rest, backward, matrix, out):
    sign = edge_sign(False)
    sites = backward.shape[0]
    for site in range(sites):
        out[site] = rest[site] - apply_faces((matrix[3, sites + site], sign * backward[site]))


def backward_face(rest, backward, matrix):
    return pl.pallas_call(
        backward_kernel,
        out_shape=pltpu.VMEM(backward.shape, F32),
        in_specs=vmem(3),
        out_specs=vmem(1)[0],
        compiler_params=params(),
        cost_estimate=cost(1e3, 1e3),
        name="backward_face",
    )(rest, backward, matrix)


def forward_kernel(front, partial, rest, forward, matrix, vectors, residual, back, keep, send, stacks):
    sign = edge_sign(True)
    sites, rows, _ = forward.shape
    for site in range(sites):
        own = rest[site] - apply_faces((matrix[2, sites + site], sign * forward[site]))
        residual[site] = front[site]
        residual[sites + site] = own
        back[site] = own
        stacks[site * 2 * rows : (site + 1) * 2 * rows] = stack(own, -1.0)
    whole = partial[...] + fold(matmul(vectors[:, stacks.shape[0] :], stacks[...]))
    half = whole.shape[0] // 2
    keep[...] = whole[:half]
    send[...] = whole[half:]


def forward_face(front, partial, rest, forward, matrix, vectors):
    sites, rows, lanes = forward.shape
    part = pltpu.VMEM((vectors.shape[0] // 4, lanes), F32)
    return pl.pallas_call(
        forward_kernel,
        out_shape=(pltpu.VMEM((2 * sites, rows, lanes), F32), pltpu.VMEM(forward.shape, F32), part, part),
        in_specs=vmem(6),
        out_specs=tuple(vmem(4)),
        scratch_shapes=[pltpu.VMEM((sites * 2 * rows, 2 * lanes), BF16)],
        compiler_params=params(),
        cost_estimate=cost(2e9, 8e6),
        name="forward_face",
    )(front, partial, rest, forward, matrix, vectors)


def split_kernel(keep, received, next_keep, next_send):
    half = next_keep.shape[0]
    next_keep[...] = keep[:half] + received[:half]
    next_send[...] = keep[half:] + received[half:]


def add_split(keep, received):
    rows, lanes = keep.shape
    part = pltpu.VMEM((rows // 2, lanes), F32)
    return pl.pallas_call(
        split_kernel,
        out_shape=(part, part),
        in_specs=vmem(2),
        out_specs=tuple(vmem(2)),
        compiler_params=params(),
        name="add_split",
    )(keep, received)


def add_kernel(left, right, out):
    out[...] = left[...] + right[...]


def add(left, right):
    return pl.pallas_call(
        add_kernel,
        out_shape=pltpu.VMEM(left.shape, F32),
        in_specs=vmem(2),
        out_specs=vmem(1)[0],
        compiler_params=params(),
        name="add",
    )(left, right)


def scaled_sum(keep, send, eigen):
    blocks, slices = lax.axis_size("space"), lax.axis_size("tm")
    if blocks != 4 or slices != 4:
        return doubling([scale(eigen, over_time(halving(keep, send)))], blocks // 2)
    keep, send = add_split(keep, crossed(send, "space", 1))
    parts = [crossed(send, "space", 2), crossed(keep, "tm", 2), crossed_both(send, "space", 2, "tm", 2)]
    d = scale(eigen, [keep] + parts)
    moved, across = crossed(d, "space", 2), crossed_both(d, "space", 2, "tm", 1)
    return [add(d, crossed(d, "tm", 1)), add(moved, across)]


def scale_kernel(eigen, *refs):
    parts, out = refs[:-1], refs[-1]
    total = parts[0][...]
    for part in parts[1:]:
        total = total + part[...]
    out[...] = eigen[0] * total + eigen[1] * turned(total)


def scale(eigen, parts):
    return pl.pallas_call(
        scale_kernel,
        out_shape=pltpu.VMEM(parts[0].shape, F32),
        in_specs=vmem(1 + len(parts)),
        out_specs=vmem(1)[0],
        compiler_params=params(),
        name="scale",
    )(eigen, *parts)


def expand(site, vectors, part, stacks):
    depth = stacks.shape[0] // 2
    total = None
    for half in range(2):
        left = vectors[site, half, :, part * depth : (part + 1) * depth]
        term = matmul(left, stacks[half * depth : (half + 1) * depth])
        total = term if total is None else total + term
    return fold(total)


def place_pieces(pieces, stacks):
    values = [piece[...] for piece in pieces]
    stacks[...] = stack(values[0] if len(values) == 1 else jnp.concatenate(values, axis=0), 1.0)


def site_of(parts, site):
    count = parts[0].shape[0]
    return parts[site // count][site % count]


def first_half_kernel(count, x, vectors, *refs):
    residual, pieces, (out, stacks) = refs[:count], refs[count:-2], refs[-2:]
    place_pieces(pieces, stacks)
    for site in range(x.shape[0]):
        out[site] = x[site] + 0.5 * site_of(residual, site) + expand(site, vectors, 0, stacks)


def first_half(x, residual, pieces, vectors):
    return pl.pallas_call(
        functools.partial(first_half_kernel, len(residual)),
        out_shape=pltpu.VMEM(x.shape, F32),
        in_specs=vmem(2 + len(residual) + len(pieces)),
        out_specs=vmem(1)[0],
        scratch_shapes=[pltpu.VMEM((vectors.shape[-1], 2 * x.shape[-1]), BF16)],
        compiler_params=params(),
        cost_estimate=cost(1e9, 4e6),
        name="first_half",
    )(x, vectors, *residual, *pieces)


def second_half_kernel(count, base, vectors, *refs):
    pieces, (outs, stacks) = refs[:count], (refs[count:-1], refs[-1])
    place_pieces(pieces, stacks)
    for site in range(base.shape[0]):
        value = base[site] + expand(site, vectors, 1, stacks)
        if len(outs) == 1:
            outs[0][site] = value
        else:
            put(site, value, *outs)


def second_half(base, pieces, vectors, halves):
    return pl.pallas_call(
        functools.partial(second_half_kernel, len(pieces)),
        out_shape=with_halves(base.shape) if halves else pltpu.VMEM(base.shape, F32),
        in_specs=vmem(2 + len(pieces)),
        out_specs=tuple(vmem(3)) if halves else vmem(1)[0],
        scratch_shapes=[pltpu.VMEM((vectors.shape[-1], 2 * base.shape[-1]), BF16)],
        compiler_params=params(),
        cost_estimate=cost(1e9, 4e6),
        name="second_half",
    )(base, vectors, *pieces)


def join_kernel(own, front, back, full, held, sems):
    group = lax.axis_index("groups")
    copies = []
    for site in range(own.shape[0]):
        held[site] = join_halves(own[site], site_of((front, back), site), group)
        copies.append(pltpu.make_async_copy(held.at[site], full.at[site], sems.at[site]))
        copies[-1].start()
    for copy in copies:
        copy.wait()


def join(own, front, back):
    sites, rows, lanes = own.shape
    shape = (sites, rows, 2 * lanes)
    return pl.pallas_call(
        join_kernel,
        out_shape=jax.ShapeDtypeStruct(shape, F32),
        in_specs=vmem(3),
        out_specs=pl.BlockSpec(memory_space=pl.ANY),
        scratch_shapes=[pltpu.VMEM(shape, F32), pltpu.SemaphoreType.DMA((sites,))],
        compiler_params=params(),
        cost_estimate=cost(1e6, 2e6),
        name="join",
    )(own, front, back)


def final_kernel(own, other, vectors, *refs):
    pieces, (full, stacks, held, sems) = refs[:-4], refs[-4:]
    group = lax.axis_index("groups")
    place_pieces(pieces, stacks)
    copies = []
    for site in range(own.shape[0]):
        held[site] = join_halves(own[site], other[site] + expand(site, vectors, 1, stacks), group)
        copies.append(pltpu.make_async_copy(held.at[site], full.at[site], sems.at[site]))
        copies[-1].start()
    for copy in copies:
        copy.wait()


def final(own, other, pieces, vectors):
    sites, rows, lanes = own.shape
    shape = (sites, rows, 2 * lanes)
    return pl.pallas_call(
        final_kernel,
        out_shape=jax.ShapeDtypeStruct(shape, F32),
        in_specs=vmem(3 + len(pieces)),
        out_specs=pl.BlockSpec(memory_space=pl.ANY),
        scratch_shapes=[
            pltpu.VMEM((vectors.shape[-1], 2 * lanes), BF16),
            pltpu.VMEM(shape, F32),
            pltpu.SemaphoreType.DMA((sites,)),
        ],
        compiler_params=params(),
        cost_estimate=cost(1e9, 4e6),
        name="final",
    )(own, other, vectors, *pieces)


def shifted(value, axis, step):
    count = lax.axis_size(axis)
    return lax.ppermute(value, axis, [(i, (i + step) % count) for i in range(count)])


def crossed(value, axis, mask):
    count = lax.axis_size(axis)
    return lax.ppermute(value, axis, [(i, i ^ mask) for i in range(count)])


def crossed_both(value, first, first_mask, second, second_mask):
    count, inner = lax.axis_size(first), lax.axis_size(second)
    pairs = [(i * inner + j, (i ^ first_mask) * inner + (j ^ second_mask)) for i in range(count) for j in range(inner)]
    return lax.ppermute(value, (first, second), pairs)


def faces_of(x, front, back):
    count = lax.axis_size("space")
    early = shifted(front, "tm", 1), shifted(front, "tm", -1)
    near, back = lax.optimization_barrier((crossed(x, "space", 1), back))
    far = lax.ppermute(x, "space", [(i, (i + 1 if i % 2 else i - 1) % count) for i in range(count)])
    late = shifted(back, "tm", 1), shifted(back, "tm", -1)
    return near, far, early, late


def halving(keep, send):
    count = lax.axis_size("space")
    mask = 1
    while True:
        received = crossed(send, "space", mask)
        mask *= 2
        if mask >= count:
            return add(keep, received)
        keep, send = add_split(keep, received)


def doubling(pieces, mask):
    while mask > 1:
        if len(pieces) > 2:
            pieces = [jnp.concatenate(pieces, axis=0)]
        pieces = pieces + [crossed(piece, "space", mask) for piece in pieces]
        mask //= 2
    return pieces


def paired(pieces):
    return [crossed(piece, "space", 1) for piece in pieces]


def across_groups(part, mask):
    return [crossed(part, "groups", 1), crossed_both(part, "groups", 1, "space", mask)]


def over_time(part):
    count = lax.axis_size("tm")
    if count <= 4:
        return [part] + [crossed(part, "tm", mask) for mask in range(1, count)]
    mask = 1
    while mask < count:
        part = part + crossed(part, "tm", mask)
        mask *= 2
    return [part]


def shards(couplings, source, initial, vectors, inverse_eigen):
    directions = couplings.shape[0]
    ny, nx, rows, lanes = source.shape[2:]
    sites = ny * nx
    number = vectors.shape[0]
    blocks = lax.axis_size("space")

    x, early_x, late_x = pack(initial.reshape(sites, rows, lanes))
    faces = faces_of(x, early_x, late_x)
    matrices = couplings.reshape(directions, sites, rows, couplings.shape[-1])
    across = jnp.transpose(vectors, (1, 2, 3, 4, 5, 0)).reshape(sites * vectors.shape[-1], number)
    rest, half_source, local, halo, by_rows, by_columns = prepare(
        x, source.reshape(sites, rows, lanes), matrices, across, ny, nx
    )
    eigen = eigen_of(inverse_eigen, number // blocks, lanes // 2)

    for sweep in range(ITERS):
        last = sweep == ITERS - 1
        if sweep:
            faces = faces_of(x, early_x, late_x)
            rest = local_part(x, half_source, local, ny, nx)
        if last:
            rest, x = lax.optimization_barrier((rest, x))
            other_x = crossed(x, "groups", 1)
        near, far, early, late = faces
        back_rest, own, partial = middle(rest, near, far, front_faces(*early, halo), halo, by_rows)
        if last:
            other_front = crossed(own, "groups", 1)
        back_rest = backward_face(back_rest, late[0], halo)
        residual, back, keep, send = forward_face(own, partial, back_rest, late[1], halo, by_rows)
        if not last:
            pieces = scaled_sum(keep, send, eigen)
            base = first_half(x, [residual], pieces, by_columns)
            x, early_x, late_x = second_half(base, paired(pieces), by_columns, True)
    part, other_x = lax.optimization_barrier((halving(keep, send), other_x))
    other_back = crossed(back, "groups", 1)
    d, other_front = lax.optimization_barrier((scale(eigen, over_time(part)), other_front))
    mask = blocks // 2
    other = across_groups(d, mask)
    own = [d, crossed(d, "space", mask)]
    other, own = doubling(other, mask // 2), doubling(own, mask // 2)
    full_residual = join(residual, other_front, other_back)
    own[-1], full_residual = lax.optimization_barrier((own[-1], full_residual))
    own_x = first_half(x, [residual], own, by_columns)
    other[-1], own_x = lax.optimization_barrier((other[-1], own_x))
    own_x = second_half(own_x, paired(own), by_columns, False)
    other_second = paired(other)
    other_x = first_half(other_x, [other_front, other_back], other, by_columns)
    whole = final(own_x, other_x, other_second, by_columns)
    shape = source.shape
    return whole.reshape(shape), full_residual.reshape(shape)


def solution(mesh):
    in_specs = (
        P(None, "tm", "space", None, None, None, None),
        P("tm", "space", None, None, None, None),
        P("tm", "space", None, None, None, None),
        P(None, "tm", "space", None, None, None),
        P(),
    )
    out_specs = (
        P(("groups", "tm"), "space", None, None, None, None),
        P(("groups", "tm"), "space", None, None, None, None),
    )
    return jax.shard_map(shards, mesh=mesh, in_specs=in_specs, out_specs=out_specs, check_vma=False)
```

```python
import functools

import jax
import jax.numpy as jnp
from jax import lax
from jax.experimental import pallas as pl
from jax.experimental.pallas import tpu as pltpu
from jax.sharding import PartitionSpec as P

ITERS = 2
F32 = jnp.float32
BF16 = jnp.bfloat16
LOCAL = 5


def params(mebibytes=12):
    return pltpu.CompilerParams(vmem_limit_bytes=mebibytes * 1024 * 1024)


def cost(flops, read):
    return pl.CostEstimate(flops=int(flops), bytes_accessed=int(read), transcendentals=0)


def low_lanes(value):
    lanes = lax.broadcasted_iota(jnp.int32, value.shape, value.ndim - 1)
    return lanes < value.shape[-1] // 2


def swap(value):
    return pltpu.roll(value, value.shape[-1] // 2, value.ndim - 1)


def turned(value):
    moved = swap(value)
    return jnp.where(low_lanes(value), -moved, moved)


def high_low(value):
    high = value.astype(BF16)
    low = (value - high.astype(F32)).astype(BF16)
    return high, low


def stack(value, sign):
    high, low = high_low(jnp.concatenate([value, sign * turned(value)], axis=0))
    return jnp.concatenate([high, low], axis=1)


def matmul(left, right):
    return jnp.dot(left, right, preferred_element_type=F32)


def fold(product):
    rows, lanes = product.shape[0] // 2, product.shape[1] // 2
    high = product[:rows, :lanes] + (product[:rows, lanes:] + product[rows:, :lanes])
    return high + product[rows:, lanes:]


def pick_half(value, group):
    middle = value.shape[-1] // 2
    real, imag = value[:, :middle], value[:, middle:]
    low = low_lanes(real)
    first = jnp.where(low, real, swap(imag))
    second = jnp.where(low, swap(real), imag)
    return jnp.where(group == 0, first, second)


def join_halves(own, other, group):
    first = jnp.where(group == 0, own, other)
    second = jnp.where(group == 0, other, own)
    low = low_lanes(own)
    real = jnp.where(low, first, swap(second))
    imag = jnp.where(low, swap(first), second)
    return jnp.concatenate([real, imag], axis=1)


def vmem(count):
    return [pl.BlockSpec(memory_space=pltpu.VMEM)] * count


def in_hbm(value):
    return pltpu.with_memory_space_constraint(value, pltpu.HBM)


def put(site, value, whole, front, back):
    count = front.shape[0]
    whole[site] = value
    if site < count:
        front[site] = value
    else:
        back[site - count] = value


def with_halves(shape):
    part = pltpu.VMEM((shape[0] // 2,) + tuple(shape[1:]), F32)
    return pltpu.VMEM(shape, F32), part, part


def pack_kernel(full, half, front, back):
    group = lax.axis_index("groups")
    for site in range(full.shape[0]):
        put(site, pick_half(full[site], group), half, front, back)


def pack(full):
    sites, rows, lanes = full.shape
    return pl.pallas_call(
        pack_kernel,
        out_shape=with_halves((sites, rows, lanes // 2)),
        in_specs=vmem(1),
        out_specs=tuple(vmem(3)),
        compiler_params=params(),
        cost_estimate=cost(1e6, 1e6),
        name="pack",
    )(full)


def around(site, ny, nx):
    y, x = site // nx, site % nx
    right, left = (x + 1) % nx, (x - 1) % nx
    up, down = (y + 1) % ny, (y - 1) % ny
    return (site, y * nx + right, y * nx + left, up * nx + x, down * nx + x)


def local_sum(site, ny, nx, stacks, local):
    total = None
    for direction, neighbour in enumerate(around(site, ny, nx)):
        term = matmul(local[direction, site], stacks[neighbour])
        total = term if total is None else total + term
    return fold(total)


def local_kernel(ny, nx, x_ref, source, local, rest, stacks):
    for site in range(x_ref.shape[0]):
        stacks[site] = stack(x_ref[site], 1.0)
    for site in range(x_ref.shape[0]):
        rest[site] = source[site] - local_sum(site, ny, nx, stacks, local)


def local_part(x, source, local, ny, nx):
    sites, rows, lanes = x.shape
    return pl.pallas_call(
        functools.partial(local_kernel, ny, nx),
        out_shape=pltpu.VMEM(x.shape, F32),
        in_specs=vmem(3),
        out_specs=vmem(1)[0],
        scratch_shapes=[pltpu.VMEM((sites, 2 * rows, 2 * lanes), BF16)],
        compiler_params=params(),
        cost_estimate=cost(8e9, 8e6),
        name="local_part",
    )(x, source, local)


def block_order(count):
    bits = count.bit_length() - 1
    return [int(format(index, "b").zfill(bits)[::-1], 2) if bits else 0 for index in range(count)]


def ordered_rows(rows, chunk, taken):
    blocks = lax.axis_size("space")
    space = lax.axis_index("space")
    size = rows.shape[0] // blocks
    unit = min(size, taken)
    parts = []
    for start in range(chunk * taken, (chunk + 1) * taken, unit):
        block = space ^ block_order(blocks)[start // size]
        parts.append(rows[pl.ds(pl.multiple_of(block * size + start % size, unit), unit)])
    return parts[0] if len(parts) == 1 else jnp.concatenate(parts, axis=0)


def prepare_kernel(ny, nx, x_ref, source, couplings, across, rest, half_source, local, halo, by_rows, by_columns, stacks, held, held_source, held_across, turned_rows, sems):
    group = lax.axis_index("groups")
    sites, directions, rows = held.shape[:3]
    number = held_across.shape[1]
    taken, step = 128, turned_rows.shape[1]
    arriving = []
    for site in range(sites):
        arriving.append(pltpu.make_async_copy(couplings.at[:, site], held.at[site], sems.at[site]))
    arriving.append(pltpu.make_async_copy(source, held_source, sems.at[sites]))
    for index in range(held_across.shape[0] // step):
        at = pl.ds(index * step, step)
        arriving.append(pltpu.make_async_copy(across.at[at], held_across.at[at], sems.at[sites + 1 + index]))
    for copy in arriving:
        copy.start()
    for site in range(sites):
        stacks[site] = stack(x_ref[site], 1.0)
    for site in range(sites):
        arriving[site].wait()
        for direction in range(directions):
            high, low = high_low(held[site, direction])
            both = jnp.concatenate([high, low], axis=0)
            if direction < LOCAL:
                local[direction, site] = both
            else:
                halo[direction - LOCAL, site] = both
        if site == 0:
            arriving[sites].wait()
        own = pick_half(held_source[site], group)
        half_source[site] = own
        rest[site] = own - local_sum(site, ny, nx, stacks, local)
    for index, copy in enumerate(arriving[sites + 1 :]):
        copy.wait()
        at = slice(index * step, (index + 1) * step)
        turned_rows[...] = held_across[at].T
        for chunk in range(number // taken):
            part = ordered_rows(turned_rows, chunk, taken)
            high, low = high_low(part)
            by_rows[chunk * taken : (chunk + 1) * taken, at] = high
            by_rows[number + chunk * taken : number + (chunk + 1) * taken, at] = low
            back = part.T
            for half in range(step // rows):
                high, low = high_low(back[half * rows : (half + 1) * rows])
                site, which = divmod(index * (step // rows) + half, 2)
                lanes = slice(chunk * taken, (chunk + 1) * taken)
                by_columns[site, which, :rows, lanes] = high
                by_columns[site, which, rows:, lanes] = low


def prepare(x, source, couplings, across, ny, nx):
    sites, rows, lanes = x.shape
    directions, _, _, columns = couplings.shape
    width, number = across.shape
    outer = directions - LOCAL
    step = width // (sites // 2)
    return pl.pallas_call(
        functools.partial(prepare_kernel, ny, nx),
        out_shape=(
            pltpu.VMEM(x.shape, F32),
            pltpu.VMEM(x.shape, F32),
            pltpu.VMEM((LOCAL, sites, 2 * rows, columns), BF16),
            pltpu.VMEM((outer, sites, 2 * rows, columns), BF16),
            pltpu.VMEM((2 * number, width), BF16),
            pltpu.VMEM((sites, 2, 2 * rows, number), BF16),
        ),
        in_specs=vmem(1) + [pl.BlockSpec(memory_space=pl.ANY)] * 3,
        out_specs=tuple(vmem(6)),
        scratch_shapes=[
            pltpu.VMEM((sites, 2 * rows, 2 * lanes), BF16),
            pltpu.VMEM((sites, directions, rows, columns), F32),
            pltpu.VMEM(source.shape, F32),
            pltpu.VMEM(across.shape, F32),
            pltpu.VMEM((number, step), F32),
            pltpu.SemaphoreType.DMA((sites + 1 + width // step,)),
        ],
        compiler_params=params(24),
        cost_estimate=cost(8e9, 25e6),
        name="prepare",
    )(x, in_hbm(source), in_hbm(couplings), in_hbm(across))


def eigen_kernel(inverse, out):
    size, lanes = out.shape[1:]
    number = inverse.shape[1]
    start = lax.axis_index("space") * size
    row = lax.broadcasted_iota(jnp.int32, (size, number), 0) + start
    chosen = lax.broadcasted_iota(jnp.int32, (size, number), 1) == row
    for part in range(2):
        value = jnp.where(chosen, inverse[part : part + 1], 0.0)
        out[part] = jnp.broadcast_to(jnp.sum(value, axis=1, keepdims=True), (size, lanes))


def eigen_of(inverse, size, lanes):
    return pl.pallas_call(
        eigen_kernel,
        out_shape=pltpu.VMEM((2, size, lanes), F32),
        in_specs=vmem(1),
        out_specs=vmem(1)[0],
        compiler_params=params(),
        cost_estimate=cost(1e6, 1e6),
        name="eigen",
    )(inverse)


def apply_faces(*pairs):
    summed = None
    for matrix, face in pairs:
        term = matmul(matrix, stack(face, 1.0))
        summed = term if summed is None else summed + term
    return fold(summed)


def edge_sign(last):
    count = lax.axis_size("tm")
    return jnp.where(lax.axis_index("tm") == (count - 1 if last else 0), -1.0, 1.0).astype(F32)


def front_kernel(backward, forward, matrix, out):
    behind, ahead = edge_sign(False), edge_sign(True)
    for site in range(out.shape[0]):
        out[site] = apply_faces((matrix[2, site], ahead * forward[site]), (matrix[3, site], behind * backward[site]))


def front_faces(backward, forward, matrix):
    return pl.pallas_call(
        front_kernel,
        out_shape=pltpu.VMEM(forward.shape, F32),
        in_specs=vmem(3),
        out_specs=vmem(1)[0],
        compiler_params=params(),
        cost_estimate=cost(1e3, 1e3),
        name="front_faces",
    )(backward, forward, matrix)


def middle_kernel(rest, near, far, front, matrix, vectors, back, residual, partial, stacks):
    parity = lax.rem(lax.axis_index("space"), 2)
    sites, rows, _ = front.shape
    for site in range(rest.shape[0]):
        own = rest[site] - apply_faces((matrix[parity, site], near[site]), (matrix[1 - parity, site], far[site]))
        if site < sites:
            own = own - front[site]
            residual[site] = own
            stacks[site * 2 * rows : (site + 1) * 2 * rows] = stack(own, -1.0)
        else:
            back[site - sites] = own
    partial[...] = fold(matmul(vectors[:, : stacks.shape[0]], stacks[...]))


def middle(rest, near, far, front, matrix, vectors):
    sites, rows, lanes = front.shape
    half = pltpu.VMEM(front.shape, F32)
    return pl.pallas_call(
        middle_kernel,
        out_shape=(half, half, pltpu.VMEM((vectors.shape[0] // 2, lanes), F32)),
        in_specs=vmem(6),
        out_specs=tuple(vmem(3)),
        scratch_shapes=[pltpu.VMEM((sites * 2 * rows, 2 * lanes), BF16)],
        compiler_params=params(),
        cost_estimate=cost(1e3, 1e3),
        name="middle",
    )(rest, near, far, front, matrix, vectors)


def backward_kernel(rest, backward, matrix, out):
    sign = edge_sign(False)
    sites = backward.shape[0]
    for site in range(sites):
        out[site] = rest[site] - apply_faces((matrix[3, sites + site], sign * backward[site]))


def backward_face(rest, backward, matrix):
    return pl.pallas_call(
        backward_kernel,
        out_shape=pltpu.VMEM(backward.shape, F32),
        in_specs=vmem(3),
        out_specs=vmem(1)[0],
        compiler_params=params(),
        cost_estimate=cost(1e3, 1e3),
        name="backward_face",
    )(rest, backward, matrix)


def forward_kernel(front, partial, rest, forward, matrix, vectors, residual, back, keep, send, stacks):
    sign = edge_sign(True)
    sites, rows, _ = forward.shape
    for site in range(sites):
        own = rest[site] - apply_faces((matrix[2, sites + site], sign * forward[site]))
        residual[site] = front[site]
        residual[sites + site] = own
        back[site] = own
        stacks[site * 2 * rows : (site + 1) * 2 * rows] = stack(own, -1.0)
    whole = partial[...] + fold(matmul(vectors[:, stacks.shape[0] :], stacks[...]))
    half = whole.shape[0] // 2
    keep[...] = whole[:half]
    send[...] = whole[half:]


def forward_face(front, partial, rest, forward, matrix, vectors):
    sites, rows, lanes = forward.shape
    part = pltpu.VMEM((vectors.shape[0] // 4, lanes), F32)
    return pl.pallas_call(
        forward_kernel,
        out_shape=(pltpu.VMEM((2 * sites, rows, lanes), F32), pltpu.VMEM(forward.shape, F32), part, part),
        in_specs=vmem(6),
        out_specs=tuple(vmem(4)),
        scratch_shapes=[pltpu.VMEM((sites * 2 * rows, 2 * lanes), BF16)],
        compiler_params=params(),
        cost_estimate=cost(2e9, 8e6),
        name="forward_face",
    )(front, partial, rest, forward, matrix, vectors)


def split_kernel(keep, received, next_keep, next_send):
    half = next_keep.shape[0]
    next_keep[...] = keep[:half] + received[:half]
    next_send[...] = keep[half:] + received[half:]


def add_split(keep, received):
    rows, lanes = keep.shape
    part = pltpu.VMEM((rows // 2, lanes), F32)
    return pl.pallas_call(
        split_kernel,
        out_shape=(part, part),
        in_specs=vmem(2),
        out_specs=tuple(vmem(2)),
        compiler_params=params(),
        name="add_split",
    )(keep, received)


def add_kernel(left, right, out):
    out[...] = left[...] + right[...]


def add(left, right):
    return pl.pallas_call(
        add_kernel,
        out_shape=pltpu.VMEM(left.shape, F32),
        in_specs=vmem(2),
        out_specs=vmem(1)[0],
        compiler_params=params(),
        name="add",
    )(left, right)


def scaled_sum(keep, send, eigen):
    blocks, slices = lax.axis_size("space"), lax.axis_size("tm")
    if blocks != 4 or slices != 4:
        return doubling([scale(eigen, over_time(halving(keep, send)))], blocks // 2)
    keep, send = add_split(keep, crossed(send, "space", 1))
    parts = [crossed_both(send, "space", 2, "tm", 2), crossed(keep, "tm", 2), crossed(send, "space", 2)]
    d = scale(eigen, [keep] + parts)
    moved, across = crossed(d, "space", 2), crossed_both(d, "space", 2, "tm", 1)
    return [add(d, crossed(d, "tm", 1)), add(moved, across)]


def scale_kernel(eigen, *refs):
    parts, out = refs[:-1], refs[-1]
    total = parts[0][...]
    for part in parts[1:]:
        total = total + part[...]
    out[...] = eigen[0] * total + eigen[1] * turned(total)


def scale(eigen, parts):
    return pl.pallas_call(
        scale_kernel,
        out_shape=pltpu.VMEM(parts[0].shape, F32),
        in_specs=vmem(1 + len(parts)),
        out_specs=vmem(1)[0],
        compiler_params=params(),
        name="scale",
    )(eigen, *parts)


def expand(site, vectors, part, stacks):
    depth = stacks.shape[0] // 2
    total = None
    for half in range(2):
        left = vectors[site, half, :, part * depth : (part + 1) * depth]
        term = matmul(left, stacks[half * depth : (half + 1) * depth])
        total = term if total is None else total + term
    return fold(total)


def place_pieces(pieces, stacks):
    values = [piece[...] for piece in pieces]
    stacks[...] = stack(values[0] if len(values) == 1 else jnp.concatenate(values, axis=0), 1.0)


def site_of(parts, site):
    count = parts[0].shape[0]
    return parts[site // count][site % count]


def first_half_kernel(count, x, vectors, *refs):
    residual, pieces, (out, stacks) = refs[:count], refs[count:-2], refs[-2:]
    place_pieces(pieces, stacks)
    for site in range(x.shape[0]):
        out[site] = x[site] + 0.5 * site_of(residual, site) + expand(site, vectors, 0, stacks)


def first_half(x, residual, pieces, vectors):
    return pl.pallas_call(
        functools.partial(first_half_kernel, len(residual)),
        out_shape=pltpu.VMEM(x.shape, F32),
        in_specs=vmem(2 + len(residual) + len(pieces)),
        out_specs=vmem(1)[0],
        scratch_shapes=[pltpu.VMEM((vectors.shape[-1], 2 * x.shape[-1]), BF16)],
        compiler_params=params(),
        cost_estimate=cost(1e9, 4e6),
        name="first_half",
    )(x, vectors, *residual, *pieces)


def second_half_kernel(count, base, vectors, *refs):
    pieces, (outs, stacks) = refs[:count], (refs[count:-1], refs[-1])
    place_pieces(pieces, stacks)
    for site in range(base.shape[0]):
        value = base[site] + expand(site, vectors, 1, stacks)
        if len(outs) == 1:
            outs[0][site] = value
        else:
            put(site, value, *outs)


def second_half(base, pieces, vectors, halves):
    return pl.pallas_call(
        functools.partial(second_half_kernel, len(pieces)),
        out_shape=with_halves(base.shape) if halves else pltpu.VMEM(base.shape, F32),
        in_specs=vmem(2 + len(pieces)),
        out_specs=tuple(vmem(3)) if halves else vmem(1)[0],
        scratch_shapes=[pltpu.VMEM((vectors.shape[-1], 2 * base.shape[-1]), BF16)],
        compiler_params=params(),
        cost_estimate=cost(1e9, 4e6),
        name="second_half",
    )(base, vectors, *pieces)


def join_kernel(own, front, back, full, held, sems):
    group = lax.axis_index("groups")
    copies = []
    for site in range(own.shape[0]):
        held[site] = join_halves(own[site], site_of((front, back), site), group)
        copies.append(pltpu.make_async_copy(held.at[site], full.at[site], sems.at[site]))
        copies[-1].start()
    for copy in copies:
        copy.wait()


def join(own, front, back):
    sites, rows, lanes = own.shape
    shape = (sites, rows, 2 * lanes)
    return pl.pallas_call(
        join_kernel,
        out_shape=jax.ShapeDtypeStruct(shape, F32),
        in_specs=vmem(3),
        out_specs=pl.BlockSpec(memory_space=pl.ANY),
        scratch_shapes=[pltpu.VMEM(shape, F32), pltpu.SemaphoreType.DMA((sites,))],
        compiler_params=params(),
        cost_estimate=cost(1e6, 2e6),
        name="join",
    )(own, front, back)


def final_kernel(own, other, vectors, *refs):
    pieces, (full, stacks, held, sems) = refs[:-4], refs[-4:]
    group = lax.axis_index("groups")
    place_pieces(pieces, stacks)
    copies = []
    for site in range(own.shape[0]):
        held[site] = join_halves(own[site], other[site] + expand(site, vectors, 1, stacks), group)
        copies.append(pltpu.make_async_copy(held.at[site], full.at[site], sems.at[site]))
        copies[-1].start()
    for copy in copies:
        copy.wait()


def final(own, other, pieces, vectors):
    sites, rows, lanes = own.shape
    shape = (sites, rows, 2 * lanes)
    return pl.pallas_call(
        final_kernel,
        out_shape=jax.ShapeDtypeStruct(shape, F32),
        in_specs=vmem(3 + len(pieces)),
        out_specs=pl.BlockSpec(memory_space=pl.ANY),
        scratch_shapes=[
            pltpu.VMEM((vectors.shape[-1], 2 * lanes), BF16),
            pltpu.VMEM(shape, F32),
            pltpu.SemaphoreType.DMA((sites,)),
        ],
        compiler_params=params(),
        cost_estimate=cost(1e9, 4e6),
        name="final",
    )(own, other, vectors, *pieces)


def shifted(value, axis, step):
    count = lax.axis_size(axis)
    return lax.ppermute(value, axis, [(i, (i + step) % count) for i in range(count)])


def crossed(value, axis, mask):
    count = lax.axis_size(axis)
    return lax.ppermute(value, axis, [(i, i ^ mask) for i in range(count)])


def crossed_both(value, first, first_mask, second, second_mask):
    count, inner = lax.axis_size(first), lax.axis_size(second)
    pairs = [(i * inner + j, (i ^ first_mask) * inner + (j ^ second_mask)) for i in range(count) for j in range(inner)]
    return lax.ppermute(value, (first, second), pairs)


def faces_of(x, front, back):
    count = lax.axis_size("space")
    early = shifted(front, "tm", 1), shifted(front, "tm", -1)
    near, back = lax.optimization_barrier((crossed(x, "space", 1), back))
    far = lax.ppermute(x, "space", [(i, (i + 1 if i % 2 else i - 1) % count) for i in range(count)])
    late = shifted(back, "tm", 1), shifted(back, "tm", -1)
    return near, far, early, late


def halving(keep, send):
    count = lax.axis_size("space")
    mask = 1
    while True:
        received = crossed(send, "space", mask)
        mask *= 2
        if mask >= count:
            return add(keep, received)
        keep, send = add_split(keep, received)


def doubling(pieces, mask):
    while mask > 1:
        if len(pieces) > 2:
            pieces = [jnp.concatenate(pieces, axis=0)]
        pieces = pieces + [crossed(piece, "space", mask) for piece in pieces]
        mask //= 2
    return pieces


def paired(pieces):
    return [crossed(piece, "space", 1) for piece in pieces]


def across_groups(part, mask):
    return [crossed(part, "groups", 1), crossed_both(part, "groups", 1, "space", mask)]


def over_time(part):
    count = lax.axis_size("tm")
    if count <= 4:
        return [part] + [crossed(part, "tm", mask) for mask in range(1, count)]
    mask = 1
    while mask < count:
        part = part + crossed(part, "tm", mask)
        mask *= 2
    return [part]


def shards(couplings, source, initial, vectors, inverse_eigen):
    directions = couplings.shape[0]
    ny, nx, rows, lanes = source.shape[2:]
    sites = ny * nx
    number = vectors.shape[0]
    blocks = lax.axis_size("space")

    x, early_x, late_x = pack(initial.reshape(sites, rows, lanes))
    faces = faces_of(x, early_x, late_x)
    matrices = couplings.reshape(directions, sites, rows, couplings.shape[-1])
    across = jnp.transpose(vectors, (1, 2, 3, 4, 5, 0)).reshape(sites * vectors.shape[-1], number)
    rest, half_source, local, halo, by_rows, by_columns = prepare(
        x, source.reshape(sites, rows, lanes), matrices, across, ny, nx
    )
    eigen = eigen_of(inverse_eigen, number // blocks, lanes // 2)

    for sweep in range(ITERS):
        last = sweep == ITERS - 1
        if sweep:
            faces = faces_of(x, early_x, late_x)
            rest = local_part(x, half_source, local, ny, nx)
        if last:
            rest, x = lax.optimization_barrier((rest, x))
            other_x = crossed(x, "groups", 1)
        near, far, early, late = faces
        back_rest, own, partial = middle(rest, near, far, front_faces(*early, halo), halo, by_rows)
        if last:
            other_front = crossed(own, "groups", 1)
        back_rest = backward_face(back_rest, late[0], halo)
        residual, back, keep, send = forward_face(own, partial, back_rest, late[1], halo, by_rows)
        if not last:
            pieces = scaled_sum(keep, send, eigen)
            base = first_half(x, [residual], pieces, by_columns)
            x, early_x, late_x = second_half(base, paired(pieces), by_columns, True)
    part, other_x = lax.optimization_barrier((halving(keep, send), other_x))
    other_back = crossed(back, "groups", 1)
    d, other_front = lax.optimization_barrier((scale(eigen, over_time(part)), other_front))
    mask = blocks // 2
    other = across_groups(d, mask)
    own = [d, crossed(d, "space", mask)]
    other, own = doubling(other, mask // 2), doubling(own, mask // 2)
    full_residual = join(residual, other_front, other_back)
    own[-1], full_residual = lax.optimization_barrier((own[-1], full_residual))
    own_x = first_half(x, [residual], own, by_columns)
    other[-1], own_x = lax.optimization_barrier((other[-1], own_x))
    own_x = second_half(own_x, paired(own), by_columns, False)
    other_second = paired(other)
    other_x = first_half(other_x, [other_front, other_back], other, by_columns)
    whole = final(own_x, other_x, other_second, by_columns)
    shape = source.shape
    return whole.reshape(shape), full_residual.reshape(shape)


def solution(mesh):
    in_specs = (
        P(None, "tm", "space", None, None, None, None),
        P("tm", "space", None, None, None, None),
        P("tm", "space", None, None, None, None),
        P(None, "tm", "space", None, None, None),
        P(),
    )
    out_specs = (
        P(("groups", "tm"), "space", None, None, None, None),
        P(("groups", "tm"), "space", None, None, None, None),
    )
    return jax.shard_map(shards, mesh=mesh, in_specs=in_specs, out_specs=out_specs, check_vma=False)
```

```python
import functools

import jax
import jax.numpy as jnp
from jax import lax
from jax.experimental import pallas as pl
from jax.experimental.pallas import tpu as pltpu
from jax.sharding import PartitionSpec as P

ITERS = 2
F32 = jnp.float32
BF16 = jnp.bfloat16
LOCAL = 5


def params(mebibytes=12):
    return pltpu.CompilerParams(vmem_limit_bytes=mebibytes * 1024 * 1024)


def cost(flops, read):
    return pl.CostEstimate(flops=int(flops), bytes_accessed=int(read), transcendentals=0)


def low_lanes(value):
    lanes = lax.broadcasted_iota(jnp.int32, value.shape, value.ndim - 1)
    return lanes < value.shape[-1] // 2


def swap(value):
    return pltpu.roll(value, value.shape[-1] // 2, value.ndim - 1)


def turned(value):
    moved = swap(value)
    return jnp.where(low_lanes(value), -moved, moved)


def high_low(value):
    high = value.astype(BF16)
    low = (value - high.astype(F32)).astype(BF16)
    return high, low


def stack(value, sign):
    high, low = high_low(jnp.concatenate([value, sign * turned(value)], axis=0))
    return jnp.concatenate([high, low], axis=1)


def matmul(left, right):
    return jnp.dot(left, right, preferred_element_type=F32)


def fold(product):
    rows, lanes = product.shape[0] // 2, product.shape[1] // 2
    high = product[:rows, :lanes] + (product[:rows, lanes:] + product[rows:, :lanes])
    return high + product[rows:, lanes:]


def pick_half(value, group):
    middle = value.shape[-1] // 2
    real, imag = value[:, :middle], value[:, middle:]
    low = low_lanes(real)
    first = jnp.where(low, real, swap(imag))
    second = jnp.where(low, swap(real), imag)
    return jnp.where(group == 0, first, second)


def join_halves(own, other, group):
    first = jnp.where(group == 0, own, other)
    second = jnp.where(group == 0, other, own)
    low = low_lanes(own)
    real = jnp.where(low, first, swap(second))
    imag = jnp.where(low, swap(first), second)
    return jnp.concatenate([real, imag], axis=1)


def vmem(count):
    return [pl.BlockSpec(memory_space=pltpu.VMEM)] * count


def in_hbm(value):
    return pltpu.with_memory_space_constraint(value, pltpu.HBM)


def put(site, value, whole, front, back):
    count = front.shape[0]
    whole[site] = value
    if site < count:
        front[site] = value
    else:
        back[site - count] = value


def with_halves(shape):
    part = pltpu.VMEM((shape[0] // 2,) + tuple(shape[1:]), F32)
    return pltpu.VMEM(shape, F32), part, part


def pack_kernel(full, half, front, back):
    group = lax.axis_index("groups")
    for site in range(full.shape[0]):
        put(site, pick_half(full[site], group), half, front, back)


def pack(full):
    sites, rows, lanes = full.shape
    return pl.pallas_call(
        pack_kernel,
        out_shape=with_halves((sites, rows, lanes // 2)),
        in_specs=vmem(1),
        out_specs=tuple(vmem(3)),
        compiler_params=params(),
        cost_estimate=cost(1e6, 1e6),
        name="pack",
    )(full)


def around(site, ny, nx):
    y, x = site // nx, site % nx
    right, left = (x + 1) % nx, (x - 1) % nx
    up, down = (y + 1) % ny, (y - 1) % ny
    return (site, y * nx + right, y * nx + left, up * nx + x, down * nx + x)


def local_sum(site, ny, nx, stacks, local):
    total = None
    for direction, neighbour in enumerate(around(site, ny, nx)):
        term = matmul(local[direction, site], stacks[neighbour])
        total = term if total is None else total + term
    return fold(total)


def local_kernel(ny, nx, x_ref, source, local, rest, stacks):
    for site in range(x_ref.shape[0]):
        stacks[site] = stack(x_ref[site], 1.0)
    for site in range(x_ref.shape[0]):
        rest[site] = source[site] - local_sum(site, ny, nx, stacks, local)


def local_part(x, source, local, ny, nx):
    sites, rows, lanes = x.shape
    return pl.pallas_call(
        functools.partial(local_kernel, ny, nx),
        out_shape=pltpu.VMEM(x.shape, F32),
        in_specs=vmem(3),
        out_specs=vmem(1)[0],
        scratch_shapes=[pltpu.VMEM((sites, 2 * rows, 2 * lanes), BF16)],
        compiler_params=params(),
        cost_estimate=cost(8e9, 8e6),
        name="local_part",
    )(x, source, local)


def block_order(count):
    bits = count.bit_length() - 1
    return [int(format(index, "b").zfill(bits)[::-1], 2) if bits else 0 for index in range(count)]


def ordered_rows(rows, chunk, taken):
    blocks = lax.axis_size("space")
    space = lax.axis_index("space")
    size = rows.shape[0] // blocks
    unit = min(size, taken)
    parts = []
    for start in range(chunk * taken, (chunk + 1) * taken, unit):
        block = space ^ block_order(blocks)[start // size]
        parts.append(rows[pl.ds(pl.multiple_of(block * size + start % size, unit), unit)])
    return parts[0] if len(parts) == 1 else jnp.concatenate(parts, axis=0)


def prepare_kernel(ny, nx, x_ref, source, couplings, across, rest, half_source, local, halo, by_rows, by_columns, stacks, held, held_source, held_across, turned_rows, sems):
    group = lax.axis_index("groups")
    sites, directions, rows = held.shape[:3]
    number = held_across.shape[1]
    taken, step = 128, turned_rows.shape[1]
    arriving = []
    for site in range(sites):
        arriving.append(pltpu.make_async_copy(couplings.at[:, site], held.at[site], sems.at[site]))
    arriving.append(pltpu.make_async_copy(source, held_source, sems.at[sites]))
    for index in range(held_across.shape[0] // step):
        at = pl.ds(index * step, step)
        arriving.append(pltpu.make_async_copy(across.at[at], held_across.at[at], sems.at[sites + 1 + index]))
    for copy in arriving:
        copy.start()
    for site in range(sites):
        stacks[site] = stack(x_ref[site], 1.0)
    for site in range(sites):
        arriving[site].wait()
        for direction in range(directions):
            high, low = high_low(held[site, direction])
            both = jnp.concatenate([high, low], axis=0)
            if direction < LOCAL:
                local[direction, site] = both
            else:
                halo[direction - LOCAL, site] = both
        if site == 0:
            arriving[sites].wait()
        own = pick_half(held_source[site], group)
        half_source[site] = own
        rest[site] = own - local_sum(site, ny, nx, stacks, local)
    for index, copy in enumerate(arriving[sites + 1 :]):
        copy.wait()
        at = slice(index * step, (index + 1) * step)
        turned_rows[...] = held_across[at].T
        for chunk in range(number // taken):
            part = ordered_rows(turned_rows, chunk, taken)
            high, low = high_low(part)
            by_rows[chunk * taken : (chunk + 1) * taken, at] = high
            by_rows[number + chunk * taken : number + (chunk + 1) * taken, at] = low
            back = part.T
            for half in range(step // rows):
                high, low = high_low(back[half * rows : (half + 1) * rows])
                site, which = divmod(index * (step // rows) + half, 2)
                lanes = slice(chunk * taken, (chunk + 1) * taken)
                by_columns[site, which, :rows, lanes] = high
                by_columns[site, which, rows:, lanes] = low


def prepare(x, source, couplings, across, ny, nx):
    sites, rows, lanes = x.shape
    directions, _, _, columns = couplings.shape
    width, number = across.shape
    outer = directions - LOCAL
    step = width // (sites // 2)
    return pl.pallas_call(
        functools.partial(prepare_kernel, ny, nx),
        out_shape=(
            pltpu.VMEM(x.shape, F32),
            pltpu.VMEM(x.shape, F32),
            pltpu.VMEM((LOCAL, sites, 2 * rows, columns), BF16),
            pltpu.VMEM((outer, sites, 2 * rows, columns), BF16),
            pltpu.VMEM((2 * number, width), BF16),
            pltpu.VMEM((sites, 2, 2 * rows, number), BF16),
        ),
        in_specs=vmem(1) + [pl.BlockSpec(memory_space=pl.ANY)] * 3,
        out_specs=tuple(vmem(6)),
        scratch_shapes=[
            pltpu.VMEM((sites, 2 * rows, 2 * lanes), BF16),
            pltpu.VMEM((sites, directions, rows, columns), F32),
            pltpu.VMEM(source.shape, F32),
            pltpu.VMEM(across.shape, F32),
            pltpu.VMEM((number, step), F32),
            pltpu.SemaphoreType.DMA((sites + 1 + width // step,)),
        ],
        compiler_params=params(24),
        cost_estimate=cost(8e9, 25e6),
        name="prepare",
    )(x, in_hbm(source), in_hbm(couplings), in_hbm(across))


def eigen_kernel(inverse, out):
    size, lanes = out.shape[1:]
    number = inverse.shape[1]
    start = lax.axis_index("space") * size
    row = lax.broadcasted_iota(jnp.int32, (size, number), 0) + start
    chosen = lax.broadcasted_iota(jnp.int32, (size, number), 1) == row
    for part in range(2):
        value = jnp.where(chosen, inverse[part : part + 1], 0.0)
        out[part] = jnp.broadcast_to(jnp.sum(value, axis=1, keepdims=True), (size, lanes))


def eigen_of(inverse, size, lanes):
    return pl.pallas_call(
        eigen_kernel,
        out_shape=pltpu.VMEM((2, size, lanes), F32),
        in_specs=vmem(1),
        out_specs=vmem(1)[0],
        compiler_params=params(),
        cost_estimate=cost(1e6, 1e6),
        name="eigen",
    )(inverse)


def apply_faces(*pairs):
    summed = None
    for matrix, face in pairs:
        term = matmul(matrix, stack(face, 1.0))
        summed = term if summed is None else summed + term
    return fold(summed)


def edge_sign(last):
    count = lax.axis_size("tm")
    return jnp.where(lax.axis_index("tm") == (count - 1 if last else 0), -1.0, 1.0).astype(F32)


def front_kernel(backward, forward, matrix, out):
    behind, ahead = edge_sign(False), edge_sign(True)
    for site in range(out.shape[0]):
        out[site] = apply_faces((matrix[2, site], ahead * forward[site]), (matrix[3, site], behind * backward[site]))


def front_faces(backward, forward, matrix):
    return pl.pallas_call(
        front_kernel,
        out_shape=pltpu.VMEM(forward.shape, F32),
        in_specs=vmem(3),
        out_specs=vmem(1)[0],
        compiler_params=params(),
        cost_estimate=cost(1e3, 1e3),
        name="front_faces",
    )(backward, forward, matrix)


def middle_kernel(rest, near, far, front, matrix, vectors, back, residual, partial, stacks):
    parity = lax.rem(lax.axis_index("space"), 2)
    sites, rows, _ = front.shape
    for site in range(rest.shape[0]):
        own = rest[site] - apply_faces((matrix[parity, site], near[site]), (matrix[1 - parity, site], far[site]))
        if site < sites:
            own = own - front[site]
            residual[site] = own
            stacks[site * 2 * rows : (site + 1) * 2 * rows] = stack(own, -1.0)
        else:
            back[site - sites] = own
    partial[...] = fold(matmul(vectors[:, : stacks.shape[0]], stacks[...]))


def middle(rest, near, far, front, matrix, vectors):
    sites, rows, lanes = front.shape
    half = pltpu.VMEM(front.shape, F32)
    return pl.pallas_call(
        middle_kernel,
        out_shape=(half, half, pltpu.VMEM((vectors.shape[0] // 2, lanes), F32)),
        in_specs=vmem(6),
        out_specs=tuple(vmem(3)),
        scratch_shapes=[pltpu.VMEM((sites * 2 * rows, 2 * lanes), BF16)],
        compiler_params=params(),
        cost_estimate=cost(1e3, 1e3),
        name="middle",
    )(rest, near, far, front, matrix, vectors)


def backward_kernel(rest, backward, matrix, out):
    sign = edge_sign(False)
    sites = backward.shape[0]
    for site in range(sites):
        out[site] = rest[site] - apply_faces((matrix[3, sites + site], sign * backward[site]))


def backward_face(rest, backward, matrix):
    return pl.pallas_call(
        backward_kernel,
        out_shape=pltpu.VMEM(backward.shape, F32),
        in_specs=vmem(3),
        out_specs=vmem(1)[0],
        compiler_params=params(),
        cost_estimate=cost(1e3, 1e3),
        name="backward_face",
    )(rest, backward, matrix)


def forward_kernel(front, partial, rest, forward, matrix, vectors, residual, back, keep, send, stacks):
    sign = edge_sign(True)
    sites, rows, _ = forward.shape
    for site in range(sites):
        own = rest[site] - apply_faces((matrix[2, sites + site], sign * forward[site]))
        residual[site] = front[site]
        residual[sites + site] = own
        back[site] = own
        stacks[site * 2 * rows : (site + 1) * 2 * rows] = stack(own, -1.0)
    whole = partial[...] + fold(matmul(vectors[:, stacks.shape[0] :], stacks[...]))
    half = whole.shape[0] // 2
    keep[...] = whole[:half]
    send[...] = whole[half:]


def forward_face(front, partial, rest, forward, matrix, vectors):
    sites, rows, lanes = forward.shape
    part = pltpu.VMEM((vectors.shape[0] // 4, lanes), F32)
    return pl.pallas_call(
        forward_kernel,
        out_shape=(pltpu.VMEM((2 * sites, rows, lanes), F32), pltpu.VMEM(forward.shape, F32), part, part),
        in_specs=vmem(6),
        out_specs=tuple(vmem(4)),
        scratch_shapes=[pltpu.VMEM((sites * 2 * rows, 2 * lanes), BF16)],
        compiler_params=params(),
        cost_estimate=cost(2e9, 8e6),
        name="forward_face",
    )(front, partial, rest, forward, matrix, vectors)


def split_kernel(keep, received, next_keep, next_send):
    half = next_keep.shape[0]
    next_keep[...] = keep[:half] + received[:half]
    next_send[...] = keep[half:] + received[half:]


def add_split(keep, received):
    rows, lanes = keep.shape
    part = pltpu.VMEM((rows // 2, lanes), F32)
    return pl.pallas_call(
        split_kernel,
        out_shape=(part, part),
        in_specs=vmem(2),
        out_specs=tuple(vmem(2)),
        compiler_params=params(),
        name="add_split",
    )(keep, received)


def add_kernel(left, right, out):
    out[...] = left[...] + right[...]


def add(left, right):
    return pl.pallas_call(
        add_kernel,
        out_shape=pltpu.VMEM(left.shape, F32),
        in_specs=vmem(2),
        out_specs=vmem(1)[0],
        compiler_params=params(),
        name="add",
    )(left, right)


def scaled_sum(keep, send, eigen):
    blocks, slices = lax.axis_size("space"), lax.axis_size("tm")
    if blocks != 4 or slices != 4:
        return doubling([scale(eigen, over_time(halving(keep, send)))], blocks // 2)
    keep, send = add_split(keep, crossed(send, "space", 1))
    parts = [crossed_both(send, "space", 2, "tm", 2), crossed(keep, "tm", 2), crossed(send, "space", 2)]
    d = scale(eigen, [keep] + parts)
    moved, across = crossed(d, "space", 2), crossed_both(d, "space", 2, "tm", 1)
    return [add(d, crossed(d, "tm", 1)), add(moved, across)]


def scale_kernel(eigen, *refs):
    parts, out = refs[:-1], refs[-1]
    total = parts[0][...]
    for part in parts[1:]:
        total = total + part[...]
    out[...] = eigen[0] * total + eigen[1] * turned(total)


def scale(eigen, parts):
    return pl.pallas_call(
        scale_kernel,
        out_shape=pltpu.VMEM(parts[0].shape, F32),
        in_specs=vmem(1 + len(parts)),
        out_specs=vmem(1)[0],
        compiler_params=params(),
        name="scale",
    )(eigen, *parts)


def expand(site, vectors, part, stacks):
    depth = stacks.shape[0] // 2
    total = None
    for half in range(2):
        left = vectors[site, half, :, part * depth : (part + 1) * depth]
        term = matmul(left, stacks[half * depth : (half + 1) * depth])
        total = term if total is None else total + term
    return fold(total)


def place_pieces(pieces, stacks):
    values = [piece[...] for piece in pieces]
    stacks[...] = stack(values[0] if len(values) == 1 else jnp.concatenate(values, axis=0), 1.0)


def site_of(parts, site):
    count = parts[0].shape[0]
    return parts[site // count][site % count]


def first_half_kernel(count, x, vectors, *refs):
    residual, pieces, (out, stacks) = refs[:count], refs[count:-2], refs[-2:]
    place_pieces(pieces, stacks)
    for site in range(x.shape[0]):
        out[site] = x[site] + 0.5 * site_of(residual, site) + expand(site, vectors, 0, stacks)


def first_half(x, residual, pieces, vectors):
    return pl.pallas_call(
        functools.partial(first_half_kernel, len(residual)),
        out_shape=pltpu.VMEM(x.shape, F32),
        in_specs=vmem(2 + len(residual) + len(pieces)),
        out_specs=vmem(1)[0],
        scratch_shapes=[pltpu.VMEM((vectors.shape[-1], 2 * x.shape[-1]), BF16)],
        compiler_params=params(),
        cost_estimate=cost(1e9, 4e6),
        name="first_half",
    )(x, vectors, *residual, *pieces)


def second_half_kernel(count, base, vectors, *refs):
    pieces, (outs, stacks) = refs[:count], (refs[count:-1], refs[-1])
    place_pieces(pieces, stacks)
    for site in range(base.shape[0]):
        value = base[site] + expand(site, vectors, 1, stacks)
        if len(outs) == 1:
            outs[0][site] = value
        else:
            put(site, value, *outs)


def second_half(base, pieces, vectors, halves):
    return pl.pallas_call(
        functools.partial(second_half_kernel, len(pieces)),
        out_shape=with_halves(base.shape) if halves else pltpu.VMEM(base.shape, F32),
        in_specs=vmem(2 + len(pieces)),
        out_specs=tuple(vmem(3)) if halves else vmem(1)[0],
        scratch_shapes=[pltpu.VMEM((vectors.shape[-1], 2 * base.shape[-1]), BF16)],
        compiler_params=params(),
        cost_estimate=cost(1e9, 4e6),
        name="second_half",
    )(base, vectors, *pieces)


def join_kernel(own, front, back, full, held, sems):
    group = lax.axis_index("groups")
    copies = []
    for site in range(own.shape[0]):
        held[site] = join_halves(own[site], site_of((front, back), site), group)
        copies.append(pltpu.make_async_copy(held.at[site], full.at[site], sems.at[site]))
        copies[-1].start()
    for copy in copies:
        copy.wait()


def join(own, front, back):
    sites, rows, lanes = own.shape
    shape = (sites, rows, 2 * lanes)
    return pl.pallas_call(
        join_kernel,
        out_shape=jax.ShapeDtypeStruct(shape, F32),
        in_specs=vmem(3),
        out_specs=pl.BlockSpec(memory_space=pl.ANY),
        scratch_shapes=[pltpu.VMEM(shape, F32), pltpu.SemaphoreType.DMA((sites,))],
        compiler_params=params(),
        cost_estimate=cost(1e6, 2e6),
        name="join",
    )(own, front, back)


def final_kernel(own, other, vectors, *refs):
    pieces, (full, stacks, held, sems) = refs[:-4], refs[-4:]
    group = lax.axis_index("groups")
    place_pieces(pieces, stacks)
    copies = []
    for site in range(own.shape[0]):
        held[site] = join_halves(own[site], other[site] + expand(site, vectors, 1, stacks), group)
        copies.append(pltpu.make_async_copy(held.at[site], full.at[site], sems.at[site]))
        copies[-1].start()
    for copy in copies:
        copy.wait()


def final(own, other, pieces, vectors):
    sites, rows, lanes = own.shape
    shape = (sites, rows, 2 * lanes)
    return pl.pallas_call(
        final_kernel,
        out_shape=jax.ShapeDtypeStruct(shape, F32),
        in_specs=vmem(3 + len(pieces)),
        out_specs=pl.BlockSpec(memory_space=pl.ANY),
        scratch_shapes=[
            pltpu.VMEM((vectors.shape[-1], 2 * lanes), BF16),
            pltpu.VMEM(shape, F32),
            pltpu.SemaphoreType.DMA((sites,)),
        ],
        compiler_params=params(),
        cost_estimate=cost(1e9, 4e6),
        name="final",
    )(own, other, vectors, *pieces)


def shifted(value, axis, step):
    count = lax.axis_size(axis)
    return lax.ppermute(value, axis, [(i, (i + step) % count) for i in range(count)])


def crossed(value, axis, mask):
    count = lax.axis_size(axis)
    return lax.ppermute(value, axis, [(i, i ^ mask) for i in range(count)])


def crossed_both(value, first, first_mask, second, second_mask):
    count, inner = lax.axis_size(first), lax.axis_size(second)
    pairs = [(i * inner + j, (i ^ first_mask) * inner + (j ^ second_mask)) for i in range(count) for j in range(inner)]
    return lax.ppermute(value, (first, second), pairs)


def faces_of(x, front, back):
    count = lax.axis_size("space")
    early = shifted(front, "tm", 1), shifted(front, "tm", -1)
    near, back = lax.optimization_barrier((crossed(x, "space", 1), back))
    far = lax.ppermute(x, "space", [(i, (i + 1 if i % 2 else i - 1) % count) for i in range(count)])
    late = shifted(back, "tm", 1), shifted(back, "tm", -1)
    return near, far, early, late


def halving(keep, send):
    count = lax.axis_size("space")
    mask = 1
    while True:
        received = crossed(send, "space", mask)
        mask *= 2
        if mask >= count:
            return add(keep, received)
        keep, send = add_split(keep, received)


def doubling(pieces, mask):
    while mask > 1:
        if len(pieces) > 2:
            pieces = [jnp.concatenate(pieces, axis=0)]
        pieces = pieces + [crossed(piece, "space", mask) for piece in pieces]
        mask //= 2
    return pieces


def paired(pieces):
    return [crossed(piece, "space", 1) for piece in pieces]


def across_groups(part, mask):
    return [crossed(part, "groups", 1), crossed_both(part, "groups", 1, "space", mask)]


def over_time(part):
    count = lax.axis_size("tm")
    if count <= 4:
        return [part] + [crossed(part, "tm", mask) for mask in reversed(range(1, count))]
    mask = 1
    while mask < count:
        part = part + crossed(part, "tm", mask)
        mask *= 2
    return [part]


def shards(couplings, source, initial, vectors, inverse_eigen):
    directions = couplings.shape[0]
    ny, nx, rows, lanes = source.shape[2:]
    sites = ny * nx
    number = vectors.shape[0]
    blocks = lax.axis_size("space")

    x, early_x, late_x = pack(initial.reshape(sites, rows, lanes))
    faces = faces_of(x, early_x, late_x)
    matrices = couplings.reshape(directions, sites, rows, couplings.shape[-1])
    across = jnp.transpose(vectors, (1, 2, 3, 4, 5, 0)).reshape(sites * vectors.shape[-1], number)
    rest, half_source, local, halo, by_rows, by_columns = prepare(
        x, source.reshape(sites, rows, lanes), matrices, across, ny, nx
    )
    eigen = eigen_of(inverse_eigen, number // blocks, lanes // 2)

    for sweep in range(ITERS):
        last = sweep == ITERS - 1
        if sweep:
            faces = faces_of(x, early_x, late_x)
            rest = local_part(x, half_source, local, ny, nx)
        if last:
            rest, x = lax.optimization_barrier((rest, x))
            other_x = crossed(x, "groups", 1)
        near, far, early, late = faces
        back_rest, own, partial = middle(rest, near, far, front_faces(*early, halo), halo, by_rows)
        if last:
            other_front = crossed(own, "groups", 1)
        back_rest = backward_face(back_rest, late[0], halo)
        residual, back, keep, send = forward_face(own, partial, back_rest, late[1], halo, by_rows)
        if not last:
            pieces = scaled_sum(keep, send, eigen)
            base = first_half(x, [residual], pieces, by_columns)
            x, early_x, late_x = second_half(base, paired(pieces), by_columns, True)
    part, other_x = lax.optimization_barrier((halving(keep, send), other_x))
    other_back = crossed(back, "groups", 1)
    d, other_front = lax.optimization_barrier((scale(eigen, over_time(part)), other_front))
    mask = blocks // 2
    other = across_groups(d, mask)
    own = [d, crossed(d, "space", mask)]
    other, own = doubling(other, mask // 2), doubling(own, mask // 2)
    full_residual = join(residual, other_front, other_back)
    own[-1], full_residual = lax.optimization_barrier((own[-1], full_residual))
    own_x = first_half(x, [residual], own, by_columns)
    other[-1], own_x = lax.optimization_barrier((other[-1], own_x))
    own_x = second_half(own_x, paired(own), by_columns, False)
    other_second = paired(other)
    other_x = first_half(other_x, [other_front, other_back], other, by_columns)
    whole = final(own_x, other_x, other_second, by_columns)
    shape = source.shape
    return whole.reshape(shape), full_residual.reshape(shape)


def solution(mesh):
    in_specs = (
        P(None, "tm", "space", None, None, None, None),
        P("tm", "space", None, None, None, None),
        P("tm", "space", None, None, None, None),
        P(None, "tm", "space", None, None, None),
        P(),
    )
    out_specs = (
        P(("groups", "tm"), "space", None, None, None, None),
        P(("groups", "tm"), "space", None, None, None, None),
    )
    return jax.shard_map(shards, mesh=mesh, in_specs=in_specs, out_specs=out_specs, check_vma=False)
```

```python
import functools

import jax
import jax.numpy as jnp
from jax import lax
from jax.experimental import pallas as pl
from jax.experimental.pallas import tpu as pltpu
from jax.sharding import PartitionSpec as P

ITERS = 2
F32 = jnp.float32
BF16 = jnp.bfloat16
LOCAL = 5


def params(mebibytes=12):
    return pltpu.CompilerParams(vmem_limit_bytes=mebibytes * 1024 * 1024)


def cost(flops, read):
    return pl.CostEstimate(flops=int(flops), bytes_accessed=int(read), transcendentals=0)


def low_lanes(value):
    lanes = lax.broadcasted_iota(jnp.int32, value.shape, value.ndim - 1)
    return lanes < value.shape[-1] // 2


def swap(value):
    return pltpu.roll(value, value.shape[-1] // 2, value.ndim - 1)


def turned(value):
    moved = swap(value)
    return jnp.where(low_lanes(value), -moved, moved)


def high_low(value):
    high = value.astype(BF16)
    low = (value - high.astype(F32)).astype(BF16)
    return high, low


def stack(value, sign):
    high, low = high_low(jnp.concatenate([value, sign * turned(value)], axis=0))
    return jnp.concatenate([high, low], axis=1)


def matmul(left, right):
    return jnp.dot(left, right, preferred_element_type=F32)


def fold(product):
    rows, lanes = product.shape[0] // 2, product.shape[1] // 2
    high = product[:rows, :lanes] + (product[:rows, lanes:] + product[rows:, :lanes])
    return high + product[rows:, lanes:]


def pick_half(value, group):
    middle = value.shape[-1] // 2
    real, imag = value[:, :middle], value[:, middle:]
    low = low_lanes(real)
    first = jnp.where(low, real, swap(imag))
    second = jnp.where(low, swap(real), imag)
    return jnp.where(group == 0, first, second)


def join_halves(own, other, group):
    first = jnp.where(group == 0, own, other)
    second = jnp.where(group == 0, other, own)
    low = low_lanes(own)
    real = jnp.where(low, first, swap(second))
    imag = jnp.where(low, swap(first), second)
    return jnp.concatenate([real, imag], axis=1)


def vmem(count):
    return [pl.BlockSpec(memory_space=pltpu.VMEM)] * count


def in_hbm(value):
    return pltpu.with_memory_space_constraint(value, pltpu.HBM)


def put(site, value, whole, front, back):
    count = front.shape[0]
    whole[site] = value
    if site < count:
        front[site] = value
    else:
        back[site - count] = value


def with_halves(shape):
    part = pltpu.VMEM((shape[0] // 2,) + tuple(shape[1:]), F32)
    return pltpu.VMEM(shape, F32), part, part


def pack_kernel(full, half, front, back):
    group = lax.axis_index("groups")
    for site in range(full.shape[0]):
        put(site, pick_half(full[site], group), half, front, back)


def pack(full):
    sites, rows, lanes = full.shape
    return pl.pallas_call(
        pack_kernel,
        out_shape=with_halves((sites, rows, lanes // 2)),
        in_specs=vmem(1),
        out_specs=tuple(vmem(3)),
        compiler_params=params(),
        cost_estimate=cost(1e6, 1e6),
        name="pack",
    )(full)


def around(site, ny, nx):
    y, x = site // nx, site % nx
    right, left = (x + 1) % nx, (x - 1) % nx
    up, down = (y + 1) % ny, (y - 1) % ny
    return (site, y * nx + right, y * nx + left, up * nx + x, down * nx + x)


def local_sum(site, ny, nx, stacks, local):
    total = None
    for direction, neighbour in enumerate(around(site, ny, nx)):
        term = matmul(local[direction, site], stacks[neighbour])
        total = term if total is None else total + term
    return fold(total)


def local_kernel(ny, nx, x_ref, source, local, rest, stacks):
    for site in range(x_ref.shape[0]):
        stacks[site] = stack(x_ref[site], 1.0)
    for site in range(x_ref.shape[0]):
        rest[site] = source[site] - local_sum(site, ny, nx, stacks, local)


def local_part(x, source, local, ny, nx):
    sites, rows, lanes = x.shape
    return pl.pallas_call(
        functools.partial(local_kernel, ny, nx),
        out_shape=pltpu.VMEM(x.shape, F32),
        in_specs=vmem(3),
        out_specs=vmem(1)[0],
        scratch_shapes=[pltpu.VMEM((sites, 2 * rows, 2 * lanes), BF16)],
        compiler_params=params(),
        cost_estimate=cost(8e9, 8e6),
        name="local_part",
    )(x, source, local)


def block_order(count):
    bits = count.bit_length() - 1
    return [int(format(index, "b").zfill(bits)[::-1], 2) if bits else 0 for index in range(count)]


def ordered_rows(rows, chunk, taken):
    blocks = lax.axis_size("space")
    space = lax.axis_index("space")
    size = rows.shape[0] // blocks
    unit = min(size, taken)
    parts = []
    for start in range(chunk * taken, (chunk + 1) * taken, unit):
        block = space ^ block_order(blocks)[start // size]
        parts.append(rows[pl.ds(pl.multiple_of(block * size + start % size, unit), unit)])
    return parts[0] if len(parts) == 1 else jnp.concatenate(parts, axis=0)


def prepare_kernel(ny, nx, x_ref, source, couplings, across, rest, half_source, local, halo, by_rows, by_columns, stacks, held, held_source, held_across, turned_rows, sems):
    group = lax.axis_index("groups")
    sites, directions, rows = held.shape[:3]
    number = held_across.shape[1]
    taken, step = 128, turned_rows.shape[1]
    arriving = []
    for site in range(sites):
        arriving.append(pltpu.make_async_copy(couplings.at[:, site], held.at[site], sems.at[site]))
    arriving.append(pltpu.make_async_copy(source, held_source, sems.at[sites]))
    for index in range(held_across.shape[0] // step):
        at = pl.ds(index * step, step)
        arriving.append(pltpu.make_async_copy(across.at[at], held_across.at[at], sems.at[sites + 1 + index]))
    for copy in arriving:
        copy.start()
    for site in range(sites):
        stacks[site] = stack(x_ref[site], 1.0)
    for site in range(sites):
        arriving[site].wait()
        for direction in range(directions):
            high, low = high_low(held[site, direction])
            both = jnp.concatenate([high, low], axis=0)
            if direction < LOCAL:
                local[direction, site] = both
            else:
                halo[direction - LOCAL, site] = both
        if site == 0:
            arriving[sites].wait()
        own = pick_half(held_source[site], group)
        half_source[site] = own
        rest[site] = own - local_sum(site, ny, nx, stacks, local)
    for index, copy in enumerate(arriving[sites + 1 :]):
        copy.wait()
        at = slice(index * step, (index + 1) * step)
        turned_rows[...] = held_across[at].T
        for chunk in range(number // taken):
            part = ordered_rows(turned_rows, chunk, taken)
            high, low = high_low(part)
            by_rows[chunk * taken : (chunk + 1) * taken, at] = high
            by_rows[number + chunk * taken : number + (chunk + 1) * taken, at] = low
            back = part.T
            for half in range(step // rows):
                high, low = high_low(back[half * rows : (half + 1) * rows])
                site, which = divmod(index * (step // rows) + half, 2)
                lanes = slice(chunk * taken, (chunk + 1) * taken)
                by_columns[site, which, :rows, lanes] = high
                by_columns[site, which, rows:, lanes] = low


def prepare(x, source, couplings, across, ny, nx):
    sites, rows, lanes = x.shape
    directions, _, _, columns = couplings.shape
    width, number = across.shape
    outer = directions - LOCAL
    step = width // (sites // 2)
    return pl.pallas_call(
        functools.partial(prepare_kernel, ny, nx),
        out_shape=(
            pltpu.VMEM(x.shape, F32),
            pltpu.VMEM(x.shape, F32),
            pltpu.VMEM((LOCAL, sites, 2 * rows, columns), BF16),
            pltpu.VMEM((outer, sites, 2 * rows, columns), BF16),
            pltpu.VMEM((2 * number, width), BF16),
            pltpu.VMEM((sites, 2, 2 * rows, number), BF16),
        ),
        in_specs=vmem(1) + [pl.BlockSpec(memory_space=pl.ANY)] * 3,
        out_specs=tuple(vmem(6)),
        scratch_shapes=[
            pltpu.VMEM((sites, 2 * rows, 2 * lanes), BF16),
            pltpu.VMEM((sites, directions, rows, columns), F32),
            pltpu.VMEM(source.shape, F32),
            pltpu.VMEM(across.shape, F32),
            pltpu.VMEM((number, step), F32),
            pltpu.SemaphoreType.DMA((sites + 1 + width // step,)),
        ],
        compiler_params=params(24),
        cost_estimate=cost(8e9, 25e6),
        name="prepare",
    )(x, in_hbm(source), in_hbm(couplings), in_hbm(across))


def eigen_kernel(inverse, out):
    size, lanes = out.shape[1:]
    number = inverse.shape[1]
    start = lax.axis_index("space") * size
    row = lax.broadcasted_iota(jnp.int32, (size, number), 0) + start
    chosen = lax.broadcasted_iota(jnp.int32, (size, number), 1) == row
    for part in range(2):
        value = jnp.where(chosen, inverse[part : part + 1], 0.0)
        out[part] = jnp.broadcast_to(jnp.sum(value, axis=1, keepdims=True), (size, lanes))


def eigen_of(inverse, size, lanes):
    return pl.pallas_call(
        eigen_kernel,
        out_shape=pltpu.VMEM((2, size, lanes), F32),
        in_specs=vmem(1),
        out_specs=vmem(1)[0],
        compiler_params=params(),
        cost_estimate=cost(1e6, 1e6),
        name="eigen",
    )(inverse)


def apply_faces(*pairs):
    summed = None
    for matrix, face in pairs:
        term = matmul(matrix, stack(face, 1.0))
        summed = term if summed is None else summed + term
    return fold(summed)


def edge_sign(last):
    count = lax.axis_size("tm")
    return jnp.where(lax.axis_index("tm") == (count - 1 if last else 0), -1.0, 1.0).astype(F32)


def front_kernel(backward, forward, matrix, out):
    behind, ahead = edge_sign(False), edge_sign(True)
    for site in range(out.shape[0]):
        out[site] = apply_faces((matrix[2, site], ahead * forward[site]), (matrix[3, site], behind * backward[site]))


def front_faces(backward, forward, matrix):
    return pl.pallas_call(
        front_kernel,
        out_shape=pltpu.VMEM(forward.shape, F32),
        in_specs=vmem(3),
        out_specs=vmem(1)[0],
        compiler_params=params(),
        cost_estimate=cost(1e3, 1e3),
        name="front_faces",
    )(backward, forward, matrix)


def middle_kernel(rest, near, far, front, matrix, vectors, back, residual, partial, stacks):
    parity = lax.rem(lax.axis_index("space"), 2)
    sites, rows, _ = front.shape
    for site in range(rest.shape[0]):
        own = rest[site] - apply_faces((matrix[parity, site], near[site]), (matrix[1 - parity, site], far[site]))
        if site < sites:
            own = own - front[site]
            residual[site] = own
            stacks[site * 2 * rows : (site + 1) * 2 * rows] = stack(own, -1.0)
        else:
            back[site - sites] = own
    partial[...] = fold(matmul(vectors[:, : stacks.shape[0]], stacks[...]))


def middle(rest, near, far, front, matrix, vectors):
    sites, rows, lanes = front.shape
    half = pltpu.VMEM(front.shape, F32)
    return pl.pallas_call(
        middle_kernel,
        out_shape=(half, half, pltpu.VMEM((vectors.shape[0] // 2, lanes), F32)),
        in_specs=vmem(6),
        out_specs=tuple(vmem(3)),
        scratch_shapes=[pltpu.VMEM((sites * 2 * rows, 2 * lanes), BF16)],
        compiler_params=params(),
        cost_estimate=cost(1e3, 1e3),
        name="middle",
    )(rest, near, far, front, matrix, vectors)


def backward_kernel(rest, backward, matrix, out):
    sign = edge_sign(False)
    sites = backward.shape[0]
    for site in range(sites):
        out[site] = rest[site] - apply_faces((matrix[3, sites + site], sign * backward[site]))


def backward_face(rest, backward, matrix):
    return pl.pallas_call(
        backward_kernel,
        out_shape=pltpu.VMEM(backward.shape, F32),
        in_specs=vmem(3),
        out_specs=vmem(1)[0],
        compiler_params=params(),
        cost_estimate=cost(1e3, 1e3),
        name="backward_face",
    )(rest, backward, matrix)


def forward_kernel(front, partial, rest, forward, matrix, vectors, residual, back, keep, send, stacks):
    sign = edge_sign(True)
    sites, rows, _ = forward.shape
    for site in range(sites):
        own = rest[site] - apply_faces((matrix[2, sites + site], sign * forward[site]))
        residual[site] = front[site]
        residual[sites + site] = own
        back[site] = own
        stacks[site * 2 * rows : (site + 1) * 2 * rows] = stack(own, -1.0)
    whole = partial[...] + fold(matmul(vectors[:, stacks.shape[0] :], stacks[...]))
    half = whole.shape[0] // 2
    keep[...] = whole[:half]
    send[...] = whole[half:]


def forward_face(front, partial, rest, forward, matrix, vectors):
    sites, rows, lanes = forward.shape
    part = pltpu.VMEM((vectors.shape[0] // 4, lanes), F32)
    return pl.pallas_call(
        forward_kernel,
        out_shape=(pltpu.VMEM((2 * sites, rows, lanes), F32), pltpu.VMEM(forward.shape, F32), part, part),
        in_specs=vmem(6),
        out_specs=tuple(vmem(4)),
        scratch_shapes=[pltpu.VMEM((sites * 2 * rows, 2 * lanes), BF16)],
        compiler_params=params(),
        cost_estimate=cost(2e9, 8e6),
        name="forward_face",
    )(front, partial, rest, forward, matrix, vectors)


def split_kernel(keep, received, next_keep, next_send):
    half = next_keep.shape[0]
    next_keep[...] = keep[:half] + received[:half]
    next_send[...] = keep[half:] + received[half:]


def add_split(keep, received):
    rows, lanes = keep.shape
    part = pltpu.VMEM((rows // 2, lanes), F32)
    return pl.pallas_call(
        split_kernel,
        out_shape=(part, part),
        in_specs=vmem(2),
        out_specs=tuple(vmem(2)),
        compiler_params=params(),
        name="add_split",
    )(keep, received)


def add_kernel(left, right, out):
    out[...] = left[...] + right[...]


def add(left, right):
    return pl.pallas_call(
        add_kernel,
        out_shape=pltpu.VMEM(left.shape, F32),
        in_specs=vmem(2),
        out_specs=vmem(1)[0],
        compiler_params=params(),
        name="add",
    )(left, right)


def scaled_sum(keep, send, eigen):
    blocks, slices = lax.axis_size("space"), lax.axis_size("tm")
    if blocks != 4 or slices != 4:
        return doubling([scale(eigen, over_time(halving(keep, send)))], blocks // 2)
    keep, send = add_split(keep, crossed(send, "space", 1))
    parts = [crossed_both(send, "space", 2, "tm", 2), crossed(keep, "tm", 2), crossed(send, "space", 2)]
    d = scale(eigen, [keep] + parts)
    moved, across = crossed(d, "space", 2), crossed_both(d, "space", 2, "tm", 1)
    return [add(d, crossed(d, "tm", 1)), add(across, moved)]


def scale_kernel(eigen, *refs):
    parts, out = refs[:-1], refs[-1]
    total = parts[0][...]
    for part in parts[1:]:
        total = total + part[...]
    out[...] = eigen[0] * total + eigen[1] * turned(total)


def scale(eigen, parts):
    return pl.pallas_call(
        scale_kernel,
        out_shape=pltpu.VMEM(parts[0].shape, F32),
        in_specs=vmem(1 + len(parts)),
        out_specs=vmem(1)[0],
        compiler_params=params(),
        name="scale",
    )(eigen, *parts)


def expand(site, vectors, part, stacks):
    depth = stacks.shape[0] // 2
    total = None
    for half in range(2):
        left = vectors[site, half, :, part * depth : (part + 1) * depth]
        term = matmul(left, stacks[half * depth : (half + 1) * depth])
        total = term if total is None else total + term
    return fold(total)


def place_pieces(pieces, stacks):
    values = [piece[...] for piece in pieces]
    stacks[...] = stack(values[0] if len(values) == 1 else jnp.concatenate(values, axis=0), 1.0)


def site_of(parts, site):
    count = parts[0].shape[0]
    return parts[site // count][site % count]


def first_half_kernel(count, x, vectors, *refs):
    residual, pieces, (out, stacks) = refs[:count], refs[count:-2], refs[-2:]
    place_pieces(pieces, stacks)
    for site in range(x.shape[0]):
        out[site] = x[site] + 0.5 * site_of(residual, site) + expand(site, vectors, 0, stacks)


def first_half(x, residual, pieces, vectors):
    return pl.pallas_call(
        functools.partial(first_half_kernel, len(residual)),
        out_shape=pltpu.VMEM(x.shape, F32),
        in_specs=vmem(2 + len(residual) + len(pieces)),
        out_specs=vmem(1)[0],
        scratch_shapes=[pltpu.VMEM((vectors.shape[-1], 2 * x.shape[-1]), BF16)],
        compiler_params=params(),
        cost_estimate=cost(1e9, 4e6),
        name="first_half",
    )(x, vectors, *residual, *pieces)


def second_half_kernel(count, base, vectors, *refs):
    pieces, (outs, stacks) = refs[:count], (refs[count:-1], refs[-1])
    place_pieces(pieces, stacks)
    for site in range(base.shape[0]):
        value = base[site] + expand(site, vectors, 1, stacks)
        if len(outs) == 1:
            outs[0][site] = value
        else:
            put(site, value, *outs)


def second_half(base, pieces, vectors, halves):
    return pl.pallas_call(
        functools.partial(second_half_kernel, len(pieces)),
        out_shape=with_halves(base.shape) if halves else pltpu.VMEM(base.shape, F32),
        in_specs=vmem(2 + len(pieces)),
        out_specs=tuple(vmem(3)) if halves else vmem(1)[0],
        scratch_shapes=[pltpu.VMEM((vectors.shape[-1], 2 * base.shape[-1]), BF16)],
        compiler_params=params(),
        cost_estimate=cost(1e9, 4e6),
        name="second_half",
    )(base, vectors, *pieces)


def join_kernel(own, front, back, full, held, sems):
    group = lax.axis_index("groups")
    copies = []
    for site in range(own.shape[0]):
        held[site] = join_halves(own[site], site_of((front, back), site), group)
        copies.append(pltpu.make_async_copy(held.at[site], full.at[site], sems.at[site]))
        copies[-1].start()
    for copy in copies:
        copy.wait()


def join(own, front, back):
    sites, rows, lanes = own.shape
    shape = (sites, rows, 2 * lanes)
    return pl.pallas_call(
        join_kernel,
        out_shape=jax.ShapeDtypeStruct(shape, F32),
        in_specs=vmem(3),
        out_specs=pl.BlockSpec(memory_space=pl.ANY),
        scratch_shapes=[pltpu.VMEM(shape, F32), pltpu.SemaphoreType.DMA((sites,))],
        compiler_params=params(),
        cost_estimate=cost(1e6, 2e6),
        name="join",
    )(own, front, back)


def final_kernel(own, other, vectors, *refs):
    pieces, (full, stacks, held, sems) = refs[:-4], refs[-4:]
    group = lax.axis_index("groups")
    place_pieces(pieces, stacks)
    copies = []
    for site in range(own.shape[0]):
        held[site] = join_halves(own[site], other[site] + expand(site, vectors, 1, stacks), group)
        copies.append(pltpu.make_async_copy(held.at[site], full.at[site], sems.at[site]))
        copies[-1].start()
    for copy in copies:
        copy.wait()


def final(own, other, pieces, vectors):
    sites, rows, lanes = own.shape
    shape = (sites, rows, 2 * lanes)
    return pl.pallas_call(
        final_kernel,
        out_shape=jax.ShapeDtypeStruct(shape, F32),
        in_specs=vmem(3 + len(pieces)),
        out_specs=pl.BlockSpec(memory_space=pl.ANY),
        scratch_shapes=[
            pltpu.VMEM((vectors.shape[-1], 2 * lanes), BF16),
            pltpu.VMEM(shape, F32),
            pltpu.SemaphoreType.DMA((sites,)),
        ],
        compiler_params=params(),
        cost_estimate=cost(1e9, 4e6),
        name="final",
    )(own, other, vectors, *pieces)


def shifted(value, axis, step):
    count = lax.axis_size(axis)
    return lax.ppermute(value, axis, [(i, (i + step) % count) for i in range(count)])


def crossed(value, axis, mask):
    count = lax.axis_size(axis)
    return lax.ppermute(value, axis, [(i, i ^ mask) for i in range(count)])


def crossed_both(value, first, first_mask, second, second_mask):
    count, inner = lax.axis_size(first), lax.axis_size(second)
    pairs = [(i * inner + j, (i ^ first_mask) * inner + (j ^ second_mask)) for i in range(count) for j in range(inner)]
    return lax.ppermute(value, (first, second), pairs)


def faces_of(x, front, back):
    count = lax.axis_size("space")
    early = shifted(front, "tm", 1), shifted(front, "tm", -1)
    near, back = lax.optimization_barrier((crossed(x, "space", 1), back))
    far = lax.ppermute(x, "space", [(i, (i + 1 if i % 2 else i - 1) % count) for i in range(count)])
    late = shifted(back, "tm", 1), shifted(back, "tm", -1)
    return near, far, early, late


def halving(keep, send):
    count = lax.axis_size("space")
    mask = 1
    while True:
        received = crossed(send, "space", mask)
        mask *= 2
        if mask >= count:
            return add(keep, received)
        keep, send = add_split(keep, received)


def doubling(pieces, mask):
    while mask > 1:
        if len(pieces) > 2:
            pieces = [jnp.concatenate(pieces, axis=0)]
        pieces = pieces + [crossed(piece, "space", mask) for piece in pieces]
        mask //= 2
    return pieces


def paired(pieces):
    return [crossed(piece, "space", 1) for piece in pieces]


def across_groups(part, mask):
    return [crossed(part, "groups", 1), crossed_both(part, "groups", 1, "space", mask)]


def over_time(part):
    count = lax.axis_size("tm")
    if count <= 4:
        return [part] + [crossed(part, "tm", mask) for mask in reversed(range(1, count))]
    mask = 1
    while mask < count:
        part = part + crossed(part, "tm", mask)
        mask *= 2
    return [part]


def shards(couplings, source, initial, vectors, inverse_eigen):
    directions = couplings.shape[0]
    ny, nx, rows, lanes = source.shape[2:]
    sites = ny * nx
    number = vectors.shape[0]
    blocks = lax.axis_size("space")

    x, early_x, late_x = pack(initial.reshape(sites, rows, lanes))
    faces = faces_of(x, early_x, late_x)
    matrices = couplings.reshape(directions, sites, rows, couplings.shape[-1])
    across = jnp.transpose(vectors, (1, 2, 3, 4, 5, 0)).reshape(sites * vectors.shape[-1], number)
    rest, half_source, local, halo, by_rows, by_columns = prepare(
        x, source.reshape(sites, rows, lanes), matrices, across, ny, nx
    )
    eigen = eigen_of(inverse_eigen, number // blocks, lanes // 2)

    for sweep in range(ITERS):
        last = sweep == ITERS - 1
        if sweep:
            faces = faces_of(x, early_x, late_x)
            rest = local_part(x, half_source, local, ny, nx)
        if last:
            rest, x = lax.optimization_barrier((rest, x))
            other_x = crossed(x, "groups", 1)
        near, far, early, late = faces
        back_rest, own, partial = middle(rest, near, far, front_faces(*early, halo), halo, by_rows)
        if last:
            other_front = crossed(own, "groups", 1)
        back_rest = backward_face(back_rest, late[0], halo)
        residual, back, keep, send = forward_face(own, partial, back_rest, late[1], halo, by_rows)
        if not last:
            pieces = scaled_sum(keep, send, eigen)
            base = first_half(x, [residual], pieces, by_columns)
            x, early_x, late_x = second_half(base, paired(pieces), by_columns, True)
    part, other_x = lax.optimization_barrier((halving(keep, send), other_x))
    other_back = crossed(back, "groups", 1)
    d, other_front = lax.optimization_barrier((scale(eigen, over_time(part)), other_front))
    mask = blocks // 2
    other = across_groups(d, mask)
    own = [d, crossed(d, "space", mask)]
    other, own = doubling(other, mask // 2), doubling(own, mask // 2)
    full_residual = join(residual, other_front, other_back)
    own[-1], full_residual = lax.optimization_barrier((own[-1], full_residual))
    own_x = first_half(x, [residual], own, by_columns)
    other[-1], own_x = lax.optimization_barrier((other[-1], own_x))
    own_x = second_half(own_x, paired(own), by_columns, False)
    other_second = paired(other)
    other_x = first_half(other_x, [other_front, other_back], other, by_columns)
    whole = final(own_x, other_x, other_second, by_columns)
    shape = source.shape
    return whole.reshape(shape), full_residual.reshape(shape)


def solution(mesh):
    in_specs = (
        P(None, "tm", "space", None, None, None, None),
        P("tm", "space", None, None, None, None),
        P("tm", "space", None, None, None, None),
        P(None, "tm", "space", None, None, None),
        P(),
    )
    out_specs = (
        P(("groups", "tm"), "space", None, None, None, None),
        P(("groups", "tm"), "space", None, None, None, None),
    )
    return jax.shard_map(shards, mesh=mesh, in_specs=in_specs, out_specs=out_specs, check_vma=False)
```
